128 devices in a mesh: ctx: 64 (over z, y, x_hi, core), heads: 2 (over x_lo).
Axes of the slice: x: 4 (x_hi: 2, x_lo: 2; x = x_hi * 2 + x_lo), y: 4, z: 4, core: 2. Of those that a mesh axis runs over, the one named last changes fastest.
Arguments:
- hidden: bfloat16 [8192, 768], P('ctx'), may hold values from -6 to 6
- w_qkv: bfloat16 [3, 768, 768], P(None, 'ctx', 'heads'), may hold values from -0.21875 to 0.21875
- w_out: bfloat16 [768, 768], P('heads', 'ctx'), may hold values from -0.875 to 0.875
- b_qv: bfloat16 [2, 768], P(None, 'heads'), may hold values from -3 to 3
- w_up: bfloat16 [768, 3072], P('ctx', 'heads'), may hold values from -0.21875 to 0.21875
- w_down: bfloat16 [3072, 768], P('heads', 'ctx'), may hold values from -0.109375 to 0.109375
- b_up: bfloat16 [3072], P('heads'), may hold values from -3 to 3
- norm_gains: bfloat16 [2, 768], replicated, may hold values from 0.5 to 1.5
- norm_shifts: bfloat16 [4, 768], replicated, may hold values from -3 to 3
- segments: int32 [8192], P('ctx'), may hold values from 0 to 2, as said below
- lengths: int32 [3], replicated, may hold values from 1 to 8192, as said below
- cotangent: bfloat16 [8192, 768], P('ctx'), may hold values from -6 to 6
Outputs:
- layer_out: bfloat16 [8192, 768], P('ctx')
- hidden_grad: float32 [8192, 768], P('ctx')
- qkv_grad: float32 [3, 768, 768], P(None, 'ctx', 'heads')
- out_grad: float32 [768, 768], P('heads', 'ctx')
- qv_grad: float32 [2, 768], P(None, ('heads', 'ctx'))
- up_grad: float32 [768, 3072], P('ctx', 'heads')
- down_grad: float32 [3072, 768], P('heads', 'ctx')
- upbias_grad: float32 [3072], P(('heads', 'ctx'))
- gains_grad: float32 [2, 768], P(None, ('ctx', 'heads'))
- shifts_grad: float32 [4, 768], P(None, ('ctx', 'heads'))
The draws below stay inside these ranges and needn't reach their ends.
Inputs may be any that keep to these rules, and one draw needn't show every extreme that they name: segments never fall along the tokens and take every value from 0 to 2; each run of equal values is one sequence; one sequence, drawn from the seed, holds all but fewer than 128 of the tokens. lengths[j] counts the leading tokens of sequence j that are not padding, at most the sequence's tokens; fewer than 32 tokens of a sequence are padding.
All inputs are finite; a program needn't handle non-finite values.
Results may differ from the reference program's by a relative error of at most 0.03.
Values may be sent and summed in bfloat16 or wider, within the bound.
No kernel may reach another device: no remote copies, remote signals or barrier semaphores. Data moves between devices by JAX's collectives and lax.ppermute only.
A program may use at most 192 MiB of HBM per device.

```python
import jax
import jax.numpy as jnp
from jax import lax

D = 768
HEADS = 12
HEAD_DIM = 64
FF = 3072
TOK_DEV = 128
SEQS = 3
TOKENS = 8192


def run_sizes(key):
    long_at = jax.random.randint(jax.random.fold_in(key, 11), (), 0, SEQS)
    short_most = (TOK_DEV - 1) // (SEQS - 1)
    shorts = jax.random.randint(jax.random.fold_in(key, 12), (SEQS,), 1, short_most + 1)
    seq_index = jnp.arange(SEQS, dtype=jnp.int32)
    shorts = jnp.where(seq_index == long_at, 0, shorts).astype(jnp.int32)
    return jnp.where(seq_index == long_at, TOKENS - jnp.sum(shorts), shorts).astype(jnp.int32)


def draw_segments(key, part):
    run_size = run_sizes(key)
    run_ends = jnp.cumsum(run_size)
    places = jnp.arange(TOKENS, dtype=jnp.int32)
    return jnp.sum((places[:, None] >= run_ends[None, :SEQS - 1]).astype(jnp.int32), axis=1).astype(jnp.int32)


def draw_lengths(key, part):
    run_size = run_sizes(key)
    key = jax.random.fold_in(key, 2)
    pad_most = jnp.minimum(TOK_DEV // 4, run_size).astype(jnp.int32)
    padding = jax.random.randint(key, (SEQS,), 0, pad_most)
    return (run_size - padding).astype(jnp.int32)


def block_levels(rng, shape, cuts, smallest, largest):
    loudness, own = 1.0, jax.random.fold_in(rng, 6)
    for axis_at, shards_of in cuts:
        steps = jnp.exp(jax.random.uniform(jax.random.fold_in(own, axis_at), (shards_of,), jnp.float32, smallest / len(cuts), largest / len(cuts)))
        loudness = loudness * jnp.repeat(steps, shape[axis_at] // shards_of).reshape([-1 if axis == axis_at else 1 for axis in range(len(shape))])
    return loudness


def normal_values(key, shape, width, reach, pieces=(), kind=jnp.bfloat16):
    loudness = block_levels(key, shape, pieces, -0.22, 0.18) if pieces else 1.0
    values = jax.random.normal(key, shape, jnp.float32) * width * loudness
    return jnp.minimum(jnp.maximum(values, -reach), reach).astype(kind)


def setup_inputs(seed: int = 0) -> dict:
    splits = jax.random.split(jax.random.key(seed), 13)
    hidden = normal_values(splits[0], (TOKENS, D), 1.0, 6.0, ((0, 64),))
    w_qkv = normal_values(splits[1], (3, D, D), D ** -0.5, 0.21875, ((1, 64), (2, 2)))
    w_out = normal_values(splits[2], (D, D), (D // 16) ** -0.5, 0.875, ((0, 2), (1, 64)))
    b_qv = normal_values(splits[3], (2, D), 0.5, 3.0, ((1, 2),))
    w_up = normal_values(splits[4], (D, FF), D ** -0.5, 0.21875, ((0, 64), (1, 2)))
    w_down = normal_values(splits[5], (FF, D), FF ** -0.5, 0.109375, ((0, 2), (1, 64)))
    b_up = normal_values(splits[6], (FF,), 0.5, 3.0, ((0, 2),))
    norm_gains = jnp.clip(1.0 + 0.1 * jax.random.normal(splits[7], (2, D), jnp.float32), 0.5, 1.5).astype(jnp.bfloat16)
    norm_shifts = normal_values(splits[8], (4, D), 0.5, 3.0)
    segments = draw_segments(jax.random.fold_in(splits[12], 71), 0)
    lengths = draw_lengths(jax.random.fold_in(splits[12], 71), 0)
    cotangent = normal_values(splits[11], (TOKENS, D), 1.0, 6.0, ((0, 64),))
    return dict(hidden=hidden, w_qkv=w_qkv, w_out=w_out, b_qv=b_qv, w_up=w_up, w_down=w_down, b_up=b_up, norm_gains=norm_gains, norm_shifts=norm_shifts, segments=segments, lengths=lengths, cotangent=cotangent)


EPS = 1e-06
NEG = -1e+30

@jax.custom_vjp
def low(v):
    return lax.optimization_barrier(v.astype(jnp.bfloat16)).astype(jnp.float32)

@jax.custom_vjp
def low_back(v):
    return v

def low_keep(v):
    return (low(v), None)

def low_pass(kept, grad):
    return (grad,)

def back_keep(v):
    return (v, None)

def back_low(kept, grad):
    return (low(grad),)
low.defvjp(low_keep, low_pass)
low_back.defvjp(back_keep, back_low)

def both_ways(value_in):
    return low_back(low(value_in))

def matmul(left, right):
    return jnp.dot(left, right, precision=lax.Precision.HIGHEST)

def layer_norm(residual, gain_row, shift_row):
    centred = residual - lax.optimization_barrier(jnp.mean(residual, axis=-1, keepdims=True))
    inverse = lax.rsqrt(lax.optimization_barrier(jnp.mean(centred * centred, axis=-1, keepdims=True)) + EPS)
    return centred * inverse * gain_row + shift_row

def key_tags(segments, lengths):
    member = (segments[:, None] == jnp.arange(lengths.shape[0], dtype=jnp.int32)[None, :]).astype(jnp.int32)
    totals = lax.optimization_barrier(jnp.sum(member, axis=0))
    starts = jnp.cumsum(totals) - totals
    places = jnp.arange(segments.shape[0], dtype=jnp.int32)
    run_start = lax.optimization_barrier(jnp.sum(member * starts[None, :], axis=1))
    run_valid = lax.optimization_barrier(jnp.sum(member * lengths[None, :], axis=1))
    return jnp.where(places - run_start < run_valid, segments, -1).astype(jnp.int32)

def reference(hidden, w_qkv, w_out, b_qv, w_up, w_down, b_up, norm_gains, norm_shifts, segments, lengths, cotangent):
    key_tag = key_tags(segments, lengths)
    places = jnp.arange(TOKENS, dtype=jnp.int32)
    blocks = TOKENS // TOK_DEV

    def attention(queries, keys_all, values_all):
        query_heads = queries.reshape(blocks, TOK_DEV, HEADS, HEAD_DIM)
        key_heads = keys_all.reshape(TOKENS, HEADS, HEAD_DIM)
        value_heads = values_all.reshape(TOKENS, HEADS, HEAD_DIM)

        def one_block(block_args):
            query_block, query_tag, query_place = block_args
            scores = jnp.einsum('qhd,khd->hqk', query_block, key_heads, precision=lax.Precision.HIGHEST) * HEAD_DIM ** (-0.5)
            scores = low_back(scores)
            allowed = (query_tag[:, None] == key_tag[None, :]) | (query_place[:, None] == places[None, :])
            scores = jnp.where(allowed[None], scores, NEG)
            prob_rows = jax.nn.softmax(scores, axis=-1)
            return jnp.einsum('hqk,khd->qhd', low(prob_rows), value_heads, precision=lax.Precision.HIGHEST)
        outputs = lax.map(jax.checkpoint(one_block), (query_heads, segments.reshape(blocks, TOK_DEV), places.reshape(blocks, TOK_DEV)))
        return outputs.reshape(TOKENS, D)

    def forward(inputs, qkv_all, out_all, qv_bias, up_all, down_all, up_bias, gain_rows, shift_rows):
        queries = both_ways(matmul(inputs, qkv_all[0]) + qv_bias[0])
        keys_all = both_ways(matmul(inputs, qkv_all[1]))
        values_all = both_ways(matmul(inputs, qkv_all[2]) + qv_bias[1])
        attended = both_ways(attention(queries, keys_all, values_all))
        attn_mixed = low_back(matmul(attended, out_all))
        first_out = layer_norm(inputs + attn_mixed + shift_rows[0], gain_rows[0], shift_rows[1])
        up_proj = low_back(matmul(low(first_out), up_all) + up_bias)
        activated = low(jax.nn.gelu(up_proj, approximate=False))
        second = low_back(matmul(activated, down_all))
        return layer_norm(first_out + second + shift_rows[2], gain_rows[1], shift_rows[3])
    floats = tuple((item.astype(jnp.float32) for item in (hidden, w_qkv, w_out, b_qv, w_up, w_down, b_up, norm_gains, norm_shifts)))
    output, pull_back = jax.vjp(forward, *floats)
    gradients = pull_back(cotangent.astype(jnp.float32))
    return (output.astype(jnp.bfloat16), gradients[0], gradients[1], gradients[2], gradients[3], gradients[4], gradients[5], gradients[6], gradients[7], gradients[8])
```

```python
import jax
import jax.numpy as jnp
from jax import lax
from jax.experimental import pallas as pl
from jax.experimental.pallas import tpu as pltpu
from jax.sharding import Mesh, PartitionSpec as P

HEAD_DIM = 64
HEADS_DEV = 3
EPS = 1e-06
NEG = -1e30
CTX = ("z", "y", "xh", "core")
CHIPS = ("z", "y", "xh")
F32 = jnp.float32
BF16 = jnp.bfloat16
NT = (((1,), (1,)), ((), ()))
VMEM_LIMIT = 50 * 1024 * 1024
OFFSETS = (0, -1, 1, 2)


def shifted(x, axis, step):
    n = lax.axis_size(axis)
    return lax.ppermute(x, axis, [(i, (i + step) % n) for i in range(n)])


def ring_blocks(x, axis):
    return [x, shifted(x, axis, 1), shifted(x, axis, -1), shifted(x, axis, 2)]


def gather_relative(x, first, second):
    both = jnp.concatenate([x, shifted(x, "xh", 1)], axis=0)
    eight = jnp.concatenate(ring_blocks(both, first), axis=0)
    return ring_blocks(eight, second)


def relative_order(first, second, core_at):
    place = {a: lax.axis_index(a) for a in CHIPS}
    core = lax.axis_index("core")
    order = []
    for second_step in OFFSETS:
        for first_step in OFFSETS:
            for xh_step in (0, 1):
                at = dict(place)
                at[first] = (at[first] + first_step) % 4
                at[second] = (at[second] + second_step) % 4
                at["xh"] = (at["xh"] + xh_step) % 2
                order.append(((at["z"] * 4 + at["y"]) * 2 + at["xh"]) * 2 + (core + core_at) % 2)
    return jnp.stack(order)


def ring_ordered(x, axis):
    own, before, after, far = ring_blocks(x, axis)
    stacked = jnp.stack([own, after, far, before] * 2)
    return lax.dynamic_slice_in_dim(stacked, 4 - lax.axis_index(axis), 4, 0)


def pair_ordered(own, other, axis):
    first = lax.axis_index(axis) == 0
    return jnp.stack([jnp.where(first, own, other), jnp.where(first, other, own)])


def gather_ordered(x, z_first):
    pair = pair_ordered(x, shifted(x, "xh", 1), "xh")
    if z_first:
        whole = jnp.swapaxes(ring_ordered(ring_ordered(pair, "z"), "y"), 0, 1)
    else:
        whole = ring_ordered(ring_ordered(pair, "y"), "z")
    return whole.reshape(-1, *x.shape[1:])


def ring_summed(x, axis, dim):
    at = lax.axis_index(axis)

    def block(step):
        return lax.dynamic_index_in_dim(x, (at + step) % 4, dim, keepdims=False)

    total = block(0).astype(F32)
    for step in (1, -1, 2):
        total = total + shifted(block(step).astype(BF16), axis, step).astype(F32)
    return total


def scatter_summed(x, z_first):
    parts = x.reshape(4, 4, 2, -1, x.shape[-1])
    if z_first:
        parts = ring_summed(ring_summed(parts, "z", 0), "y", 0)
    else:
        parts = ring_summed(ring_summed(parts, "y", 1), "z", 0)
    at = lax.axis_index("xh")
    own = lax.dynamic_index_in_dim(parts, at, 0, keepdims=False)
    theirs = lax.dynamic_index_in_dim(parts, 1 - at, 0, keepdims=False)
    return own + shifted(theirs.astype(BF16), "xh", 1).astype(F32)


def team_sum(partial):
    rows = partial.shape[0] // 2
    near = partial[:rows] + shifted(partial[rows:].astype(BF16), "core", 1).astype(F32)
    low = lax.optimization_barrier(near.astype(BF16))
    return low.astype(F32) + shifted(low, "heads", 1).astype(F32)


def chip_tokens(x):
    return jnp.concatenate([x, shifted(x, "core", 1)], axis=0)


def layer_norm(residual, gain_row, shift_row):
    centred = residual - jnp.mean(residual, axis=-1, keepdims=True)
    inverse = lax.rsqrt(jnp.mean(centred * centred, axis=-1, keepdims=True) + EPS)
    normed = centred * inverse
    return (normed * gain_row + shift_row, normed, inverse)


def norm_back(incoming, normed, inverse, gain_row):
    scaled = incoming * gain_row
    projected = (
        scaled
        - jnp.mean(scaled, axis=-1, keepdims=True)
        - normed * jnp.mean(scaled * normed, axis=-1, keepdims=True)
    )
    return (inverse * projected, jnp.sum(incoming * normed, axis=0), jnp.sum(incoming, axis=0))


def exact_gelu(pre_act):
    return jax.nn.gelu(pre_act, approximate=False)


def pieces_of(column):
    high = column.astype(BF16).astype(F32)
    middle = (column - high).astype(BF16).astype(F32)
    return high, middle, column - high - middle


def head_columns(h):
    return slice(h * HEAD_DIM, (h + 1) * HEAD_DIM)


def head_block(h):
    return slice(h * 128, (h + 1) * 128)


def diagonal_scores(q_ref, kv_ref, h):
    product = q_ref[h].astype(F32) * kv_ref[:, head_block(h)].astype(F32)
    return jnp.sum(product, axis=1, keepdims=True)


def copies_in(sources, buffer, sems):
    copies = [
        pltpu.make_async_copy(source, buffer.at[j], sems.at[j]) for j, source in enumerate(sources)
    ]
    for copy in copies:
        copy.start()


def attend_kernel(q_ref, own_ref, tags_ref, seg_ref, tag_ref, *rest):
    blocks, (out_ref, stat_ref, sent_ref, buffer, top, total, acc, sems) = rest[:8], rest[8:]
    copies_in(blocks, buffer, sems)
    rows = q_ref.shape[1]
    padded = tag_ref[...] < 0
    seg_wide = jnp.broadcast_to(seg_ref[...], (rows, 128))
    for h in range(HEADS_DEV):
        diagonal = diagonal_scores(q_ref, own_ref, h)
        top[h] = jnp.broadcast_to(jnp.where(padded, diagonal, NEG), (rows, 128))
        lane = lax.broadcasted_iota(jnp.int32, (rows, 128), 1)
        total[h] = jnp.where((lane == 0) & padded, 1.0, 0.0)
        acc[h] = jnp.where(padded, own_ref[:, head_block(h)].astype(F32), 0.0)

    def step(j, carry):
        pltpu.make_async_copy(blocks[0], buffer.at[j], sems.at[j]).wait()
        tags = tags_ref[pl.ds(j, 1), :]
        keys = tags.shape[1]
        allowed = jnp.tile(seg_wide, (1, keys // 128)) == tags
        for h in range(HEADS_DEV):
            kv = buffer[j, :, head_block(h)]
            scores = lax.dot_general(q_ref[h], kv, NT, preferred_element_type=F32)
            scores = jnp.where(allowed, scores, NEG)
            before = top[h]
            now = jnp.maximum(before, jnp.max(scores, axis=1, keepdims=True))
            weights = jnp.exp(scores - jnp.tile(now, (1, keys // 128)))
            fade = jnp.exp(before - now)
            sums = weights[:, :128]
            for k in range(1, keys // 128):
                sums = sums + weights[:, k * 128 : (k + 1) * 128]
            total[h] = total[h] * fade + sums
            acc[h] = acc[h] * fade + jnp.dot(weights.astype(BF16), kv, preferred_element_type=F32)
            top[h] = now
        return carry

    lax.fori_loop(0, 8, step, 0)
    lane = lax.broadcasted_iota(jnp.int32, (rows, HEAD_DIM), 1)
    seg = seg_ref[...]
    extra = jnp.where(lane == 12, 1.0, 0.0)
    for s in range(3):
        extra = extra + jnp.where((lane == 9 + s) & (seg != s), 1.0, 0.0)
    outs, queries = [], []
    for h in range(HEADS_DEV):
        sums = jnp.sum(total[h], axis=1, keepdims=True)
        outs.append((acc[h] / sums)[:, HEAD_DIM:])
        stat = top[h] + jnp.log(sums)
        stat_ref[h] = stat
        for i, piece in enumerate(pieces_of(stat[:, :1])):
            extra = extra + jnp.where(lane == 3 * h + i, piece, 0.0)
        queries.append(q_ref[h][:, :HEAD_DIM].astype(F32))
    out_ref[...] = jnp.concatenate(outs, axis=1)
    sent_ref[...] = jnp.concatenate(queries + [extra], axis=1).astype(BF16)


def vmem_specs(n):
    return [pl.BlockSpec(memory_space=pltpu.VMEM)] * n


def any_specs(n):
    return [pl.BlockSpec(memory_space=pl.ANY)] * n


def attend(q_heads, kv_own, tags, seg, tag, blocks):
    rows = kv_own.shape[0]
    keys, width = blocks[0].shape
    pairs = rows * keys * 8 * HEADS_DEV
    return pl.pallas_call(
        attend_kernel,
        out_shape=(
            jax.ShapeDtypeStruct((rows, HEADS_DEV * HEAD_DIM), F32),
            jax.ShapeDtypeStruct((HEADS_DEV, rows, 128), F32),
            jax.ShapeDtypeStruct((rows, 256), BF16),
        ),
        in_specs=vmem_specs(5) + any_specs(8),
        out_specs=tuple(vmem_specs(3)),
        scratch_shapes=[
            pltpu.VMEM((8, keys, width), BF16),
            pltpu.VMEM((HEADS_DEV, rows, 128), F32),
            pltpu.VMEM((HEADS_DEV, rows, 128), F32),
            pltpu.VMEM((HEADS_DEV, rows, 128), F32),
            pltpu.SemaphoreType.DMA((8,)),
        ],
        compiler_params=pltpu.CompilerParams(vmem_limit_bytes=VMEM_LIMIT),
        cost_estimate=pl.CostEstimate(
            flops=pairs * 512, bytes_accessed=8 * keys * width * 2, transcendentals=pairs
        ),
        name="attend",
    )(q_heads, kv_own, tags, seg, tag, *blocks)


def query_back_kernel(q_ref, g_ref, own_ref, tags_ref, seg_ref, tag_ref, stat_ref, delta_ref, *rest):
    blocks, (dq_ref, dkv_ref, buffer, acc, sems) = rest[:8], rest[8:]
    copies_in(blocks, buffer, sems)
    rows = q_ref.shape[1]
    seg_wide = jnp.broadcast_to(seg_ref[...], (rows, 128))
    padded = tag_ref[...] < 0
    for h in range(HEADS_DEV):
        own = own_ref[:, head_block(h)].astype(F32)
        prob = jnp.exp(diagonal_scores(q_ref, own_ref, h) - stat_ref[h][:, :1])
        prob = jnp.where(padded, prob, 0.0)
        grad = diagonal_scores(g_ref, own_ref, h) - delta_ref[h][:, :1]
        score = (prob * grad).astype(BF16).astype(F32)
        acc[h] = score * own
        dkv_ref[:, head_block(h)] = score * q_ref[h].astype(F32) + prob.astype(BF16).astype(
            F32
        ) * g_ref[h].astype(F32)

    def step(j, carry):
        pltpu.make_async_copy(blocks[0], buffer.at[j], sems.at[j]).wait()
        tags = tags_ref[pl.ds(j, 1), :]
        keys = tags.shape[1]
        allowed = jnp.tile(seg_wide, (1, keys // 128)) == tags
        for h in range(HEADS_DEV):
            kv = buffer[j, :, head_block(h)]
            scores = lax.dot_general(q_ref[h], kv, NT, preferred_element_type=F32)
            scores = jnp.where(allowed, scores, NEG)
            probs = jnp.exp(scores - jnp.tile(stat_ref[h], (1, keys // 128)))
            grads = lax.dot_general(g_ref[h], kv, NT, preferred_element_type=F32)
            back = probs * (grads - jnp.tile(delta_ref[h], (1, keys // 128)))
            acc[h] = acc[h] + jnp.dot(back.astype(BF16), kv, preferred_element_type=F32)
        return carry

    lax.fori_loop(0, 8, step, 0)
    dq_ref[...] = (
        jnp.concatenate([acc[h][:, :HEAD_DIM] for h in range(HEADS_DEV)], axis=1)
        * HEAD_DIM ** (-0.5)
    ).astype(BF16)


def query_back(q_heads, g_heads, kv_own, tags, seg, tag, stat, delta, blocks):
    rows = kv_own.shape[0]
    keys, width = blocks[0].shape
    pairs = rows * keys * 8 * HEADS_DEV
    return pl.pallas_call(
        query_back_kernel,
        out_shape=(
            jax.ShapeDtypeStruct((rows, HEADS_DEV * HEAD_DIM), BF16),
            jax.ShapeDtypeStruct((rows, width), F32),
        ),
        in_specs=vmem_specs(8) + any_specs(8),
        out_specs=tuple(vmem_specs(2)),
        scratch_shapes=[
            pltpu.VMEM((8, keys, width), BF16),
            pltpu.VMEM((HEADS_DEV, rows, 128), F32),
            pltpu.SemaphoreType.DMA((8,)),
        ],
        compiler_params=pltpu.CompilerParams(vmem_limit_bytes=VMEM_LIMIT),
        cost_estimate=pl.CostEstimate(
            flops=pairs * 768, bytes_accessed=8 * keys * width * 2, transcendentals=pairs
        ),
        name="query_back",
    )(q_heads, g_heads, kv_own, tags, seg, tag, stat, delta, *blocks)


def grad_rows_kernel(mixed_ref, out_ref, attended_ref, sent_ref, g_ref, delta_ref):
    rows = mixed_ref.shape[0]
    grad = jnp.dot(mixed_ref[...], out_ref[...], preferred_element_type=F32).astype(BF16)
    grad = grad.astype(F32)
    product = grad * attended_ref[...]
    lane = lax.broadcasted_iota(jnp.int32, (rows, HEAD_DIM), 1)
    extra = jnp.zeros((rows, HEAD_DIM), F32)
    zeros = jnp.zeros((rows, HEAD_DIM), BF16)
    for h in range(HEADS_DEV):
        delta = jnp.sum(product[:, head_columns(h)], axis=1, keepdims=True)
        delta_ref[h] = jnp.broadcast_to(delta, (rows, 128))
        for i, piece in enumerate(pieces_of(delta)):
            extra = extra + jnp.where(lane == 3 * h + i, piece, 0.0)
        g_ref[h] = jnp.concatenate([zeros, grad[:, head_columns(h)].astype(BF16)], axis=1)
    sent_ref[...] = jnp.concatenate([grad, extra], axis=1).astype(BF16)


def grad_rows(mixed, w_out, attended):
    rows = mixed.shape[0]
    return pl.pallas_call(
        grad_rows_kernel,
        out_shape=(
            jax.ShapeDtypeStruct((rows, 256), BF16),
            jax.ShapeDtypeStruct((HEADS_DEV, rows, 128), BF16),
            jax.ShapeDtypeStruct((HEADS_DEV, rows, 128), F32),
        ),
        in_specs=vmem_specs(3),
        out_specs=tuple(vmem_specs(3)),
        compiler_params=pltpu.CompilerParams(vmem_limit_bytes=VMEM_LIMIT),
        name="grad_rows",
    )(mixed, w_out, attended)


def key_back_kernel(k_ref, v_ref, diag_ref, *rest):
    q_blocks, g_blocks = rest[:8], rest[8:16]
    dkv_ref, q_buffer, g_buffer, k_acc, v_acc, q_sems, g_sems = rest[16:]
    copies_in(q_blocks, q_buffer, q_sems)
    copies_in(g_blocks, g_buffer, g_sems)
    k_acc[...] = jnp.zeros_like(k_acc)
    v_acc[...] = jnp.zeros_like(v_acc)

    def step(j, carry):
        pltpu.make_async_copy(q_blocks[0], q_buffer.at[j], q_sems.at[j]).wait()
        pltpu.make_async_copy(g_blocks[0], g_buffer.at[j], g_sems.at[j]).wait()
        queries, grads = q_buffer[j], g_buffer[j]
        for h in range(HEADS_DEV):
            scores = lax.dot_general(k_ref[h], queries, NT, preferred_element_type=F32)
            probs = jnp.exp(scores)
            v_acc[h] = v_acc[h] + jnp.dot(probs.astype(BF16), grads, preferred_element_type=F32)
            back = probs * lax.dot_general(v_ref[h], grads, NT, preferred_element_type=F32)
            k_acc[h] = k_acc[h] + jnp.dot(back.astype(BF16), queries, preferred_element_type=F32)
        return carry

    lax.fori_loop(0, 8, step, 0)
    parts = []
    for h in range(HEADS_DEV):
        parts += [k_acc[h][:, head_columns(h)], v_acc[h][:, head_columns(h)]]
    dkv_ref[...] = (jnp.concatenate(parts, axis=1) + diag_ref[...]).astype(BF16)


def key_back(k_heads, v_heads, diagonal, q_blocks, g_blocks):
    rows = k_heads.shape[1]
    queries, width = q_blocks[0].shape
    pairs = rows * queries * 8 * HEADS_DEV
    return pl.pallas_call(
        key_back_kernel,
        out_shape=jax.ShapeDtypeStruct(diagonal.shape, BF16),
        in_specs=vmem_specs(3) + any_specs(16),
        out_specs=vmem_specs(1)[0],
        scratch_shapes=[
            pltpu.VMEM((8, queries, width), BF16),
            pltpu.VMEM((8, queries, width), BF16),
            pltpu.VMEM((HEADS_DEV, rows, width), F32),
            pltpu.VMEM((HEADS_DEV, rows, width), F32),
            pltpu.SemaphoreType.DMA((8,)),
            pltpu.SemaphoreType.DMA((8,)),
        ],
        compiler_params=pltpu.CompilerParams(vmem_limit_bytes=VMEM_LIMIT),
        cost_estimate=pl.CostEstimate(
            flops=pairs * 2048, bytes_accessed=16 * queries * width * 2, transcendentals=pairs
        ),
        name="key_back",
    )(k_heads, v_heads, diagonal, *q_blocks, *g_blocks)


def dot(a, b):
    return jnp.dot(a, b, preferred_element_type=F32)


def dot_nt(a, b):
    return lax.dot_general(a, b, NT, preferred_element_type=F32)


def dot_tn(a, b):
    return lax.dot_general(a, b, (((0,), (0,)), ((), ())), preferred_element_type=F32)


def core_half(x, axis, at):
    size = x.shape[axis] // 2
    return lax.dynamic_slice_in_dim(x, at * size, size, axis)


def interleaved(k, v):
    shape = (*k.shape[:-1], -1, HEAD_DIM)
    return jnp.stack([k.reshape(shape), v.reshape(shape)], axis=-2).reshape(*k.shape[:-1], -1)


def per_device(
    hidden,
    w_qkv,
    w_out,
    b_qv,
    w_up,
    w_down,
    b_up,
    norm_gains,
    norm_shifts,
    segments,
    lengths,
    cotangent,
):
    core = lax.axis_index("core")
    heads_at = lax.axis_index("heads")
    own_ctx = ((lax.axis_index("z") * 4 + lax.axis_index("y")) * 2 + lax.axis_index("xh")) * 2 + core
    tok = hidden.shape[0]
    rows = w_up.shape[0]
    feat = HEADS_DEV * HEAD_DIM
    hidden_units = w_up.shape[1] // 2

    hid = chip_tokens(hidden)
    out_turned, down_turned = w_out.T, w_down.T
    segs_low = segments.astype(BF16).reshape(2, tok // 2)

    def packed(at):
        q, k, v = (core_half(w_qkv[i], 1, at) for i in range(3))
        tail = jnp.pad(segs_low, ((0, rows - 2), (0, 0)))
        urgent = jnp.concatenate([interleaved(k, v), q, tail], axis=1)
        later = [core_half(w, 1, at) for w in (out_turned, w_up, down_turned)]
        return urgent, jnp.concatenate(later, axis=1)

    mine, theirs = packed(core), packed(1 - core)
    urgent = pair_ordered(mine[0], shifted(theirs[0], "core", 1), "core").reshape(2 * rows, -1)
    later = pair_ordered(mine[1], shifted(theirs[1], "core", 1), "core").reshape(2 * rows, -1)
    kv_cols = 2 * feat
    w_kv = gather_ordered(urgent[:, :kv_cols], True)
    w_q_tail = gather_ordered(urgent[:, kv_cols:], False)
    w_q = w_q_tail[:, :feat]
    seg_all = w_q_tail[:, feat:].reshape(-1, 2, rows, tok // 2)[:, :, :2].reshape(-1, tok)
    seg_all = seg_all.astype(jnp.int32)
    rest = lax.all_gather(later, CHIPS, axis=0, tiled=True)
    w_out_t = rest[:, :feat]
    w_up_all = rest[:, feat : feat + hidden_units]
    w_down_t = rest[:, feat + hidden_units :]

    bias = b_qv.astype(F32)
    q_bias, v_bias = core_half(bias[0], 0, core), core_half(bias[1], 0, core)
    kv_own = (dot(hid, w_kv) + interleaved(jnp.zeros_like(v_bias), v_bias)).astype(BF16)
    queries = ((dot(hid, w_q) + q_bias).astype(BF16) * HEAD_DIM ** (-0.5)).astype(BF16)
    q_heads = jnp.pad(
        jnp.swapaxes(queries.reshape(2 * tok, HEADS_DEV, HEAD_DIM), 0, 1),
        ((0, 0), (0, 0), (0, HEAD_DIM)),
    )

    starts = [jnp.sum((seg_all < s).astype(jnp.int32)) for s in range(3)]
    places = jnp.arange(seg_all.size, dtype=jnp.int32).reshape(seg_all.shape)
    run_end = jnp.zeros_like(seg_all)
    for s in range(3):
        run_end = jnp.where(seg_all == s, starts[s] + lengths[s], run_end)
    tag_all = jnp.where(places < run_end, seg_all, -1).astype(F32)
    order = jnp.concatenate([relative_order("z", "y", 0), relative_order("y", "z", 1)])
    tags = jnp.take(tag_all, order, axis=0).reshape(8, -1)
    both = jnp.stack([own_ctx, own_ctx + 1 - 2 * core])
    tag_own = jnp.take(tag_all, both, axis=0).reshape(-1, 1)
    seg_own = jnp.take(seg_all, both, axis=0).astype(F32).reshape(-1, 1)

    kv_blocks = gather_relative(kv_own[:tok], "z", "y") + gather_relative(kv_own[tok:], "y", "z")
    attended, stat, q_sent = attend(q_heads, kv_own, tags, seg_own, tag_own, kv_blocks)
    attended_low = attended.astype(BF16)
    q_blocks = gather_relative(q_sent[:tok], "z", "y") + gather_relative(q_sent[tok:], "y", "z")

    gain_rows = norm_gains.astype(F32)
    shifts = norm_shifts.astype(F32)
    attn_mixed = team_sum(dot_nt(attended_low, w_out_t))
    first_out, normed_one, inverse_one = layer_norm(
        hidden.astype(F32) + attn_mixed + shifts[0], gain_rows[0], shifts[1]
    )
    first_low = chip_tokens(first_out.astype(BF16))
    up_bias = core_half(b_up, 0, core).astype(F32)
    up_proj = dot(first_low, w_up_all) + up_bias
    activated = exact_gelu(up_proj).astype(BF16)
    second = team_sum(dot_nt(activated, w_down_t))
    output, normed_two, inverse_two = layer_norm(
        first_out + second + shifts[2], gain_rows[1], shifts[3]
    )
    resid_two, gain_two_grad, beta_two_grad = norm_back(
        cotangent.astype(F32), normed_two, inverse_two, gain_rows[1]
    )
    branch_low = chip_tokens(resid_two.astype(BF16))
    act_grad = dot(branch_low, w_down_t)
    up_low = jax.vjp(exact_gelu, up_proj)[1](act_grad)[0].astype(BF16)
    first_grad = resid_two + team_sum(dot_nt(up_low, w_up_all))
    down_grad = dot_tn(branch_low, activated)
    up_grad = dot_tn(first_low, up_low)
    upbias_grad = jnp.sum(up_low.astype(F32), axis=0)
    resid_one, gain_one_grad, beta_one_grad = norm_back(
        first_grad, normed_one, inverse_one, gain_rows[0]
    )
    mixed_low = chip_tokens(resid_one.astype(BF16))
    g_sent, g_heads, delta = grad_rows(mixed_low, w_out_t, attended)
    g_blocks = gather_relative(g_sent[:tok], "z", "y") + gather_relative(g_sent[tok:], "y", "z")
    out_grad = dot_tn(mixed_low, attended_low)
    up_done = scatter_summed(up_grad, True)
    down_done = scatter_summed(jnp.concatenate([down_grad, out_grad], axis=1), False)

    dq, diagonal = query_back(
        q_heads, g_heads, kv_own, tags, seg_own, tag_own, stat, delta, kv_blocks
    )
    lane = jnp.arange(256, dtype=jnp.int32)
    split = kv_own.reshape(2 * tok, HEADS_DEV, 2, HEAD_DIM)
    extras = jnp.where(
        (lane >= feat + 9) & (lane < feat + 12),
        jnp.where(tag_own == (lane - feat - 9).astype(F32), NEG, 0.0),
        jnp.where((lane == feat + 12) & (tag_own < 0), NEG, 0.0),
    )

    def spread_heads(x, more):
        wide = jnp.pad(x.reshape(2 * tok, feat).astype(F32), ((0, 0), (0, 256 - feat)))
        made = []
        for h in range(HEADS_DEV):
            in_head = (lane >= h * HEAD_DIM) & (lane < (h + 1) * HEAD_DIM)
            in_stat = (lane >= feat + 3 * h) & (lane < feat + 3 * h + 3)
            made.append(jnp.where(in_head, wide, jnp.where(in_stat, -1.0, more)))
        return jnp.stack(made).astype(BF16)

    k_heads = spread_heads(split[:, :, 0], extras)
    v_heads = spread_heads(split[:, :, 1], jnp.zeros_like(extras))
    dkv = key_back(k_heads, v_heads, diagonal, q_blocks, g_blocks)

    hidden_grad = resid_one + team_sum(dot_nt(dkv, w_kv) + dot_nt(dq, w_q))

    def placed_half(x):
        zero = jnp.zeros_like(x)
        return jnp.concatenate(
            [jnp.where(core == 0, x, zero), jnp.where(core == 0, zero, x)], axis=-1
        )

    dv = dkv.reshape(2 * tok, HEADS_DEV, 2, HEAD_DIM)[:, :, 1].reshape(2 * tok, feat)
    qv_grad = jnp.stack([jnp.sum(dq.astype(F32), axis=0), jnp.sum(dv.astype(F32), axis=0)])
    vectors = jnp.stack(
        [
            gain_one_grad,
            gain_two_grad,
            jnp.sum(resid_one, axis=0),
            beta_one_grad,
            jnp.sum(resid_two, axis=0),
            beta_two_grad,
        ]
    )

    def by_owner(x):
        return jnp.swapaxes(x.reshape(x.shape[0], 64, -1), 0, 1).reshape(64, -1)

    small = jnp.concatenate(
        [by_owner(placed_half(qv_grad)), by_owner(placed_half(upbias_grad)[None]), by_owner(vectors)],
        axis=1,
    )
    small = jnp.pad(small, ((0, 0), (0, 128 - small.shape[1]))).reshape(64, 2, 64)
    small = jnp.pad(small, ((0, 0), (0, rows - 2), (0, 0))).reshape(64 * rows, 64)
    kv_done = scatter_summed(dot_tn(hid, dkv), True)
    q_done = scatter_summed(jnp.concatenate([dot_tn(hid, dq), small], axis=1), False)

    done = jnp.concatenate([kv_done, q_done, up_done, down_done], axis=1)
    own_rows = core_half(done, 0, core)
    got = shifted(core_half(done, 0, 1 - core), "core", 1)
    low = jnp.where(core == 0, own_rows, got)
    high = jnp.where(core == 0, got, own_rows)

    def columns(start, size):
        return jnp.concatenate(
            [low[:, start : start + size], high[:, start : start + size]], axis=1
        )

    kv_pairs = columns(0, kv_cols).reshape(rows, 2 * HEADS_DEV, 2, HEAD_DIM)
    k_cols = kv_pairs[:, :, 0].reshape(rows, -1)
    v_cols = kv_pairs[:, :, 1].reshape(rows, -1)
    q_cols = columns(kv_cols, feat)
    at = kv_cols + feat
    tail = (own_rows + got)[:2, at : at + 64].reshape(-1)
    at += 64
    up_cols = columns(at, hidden_units)
    down_cols = columns(at + hidden_units, hidden_units)
    out_cols = columns(at + 2 * hidden_units, feat)
    qv_out = tail[:12].reshape(2, 6)
    bias_out = tail[12:36]
    vec_out = tail[36:108].reshape(6, 2, 6)
    vec_out = lax.dynamic_index_in_dim(vec_out, heads_at, 1, keepdims=False)
    return (
        output.astype(BF16),
        hidden_grad,
        jnp.stack([q_cols, k_cols, v_cols]),
        out_cols.T,
        qv_out,
        up_cols,
        down_cols.T,
        bias_out,
        vec_out[:2],
        vec_out[2:],
    )


def solution(mesh):
    fine = Mesh(mesh.devices.reshape(4, 4, 2, 2, 2), ("z", "y", "xh", "core", "heads"))
    return jax.shard_map(
        per_device,
        mesh=fine,
        in_specs=(
            P(CTX, None),
            P(None, CTX, "heads"),
            P("heads", CTX),
            P(None, "heads"),
            P(CTX, "heads"),
            P("heads", CTX),
            P("heads"),
            P(),
            P(),
            P(CTX),
            P(),
            P(CTX, None),
        ),
        out_specs=(
            P(CTX, None),
            P(CTX, None),
            P(None, CTX, "heads"),
            P("heads", CTX),
            P(None, ("heads", *CTX)),
            P(CTX, "heads"),
            P("heads", CTX),
            P(("heads", *CTX)),
            P(None, (*CTX, "heads")),
            P(None, (*CTX, "heads")),
        ),
        check_vma=False,
    )
```

```python
import jax
import jax.numpy as jnp
from jax import lax
from jax.experimental import pallas as pl
from jax.experimental.pallas import tpu as pltpu
from jax.sharding import Mesh, PartitionSpec as P

HEAD_DIM = 64
HEADS_DEV = 3
EPS = 1e-06
NEG = -1e30
CTX = ("z", "y", "xh", "core")
CHIPS = ("z", "y", "xh")
F32 = jnp.float32
BF16 = jnp.bfloat16
NT = (((1,), (1,)), ((), ()))
VMEM_LIMIT = 50 * 1024 * 1024
OFFSETS = (0, -1, 1, 2)


def shifted(x, axis, step):
    n = lax.axis_size(axis)
    return lax.ppermute(x, axis, [(i, (i + step) % n) for i in range(n)])


def ring_blocks(x, axis):
    return [x, shifted(x, axis, 1), shifted(x, axis, -1), shifted(x, axis, 2)]


def ring_halves(x, axis):
    half = x.shape[0] // 2
    before, after = shifted(x, axis, 1), shifted(x, axis, -1)
    return [x, before, after, shifted(before[:half], axis, 1), shifted(after[half:], axis, -1)]


def gather_first(x):
    half = x.shape[0] // 2
    streams = []
    for part, axis in ((x[:half], "z"), (x[half:], "y")):
        both = jnp.concatenate([part, shifted(part, "xh", 1)], axis=0)
        streams.append(jnp.concatenate(ring_halves(both, axis), axis=0))
    return tuple(streams)


def gather_second(streams):
    blocks = ring_halves(streams[0], "y") + ring_halves(streams[1], "z")
    return [b.reshape(-1, streams[0].shape[0] // 2, b.shape[1]) for b in blocks]


def relative_order(first, second, core_at):
    place = {a: lax.axis_index(a) for a in CHIPS}
    core = lax.axis_index("core")
    order = []
    for second_step in OFFSETS:
        for first_step in OFFSETS:
            for xh_step in (0, 1):
                at = dict(place)
                at[first] = (at[first] + first_step) % 4
                at[second] = (at[second] + second_step) % 4
                at["xh"] = (at["xh"] + xh_step) % 2
                order.append(((at["z"] * 4 + at["y"]) * 2 + at["xh"]) * 2 + (core + core_at) % 2)
    return jnp.stack(order)


def ring_ordered(x, axis):
    own, before, after, far = ring_blocks(x, axis)
    stacked = jnp.stack([own, after, far, before] * 2)
    return lax.dynamic_slice_in_dim(stacked, 4 - lax.axis_index(axis), 4, 0)


def pair_ordered(own, other, axis):
    first = lax.axis_index(axis) == 0
    return jnp.stack([jnp.where(first, own, other), jnp.where(first, other, own)])


def gather_ordered(x):
    pair = pair_ordered(x, shifted(x, "xh", 1), "xh")
    return ring_ordered(ring_ordered(pair, "y"), "z").reshape(-1, *x.shape[1:])


def ring_summed(x, axis, dim):
    at = lax.axis_index(axis)
    half = x.shape[-1] // 256 * 128

    def block(step):
        return lax.dynamic_index_in_dim(x, (at + step) % 4, dim, keepdims=False).astype(F32)

    far = block(2).astype(BF16)
    from_before = shifted(far[..., :half], axis, 1).astype(F32)
    from_after = shifted(far[..., half:], axis, -1).astype(F32)
    ahead, behind = block(1), block(-1)
    ahead = jnp.concatenate([ahead[..., :half] + from_before, ahead[..., half:]], axis=-1)
    behind = jnp.concatenate([behind[..., :half], behind[..., half:] + from_after], axis=-1)
    got = shifted(ahead.astype(BF16), axis, 1).astype(F32)
    return block(0) + got + shifted(behind.astype(BF16), axis, -1).astype(F32)


def scatter_first(z_stream, y_stream):
    def parts(x):
        return x.reshape(4, 4, 2, -1, x.shape[-1])

    return ring_summed(parts(z_stream), "z", 0), ring_summed(parts(y_stream), "y", 1)


def scatter_second(z_stream, y_stream):
    both = [ring_summed(z_stream, "y", 0), ring_summed(y_stream, "z", 0)]
    widths = [b.shape[-1] for b in both]
    parts = jnp.concatenate(both, axis=-1)
    at = lax.axis_index("xh")
    own = lax.dynamic_index_in_dim(parts, at, 0, keepdims=False)
    theirs = lax.dynamic_index_in_dim(parts, 1 - at, 0, keepdims=False)
    done = own + shifted(theirs.astype(BF16), "xh", 1).astype(F32)
    return done[:, : widths[0]], done[:, widths[0] :]


def team_sum(partial):
    rows = partial.shape[0] // 2
    near = partial[:rows] + shifted(partial[rows:].astype(BF16), "core", 1).astype(F32)
    low = lax.optimization_barrier(near.astype(BF16))
    return low.astype(F32) + shifted(low, "heads", 1).astype(F32)


def chip_tokens(x):
    return jnp.concatenate([x, shifted(x, "core", 1)], axis=0)


def layer_norm(residual, gain_row, shift_row):
    centred = residual - jnp.mean(residual, axis=-1, keepdims=True)
    inverse = lax.rsqrt(jnp.mean(centred * centred, axis=-1, keepdims=True) + EPS)
    normed = centred * inverse
    return (normed * gain_row + shift_row, normed, inverse)


def norm_back(incoming, normed, inverse, gain_row):
    scaled = incoming * gain_row
    projected = (
        scaled
        - jnp.mean(scaled, axis=-1, keepdims=True)
        - normed * jnp.mean(scaled * normed, axis=-1, keepdims=True)
    )
    return (inverse * projected, jnp.sum(incoming * normed, axis=0), jnp.sum(incoming, axis=0))


def exact_gelu(pre_act):
    return jax.nn.gelu(pre_act, approximate=False)


def pieces_of(column):
    high = column.astype(BF16).astype(F32)
    middle = (column - high).astype(BF16).astype(F32)
    return high, middle, column - high - middle


def head_columns(h):
    return slice(h * HEAD_DIM, (h + 1) * HEAD_DIM)


def head_block(h):
    return slice(h * 128, (h + 1) * 128)


def diagonal_scores(q_ref, kv_ref, h):
    product = q_ref[h].astype(F32) * kv_ref[:, head_block(h)].astype(F32)
    return jnp.sum(product, axis=1, keepdims=True)


def copies_in(sources, buffer, sems):
    at = 0
    for source in sources:
        size = source.shape[0]
        pltpu.make_async_copy(source, buffer.at[pl.ds(at, size)], sems.at[at // 2]).start()
        at += size


def block_of(buffer, sems, j):
    block = buffer.at[pl.ds(2 * j, 2)]
    pltpu.make_async_copy(block, block, sems.at[j]).wait()
    return buffer[pl.ds(2 * j, 2)].reshape(-1, buffer.shape[2])


def attend_kernel(q_ref, own_ref, tags_ref, seg_ref, tag_ref, *rest):
    blocks, (out_ref, stat_ref, sent_ref, buffer, top, total, acc, sems) = rest[:10], rest[10:]
    copies_in(blocks, buffer, sems)
    rows = q_ref.shape[1]
    padded = tag_ref[...] < 0
    seg_wide = jnp.broadcast_to(seg_ref[...], (rows, 128))
    for h in range(HEADS_DEV):
        diagonal = diagonal_scores(q_ref, own_ref, h)
        top[h] = jnp.broadcast_to(jnp.where(padded, diagonal, NEG), (rows, 128))
        lane = lax.broadcasted_iota(jnp.int32, (rows, 128), 1)
        total[h] = jnp.where((lane == 0) & padded, 1.0, 0.0)
        acc[h] = jnp.where(padded, own_ref[:, head_block(h)].astype(F32), 0.0)

    def step(j, carry):
        whole = block_of(buffer, sems, j)
        tags = tags_ref[pl.ds(j, 1), :]
        keys = tags.shape[1]
        allowed = jnp.tile(seg_wide, (1, keys // 128)) == tags
        for h in range(HEADS_DEV):
            kv = whole[:, head_block(h)]
            scores = lax.dot_general(q_ref[h], kv, NT, preferred_element_type=F32)
            scores = jnp.where(allowed, scores, NEG)
            before = top[h]
            now = jnp.maximum(before, jnp.max(scores, axis=1, keepdims=True))
            weights = jnp.exp(scores - jnp.tile(now, (1, keys // 128)))
            fade = jnp.exp(before - now)
            sums = weights[:, :128]
            for k in range(1, keys // 128):
                sums = sums + weights[:, k * 128 : (k + 1) * 128]
            total[h] = total[h] * fade + sums
            acc[h] = acc[h] * fade + jnp.dot(weights.astype(BF16), kv, preferred_element_type=F32)
            top[h] = now
        return carry

    lax.fori_loop(0, 8, step, 0)
    lane = lax.broadcasted_iota(jnp.int32, (rows, HEAD_DIM), 1)
    seg = seg_ref[...]
    extra = jnp.where(lane == 12, 1.0, 0.0)
    for s in range(3):
        extra = extra + jnp.where((lane == 9 + s) & (seg != s), 1.0, 0.0)
    outs, queries = [], []
    for h in range(HEADS_DEV):
        sums = jnp.sum(total[h], axis=1, keepdims=True)
        outs.append((acc[h] / sums)[:, HEAD_DIM:])
        stat = top[h] + jnp.log(sums)
        stat_ref[h] = stat
        for i, piece in enumerate(pieces_of(stat[:, :1])):
            extra = extra + jnp.where(lane == 3 * h + i, piece, 0.0)
        queries.append(q_ref[h][:, :HEAD_DIM].astype(F32))
    out_ref[...] = jnp.concatenate(outs, axis=1)
    sent_ref[...] = jnp.concatenate(queries + [extra], axis=1).astype(BF16)


def vmem_specs(n):
    return [pl.BlockSpec(memory_space=pltpu.VMEM)] * n


def any_specs(n):
    return [pl.BlockSpec(memory_space=pl.ANY)] * n


def attend(q_heads, kv_own, tags, seg, tag, blocks):
    rows = kv_own.shape[0]
    keys, width = 2 * blocks[0].shape[1], blocks[0].shape[2]
    pairs = rows * keys * 8 * HEADS_DEV
    return pl.pallas_call(
        attend_kernel,
        out_shape=(
            jax.ShapeDtypeStruct((rows, HEADS_DEV * HEAD_DIM), F32),
            jax.ShapeDtypeStruct((HEADS_DEV, rows, 128), F32),
            jax.ShapeDtypeStruct((rows, 256), BF16),
        ),
        in_specs=vmem_specs(5) + any_specs(10),
        out_specs=tuple(vmem_specs(3)),
        scratch_shapes=[
            pltpu.VMEM((16, keys // 2, width), BF16),
            pltpu.VMEM((HEADS_DEV, rows, 128), F32),
            pltpu.VMEM((HEADS_DEV, rows, 128), F32),
            pltpu.VMEM((HEADS_DEV, rows, 128), F32),
            pltpu.SemaphoreType.DMA((8,)),
        ],
        compiler_params=pltpu.CompilerParams(vmem_limit_bytes=VMEM_LIMIT),
        cost_estimate=pl.CostEstimate(
            flops=pairs * 512, bytes_accessed=8 * keys * width * 2, transcendentals=pairs
        ),
        name="attend",
    )(q_heads, kv_own, tags, seg, tag, *blocks)


def query_back_kernel(q_ref, g_ref, own_ref, tags_ref, seg_ref, tag_ref, stat_ref, delta_ref, *rest):
    blocks, (dq_ref, dkv_ref, buffer, acc, sems) = rest[:10], rest[10:]
    copies_in(blocks, buffer, sems)
    rows = q_ref.shape[1]
    seg_wide = jnp.broadcast_to(seg_ref[...], (rows, 128))
    padded = tag_ref[...] < 0
    for h in range(HEADS_DEV):
        own = own_ref[:, head_block(h)].astype(F32)
        prob = jnp.exp(diagonal_scores(q_ref, own_ref, h) - stat_ref[h][:, :1])
        prob = jnp.where(padded, prob, 0.0)
        grad = diagonal_scores(g_ref, own_ref, h) - delta_ref[h][:, :1]
        score = (prob * grad).astype(BF16).astype(F32)
        acc[h] = score * own
        dkv_ref[:, head_block(h)] = score * q_ref[h].astype(F32) + prob.astype(BF16).astype(
            F32
        ) * g_ref[h].astype(F32)

    def step(j, carry):
        whole = block_of(buffer, sems, j)
        tags = tags_ref[pl.ds(j, 1), :]
        keys = tags.shape[1]
        allowed = jnp.tile(seg_wide, (1, keys // 128)) == tags
        for h in range(HEADS_DEV):
            kv = whole[:, head_block(h)]
            scores = lax.dot_general(q_ref[h], kv, NT, preferred_element_type=F32)
            scores = jnp.where(allowed, scores, NEG)
            probs = jnp.exp(scores - jnp.tile(stat_ref[h], (1, keys // 128)))
            grads = lax.dot_general(g_ref[h], kv, NT, preferred_element_type=F32)
            back = probs * (grads - jnp.tile(delta_ref[h], (1, keys // 128)))
            acc[h] = acc[h] + jnp.dot(back.astype(BF16), kv, preferred_element_type=F32)
        return carry

    lax.fori_loop(0, 8, step, 0)
    dq_ref[...] = (
        jnp.concatenate([acc[h][:, :HEAD_DIM] for h in range(HEADS_DEV)], axis=1)
        * HEAD_DIM ** (-0.5)
    ).astype(BF16)


def query_back(q_heads, g_heads, kv_own, tags, seg, tag, stat, delta, blocks):
    rows = kv_own.shape[0]
    keys, width = 2 * blocks[0].shape[1], blocks[0].shape[2]
    pairs = rows * keys * 8 * HEADS_DEV
    return pl.pallas_call(
        query_back_kernel,
        out_shape=(
            jax.ShapeDtypeStruct((rows, HEADS_DEV * HEAD_DIM), BF16),
            jax.ShapeDtypeStruct((rows, width), F32),
        ),
        in_specs=vmem_specs(8) + any_specs(10),
        out_specs=tuple(vmem_specs(2)),
        scratch_shapes=[
            pltpu.VMEM((16, keys // 2, width), BF16),
            pltpu.VMEM((HEADS_DEV, rows, 128), F32),
            pltpu.SemaphoreType.DMA((8,)),
        ],
        compiler_params=pltpu.CompilerParams(vmem_limit_bytes=VMEM_LIMIT),
        cost_estimate=pl.CostEstimate(
            flops=pairs * 768, bytes_accessed=8 * keys * width * 2, transcendentals=pairs
        ),
        name="query_back",
    )(q_heads, g_heads, kv_own, tags, seg, tag, stat, delta, *blocks)


def grad_rows_kernel(mixed_ref, out_ref, attended_ref, sent_ref, g_ref, delta_ref):
    rows = mixed_ref.shape[0]
    grad = jnp.dot(mixed_ref[...], out_ref[...], preferred_element_type=F32).astype(BF16)
    grad = grad.astype(F32)
    product = grad * attended_ref[...]
    lane = lax.broadcasted_iota(jnp.int32, (rows, HEAD_DIM), 1)
    extra = jnp.zeros((rows, HEAD_DIM), F32)
    zeros = jnp.zeros((rows, HEAD_DIM), BF16)
    for h in range(HEADS_DEV):
        delta = jnp.sum(product[:, head_columns(h)], axis=1, keepdims=True)
        delta_ref[h] = jnp.broadcast_to(delta, (rows, 128))
        for i, piece in enumerate(pieces_of(delta)):
            extra = extra + jnp.where(lane == 3 * h + i, piece, 0.0)
        g_ref[h] = jnp.concatenate([zeros, grad[:, head_columns(h)].astype(BF16)], axis=1)
    sent_ref[...] = jnp.concatenate([grad, extra], axis=1).astype(BF16)


def grad_rows(mixed, w_out, attended):
    rows = mixed.shape[0]
    return pl.pallas_call(
        grad_rows_kernel,
        out_shape=(
            jax.ShapeDtypeStruct((rows, 256), BF16),
            jax.ShapeDtypeStruct((HEADS_DEV, rows, 128), BF16),
            jax.ShapeDtypeStruct((HEADS_DEV, rows, 128), F32),
        ),
        in_specs=vmem_specs(3),
        out_specs=tuple(vmem_specs(3)),
        compiler_params=pltpu.CompilerParams(vmem_limit_bytes=VMEM_LIMIT),
        name="grad_rows",
    )(mixed, w_out, attended)


def key_back_kernel(order_ref, k_ref, v_ref, diag_ref, q_ref, *rest):
    g_blocks = rest[:10]
    dkv_ref, q_buffer, g_buffer, k_acc, v_acc, q_sems, g_sems = rest[10:]
    copies_in(g_blocks, g_buffer, g_sems)
    for i in range(64):
        pltpu.make_async_copy(
            q_ref.at[order_ref[i]], q_buffer.at[i], q_sems.at[i // 8]
        ).start()
    k_acc[...] = jnp.zeros_like(k_acc)
    v_acc[...] = jnp.zeros_like(v_acc)

    def step(j, carry):
        eight = q_buffer.at[pl.ds(8 * j, 8)]
        pltpu.make_async_copy(eight, eight, q_sems.at[j]).wait()
        queries = q_buffer[pl.ds(8 * j, 8)].reshape(-1, q_buffer.shape[2])
        grads = block_of(g_buffer, g_sems, j)
        for h in range(HEADS_DEV):
            scores = lax.dot_general(k_ref[h], queries, NT, preferred_element_type=F32)
            probs = jnp.exp(scores)
            v_acc[h] = v_acc[h] + jnp.dot(probs.astype(BF16), grads, preferred_element_type=F32)
            back = probs * lax.dot_general(v_ref[h], grads, NT, preferred_element_type=F32)
            k_acc[h] = k_acc[h] + jnp.dot(back.astype(BF16), queries, preferred_element_type=F32)
        return carry

    lax.fori_loop(0, 8, step, 0)
    parts = []
    for h in range(HEADS_DEV):
        parts += [k_acc[h][:, head_columns(h)], v_acc[h][:, head_columns(h)]]
    dkv_ref[...] = (jnp.concatenate(parts, axis=1) + diag_ref[...]).astype(BF16)


def key_back(order, k_heads, v_heads, diagonal, q_all, g_blocks):
    rows = k_heads.shape[1]
    queries, width = 2 * g_blocks[0].shape[1], g_blocks[0].shape[2]
    pairs = rows * queries * 8 * HEADS_DEV
    return pl.pallas_call(
        key_back_kernel,
        out_shape=jax.ShapeDtypeStruct(diagonal.shape, BF16),
        in_specs=[pl.BlockSpec(memory_space=pltpu.SMEM)] + vmem_specs(3) + any_specs(11),
        out_specs=vmem_specs(1)[0],
        scratch_shapes=[
            pltpu.VMEM((64, queries // 8, width), BF16),
            pltpu.VMEM((16, queries // 2, width), BF16),
            pltpu.VMEM((HEADS_DEV, rows, width), F32),
            pltpu.VMEM((HEADS_DEV, rows, width), F32),
            pltpu.SemaphoreType.DMA((8,)),
            pltpu.SemaphoreType.DMA((8,)),
        ],
        compiler_params=pltpu.CompilerParams(vmem_limit_bytes=VMEM_LIMIT),
        cost_estimate=pl.CostEstimate(
            flops=pairs * 2048, bytes_accessed=16 * queries * width * 2, transcendentals=pairs
        ),
        name="key_back",
    )(order, k_heads, v_heads, diagonal, q_all, *g_blocks)


def dot(a, b):
    return jnp.dot(a, b, preferred_element_type=F32)


def dot_nt(a, b):
    return lax.dot_general(a, b, NT, preferred_element_type=F32)


def dot_tn(a, b):
    return lax.dot_general(a, b, (((0,), (0,)), ((), ())), preferred_element_type=F32)


def core_half(x, axis, at):
    size = x.shape[axis] // 2
    return lax.dynamic_slice_in_dim(x, at * size, size, axis)


def interleaved(k, v):
    shape = (*k.shape[:-1], -1, HEAD_DIM)
    return jnp.stack([k.reshape(shape), v.reshape(shape)], axis=-2).reshape(*k.shape[:-1], -1)


def per_device(
    hidden,
    w_qkv,
    w_out,
    b_qv,
    w_up,
    w_down,
    b_up,
    norm_gains,
    norm_shifts,
    segments,
    lengths,
    cotangent,
):
    core = lax.axis_index("core")
    heads_at = lax.axis_index("heads")
    own_ctx = ((lax.axis_index("z") * 4 + lax.axis_index("y")) * 2 + lax.axis_index("xh")) * 2 + core
    tok = hidden.shape[0]
    rows = w_up.shape[0]
    feat = HEADS_DEV * HEAD_DIM
    hidden_units = w_up.shape[1] // 2

    hid = chip_tokens(hidden)
    out_turned, down_turned = w_out.T, w_down.T
    segs_low = segments.astype(BF16).reshape(2, tok // 2)

    def packed(at):
        q, k, v = (core_half(w_qkv[i], 1, at) for i in range(3))
        tail = jnp.pad(segs_low, ((0, rows - 2), (0, 0)))
        urgent = jnp.concatenate([interleaved(k, v), q, tail], axis=1)
        later = [core_half(w, 1, at) for w in (out_turned, w_up, down_turned)]
        return urgent, jnp.concatenate(later, axis=1)

    mine, theirs = packed(core), packed(1 - core)
    urgent = pair_ordered(mine[0], shifted(theirs[0], "core", 1), "core").reshape(2 * rows, -1)
    later = pair_ordered(mine[1], shifted(theirs[1], "core", 1), "core").reshape(2 * rows, -1)
    kv_cols = 2 * feat
    w_urgent = gather_ordered(urgent)
    w_kv = w_urgent[:, :kv_cols]
    w_q = w_urgent[:, kv_cols : kv_cols + feat]
    seg_all = w_urgent[:, kv_cols + feat :].reshape(-1, 2, rows, tok // 2)[:, :, :2].reshape(-1, tok)
    seg_all = seg_all.astype(jnp.int32)
    rest = lax.all_gather(later, CHIPS, axis=0, tiled=True)
    w_out_t = rest[:, :feat]
    w_up_all = rest[:, feat : feat + hidden_units]
    w_down_t = rest[:, feat + hidden_units :]

    bias = b_qv.astype(F32)
    q_bias, v_bias = core_half(bias[0], 0, core), core_half(bias[1], 0, core)
    kv_own = (dot(hid, w_kv) + interleaved(jnp.zeros_like(v_bias), v_bias)).astype(BF16)
    queries = ((dot(hid, w_q) + q_bias).astype(BF16) * HEAD_DIM ** (-0.5)).astype(BF16)
    q_heads = jnp.pad(
        jnp.swapaxes(queries.reshape(2 * tok, HEADS_DEV, HEAD_DIM), 0, 1),
        ((0, 0), (0, 0), (0, HEAD_DIM)),
    )

    starts = [jnp.sum((seg_all < s).astype(jnp.int32)) for s in range(3)]
    places = jnp.arange(seg_all.size, dtype=jnp.int32).reshape(seg_all.shape)
    run_end = jnp.zeros_like(seg_all)
    for s in range(3):
        run_end = jnp.where(seg_all == s, starts[s] + lengths[s], run_end)
    tag_all = jnp.where(places < run_end, seg_all, -1).astype(F32)
    order = jnp.concatenate([relative_order("z", "y", 0), relative_order("y", "z", 1)])
    tags = jnp.take(tag_all, order, axis=0).reshape(8, -1)
    both = jnp.stack([own_ctx, own_ctx + 1 - 2 * core])
    tag_own = jnp.take(tag_all, both, axis=0).reshape(-1, 1)
    seg_own = jnp.take(seg_all, both, axis=0).astype(F32).reshape(-1, 1)

    kv_blocks = gather_second(lax.optimization_barrier(gather_first(kv_own)))
    attended, stat, q_sent = attend(q_heads, kv_own, tags, seg_own, tag_own, kv_blocks)
    attended_low = attended.astype(BF16)
    q_all = lax.all_gather(q_sent, CHIPS, axis=0, tiled=True).reshape(64, tok, -1)
    q_order = jnp.where(core == 0, order, order + 1 - 2 * (order % 2))

    gain_rows = norm_gains.astype(F32)
    shifts = norm_shifts.astype(F32)
    attn_mixed = team_sum(dot_nt(attended_low, w_out_t))
    first_out, normed_one, inverse_one = layer_norm(
        hidden.astype(F32) + attn_mixed + shifts[0], gain_rows[0], shifts[1]
    )
    first_low = chip_tokens(first_out.astype(BF16))
    up_bias = core_half(b_up, 0, core).astype(F32)
    up_proj = dot(first_low, w_up_all) + up_bias
    activated = exact_gelu(up_proj).astype(BF16)
    second = team_sum(dot_nt(activated, w_down_t))
    output, normed_two, inverse_two = layer_norm(
        first_out + second + shifts[2], gain_rows[1], shifts[3]
    )
    resid_two, gain_two_grad, beta_two_grad = norm_back(
        cotangent.astype(F32), normed_two, inverse_two, gain_rows[1]
    )
    branch_low = chip_tokens(resid_two.astype(BF16))
    act_grad = dot(branch_low, w_down_t)
    up_low = jax.vjp(exact_gelu, up_proj)[1](act_grad)[0].astype(BF16)
    first_grad = resid_two + team_sum(dot_nt(up_low, w_up_all))
    down_grad = dot_tn(branch_low, activated)
    up_grad = dot_tn(first_low, up_low)
    upbias_grad = jnp.sum(up_low.astype(F32), axis=0)
    resid_one, gain_one_grad, beta_one_grad = norm_back(
        first_grad, normed_one, inverse_one, gain_rows[0]
    )
    mixed_low = chip_tokens(resid_one.astype(BF16))
    g_sent, g_heads, delta = grad_rows(mixed_low, w_out_t, attended)
    g_first, g_heads = lax.optimization_barrier((gather_first(g_sent), g_heads))
    g_blocks = gather_second(g_first)
    out_grad = dot_tn(mixed_low, attended_low)

    dq, diagonal = query_back(
        q_heads, g_heads, kv_own, tags, seg_own, tag_own, stat, delta, kv_blocks
    )
    early = (
        jnp.concatenate([up_grad, dot_tn(hid, dq)], axis=1),
        jnp.concatenate([down_grad, out_grad], axis=1),
    )
    early, g_blocks = lax.optimization_barrier((early, g_blocks))
    early_z, early_y = scatter_first(*early)
    lane = jnp.arange(256, dtype=jnp.int32)
    split = kv_own.reshape(2 * tok, HEADS_DEV, 2, HEAD_DIM)
    extras = jnp.where(
        (lane >= feat + 9) & (lane < feat + 12),
        jnp.where(tag_own == (lane - feat - 9).astype(F32), NEG, 0.0),
        jnp.where((lane == feat + 12) & (tag_own < 0), NEG, 0.0),
    )

    def spread_heads(x, more):
        wide = jnp.pad(x.reshape(2 * tok, feat).astype(F32), ((0, 0), (0, 256 - feat)))
        made = []
        for h in range(HEADS_DEV):
            in_head = (lane >= h * HEAD_DIM) & (lane < (h + 1) * HEAD_DIM)
            in_stat = (lane >= feat + 3 * h) & (lane < feat + 3 * h + 3)
            made.append(jnp.where(in_head, wide, jnp.where(in_stat, -1.0, more)))
        return jnp.stack(made).astype(BF16)

    k_heads = spread_heads(split[:, :, 0], extras)
    v_heads = spread_heads(split[:, :, 1], jnp.zeros_like(extras))
    dkv = key_back(q_order, k_heads, v_heads, diagonal, q_all, g_blocks)

    hidden_grad = resid_one + team_sum(dot_nt(dkv, w_kv) + dot_nt(dq, w_q))

    def placed_half(x):
        zero = jnp.zeros_like(x)
        return jnp.concatenate(
            [jnp.where(core == 0, x, zero), jnp.where(core == 0, zero, x)], axis=-1
        )

    dv = dkv.reshape(2 * tok, HEADS_DEV, 2, HEAD_DIM)[:, :, 1].reshape(2 * tok, feat)
    qv_grad = jnp.stack([jnp.sum(dq.astype(F32), axis=0), jnp.sum(dv.astype(F32), axis=0)])
    vectors = jnp.stack(
        [
            gain_one_grad,
            gain_two_grad,
            jnp.sum(resid_one, axis=0),
            beta_one_grad,
            jnp.sum(resid_two, axis=0),
            beta_two_grad,
        ]
    )

    def by_owner(x):
        return jnp.swapaxes(x.reshape(x.shape[0], 64, -1), 0, 1).reshape(64, -1)

    small = jnp.concatenate(
        [by_owner(placed_half(qv_grad)), by_owner(placed_half(upbias_grad)[None]), by_owner(vectors)],
        axis=1,
    )
    small = jnp.pad(small, ((0, 0), (0, 128 - small.shape[1]))).reshape(64, 2, 64)
    small = jnp.pad(small, ((0, 0), (0, rows - 2), (0, 0))).reshape(64 * rows, 64)
    kv_grad = dot_tn(hid, dkv)
    late_z, late_y = scatter_first(
        kv_grad[:, :256], jnp.concatenate([kv_grad[:, 256:], small], axis=1)
    )
    done_z, done_y = scatter_second(
        jnp.concatenate([late_z, early_z], axis=-1), jnp.concatenate([late_y, early_y], axis=-1)
    )
    done = jnp.concatenate(
        [done_z[:, :256], done_y[:, : 2 * HEAD_DIM], done_y[:, 2 * HEAD_DIM : 3 * HEAD_DIM]]
        + [done_z[:, 256:], done_y[:, 3 * HEAD_DIM :]],
        axis=1,
    )
    own_rows = core_half(done, 0, core)
    got = shifted(core_half(done, 0, 1 - core), "core", 1)
    low = jnp.where(core == 0, own_rows, got)
    high = jnp.where(core == 0, got, own_rows)

    def columns(start, size):
        return jnp.concatenate(
            [low[:, start : start + size], high[:, start : start + size]], axis=1
        )

    kv_pairs = columns(0, kv_cols).reshape(rows, 2 * HEADS_DEV, 2, HEAD_DIM)
    k_cols = kv_pairs[:, :, 0].reshape(rows, -1)
    v_cols = kv_pairs[:, :, 1].reshape(rows, -1)
    tail = (own_rows + got)[:2, kv_cols : kv_cols + 64].reshape(-1)
    at = kv_cols + 64
    up_cols = columns(at, hidden_units)
    q_cols = columns(at + hidden_units, feat)
    at += hidden_units + feat
    down_cols = columns(at, hidden_units)
    out_cols = columns(at + hidden_units, feat)
    qv_out = tail[:12].reshape(2, 6)
    bias_out = tail[12:36]
    vec_out = tail[36:108].reshape(6, 2, 6)
    vec_out = lax.dynamic_index_in_dim(vec_out, heads_at, 1, keepdims=False)
    return (
        output.astype(BF16),
        hidden_grad,
        jnp.stack([q_cols, k_cols, v_cols]),
        out_cols.T,
        qv_out,
        up_cols,
        down_cols.T,
        bias_out,
        vec_out[:2],
        vec_out[2:],
    )


def solution(mesh):
    fine = Mesh(mesh.devices.reshape(4, 4, 2, 2, 2), ("z", "y", "xh", "core", "heads"))
    return jax.shard_map(
        per_device,
        mesh=fine,
        in_specs=(
            P(CTX, None),
            P(None, CTX, "heads"),
            P("heads", CTX),
            P(None, "heads"),
            P(CTX, "heads"),
            P("heads", CTX),
            P("heads"),
            P(),
            P(),
            P(CTX),
            P(),
            P(CTX, None),
        ),
        out_specs=(
            P(CTX, None),
            P(CTX, None),
            P(None, CTX, "heads"),
            P("heads", CTX),
            P(None, ("heads", *CTX)),
            P(CTX, "heads"),
            P("heads", CTX),
            P(("heads", *CTX)),
            P(None, (*CTX, "heads")),
            P(None, (*CTX, "heads")),
        ),
        check_vma=False,
    )
```

```python
import jax
import jax.numpy as jnp
from jax import lax
from jax.experimental import pallas as pl
from jax.experimental.pallas import tpu as pltpu
from jax.sharding import Mesh, PartitionSpec as P

HEAD_DIM = 64
HEADS_DEV = 3
EPS = 1e-06
NEG = -1e30
CTX = ("z", "y", "xh", "core")
CHIPS = ("z", "y", "xh")
F32 = jnp.float32
BF16 = jnp.bfloat16
NT = (((1,), (1,)), ((), ()))
VMEM_LIMIT = 50 * 1024 * 1024
OFFSETS = (0, -1, 1, 2)


def shifted(x, axis, step):
    n = lax.axis_size(axis)
    return lax.ppermute(x, axis, [(i, (i + step) % n) for i in range(n)])


def ring_halves(x, axis):
    half = x.shape[0] // 2
    before, after = shifted(x, axis, 1), shifted(x, axis, -1)
    return [x, before, after, shifted(before[:half], axis, 1), shifted(after[half:], axis, -1)]


def gather_first(x, widths):
    half = x.shape[0] // 2
    streams = []
    for part, axis in ((x[:half], "z"), (x[half:], "y")):
        both = jnp.concatenate([part, shifted(part, "xh", 1)], axis=0)
        pieces, at = ring_halves(both, axis), 0
        for width in widths:
            streams.append(jnp.concatenate([p[:, at : at + width] for p in pieces], axis=0))
            at += width
    return tuple(streams)


def gather_second(z_stream, y_stream):
    blocks = ring_halves(z_stream, "y") + ring_halves(y_stream, "z")
    return [b.reshape(-1, z_stream.shape[0] // 2, b.shape[1]) for b in blocks]


def near_blocks(blocks):
    return blocks[:3] + blocks[5:8]


def far_blocks(blocks):
    return blocks[3:5] + blocks[8:]


def relative_order(first, second, core_at):
    place = {a: lax.axis_index(a) for a in CHIPS}
    core = lax.axis_index("core")
    order = []
    for second_step in OFFSETS:
        for first_step in OFFSETS:
            for xh_step in (0, 1):
                at = dict(place)
                at[first] = (at[first] + first_step) % 4
                at[second] = (at[second] + second_step) % 4
                at["xh"] = (at["xh"] + xh_step) % 2
                order.append(((at["z"] * 4 + at["y"]) * 2 + at["xh"]) * 2 + (core + core_at) % 2)
    return jnp.stack(order)


def pair_ordered(own, other, axis):
    first = lax.axis_index(axis) == 0
    return jnp.stack([jnp.where(first, own, other), jnp.where(first, other, own)])


def sums_by_owner(x):
    parts = lax.all_to_all(x, CTX, 0, 0, tiled=True)
    return jnp.sum(parts.reshape(-1, 2, *x.shape[1:]).astype(F32), axis=0)


def team_sum(partial):
    rows = partial.shape[0] // 2
    near = partial[:rows] + shifted(partial[rows:].astype(BF16), "core", 1).astype(F32)
    low = lax.optimization_barrier(near.astype(BF16))
    return low.astype(F32) + shifted(low, "heads", 1).astype(F32)


def chip_tokens(x):
    return jnp.concatenate([x, shifted(x, "core", 1)], axis=0)


def layer_norm(residual, gain_row, shift_row):
    centred = residual - jnp.mean(residual, axis=-1, keepdims=True)
    inverse = lax.rsqrt(jnp.mean(centred * centred, axis=-1, keepdims=True) + EPS)
    normed = centred * inverse
    return (normed * gain_row + shift_row, normed, inverse)


def norm_back(incoming, normed, inverse, gain_row):
    scaled = incoming * gain_row
    projected = (
        scaled
        - jnp.mean(scaled, axis=-1, keepdims=True)
        - normed * jnp.mean(scaled * normed, axis=-1, keepdims=True)
    )
    return (inverse * projected, jnp.sum(incoming * normed, axis=0), jnp.sum(incoming, axis=0))


def exact_gelu(pre_act):
    return jax.nn.gelu(pre_act, approximate=False)


def pieces_of(column):
    high = column.astype(BF16).astype(F32)
    middle = (column - high).astype(BF16).astype(F32)
    return high, middle, column - high - middle


def head_columns(h):
    return slice(h * HEAD_DIM, (h + 1) * HEAD_DIM)


def head_block(h):
    return slice(h * 128, (h + 1) * 128)


def diagonal_scores(q_ref, kv_ref, h):
    product = q_ref[h].astype(F32) * kv_ref[:, head_block(h)].astype(F32)
    return jnp.sum(product, axis=1, keepdims=True)


def copies_in(sources, buffer, sems):
    at = 0
    for source in sources:
        size = source.shape[0]
        pltpu.make_async_copy(source, buffer.at[pl.ds(at, size)], sems.at[at // 2]).start()
        at += size


def block_of(buffer, sems, j):
    block = buffer.at[pl.ds(2 * j, 2)]
    pltpu.make_async_copy(block, block, sems.at[j]).wait()
    return buffer[pl.ds(2 * j, 2)].reshape(-1, buffer.shape[2])


def attend_blocks(q_ref, tags_ref, seg_ref, top, total, acc, buffer, sems):
    rows = q_ref.shape[1]
    seg_wide = jnp.broadcast_to(seg_ref[...], (rows, 128))

    def step(j, carry):
        whole = block_of(buffer, sems, j)
        tags = tags_ref[pl.ds(j, 1), :]
        keys = tags.shape[1]
        allowed = jnp.tile(seg_wide, (1, keys // 128)) == tags
        for h in range(HEADS_DEV):
            kv = whole[:, head_block(h)]
            scores = lax.dot_general(q_ref[h], kv, NT, preferred_element_type=F32)
            scores = jnp.where(allowed, scores, NEG)
            before = top[h]
            now = jnp.maximum(before, jnp.max(scores, axis=1, keepdims=True))
            weights = jnp.exp(scores - jnp.tile(now, (1, keys // 128)))
            fade = jnp.exp(before - now)
            sums = weights[:, :128]
            for k in range(1, keys // 128):
                sums = sums + weights[:, k * 128 : (k + 1) * 128]
            total[h] = total[h] * fade + sums
            acc[h] = acc[h] * fade + jnp.dot(weights.astype(BF16), kv, preferred_element_type=F32)
            top[h] = now
        return carry

    lax.fori_loop(0, tags_ref.shape[0], step, 0)


def attend_near_kernel(q_ref, own_ref, tags_ref, seg_ref, tag_ref, *rest):
    blocks, (top, total, acc, buffer, sems) = rest[:6], rest[6:]
    copies_in(blocks, buffer, sems)
    rows = q_ref.shape[1]
    padded = tag_ref[...] < 0
    for h in range(HEADS_DEV):
        diagonal = diagonal_scores(q_ref, own_ref, h)
        top[h] = jnp.broadcast_to(jnp.where(padded, diagonal, NEG), (rows, 128))
        lane = lax.broadcasted_iota(jnp.int32, (rows, 128), 1)
        total[h] = jnp.where((lane == 0) & padded, 1.0, 0.0)
        acc[h] = jnp.where(padded, own_ref[:, head_block(h)].astype(F32), 0.0)
    attend_blocks(q_ref, tags_ref, seg_ref, top, total, acc, buffer, sems)


def attend_far_kernel(q_ref, tags_ref, seg_ref, top_in, total_in, acc_in, *rest):
    blocks, (out_ref, stat_ref, top, total, acc, buffer, sems) = rest[:4], rest[4:]
    copies_in(blocks, buffer, sems)
    top[...], total[...], acc[...] = top_in[...], total_in[...], acc_in[...]
    attend_blocks(q_ref, tags_ref, seg_ref, top, total, acc, buffer, sems)
    outs = []
    for h in range(HEADS_DEV):
        sums = jnp.sum(total[h], axis=1, keepdims=True)
        outs.append((acc[h] / sums)[:, HEAD_DIM:])
        stat_ref[h] = top[h] + jnp.log(sums)
    out_ref[...] = jnp.concatenate(outs, axis=1)


def vmem_specs(n):
    return [pl.BlockSpec(memory_space=pltpu.VMEM)] * n


def any_specs(n):
    return [pl.BlockSpec(memory_space=pl.ANY)] * n


def head_state(rows, lanes=128):
    return jax.ShapeDtypeStruct((HEADS_DEV, rows, lanes), F32)


def cost(rows, blocks, flops):
    keys = sum(b.shape[0] * b.shape[1] for b in blocks)
    pairs = rows * keys * HEADS_DEV
    return pl.CostEstimate(
        flops=pairs * flops, bytes_accessed=keys * 1024, transcendentals=pairs
    )


def buffers(blocks):
    count = sum(b.shape[0] for b in blocks)
    return [
        pltpu.VMEM((count, *blocks[0].shape[1:]), BF16),
        pltpu.SemaphoreType.DMA((count // 2,)),
    ]


def attend_near(q_heads, kv_own, tags, seg, tag, blocks):
    rows = kv_own.shape[0]
    return pl.pallas_call(
        attend_near_kernel,
        out_shape=(head_state(rows),) * 3,
        in_specs=vmem_specs(5) + any_specs(6),
        out_specs=tuple(vmem_specs(3)),
        scratch_shapes=buffers(blocks),
        compiler_params=pltpu.CompilerParams(vmem_limit_bytes=VMEM_LIMIT),
        cost_estimate=cost(rows, blocks, 512),
        name="attend_near",
    )(q_heads, kv_own, tags, seg, tag, *blocks)


def attend_far(q_heads, tags, seg, state, blocks):
    rows = q_heads.shape[1]
    return pl.pallas_call(
        attend_far_kernel,
        out_shape=(jax.ShapeDtypeStruct((rows, HEADS_DEV * HEAD_DIM), F32), head_state(rows)),
        in_specs=vmem_specs(6) + any_specs(4),
        out_specs=tuple(vmem_specs(2)),
        scratch_shapes=[pltpu.VMEM((HEADS_DEV, rows, 128), F32)] * 3 + buffers(blocks),
        compiler_params=pltpu.CompilerParams(vmem_limit_bytes=VMEM_LIMIT),
        cost_estimate=cost(rows, blocks, 512),
        name="attend_far",
    )(q_heads, tags, seg, *state, *blocks)


def query_back_kernel(q_ref, g_ref, own_ref, tags_ref, seg_ref, tag_ref, stat_ref, delta_ref, *rest):
    blocks, (dq_ref, dkv_ref, buffer, acc, sems) = rest[:10], rest[10:]
    copies_in(blocks, buffer, sems)
    rows = q_ref.shape[1]
    seg_wide = jnp.broadcast_to(seg_ref[...], (rows, 128))
    padded = tag_ref[...] < 0
    for h in range(HEADS_DEV):
        own = own_ref[:, head_block(h)].astype(F32)
        prob = jnp.exp(diagonal_scores(q_ref, own_ref, h) - stat_ref[h][:, :1])
        prob = jnp.where(padded, prob, 0.0)
        grad = diagonal_scores(g_ref, own_ref, h) - delta_ref[h][:, :1]
        score = (prob * grad).astype(BF16).astype(F32)
        acc[h] = score * own
        dkv_ref[:, head_block(h)] = score * q_ref[h].astype(F32) + prob.astype(BF16).astype(
            F32
        ) * g_ref[h].astype(F32)

    def step(j, carry):
        whole = block_of(buffer, sems, j)
        tags = tags_ref[pl.ds(j, 1), :]
        keys = tags.shape[1]
        allowed = jnp.tile(seg_wide, (1, keys // 128)) == tags
        for h in range(HEADS_DEV):
            kv = whole[:, head_block(h)]
            scores = lax.dot_general(q_ref[h], kv, NT, preferred_element_type=F32)
            scores = jnp.where(allowed, scores, NEG)
            probs = jnp.exp(scores - jnp.tile(stat_ref[h], (1, keys // 128)))
            grads = lax.dot_general(g_ref[h], kv, NT, preferred_element_type=F32)
            back = probs * (grads - jnp.tile(delta_ref[h], (1, keys // 128)))
            acc[h] = acc[h] + jnp.dot(back.astype(BF16), kv, preferred_element_type=F32)
        return carry

    lax.fori_loop(0, 8, step, 0)
    dq_ref[...] = (
        jnp.concatenate([acc[h][:, :HEAD_DIM] for h in range(HEADS_DEV)], axis=1)
        * HEAD_DIM ** (-0.5)
    ).astype(BF16)


def query_back(q_heads, g_heads, kv_own, tags, seg, tag, stat, delta, blocks):
    rows = kv_own.shape[0]
    keys, width = 2 * blocks[0].shape[1], blocks[0].shape[2]
    return pl.pallas_call(
        query_back_kernel,
        out_shape=(
            jax.ShapeDtypeStruct((rows, HEADS_DEV * HEAD_DIM), BF16),
            jax.ShapeDtypeStruct((rows, width), F32),
        ),
        in_specs=vmem_specs(8) + any_specs(10),
        out_specs=tuple(vmem_specs(2)),
        scratch_shapes=[
            pltpu.VMEM((16, keys // 2, width), BF16),
            pltpu.VMEM((HEADS_DEV, rows, 128), F32),
            pltpu.SemaphoreType.DMA((8,)),
        ],
        compiler_params=pltpu.CompilerParams(vmem_limit_bytes=VMEM_LIMIT),
        cost_estimate=cost(rows, blocks, 768),
        name="query_back",
    )(q_heads, g_heads, kv_own, tags, seg, tag, stat, delta, *blocks)


def grad_rows_kernel(
    mixed_ref, out_ref, attended_ref, stat_ref, seg_ref, sent_ref, g_ref, delta_ref
):
    rows = mixed_ref.shape[0]
    grad = jnp.dot(mixed_ref[...], out_ref[...], preferred_element_type=F32).astype(BF16)
    grad = grad.astype(F32)
    product = grad * attended_ref[...]
    lane = lax.broadcasted_iota(jnp.int32, (rows, HEAD_DIM), 1)
    seg = seg_ref[...]
    extra = jnp.where(lane == 21, 1.0, 0.0)
    for s in range(3):
        extra = extra + jnp.where((lane == 18 + s) & (seg != s), 1.0, 0.0)
    zeros = jnp.zeros((rows, HEAD_DIM), BF16)
    for h in range(HEADS_DEV):
        delta = jnp.sum(product[:, head_columns(h)], axis=1, keepdims=True)
        delta_ref[h] = jnp.broadcast_to(delta, (rows, 128))
        for i, piece in enumerate(pieces_of(delta)):
            extra = extra + jnp.where(lane == 3 * h + i, piece, 0.0)
        for i, piece in enumerate(pieces_of(stat_ref[h][:, :1])):
            extra = extra + jnp.where(lane == 9 + 3 * h + i, piece, 0.0)
        g_ref[h] = jnp.concatenate([zeros, grad[:, head_columns(h)].astype(BF16)], axis=1)
    sent_ref[...] = jnp.concatenate([grad, extra], axis=1).astype(BF16)


def grad_rows(mixed, w_out, attended, stat, seg):
    rows = mixed.shape[0]
    return pl.pallas_call(
        grad_rows_kernel,
        out_shape=(
            jax.ShapeDtypeStruct((rows, 256), BF16),
            jax.ShapeDtypeStruct((HEADS_DEV, rows, 128), BF16),
            jax.ShapeDtypeStruct((HEADS_DEV, rows, 128), F32),
        ),
        in_specs=vmem_specs(5),
        out_specs=tuple(vmem_specs(3)),
        compiler_params=pltpu.CompilerParams(vmem_limit_bytes=VMEM_LIMIT),
        name="grad_rows",
    )(mixed, w_out, attended, stat, seg)


def hidden_grads_kernel(spread_ref, branch_ref, activated_ref, first_ref, up_ref, out_ref, held, sems):
    for i, (left, right) in enumerate(((first_ref, up_ref), (branch_ref, activated_ref))):
        wide = jnp.dot(left[...], spread_ref[...], preferred_element_type=F32).astype(BF16)
        held[i] = dot_tn(wide, right[...]).astype(BF16)
        columns = pl.ds(i * held.shape[2], held.shape[2])
        pltpu.make_async_copy(held.at[i], out_ref.at[:, columns], sems.at[i]).start()
    for i in range(2):
        columns = pl.ds(i * held.shape[2], held.shape[2])
        pltpu.make_async_copy(held.at[i], out_ref.at[:, columns], sems.at[i]).wait()


def hidden_grads(spread, branch, activated, first, up):
    wide, units = spread.shape[1], up.shape[1]
    return pl.pallas_call(
        hidden_grads_kernel,
        out_shape=jax.ShapeDtypeStruct((wide, 2 * units), BF16),
        in_specs=vmem_specs(5),
        out_specs=pl.BlockSpec(memory_space=pltpu.HBM),
        scratch_shapes=[pltpu.VMEM((2, wide, units), BF16), pltpu.SemaphoreType.DMA((2,))],
        compiler_params=pltpu.CompilerParams(vmem_limit_bytes=VMEM_LIMIT),
        name="hidden_grads",
    )(spread, branch, activated, first, up)


def key_back_blocks(k_ref, v_ref, k_acc, v_acc, q_buffer, g_buffer, q_sems, g_sems):
    def step(j, carry):
        queries = block_of(q_buffer, q_sems, j)
        grads = block_of(g_buffer, g_sems, j)
        lane = lax.broadcasted_iota(jnp.int32, queries.shape, 1)
        queries = jnp.where(lane < HEADS_DEV * HEAD_DIM, queries, grads)
        for h in range(HEADS_DEV):
            scores = lax.dot_general(k_ref[h], queries, NT, preferred_element_type=F32)
            probs = jnp.exp(scores)
            v_acc[h] = v_acc[h] + jnp.dot(probs.astype(BF16), grads, preferred_element_type=F32)
            back = probs * lax.dot_general(v_ref[h], grads, NT, preferred_element_type=F32)
            k_acc[h] = k_acc[h] + jnp.dot(back.astype(BF16), queries, preferred_element_type=F32)
        return carry

    lax.fori_loop(0, q_sems.shape[0], step, 0)


def key_near_kernel(k_ref, v_ref, *rest):
    q_blocks, g_blocks = rest[:6], rest[6:12]
    k_acc, v_acc, q_buffer, q_sems, g_buffer, g_sems = rest[12:]
    copies_in(q_blocks, q_buffer, q_sems)
    copies_in(g_blocks, g_buffer, g_sems)
    k_acc[...] = jnp.zeros_like(k_acc)
    v_acc[...] = jnp.zeros_like(v_acc)
    key_back_blocks(k_ref, v_ref, k_acc, v_acc, q_buffer, g_buffer, q_sems, g_sems)


def key_far_kernel(k_ref, v_ref, diag_ref, k_in, v_in, *rest):
    q_blocks, g_blocks = rest[:4], rest[4:8]
    dkv_ref, k_acc, v_acc, q_buffer, q_sems, g_buffer, g_sems = rest[8:]
    copies_in(q_blocks, q_buffer, q_sems)
    copies_in(g_blocks, g_buffer, g_sems)
    k_acc[...], v_acc[...] = k_in[...], v_in[...]
    key_back_blocks(k_ref, v_ref, k_acc, v_acc, q_buffer, g_buffer, q_sems, g_sems)
    parts = []
    for h in range(HEADS_DEV):
        parts += [k_acc[h][:, head_columns(h)], v_acc[h][:, head_columns(h)]]
    dkv_ref[...] = (jnp.concatenate(parts, axis=1) + diag_ref[...]).astype(BF16)


def key_near(k_heads, v_heads, q_blocks, g_blocks):
    rows, width = k_heads.shape[1:]
    return pl.pallas_call(
        key_near_kernel,
        out_shape=(head_state(rows, width),) * 2,
        in_specs=vmem_specs(2) + any_specs(12),
        out_specs=tuple(vmem_specs(2)),
        scratch_shapes=buffers(q_blocks) + buffers(g_blocks),
        compiler_params=pltpu.CompilerParams(vmem_limit_bytes=VMEM_LIMIT),
        cost_estimate=cost(rows, q_blocks, 2048),
        name="key_near",
    )(k_heads, v_heads, *q_blocks, *g_blocks)


def key_far(k_heads, v_heads, diagonal, state, q_blocks, g_blocks):
    rows, width = k_heads.shape[1:]
    return pl.pallas_call(
        key_far_kernel,
        out_shape=jax.ShapeDtypeStruct(diagonal.shape, BF16),
        in_specs=vmem_specs(5) + any_specs(8),
        out_specs=vmem_specs(1)[0],
        scratch_shapes=[pltpu.VMEM((HEADS_DEV, rows, width), F32)] * 2
        + buffers(q_blocks)
        + buffers(g_blocks),
        compiler_params=pltpu.CompilerParams(vmem_limit_bytes=VMEM_LIMIT),
        cost_estimate=cost(rows, q_blocks, 2048),
        name="key_far",
    )(k_heads, v_heads, diagonal, *state, *q_blocks, *g_blocks)


def dot(a, b):
    return jnp.dot(a, b, preferred_element_type=F32)


def dot_nt(a, b):
    return lax.dot_general(a, b, NT, preferred_element_type=F32)


def dot_tn(a, b):
    return lax.dot_general(a, b, (((0,), (0,)), ((), ())), preferred_element_type=F32)


def core_half(x, axis, at):
    size = x.shape[axis] // 2
    return lax.dynamic_slice_in_dim(x, at * size, size, axis)


def interleaved(k, v):
    shape = (*k.shape[:-1], -1, HEAD_DIM)
    return jnp.stack([k.reshape(shape), v.reshape(shape)], axis=-2).reshape(*k.shape[:-1], -1)


def per_device(
    hidden,
    w_qkv,
    w_out,
    b_qv,
    w_up,
    w_down,
    b_up,
    norm_gains,
    norm_shifts,
    segments,
    lengths,
    cotangent,
):
    core = lax.axis_index("core")
    heads_at = lax.axis_index("heads")
    own_ctx = ((lax.axis_index("z") * 4 + lax.axis_index("y")) * 2 + lax.axis_index("xh")) * 2 + core
    tok = hidden.shape[0]
    rows = w_up.shape[0]
    feat = HEADS_DEV * HEAD_DIM
    hidden_units = w_up.shape[1] // 2

    hid = chip_tokens(hidden)
    out_turned, down_turned = w_out.T, w_down.T
    low_tok = segments.astype(BF16).reshape(2, tok // 2)
    kv_cols = 2 * feat

    def halves(x):
        return jnp.swapaxes(x.reshape(rows, 2, -1), 0, 1)

    q_half, k_half, v_half = (halves(w_qkv[i]) for i in range(3))
    tail = jnp.broadcast_to(jnp.pad(low_tok, ((0, rows - 2), (0, 0))), (2, rows, tok // 2))
    urgent = jnp.concatenate([interleaved(k_half, v_half), q_half, tail], axis=2)
    urgent = jnp.pad(urgent, ((0, 0), (0, 16 - rows), (0, 0)))
    urgent = jnp.broadcast_to(urgent[None], (32, *urgent.shape)).reshape(64, 16, -1)
    w_urgent = lax.all_to_all(urgent, CTX, 0, 0, tiled=True)
    seg_all = w_urgent[:, :2, kv_cols + feat :].reshape(-1, tok).astype(jnp.int32)
    w_urgent = w_urgent.reshape(64 * 16, -1)
    at_wide = jnp.arange(64 * 16, dtype=jnp.int32)
    at_feature = jnp.arange(64 * rows, dtype=jnp.int32)
    spread = (
        (at_feature // rows * 16 + at_feature % rows)[:, None] == at_wide[None, :]
    ).astype(BF16)
    hid_wide = dot(hid, spread).astype(BF16)

    later = jnp.concatenate([halves(w) for w in (out_turned, w_up, down_turned)], axis=2)
    mine = lax.dynamic_index_in_dim(later, core, 0, keepdims=False)
    theirs = lax.dynamic_index_in_dim(later, 1 - core, 0, keepdims=False)
    later = pair_ordered(mine, shifted(theirs, "core", 1), "core").reshape(2 * rows, -1)
    rest = lax.all_gather(later, CHIPS, axis=0, tiled=True)
    w_out_t = rest[:, :feat]
    w_up_all = rest[:, feat : feat + hidden_units]
    w_down_t = rest[:, feat + hidden_units :]

    bias = b_qv.astype(F32)
    q_bias, v_bias = core_half(bias[0], 0, core), core_half(bias[1], 0, core)
    no_bias = jnp.zeros((tok // 2,), F32)
    bias_row = jnp.concatenate([interleaved(jnp.zeros_like(v_bias), v_bias), q_bias, no_bias])
    projected = (dot(hid_wide, w_urgent) + bias_row).astype(BF16)
    kv_own = projected[:, :kv_cols]
    queries = (projected[:, kv_cols : kv_cols + feat] * HEAD_DIM ** (-0.5)).astype(BF16)
    q_heads = jnp.pad(
        jnp.swapaxes(queries.reshape(2 * tok, HEADS_DEV, HEAD_DIM), 0, 1),
        ((0, 0), (0, 0), (0, HEAD_DIM)),
    )

    starts = [jnp.sum((seg_all < s).astype(jnp.int32)) for s in range(3)]
    places = jnp.arange(seg_all.size, dtype=jnp.int32).reshape(seg_all.shape)
    run_end = jnp.zeros_like(seg_all)
    for s in range(3):
        run_end = jnp.where(seg_all == s, starts[s] + lengths[s], run_end)
    tag_all = jnp.where(places < run_end, seg_all, -1).astype(F32)
    order = jnp.concatenate([relative_order("z", "y", 0), relative_order("y", "z", 1)])
    tags = jnp.take(tag_all, order, axis=0).reshape(8, -1)
    both = jnp.stack([own_ctx, own_ctx + 1 - 2 * core])
    tag_own = jnp.take(tag_all, both, axis=0).reshape(-1, 1)
    seg_own = jnp.take(seg_all, both, axis=0).astype(F32).reshape(-1, 1)

    sent = jnp.concatenate([kv_own, queries, jnp.zeros((2 * tok, HEAD_DIM), BF16)], axis=1)
    kv_z, q_z, kv_y, q_y = lax.optimization_barrier(gather_first(sent, (kv_cols, 256)))
    kv_blocks = gather_second(kv_z, kv_y)
    near_tags = jnp.concatenate([tags[:3], tags[4:7]], axis=0)
    far_tags = jnp.concatenate([tags[3:4], tags[7:]], axis=0)
    state = attend_near(q_heads, kv_own, near_tags, seg_own, tag_own, near_blocks(kv_blocks))
    kv_far, q_z, q_y = lax.optimization_barrier((far_blocks(kv_blocks), q_z, q_y))
    kv_blocks = kv_blocks[:3] + kv_far[:2] + kv_blocks[5:8] + kv_far[2:]
    q_blocks = gather_second(q_z, q_y)
    attended, stat = attend_far(q_heads, far_tags, seg_own, state, kv_far)
    attended_low = attended.astype(BF16)

    gain_rows = norm_gains.astype(F32)
    shifts = norm_shifts.astype(F32)
    attn_mixed = team_sum(dot_nt(attended_low, w_out_t))
    first_out, normed_one, inverse_one = layer_norm(
        hidden.astype(F32) + attn_mixed + shifts[0], gain_rows[0], shifts[1]
    )
    first_low = chip_tokens(first_out.astype(BF16))
    up_bias = core_half(b_up, 0, core).astype(F32)
    up_proj = dot(first_low, w_up_all) + up_bias
    activated = exact_gelu(up_proj).astype(BF16)
    second = team_sum(dot_nt(activated, w_down_t))
    output, normed_two, inverse_two = layer_norm(
        first_out + second + shifts[2], gain_rows[1], shifts[3]
    )
    resid_two, gain_two_grad, beta_two_grad = norm_back(
        cotangent.astype(F32), normed_two, inverse_two, gain_rows[1]
    )
    branch_low = chip_tokens(resid_two.astype(BF16))
    act_grad = dot(branch_low, w_down_t)
    up_low = jax.vjp(exact_gelu, up_proj)[1](act_grad)[0].astype(BF16)
    first_grad = resid_two + team_sum(dot_nt(up_low, w_up_all))
    up_sums = sums_by_owner(
        hidden_grads(spread, branch_low, activated, first_low, up_low).reshape(64, 16, -1)
    )
    upbias_grad = jnp.sum(up_low.astype(F32), axis=0)
    resid_one, gain_one_grad, beta_one_grad = norm_back(
        first_grad, normed_one, inverse_one, gain_rows[0]
    )
    mixed_low = chip_tokens(resid_one.astype(BF16))
    g_sent, g_heads, delta = grad_rows(mixed_low, w_out_t, attended, stat, seg_own)
    (g_z, g_y), g_heads = lax.optimization_barrier((gather_first(g_sent, (256,)), g_heads))
    g_blocks = gather_second(g_z, g_y)

    dq, diagonal = query_back(
        q_heads, g_heads, kv_own, tags, seg_own, tag_own, stat, delta, kv_blocks
    )
    wide_mixed = dot(mixed_low, spread).astype(BF16)
    q_part = jnp.concatenate([dot_tn(hid_wide, dq), dot_tn(wide_mixed, attended_low)], axis=1)
    q_sums = sums_by_owner(q_part.astype(BF16).reshape(64, 16, -1))
    lane = jnp.arange(256, dtype=jnp.int32)
    split = kv_own.reshape(2 * tok, HEADS_DEV, 2, HEAD_DIM)
    extras = jnp.where(
        (lane >= feat + 18) & (lane < feat + 21),
        jnp.where(tag_own == (lane - feat - 18).astype(F32), NEG, 0.0),
        jnp.where((lane == feat + 21) & (tag_own < 0), NEG, 0.0),
    )

    def spread_heads(x, stat_at, more):
        wide = jnp.pad(x.reshape(2 * tok, feat).astype(F32), ((0, 0), (0, 256 - feat)))
        made = []
        for h in range(HEADS_DEV):
            in_head = (lane >= h * HEAD_DIM) & (lane < (h + 1) * HEAD_DIM)
            in_stat = (lane >= stat_at + 3 * h) & (lane < stat_at + 3 * h + 3)
            made.append(jnp.where(in_head, wide, jnp.where(in_stat, -1.0, more)))
        return jnp.stack(made).astype(BF16)

    k_heads = spread_heads(split[:, :, 0], feat + 9, extras)
    v_heads = spread_heads(split[:, :, 1], feat, jnp.zeros_like(extras))
    key_state = key_near(k_heads, v_heads, near_blocks(q_blocks), near_blocks(g_blocks))
    dkv = key_far(
        k_heads, v_heads, diagonal, key_state, far_blocks(q_blocks), far_blocks(g_blocks)
    )

    w_compact = dot(spread, w_urgent[:, : kv_cols + feat]).astype(BF16)
    back = jnp.concatenate([dkv, dq], axis=1)
    hidden_grad = resid_one + team_sum(dot_nt(back, w_compact))

    def placed_half(x):
        zero = jnp.zeros_like(x)
        return jnp.concatenate(
            [jnp.where(core == 0, x, zero), jnp.where(core == 0, zero, x)], axis=-1
        )

    dv = dkv.reshape(2 * tok, HEADS_DEV, 2, HEAD_DIM)[:, :, 1].reshape(2 * tok, feat)
    qv_grad = jnp.stack([jnp.sum(dq.astype(F32), axis=0), jnp.sum(dv.astype(F32), axis=0)])
    vectors = jnp.stack(
        [
            gain_one_grad,
            gain_two_grad,
            jnp.sum(resid_one, axis=0),
            beta_one_grad,
            jnp.sum(resid_two, axis=0),
            beta_two_grad,
        ]
    )

    def by_owner(x):
        return jnp.swapaxes(x.reshape(x.shape[0], 64, -1), 0, 1).reshape(64, -1)

    small = jnp.concatenate(
        [by_owner(placed_half(qv_grad)), by_owner(placed_half(upbias_grad)[None]), by_owner(vectors)],
        axis=1,
    )
    small = jnp.pad(small, ((0, 0), (0, 128 - small.shape[1]))).reshape(64, 2, 64)
    small = jnp.pad(small, ((0, 0), (0, 14), (0, 0))).astype(BF16)
    kv_part = dot_tn(hid_wide, dkv).astype(BF16).reshape(64, 16, -1)
    kv_sums = sums_by_owner(jnp.concatenate([kv_part, small], axis=2))

    def columns(x, start, size):
        return jnp.concatenate([x[c, :rows, start : start + size] for c in range(2)], axis=1)

    kv_pairs = columns(kv_sums, 0, kv_cols).reshape(rows, 2 * HEADS_DEV, 2, HEAD_DIM)
    k_cols = kv_pairs[:, :, 0].reshape(rows, -1)
    v_cols = kv_pairs[:, :, 1].reshape(rows, -1)
    q_cols = columns(q_sums, 0, feat)
    out_cols = columns(q_sums, feat, feat)
    up_cols = columns(up_sums, 0, hidden_units)
    down_cols = columns(up_sums, hidden_units, hidden_units)
    tail = (kv_sums[0] + kv_sums[1])[:2, kv_cols:].reshape(-1)
    qv_out = tail[:12].reshape(2, 6)
    bias_out = tail[12:36]
    vec_out = tail[36:108].reshape(6, 2, 6)
    vec_out = lax.dynamic_index_in_dim(vec_out, heads_at, 1, keepdims=False)
    return (
        output.astype(BF16),
        hidden_grad,
        jnp.stack([q_cols, k_cols, v_cols]),
        out_cols.T,
        qv_out,
        up_cols,
        down_cols.T,
        bias_out,
        vec_out[:2],
        vec_out[2:],
    )


def solution(mesh):
    fine = Mesh(mesh.devices.reshape(4, 4, 2, 2, 2), ("z", "y", "xh", "core", "heads"))
    return jax.shard_map(
        per_device,
        mesh=fine,
        in_specs=(
            P(CTX, None),
            P(None, CTX, "heads"),
            P("heads", CTX),
            P(None, "heads"),
            P(CTX, "heads"),
            P("heads", CTX),
            P("heads"),
            P(),
            P(),
            P(CTX),
            P(),
            P(CTX, None),
        ),
        out_specs=(
            P(CTX, None),
            P(CTX, None),
            P(None, CTX, "heads"),
            P("heads", CTX),
            P(None, ("heads", *CTX)),
            P(CTX, "heads"),
            P("heads", CTX),
            P(("heads", *CTX)),
            P(None, (*CTX, "heads")),
            P(None, (*CTX, "heads")),
        ),
        check_vma=False,
    )
```

```python
import jax
import jax.numpy as jnp
from jax import lax
from jax.experimental import pallas as pl
from jax.experimental.pallas import tpu as pltpu
from jax.sharding import Mesh, PartitionSpec as P

HEAD_DIM = 64
HEADS_DEV = 3
EPS = 1e-06
NEG = -1e30
CTX = ("z", "y", "xh", "core")
CHIPS = ("z", "y", "xh")
F32 = jnp.float32
BF16 = jnp.bfloat16
NT = (((1,), (1,)), ((), ()))
VMEM_LIMIT = 50 * 1024 * 1024
OFFSETS = (0, -1, 1, 2)


def shifted(x, axis, step):
    n = lax.axis_size(axis)
    return lax.ppermute(x, axis, [(i, (i + step) % n) for i in range(n)])


def ring_halves(x, axis):
    half = x.shape[0] // 2
    before, after = shifted(x, axis, 1), shifted(x, axis, -1)
    return [x, before, after, shifted(before[:half], axis, 1), shifted(after[half:], axis, -1)]


def gather_first(x):
    half = x.shape[0] // 2
    streams = []
    for part, axis in ((x[:half], "z"), (x[half:], "y")):
        both = jnp.concatenate([part, shifted(part, "xh", 1)], axis=0)
        streams.append(jnp.concatenate(ring_halves(both, axis), axis=0))
    return tuple(streams)


def gather_second(z_stream, y_stream):
    blocks = ring_halves(z_stream, "y") + ring_halves(y_stream, "z")
    return [b.reshape(-1, z_stream.shape[0] // 2, b.shape[1]) for b in blocks]


def near_blocks(blocks):
    return blocks[:3] + blocks[5:8]


def far_blocks(blocks):
    return blocks[3:5] + blocks[8:]


def relative_order(first, second, core_at):
    place = {a: lax.axis_index(a) for a in CHIPS}
    core = lax.axis_index("core")
    order = []
    for second_step in OFFSETS:
        for first_step in OFFSETS:
            for xh_step in (0, 1):
                at = dict(place)
                at[first] = (at[first] + first_step) % 4
                at[second] = (at[second] + second_step) % 4
                at["xh"] = (at["xh"] + xh_step) % 2
                order.append(((at["z"] * 4 + at["y"]) * 2 + at["xh"]) * 2 + (core + core_at) % 2)
    return jnp.stack(order)


def pair_ordered(own, other, axis):
    first = lax.axis_index(axis) == 0
    return jnp.stack([jnp.where(first, own, other), jnp.where(first, other, own)])


def to_owners(x):
    return lax.all_to_all(x.reshape(64, 16, -1), CTX, 0, 0, tiled=True)


def owner_sums(parts):
    return jnp.sum(parts.reshape(-1, 2, *parts.shape[1:]).astype(F32), axis=0)


def team_sum(partial):
    rows = partial.shape[0] // 2
    near = partial[:rows] + shifted(partial[rows:].astype(BF16), "core", 1).astype(F32)
    low = lax.optimization_barrier(near.astype(BF16))
    return low.astype(F32) + shifted(low, "heads", 1).astype(F32)


def chip_tokens(x):
    return jnp.concatenate([x, shifted(x, "core", 1)], axis=0)


def layer_norm(residual, gain_row, shift_row):
    centred = residual - jnp.mean(residual, axis=-1, keepdims=True)
    inverse = lax.rsqrt(jnp.mean(centred * centred, axis=-1, keepdims=True) + EPS)
    normed = centred * inverse
    return (normed * gain_row + shift_row, normed, inverse)


def norm_back(incoming, normed, inverse, gain_row):
    scaled = incoming * gain_row
    projected = (
        scaled
        - jnp.mean(scaled, axis=-1, keepdims=True)
        - normed * jnp.mean(scaled * normed, axis=-1, keepdims=True)
    )
    return inverse * projected


def exact_gelu(pre_act):
    return jax.nn.gelu(pre_act, approximate=False)


def pieces_of(column):
    high = column.astype(BF16).astype(F32)
    middle = (column - high).astype(BF16).astype(F32)
    return high, middle, column - high - middle


def head_columns(h):
    return slice(h * HEAD_DIM, (h + 1) * HEAD_DIM)


def head_block(h):
    return slice(h * 128, (h + 1) * 128)


def diagonal_scores(q_ref, kv_ref, h):
    product = q_ref[h].astype(F32) * kv_ref[:, head_block(h)].astype(F32)
    return jnp.sum(product, axis=1, keepdims=True)


def copies_in(sources, buffer, sems, first_lane=0):
    at = 0
    lanes = pl.ds(first_lane, buffer.shape[2])
    for source in sources:
        size = source.shape[0]
        pltpu.make_async_copy(
            source.at[:, :, lanes], buffer.at[pl.ds(at, size)], sems.at[at // 2]
        ).start()
        at += size


def block_of(buffer, sems, j):
    block = buffer.at[pl.ds(2 * j, 2)]
    pltpu.make_async_copy(block, block, sems.at[j]).wait()
    return buffer[pl.ds(2 * j, 2)].reshape(-1, buffer.shape[2])


def attend_blocks(q_ref, tags_ref, seg_ref, top, total, acc, buffer, sems, row_of):
    rows = q_ref.shape[1]
    seg_wide = jnp.broadcast_to(seg_ref[...], (rows, 128))

    def step(j, carry):
        whole = block_of(buffer, sems, j)
        tags = tags_ref[pl.ds(row_of(j), 1), :]
        keys = tags.shape[1]
        allowed = jnp.tile(seg_wide, (1, keys // 128)) == tags
        for h in range(HEADS_DEV):
            kv = whole[:, head_block(h)]
            scores = lax.dot_general(q_ref[h], kv, NT, preferred_element_type=F32)
            scores = jnp.where(allowed, scores, NEG)
            before = top[h]
            now = jnp.maximum(before, jnp.max(scores, axis=1, keepdims=True))
            weights = jnp.exp(scores - jnp.tile(now, (1, keys // 128)))
            fade = jnp.exp(before - now)
            sums = weights[:, :128]
            for k in range(1, keys // 128):
                sums = sums + weights[:, k * 128 : (k + 1) * 128]
            total[h] = total[h] * fade + sums
            acc[h] = acc[h] * fade + jnp.dot(weights.astype(BF16), kv, preferred_element_type=F32)
            top[h] = now
        return carry

    lax.fori_loop(0, sems.shape[0], step, 0)


def near_row(j):
    return j + (j >= 3).astype(jnp.int32)


def far_row(j):
    return 4 * j + 3


def attend_near_kernel(q_ref, own_ref, tags_ref, seg_ref, tag_ref, *rest):
    blocks, (top, total, acc, buffer, sems) = rest[:6], rest[6:]
    copies_in(blocks, buffer, sems)
    rows = q_ref.shape[1]
    padded = tag_ref[...] < 0
    for h in range(HEADS_DEV):
        diagonal = diagonal_scores(q_ref, own_ref, h)
        top[h] = jnp.broadcast_to(jnp.where(padded, diagonal, NEG), (rows, 128))
        lane = lax.broadcasted_iota(jnp.int32, (rows, 128), 1)
        total[h] = jnp.where((lane == 0) & padded, 1.0, 0.0)
        acc[h] = jnp.where(padded, own_ref[:, head_block(h)].astype(F32), 0.0)
    attend_blocks(q_ref, tags_ref, seg_ref, top, total, acc, buffer, sems, near_row)


def attend_far_kernel(q_ref, tags_ref, seg_ref, top_in, total_in, acc_in, *rest):
    blocks, (out_ref, stat_ref, top, total, acc, buffer, sems) = rest[:4], rest[4:]
    copies_in(blocks, buffer, sems)
    top[...], total[...], acc[...] = top_in[...], total_in[...], acc_in[...]
    attend_blocks(q_ref, tags_ref, seg_ref, top, total, acc, buffer, sems, far_row)
    outs = []
    for h in range(HEADS_DEV):
        sums = jnp.sum(total[h], axis=1, keepdims=True)
        outs.append((acc[h] / sums)[:, HEAD_DIM:])
        stat_ref[h] = top[h] + jnp.log(sums)
    out_ref[...] = jnp.concatenate(outs, axis=1)


def vmem_specs(n):
    return [pl.BlockSpec(memory_space=pltpu.VMEM)] * n


def any_specs(n):
    return [pl.BlockSpec(memory_space=pl.ANY)] * n


def head_state(rows, lanes=128):
    return jax.ShapeDtypeStruct((HEADS_DEV, rows, lanes), F32)


def cost(rows, blocks, flops):
    keys = sum(b.shape[0] * b.shape[1] for b in blocks)
    pairs = rows * keys * HEADS_DEV
    return pl.CostEstimate(
        flops=pairs * flops, bytes_accessed=keys * 1024, transcendentals=pairs
    )


def buffers(blocks, lanes):
    count = sum(b.shape[0] for b in blocks)
    return [
        pltpu.VMEM((count, blocks[0].shape[1], lanes), BF16),
        pltpu.SemaphoreType.DMA((count // 2,)),
    ]


def attend_near(q_heads, kv_own, tags, seg, tag, blocks):
    rows = kv_own.shape[0]
    return pl.pallas_call(
        attend_near_kernel,
        out_shape=(head_state(rows),) * 3,
        in_specs=vmem_specs(5) + any_specs(6),
        out_specs=tuple(vmem_specs(3)),
        scratch_shapes=buffers(blocks, kv_own.shape[1]),
        compiler_params=pltpu.CompilerParams(vmem_limit_bytes=VMEM_LIMIT),
        cost_estimate=cost(rows, blocks, 512),
        name="attend_near",
    )(q_heads, kv_own, tags, seg, tag, *blocks)


def attend_far(q_heads, tags, seg, state, blocks):
    rows = q_heads.shape[1]
    return pl.pallas_call(
        attend_far_kernel,
        out_shape=(jax.ShapeDtypeStruct((rows, HEADS_DEV * HEAD_DIM), F32), head_state(rows)),
        in_specs=vmem_specs(6) + any_specs(4),
        out_specs=tuple(vmem_specs(2)),
        scratch_shapes=[pltpu.VMEM((HEADS_DEV, rows, 128), F32)] * 3
        + buffers(blocks, HEADS_DEV * 128),
        compiler_params=pltpu.CompilerParams(vmem_limit_bytes=VMEM_LIMIT),
        cost_estimate=cost(rows, blocks, 512),
        name="attend_far",
    )(q_heads, tags, seg, *state, *blocks)


def query_back_kernel(q_ref, g_ref, own_ref, tags_ref, seg_ref, tag_ref, stat_ref, delta_ref, *rest):
    blocks, (dq_ref, dkv_ref, buffer, sems, acc) = rest[:10], rest[10:]
    copies_in(blocks, buffer, sems)
    rows = q_ref.shape[1]
    seg_wide = jnp.broadcast_to(seg_ref[...], (rows, 128))
    padded = tag_ref[...] < 0
    for h in range(HEADS_DEV):
        own = own_ref[:, head_block(h)].astype(F32)
        prob = jnp.exp(diagonal_scores(q_ref, own_ref, h) - stat_ref[h][:, :1])
        prob = jnp.where(padded, prob, 0.0)
        grad = diagonal_scores(g_ref, own_ref, h) - delta_ref[h][:, :1]
        score = (prob * grad).astype(BF16).astype(F32)
        acc[h] = score * own
        dkv_ref[:, head_block(h)] = score * q_ref[h].astype(F32) + prob.astype(BF16).astype(
            F32
        ) * g_ref[h].astype(F32)

    def step(j, carry):
        whole = block_of(buffer, sems, j)
        tags = tags_ref[pl.ds(jnp.where(j < 6, near_row(j), far_row(j - 6)), 1), :]
        keys = tags.shape[1]
        allowed = jnp.tile(seg_wide, (1, keys // 128)) == tags
        for h in range(HEADS_DEV):
            kv = whole[:, head_block(h)]
            scores = lax.dot_general(q_ref[h], kv, NT, preferred_element_type=F32)
            scores = jnp.where(allowed, scores, NEG)
            probs = jnp.exp(scores - jnp.tile(stat_ref[h], (1, keys // 128)))
            grads = lax.dot_general(g_ref[h], kv, NT, preferred_element_type=F32)
            back = probs * (grads - jnp.tile(delta_ref[h], (1, keys // 128)))
            acc[h] = acc[h] + jnp.dot(back.astype(BF16), kv, preferred_element_type=F32)
        return carry

    lax.fori_loop(0, 8, step, 0)
    dq_ref[...] = (
        jnp.concatenate([acc[h][:, :HEAD_DIM] for h in range(HEADS_DEV)], axis=1)
        * HEAD_DIM ** (-0.5)
    ).astype(BF16)


def query_back(q_heads, g_heads, kv_own, tags, seg, tag, stat, delta, blocks):
    rows = kv_own.shape[0]
    return pl.pallas_call(
        query_back_kernel,
        out_shape=(
            jax.ShapeDtypeStruct((rows, HEADS_DEV * HEAD_DIM), BF16),
            jax.ShapeDtypeStruct(kv_own.shape, F32),
        ),
        in_specs=vmem_specs(8) + any_specs(10),
        out_specs=tuple(vmem_specs(2)),
        scratch_shapes=buffers(blocks, kv_own.shape[1]) + [pltpu.VMEM((HEADS_DEV, rows, 128), F32)],
        compiler_params=pltpu.CompilerParams(vmem_limit_bytes=VMEM_LIMIT),
        cost_estimate=cost(rows, blocks, 768),
        name="query_back",
    )(q_heads, g_heads, kv_own, tags, seg, tag, stat, delta, *blocks)


def grad_rows_kernel(
    mixed_ref, out_ref, attended_ref, stat_ref, seg_ref, sent_ref, g_ref, delta_ref
):
    rows = mixed_ref.shape[0]
    grad = jnp.dot(mixed_ref[...], out_ref[...], preferred_element_type=F32).astype(BF16)
    grad = grad.astype(F32)
    product = grad * attended_ref[...]
    lane = lax.broadcasted_iota(jnp.int32, (rows, HEAD_DIM), 1)
    seg = seg_ref[...]
    extra = jnp.where(lane == 21, 1.0, 0.0)
    for s in range(3):
        extra = extra + jnp.where((lane == 18 + s) & (seg != s), 1.0, 0.0)
    zeros = jnp.zeros((rows, HEAD_DIM), BF16)
    for h in range(HEADS_DEV):
        delta = jnp.sum(product[:, head_columns(h)], axis=1, keepdims=True)
        delta_ref[h] = jnp.broadcast_to(delta, (rows, 128))
        for i, piece in enumerate(pieces_of(delta)):
            extra = extra + jnp.where(lane == 3 * h + i, piece, 0.0)
        for i, piece in enumerate(pieces_of(stat_ref[h][:, :1])):
            extra = extra + jnp.where(lane == 9 + 3 * h + i, piece, 0.0)
        g_ref[h] = jnp.concatenate([zeros, grad[:, head_columns(h)].astype(BF16)], axis=1)
    sent_ref[...] = jnp.concatenate([grad, extra], axis=1).astype(BF16)


def grad_rows(mixed, w_out, attended, stat, seg):
    rows = mixed.shape[0]
    return pl.pallas_call(
        grad_rows_kernel,
        out_shape=(
            jax.ShapeDtypeStruct((rows, 256), BF16),
            jax.ShapeDtypeStruct((HEADS_DEV, rows, 128), BF16),
            jax.ShapeDtypeStruct((HEADS_DEV, rows, 128), F32),
        ),
        in_specs=vmem_specs(5),
        out_specs=tuple(vmem_specs(3)),
        compiler_params=pltpu.CompilerParams(vmem_limit_bytes=VMEM_LIMIT),
        name="grad_rows",
    )(mixed, w_out, attended, stat, seg)


def send_out(held, out_ref, sem):
    copy = pltpu.make_async_copy(held, out_ref, sem)
    copy.start()
    copy.wait()


def early_grads_kernel(
    spread_ref, branch_ref, activated_ref, first_ref, up_ref, mixed_ref, attended_ref, *rest
):
    out_ref, held, sem = rest
    pairs = ((first_ref, up_ref), (branch_ref, activated_ref), (mixed_ref, attended_ref))
    at = 0
    for left, right in pairs:
        wide = jnp.dot(left[...], spread_ref[...], preferred_element_type=F32).astype(BF16)
        part = dot_tn(wide, right[...]).astype(BF16)
        if part.shape[1] % 128:
            part = jnp.concatenate([part, jnp.zeros((part.shape[0], 64), BF16)], axis=1)
        held[:, at : at + part.shape[1]] = part
        at += part.shape[1]
    send_out(held, out_ref, sem)


def early_grads(spread, branch, activated, first, up, mixed, attended):
    shape = (spread.shape[1], 2 * up.shape[1] + attended.shape[1] + 64)
    return pl.pallas_call(
        early_grads_kernel,
        out_shape=jax.ShapeDtypeStruct(shape, BF16),
        in_specs=vmem_specs(7),
        out_specs=pl.BlockSpec(memory_space=pltpu.HBM),
        scratch_shapes=[pltpu.VMEM(shape, BF16), pltpu.SemaphoreType.DMA],
        compiler_params=pltpu.CompilerParams(vmem_limit_bytes=VMEM_LIMIT),
        name="early_grads",
    )(spread, branch, activated, first, up, mixed, attended)


def vector_rows_kernel(
    cot_ref, two_ref, resid_two_ref, first_ref, one_ref, resid_one_ref, up_ref, spread_ref, bias_ref,
    parts_ref, out_ref,
):
    cot, first = cot_ref[...].astype(F32), first_ref[...]
    columns = (
        first * one_ref[...],
        cot * two_ref[...],
        resid_one_ref[...],
        first,
        resid_two_ref[...],
        cot,
    )
    rows = jnp.concatenate([jnp.sum(c, axis=0, keepdims=True) for c in columns], axis=0)
    bias = jnp.sum(up_ref[...].astype(F32), axis=0, keepdims=True) * parts_ref[...]
    made = [
        jnp.dot(rows.astype(BF16), spread_ref[...], preferred_element_type=F32),
        jnp.dot(bias.astype(BF16), bias_ref[...], preferred_element_type=F32),
    ]
    out_ref[...] = jnp.concatenate(made, axis=0)


def vector_rows(spread, *args):
    return pl.pallas_call(
        vector_rows_kernel,
        out_shape=jax.ShapeDtypeStruct((8, spread.shape[1]), F32),
        in_specs=vmem_specs(10),
        out_specs=vmem_specs(1)[0],
        compiler_params=pltpu.CompilerParams(vmem_limit_bytes=VMEM_LIMIT),
        name="vector_rows",
    )(*args)


def late_grads_kernel(hid_ref, dkv_ref, dq_ref, rows_ref, q_place_ref, v_place_ref, out_ref, held, sem):
    wide = hid_ref.shape[1]
    kv_cols, feat = dkv_ref.shape[1], dq_ref.shape[1]
    held[:, :kv_cols] = dot_tn(hid_ref[...], dkv_ref[...]).astype(BF16)
    sums = [rows_ref[...]]
    for grad, place in ((dq_ref, q_place_ref), (dkv_ref, v_place_ref)):
        row = jnp.sum(grad[...].astype(F32), axis=0, keepdims=True).astype(BF16)
        sums.append(jnp.dot(row, place[...], preferred_element_type=F32))
    sums.append(jnp.zeros((128 - 10, wide), F32))
    small = jnp.transpose(jnp.concatenate(sums, axis=0))[:, :64]
    q_part = dot_tn(hid_ref[...], dq_ref[...])
    held[:, kv_cols:] = jnp.concatenate([q_part, small], axis=1).astype(BF16)
    send_out(held, out_ref, sem)


def late_grads(hid, dkv, dq, rows, q_place, v_place):
    shape = (hid.shape[1], dkv.shape[1] + dq.shape[1] + 64)
    return pl.pallas_call(
        late_grads_kernel,
        out_shape=jax.ShapeDtypeStruct(shape, BF16),
        in_specs=vmem_specs(6),
        out_specs=pl.BlockSpec(memory_space=pltpu.HBM),
        scratch_shapes=[pltpu.VMEM(shape, BF16), pltpu.SemaphoreType.DMA],
        compiler_params=pltpu.CompilerParams(vmem_limit_bytes=VMEM_LIMIT),
        name="late_grads",
    )(hid, dkv, dq, rows, q_place, v_place)


def project_kernel(hid_ref, w_ref, bias_ref, scale_ref, sent_ref, q_ref):
    made = jnp.dot(hid_ref[...], w_ref[...], preferred_element_type=F32) + bias_ref[...]
    made = (made.astype(BF16).astype(F32) * scale_ref[...]).astype(BF16)
    sent_ref[...] = made
    zeros = jnp.zeros((made.shape[0], HEAD_DIM), BF16)
    for h in range(HEADS_DEV):
        at = 2 * HEADS_DEV * HEAD_DIM + h * HEAD_DIM
        q_ref[h] = jnp.concatenate([made[:, at : at + HEAD_DIM], zeros], axis=1)


def project(hid, w, bias, scale):
    rows = hid.shape[0]
    return pl.pallas_call(
        project_kernel,
        out_shape=(
            jax.ShapeDtypeStruct((rows, w.shape[1]), BF16),
            jax.ShapeDtypeStruct((HEADS_DEV, rows, 128), BF16),
        ),
        in_specs=vmem_specs(4),
        out_specs=tuple(vmem_specs(2)),
        compiler_params=pltpu.CompilerParams(vmem_limit_bytes=VMEM_LIMIT),
        name="project",
    )(hid, w, bias, scale)


def key_back_blocks(k_ref, v_ref, k_acc, v_acc, q_buffer, g_buffer, q_sems, g_sems):
    def step(j, carry):
        queries = block_of(q_buffer, q_sems, j)
        grads = block_of(g_buffer, g_sems, j)
        lane = lax.broadcasted_iota(jnp.int32, queries.shape, 1)
        queries = jnp.where(lane < HEADS_DEV * HEAD_DIM, queries, grads)
        for h in range(HEADS_DEV):
            scores = lax.dot_general(k_ref[h], queries, NT, preferred_element_type=F32)
            probs = jnp.exp(scores)
            v_acc[h] = v_acc[h] + jnp.dot(probs.astype(BF16), grads, preferred_element_type=F32)
            back = probs * lax.dot_general(v_ref[h], grads, NT, preferred_element_type=F32)
            k_acc[h] = k_acc[h] + jnp.dot(back.astype(BF16), queries, preferred_element_type=F32)
        return carry

    lax.fori_loop(0, q_sems.shape[0], step, 0)


def key_near_kernel(k_ref, v_ref, *rest):
    q_blocks, g_blocks = rest[:6], rest[6:12]
    k_acc, v_acc, q_buffer, q_sems, g_buffer, g_sems = rest[12:]
    copies_in(q_blocks, q_buffer, q_sems, 2 * HEADS_DEV * HEAD_DIM)
    copies_in(g_blocks, g_buffer, g_sems)
    k_acc[...] = jnp.zeros_like(k_acc)
    v_acc[...] = jnp.zeros_like(v_acc)
    key_back_blocks(k_ref, v_ref, k_acc, v_acc, q_buffer, g_buffer, q_sems, g_sems)


def key_far_kernel(k_ref, v_ref, diag_ref, k_in, v_in, *rest):
    q_blocks, g_blocks = rest[:4], rest[4:8]
    dkv_ref, k_acc, v_acc, q_buffer, q_sems, g_buffer, g_sems = rest[8:]
    copies_in(q_blocks, q_buffer, q_sems, 2 * HEADS_DEV * HEAD_DIM)
    copies_in(g_blocks, g_buffer, g_sems)
    k_acc[...], v_acc[...] = k_in[...], v_in[...]
    key_back_blocks(k_ref, v_ref, k_acc, v_acc, q_buffer, g_buffer, q_sems, g_sems)
    parts = []
    for h in range(HEADS_DEV):
        parts += [k_acc[h][:, head_columns(h)], v_acc[h][:, head_columns(h)]]
    dkv_ref[...] = (jnp.concatenate(parts, axis=1) + diag_ref[...]).astype(BF16)


def key_near(k_heads, v_heads, q_blocks, g_blocks):
    rows, width = k_heads.shape[1:]
    return pl.pallas_call(
        key_near_kernel,
        out_shape=(head_state(rows, width),) * 2,
        in_specs=vmem_specs(2) + any_specs(12),
        out_specs=tuple(vmem_specs(2)),
        scratch_shapes=buffers(q_blocks, width) + buffers(g_blocks, width),
        compiler_params=pltpu.CompilerParams(vmem_limit_bytes=VMEM_LIMIT),
        cost_estimate=cost(rows, q_blocks, 2048),
        name="key_near",
    )(k_heads, v_heads, *q_blocks, *g_blocks)


def key_far(k_heads, v_heads, diagonal, state, q_blocks, g_blocks):
    rows, width = k_heads.shape[1:]
    return pl.pallas_call(
        key_far_kernel,
        out_shape=jax.ShapeDtypeStruct(diagonal.shape, BF16),
        in_specs=vmem_specs(5) + any_specs(8),
        out_specs=vmem_specs(1)[0],
        scratch_shapes=[pltpu.VMEM((HEADS_DEV, rows, width), F32)] * 2
        + buffers(q_blocks, width)
        + buffers(g_blocks, width),
        compiler_params=pltpu.CompilerParams(vmem_limit_bytes=VMEM_LIMIT),
        cost_estimate=cost(rows, q_blocks, 2048),
        name="key_far",
    )(k_heads, v_heads, diagonal, *state, *q_blocks, *g_blocks)


def dot(a, b):
    return jnp.dot(a, b, preferred_element_type=F32)


def dot_nt(a, b):
    return lax.dot_general(a, b, NT, preferred_element_type=F32)


def dot_tn(a, b):
    return lax.dot_general(a, b, (((0,), (0,)), ((), ())), preferred_element_type=F32)


def core_half(x, axis, at):
    size = x.shape[axis] // 2
    return lax.dynamic_slice_in_dim(x, at * size, size, axis)


def interleaved(k, v):
    shape = (*k.shape[:-1], -1, HEAD_DIM)
    return jnp.stack([k.reshape(shape), v.reshape(shape)], axis=-2).reshape(*k.shape[:-1], -1)


def per_device(
    hidden,
    w_qkv,
    w_out,
    b_qv,
    w_up,
    w_down,
    b_up,
    norm_gains,
    norm_shifts,
    segments,
    lengths,
    cotangent,
):
    core = lax.axis_index("core")
    heads_at = lax.axis_index("heads")
    own_ctx = ((lax.axis_index("z") * 4 + lax.axis_index("y")) * 2 + lax.axis_index("xh")) * 2 + core
    tok = hidden.shape[0]
    rows = w_up.shape[0]
    feat = HEADS_DEV * HEAD_DIM
    hidden_units = w_up.shape[1] // 2

    hid = chip_tokens(hidden)
    out_turned, down_turned = w_out.T, w_down.T
    low_tok = segments.astype(BF16).reshape(2, tok // 2)
    kv_cols = 2 * feat

    def halves(x):
        return jnp.swapaxes(x.reshape(rows, 2, -1), 0, 1)

    q_half, k_half, v_half = (halves(w_qkv[i]) for i in range(3))
    tail = jnp.broadcast_to(jnp.pad(low_tok, ((0, rows - 2), (0, 0))), (2, rows, tok // 2))
    urgent = jnp.concatenate([interleaved(k_half, v_half), q_half, tail], axis=2)
    urgent = jnp.pad(urgent, ((0, 0), (0, 16 - rows), (0, 0)))
    urgent = jnp.broadcast_to(urgent[None], (32, *urgent.shape)).reshape(64, 16, -1)
    w_urgent = lax.all_to_all(urgent, CTX, 0, 0, tiled=True)
    seg_all = w_urgent[:, :2, kv_cols + feat :].reshape(-1, tok).astype(jnp.int32)
    w_urgent = w_urgent.reshape(64 * 16, -1)
    at_wide = jnp.arange(64 * 16, dtype=jnp.int32)
    at_feature = jnp.arange(64 * rows, dtype=jnp.int32)
    spread = (
        (at_feature // rows * 16 + at_feature % rows)[:, None] == at_wide[None, :]
    ).astype(BF16)
    hid_wide = dot(hid, spread).astype(BF16)

    later = jnp.concatenate([halves(w) for w in (out_turned, w_up, down_turned)], axis=2)
    mine = lax.dynamic_index_in_dim(later, core, 0, keepdims=False)
    theirs = lax.dynamic_index_in_dim(later, 1 - core, 0, keepdims=False)
    later = pair_ordered(mine, shifted(theirs, "core", 1), "core").reshape(2 * rows, -1)
    rest = lax.all_gather(later, CHIPS, axis=0, tiled=True)
    w_out_t = rest[:, :feat]
    w_up_all = rest[:, feat : feat + hidden_units]
    w_down_t = rest[:, feat + hidden_units :]

    bias = b_qv.astype(F32)
    q_bias, v_bias = core_half(bias[0], 0, core), core_half(bias[1], 0, core)
    no_bias = jnp.zeros((tok // 2,), F32)
    bias_row = jnp.concatenate([interleaved(jnp.zeros_like(v_bias), v_bias), q_bias, no_bias])
    column = jnp.arange(bias_row.shape[0], dtype=jnp.int32)
    scale_row = jnp.where(
        column < kv_cols, 1.0, jnp.where(column < kv_cols + feat, HEAD_DIM ** (-0.5), 0.0)
    ).astype(F32)
    sent, q_heads = project(hid_wide, w_urgent, bias_row[None], scale_row[None])
    kv_own = sent[:, :kv_cols]
    starts = [jnp.sum((seg_all < s).astype(jnp.int32)) for s in range(3)]
    places = jnp.arange(seg_all.size, dtype=jnp.int32).reshape(seg_all.shape)
    run_end = jnp.zeros_like(seg_all)
    for s in range(3):
        run_end = jnp.where(seg_all == s, starts[s] + lengths[s], run_end)
    tag_all = jnp.where(places < run_end, seg_all, -1).astype(F32)
    order = jnp.concatenate([relative_order("z", "y", 0), relative_order("y", "z", 1)])
    tags = jnp.take(tag_all, order, axis=0).reshape(8, -1)
    both = jnp.stack([own_ctx, own_ctx + 1 - 2 * core])
    tag_own = jnp.take(tag_all, both, axis=0).reshape(-1, 1)
    seg_own = jnp.take(seg_all, both, axis=0).astype(F32).reshape(-1, 1)

    sent_z, sent_y = lax.optimization_barrier(gather_first(sent))
    blocks = gather_second(sent_z, sent_y)
    near, far = near_blocks(blocks), far_blocks(blocks)
    state = attend_near(q_heads, kv_own, tags, seg_own, tag_own, near)
    attended, stat = attend_far(q_heads, tags, seg_own, state, far)
    attended_low = attended.astype(BF16)

    gain_rows = norm_gains.astype(F32)
    shifts = norm_shifts.astype(F32)
    attn_mixed = team_sum(dot_nt(attended_low, w_out_t))
    first_out, normed_one, inverse_one = layer_norm(
        hidden.astype(F32) + attn_mixed + shifts[0], gain_rows[0], shifts[1]
    )
    first_low = chip_tokens(first_out.astype(BF16))
    up_bias = core_half(b_up, 0, core).astype(F32)
    up_proj = dot(first_low, w_up_all) + up_bias
    activated = exact_gelu(up_proj).astype(BF16)
    second = team_sum(dot_nt(activated, w_down_t))
    output, normed_two, inverse_two = layer_norm(
        first_out + second + shifts[2], gain_rows[1], shifts[3]
    )
    resid_two = norm_back(
        cotangent.astype(F32), normed_two, inverse_two, gain_rows[1]
    )
    branch_low = chip_tokens(resid_two.astype(BF16))
    act_grad = dot(branch_low, w_down_t)
    up_low = jax.vjp(exact_gelu, up_proj)[1](act_grad)[0].astype(BF16)
    first_grad = resid_two + team_sum(dot_nt(up_low, w_up_all))
    resid_one = norm_back(first_grad, normed_one, inverse_one, gain_rows[0])
    mixed_low = chip_tokens(resid_one.astype(BF16))
    g_sent, g_heads, delta = grad_rows(mixed_low, w_out_t, attended, stat, seg_own)
    early = to_owners(
        early_grads(spread, branch_low, activated, first_low, up_low, mixed_low, attended_low)
    )
    (g_z, g_y), g_heads = lax.optimization_barrier((gather_first(g_sent), g_heads))
    g_blocks = gather_second(g_z, g_y)
    at_bias = jnp.arange(hidden_units, dtype=jnp.int32)
    at_half = jnp.arange(feat, dtype=jnp.int32)
    at_kv = jnp.arange(kv_cols, dtype=jnp.int32)

    def placed(owner, row):
        return ((owner * 16 + row)[:, None] == at_wide[None, :]).astype(BF16)

    first_owner = 32 * core
    bias_place = placed(first_owner + at_bias // 24, at_bias % 12)
    q_place = placed(first_owner + at_half // 6, at_half % 6)
    at_value = at_kv // 128 * HEAD_DIM + at_kv % 128 - HEAD_DIM
    is_value = at_kv % 128 >= HEAD_DIM
    v_place = placed(jnp.where(is_value, first_owner + at_value // 6, -1), at_value % 6)
    parts = jnp.arange(2, dtype=jnp.int32)[:, None] == (at_bias % 24 // 12)[None, :]
    rows_made = vector_rows(
        spread,
        cotangent,
        normed_two,
        resid_two,
        first_grad,
        normed_one,
        resid_one,
        up_low,
        spread,
        bias_place,
        parts.astype(F32),
    )

    dq, diagonal = query_back(
        q_heads, g_heads, kv_own, tags, seg_own, tag_own, stat, delta, near + far
    )
    lane = jnp.arange(256, dtype=jnp.int32)
    split = kv_own.reshape(2 * tok, HEADS_DEV, 2, HEAD_DIM)
    extras = jnp.where(
        (lane >= feat + 18) & (lane < feat + 21),
        jnp.where(tag_own == (lane - feat - 18).astype(F32), NEG, 0.0),
        jnp.where((lane == feat + 21) & (tag_own < 0), NEG, 0.0),
    )

    def spread_heads(x, stat_at, more):
        wide = jnp.pad(x.reshape(2 * tok, feat).astype(F32), ((0, 0), (0, 256 - feat)))
        made = []
        for h in range(HEADS_DEV):
            in_head = (lane >= h * HEAD_DIM) & (lane < (h + 1) * HEAD_DIM)
            in_stat = (lane >= stat_at + 3 * h) & (lane < stat_at + 3 * h + 3)
            made.append(jnp.where(in_head, wide, jnp.where(in_stat, -1.0, more)))
        return jnp.stack(made).astype(BF16)

    k_heads = spread_heads(split[:, :, 0], feat + 9, extras)
    v_heads = spread_heads(split[:, :, 1], feat, jnp.zeros_like(extras))
    key_state = key_near(k_heads, v_heads, near, near_blocks(g_blocks))
    g_far, early = lax.optimization_barrier((far_blocks(g_blocks), early))
    dkv = key_far(k_heads, v_heads, diagonal, key_state, far, g_far)
    late = to_owners(late_grads(hid_wide, dkv, dq, rows_made, q_place, v_place))

    w_compact = dot(spread, w_urgent[:, : kv_cols + feat]).astype(BF16)
    back = jnp.concatenate([dkv, dq], axis=1)
    hidden_grad = resid_one + team_sum(dot_nt(back, w_compact))

    early_sums, late_sums = owner_sums(early), owner_sums(late)

    def columns(x, start, size):
        return jnp.concatenate([x[c, :rows, start : start + size] for c in range(2)], axis=1)

    kv_pairs = columns(late_sums, 0, kv_cols).reshape(rows, 2 * HEADS_DEV, 2, HEAD_DIM)
    k_cols = kv_pairs[:, :, 0].reshape(rows, -1)
    v_cols = kv_pairs[:, :, 1].reshape(rows, -1)
    q_cols = columns(late_sums, kv_cols, feat)
    up_cols = columns(early_sums, 0, hidden_units)
    down_cols = columns(early_sums, hidden_units, hidden_units)
    out_cols = columns(early_sums, 2 * hidden_units, feat)
    small = (late_sums[0] + late_sums[1])[:rows, kv_cols + feat :].T
    vec_out = small[:6].reshape(6, 2, 6)
    bias_out = small[6:8].reshape(-1)
    qv_out = small[8:10, :6]
    vec_out = lax.dynamic_index_in_dim(vec_out, heads_at, 1, keepdims=False)
    return (
        output.astype(BF16),
        hidden_grad,
        jnp.stack([q_cols, k_cols, v_cols]),
        out_cols.T,
        qv_out,
        up_cols,
        down_cols.T,
        bias_out,
        vec_out[:2],
        vec_out[2:],
    )


def solution(mesh):
    fine = Mesh(mesh.devices.reshape(4, 4, 2, 2, 2), ("z", "y", "xh", "core", "heads"))
    return jax.shard_map(
        per_device,
        mesh=fine,
        in_specs=(
            P(CTX, None),
            P(None, CTX, "heads"),
            P("heads", CTX),
            P(None, "heads"),
            P(CTX, "heads"),
            P("heads", CTX),
            P("heads"),
            P(),
            P(),
            P(CTX),
            P(),
            P(CTX, None),
        ),
        out_specs=(
            P(CTX, None),
            P(CTX, None),
            P(None, CTX, "heads"),
            P("heads", CTX),
            P(None, ("heads", *CTX)),
            P(CTX, "heads"),
            P("heads", CTX),
            P(("heads", *CTX)),
            P(None, (*CTX, "heads")),
            P(None, (*CTX, "heads")),
        ),
        check_vma=False,
    )
```

```python
import jax
import jax.numpy as jnp
from jax import lax
from jax.experimental import pallas as pl
from jax.experimental.pallas import tpu as pltpu
from jax.sharding import Mesh, PartitionSpec as P

HEAD_DIM = 64
HEADS_DEV = 3
EPS = 1e-06
NEG = -1e30
CTX = ("z", "y", "xh", "core")
CHIPS = ("z", "y", "xh")
F32 = jnp.float32
BF16 = jnp.bfloat16
NT = (((1,), (1,)), ((), ()))
VMEM_LIMIT = 50 * 1024 * 1024
OFFSETS = (0, -1, 1, 2)


def shifted(x, axis, step):
    n = lax.axis_size(axis)
    return lax.ppermute(x, axis, [(i, (i + step) % n) for i in range(n)])


def ring_halves(x, axis):
    half = x.shape[0] // 2
    before, after = shifted(x, axis, 1), shifted(x, axis, -1)
    return [x, before, after, shifted(before[:half], axis, 1), shifted(after[half:], axis, -1)]


def gather_first(x):
    half = x.shape[0] // 2
    streams = []
    for part, axis in ((x[:half], "z"), (x[half:], "y")):
        both = jnp.concatenate([part, shifted(part, "xh", 1)], axis=0)
        streams.append(jnp.concatenate(ring_halves(both, axis), axis=0))
    return tuple(streams)


def gather_second(z_stream, y_stream):
    blocks = ring_halves(z_stream, "y") + ring_halves(y_stream, "z")
    return [b.reshape(-1, z_stream.shape[0] // 2, b.shape[1]) for b in blocks]


def near_blocks(blocks):
    return blocks[:3] + blocks[5:8]


def far_blocks(blocks):
    return blocks[3:5] + blocks[8:]


def relative_order(first, second, core_at):
    place = {a: lax.axis_index(a) for a in CHIPS}
    core = lax.axis_index("core")
    order = []
    for second_step in OFFSETS:
        for first_step in OFFSETS:
            for xh_step in (0, 1):
                at = dict(place)
                at[first] = (at[first] + first_step) % 4
                at[second] = (at[second] + second_step) % 4
                at["xh"] = (at["xh"] + xh_step) % 2
                order.append(((at["z"] * 4 + at["y"]) * 2 + at["xh"]) * 2 + (core + core_at) % 2)
    return jnp.stack(order)


def pair_ordered(own, other, axis):
    first = lax.axis_index(axis) == 0
    return jnp.stack([jnp.where(first, own, other), jnp.where(first, other, own)])


def to_owners(x):
    return lax.all_to_all(x.reshape(64, 16, -1), CTX, 0, 0, tiled=True)


def owner_sums(parts):
    return jnp.sum(parts.reshape(-1, 2, *parts.shape[1:]).astype(F32), axis=0)


def team_sum(partial):
    rows = partial.shape[0] // 2
    near = partial[:rows] + shifted(partial[rows:].astype(BF16), "core", 1).astype(F32)
    low = lax.optimization_barrier(near.astype(BF16))
    return low.astype(F32) + shifted(low, "heads", 1).astype(F32)


def chip_tokens(x):
    return jnp.concatenate([x, shifted(x, "core", 1)], axis=0)


def layer_norm(residual, gain_row, shift_row):
    centred = residual - jnp.mean(residual, axis=-1, keepdims=True)
    inverse = lax.rsqrt(jnp.mean(centred * centred, axis=-1, keepdims=True) + EPS)
    normed = centred * inverse
    return (normed * gain_row + shift_row, normed, inverse)


def norm_back(incoming, normed, inverse, gain_row):
    scaled = incoming * gain_row
    projected = (
        scaled
        - jnp.mean(scaled, axis=-1, keepdims=True)
        - normed * jnp.mean(scaled * normed, axis=-1, keepdims=True)
    )
    return inverse * projected


def exact_gelu(pre_act):
    return jax.nn.gelu(pre_act, approximate=False)


def pieces_of(column):
    high = column.astype(BF16).astype(F32)
    middle = (column - high).astype(BF16).astype(F32)
    return high, middle, column - high - middle


def head_columns(h):
    return slice(h * HEAD_DIM, (h + 1) * HEAD_DIM)


def head_block(h):
    return slice(h * 128, (h + 1) * 128)


def diagonal_scores(q_ref, kv_ref, h):
    product = q_ref[h].astype(F32) * kv_ref[:, head_block(h)].astype(F32)
    return jnp.sum(product, axis=1, keepdims=True)


def copies_in(sources, buffer, sems, first_lane=0):
    at = 0
    lanes = pl.ds(first_lane, buffer.shape[2])
    for source in sources:
        size = source.shape[0]
        pltpu.make_async_copy(
            source.at[:, :, lanes], buffer.at[pl.ds(at, size)], sems.at[at // 2]
        ).start()
        at += size


def block_of(buffer, sems, j):
    block = buffer.at[pl.ds(2 * j, 2)]
    pltpu.make_async_copy(block, block, sems.at[j]).wait()
    return buffer[pl.ds(2 * j, 2)].reshape(-1, buffer.shape[2])


def attend_blocks(q_ref, tags_ref, seg_ref, top, total, acc, buffer, sems, row_of):
    rows = q_ref.shape[1]
    seg_wide = jnp.broadcast_to(seg_ref[...], (rows, 128))

    def step(j, carry):
        whole = block_of(buffer, sems, j)
        tags = tags_ref[pl.ds(row_of(j), 1), :]
        keys = tags.shape[1]
        allowed = jnp.tile(seg_wide, (1, keys // 128)) == tags
        for h in range(HEADS_DEV):
            kv = whole[:, head_block(h)]
            scores = lax.dot_general(q_ref[h], kv, NT, preferred_element_type=F32)
            scores = jnp.where(allowed, scores, NEG)
            before = top[h]
            now = jnp.maximum(before, jnp.max(scores, axis=1, keepdims=True))
            weights = jnp.exp(scores - jnp.tile(now, (1, keys // 128)))
            fade = jnp.exp(before - now)
            sums = weights[:, :128]
            for k in range(1, keys // 128):
                sums = sums + weights[:, k * 128 : (k + 1) * 128]
            total[h] = total[h] * fade + sums
            acc[h] = acc[h] * fade + jnp.dot(weights.astype(BF16), kv, preferred_element_type=F32)
            top[h] = now
        return carry

    lax.fori_loop(0, sems.shape[0], step, 0)


def near_row(j):
    return j + (j >= 3).astype(jnp.int32)


def far_row(j):
    return 4 * j + 3


def attend_near_kernel(q_ref, own_ref, tags_ref, seg_ref, tag_ref, *rest):
    blocks, (top, total, acc, buffer, sems) = rest[:6], rest[6:]
    copies_in(blocks, buffer, sems)
    rows = q_ref.shape[1]
    padded = tag_ref[...] < 0
    for h in range(HEADS_DEV):
        diagonal = diagonal_scores(q_ref, own_ref, h)
        top[h] = jnp.broadcast_to(jnp.where(padded, diagonal, NEG), (rows, 128))
        lane = lax.broadcasted_iota(jnp.int32, (rows, 128), 1)
        total[h] = jnp.where((lane == 0) & padded, 1.0, 0.0)
        acc[h] = jnp.where(padded, own_ref[:, head_block(h)].astype(F32), 0.0)
    attend_blocks(q_ref, tags_ref, seg_ref, top, total, acc, buffer, sems, near_row)


def attend_far_kernel(q_ref, tags_ref, seg_ref, top_in, total_in, acc_in, *rest):
    blocks, (out_ref, stat_ref, top, total, acc, buffer, sems) = rest[:4], rest[4:]
    copies_in(blocks, buffer, sems)
    top[...], total[...], acc[...] = top_in[...], total_in[...], acc_in[...]
    attend_blocks(q_ref, tags_ref, seg_ref, top, total, acc, buffer, sems, far_row)
    outs = []
    for h in range(HEADS_DEV):
        sums = jnp.sum(total[h], axis=1, keepdims=True)
        outs.append((acc[h] / sums)[:, HEAD_DIM:])
        stat_ref[h] = top[h] + jnp.log(sums)
    out_ref[...] = jnp.concatenate(outs, axis=1)


def vmem_specs(n):
    return [pl.BlockSpec(memory_space=pltpu.VMEM)] * n


def any_specs(n):
    return [pl.BlockSpec(memory_space=pl.ANY)] * n


def head_state(rows, lanes=128):
    return jax.ShapeDtypeStruct((HEADS_DEV, rows, lanes), F32)


def cost(rows, blocks, flops):
    keys = sum(b.shape[0] * b.shape[1] for b in blocks)
    pairs = rows * keys * HEADS_DEV
    return pl.CostEstimate(
        flops=pairs * flops, bytes_accessed=keys * 1024, transcendentals=pairs
    )


def buffers(blocks, lanes):
    count = sum(b.shape[0] for b in blocks)
    return [
        pltpu.VMEM((count, blocks[0].shape[1], lanes), BF16),
        pltpu.SemaphoreType.DMA((count // 2,)),
    ]


def attend_near(q_heads, kv_own, tags, seg, tag, blocks):
    rows = kv_own.shape[0]
    return pl.pallas_call(
        attend_near_kernel,
        out_shape=(head_state(rows),) * 3,
        in_specs=vmem_specs(5) + any_specs(6),
        out_specs=tuple(vmem_specs(3)),
        scratch_shapes=buffers(blocks, kv_own.shape[1]),
        compiler_params=pltpu.CompilerParams(vmem_limit_bytes=VMEM_LIMIT),
        cost_estimate=cost(rows, blocks, 512),
        name="attend_near",
    )(q_heads, kv_own, tags, seg, tag, *blocks)


def attend_far(q_heads, tags, seg, state, blocks):
    rows = q_heads.shape[1]
    return pl.pallas_call(
        attend_far_kernel,
        out_shape=(jax.ShapeDtypeStruct((rows, HEADS_DEV * HEAD_DIM), F32), head_state(rows)),
        in_specs=vmem_specs(6) + any_specs(4),
        out_specs=tuple(vmem_specs(2)),
        scratch_shapes=[pltpu.VMEM((HEADS_DEV, rows, 128), F32)] * 3
        + buffers(blocks, HEADS_DEV * 128),
        compiler_params=pltpu.CompilerParams(vmem_limit_bytes=VMEM_LIMIT),
        cost_estimate=cost(rows, blocks, 512),
        name="attend_far",
    )(q_heads, tags, seg, *state, *blocks)


def query_back_kernel(q_ref, g_ref, own_ref, tags_ref, seg_ref, tag_ref, stat_ref, delta_ref, *rest):
    blocks, (dq_ref, dkv_ref, buffer, sems, acc) = rest[:10], rest[10:]
    copies_in(blocks, buffer, sems)
    rows = q_ref.shape[1]
    seg_wide = jnp.broadcast_to(seg_ref[...], (rows, 128))
    padded = tag_ref[...] < 0
    for h in range(HEADS_DEV):
        own = own_ref[:, head_block(h)].astype(F32)
        prob = jnp.exp(diagonal_scores(q_ref, own_ref, h) - stat_ref[h][:, :1])
        prob = jnp.where(padded, prob, 0.0)
        grad = diagonal_scores(g_ref, own_ref, h) - delta_ref[h][:, :1]
        score = (prob * grad).astype(BF16).astype(F32)
        acc[h] = score * own
        dkv_ref[:, head_block(h)] = score * q_ref[h].astype(F32) + prob.astype(BF16).astype(
            F32
        ) * g_ref[h].astype(F32)

    def step(j, carry):
        whole = block_of(buffer, sems, j)
        tags = tags_ref[pl.ds(jnp.where(j < 6, near_row(j), far_row(j - 6)), 1), :]
        keys = tags.shape[1]
        allowed = jnp.tile(seg_wide, (1, keys // 128)) == tags
        for h in range(HEADS_DEV):
            kv = whole[:, head_block(h)]
            scores = lax.dot_general(q_ref[h], kv, NT, preferred_element_type=F32)
            scores = jnp.where(allowed, scores, NEG)
            probs = jnp.exp(scores - jnp.tile(stat_ref[h], (1, keys // 128)))
            grads = lax.dot_general(g_ref[h], kv, NT, preferred_element_type=F32)
            back = probs * (grads - jnp.tile(delta_ref[h], (1, keys // 128)))
            acc[h] = acc[h] + jnp.dot(back.astype(BF16), kv, preferred_element_type=F32)
        return carry

    lax.fori_loop(0, 8, step, 0)
    dq_ref[...] = (
        jnp.concatenate([acc[h][:, :HEAD_DIM] for h in range(HEADS_DEV)], axis=1)
        * HEAD_DIM ** (-0.5)
    ).astype(BF16)


def query_back(q_heads, g_heads, kv_own, tags, seg, tag, stat, delta, blocks):
    rows = kv_own.shape[0]
    return pl.pallas_call(
        query_back_kernel,
        out_shape=(
            jax.ShapeDtypeStruct((rows, HEADS_DEV * HEAD_DIM), BF16),
            jax.ShapeDtypeStruct(kv_own.shape, F32),
        ),
        in_specs=vmem_specs(8) + any_specs(10),
        out_specs=tuple(vmem_specs(2)),
        scratch_shapes=buffers(blocks, kv_own.shape[1]) + [pltpu.VMEM((HEADS_DEV, rows, 128), F32)],
        compiler_params=pltpu.CompilerParams(vmem_limit_bytes=VMEM_LIMIT),
        cost_estimate=cost(rows, blocks, 768),
        name="query_back",
    )(q_heads, g_heads, kv_own, tags, seg, tag, stat, delta, *blocks)


def grad_rows_kernel(
    mixed_ref, out_ref, attended_ref, stat_ref, seg_ref, sent_ref, g_ref, delta_ref
):
    rows = mixed_ref.shape[0]
    grad = jnp.dot(mixed_ref[...], out_ref[...], preferred_element_type=F32).astype(BF16)
    grad = grad.astype(F32)
    product = grad * attended_ref[...]
    lane = lax.broadcasted_iota(jnp.int32, (rows, HEAD_DIM), 1)
    seg = seg_ref[...]
    extra = jnp.where(lane == 21, 1.0, 0.0)
    for s in range(3):
        extra = extra + jnp.where((lane == 18 + s) & (seg != s), 1.0, 0.0)
    zeros = jnp.zeros((rows, HEAD_DIM), BF16)
    for h in range(HEADS_DEV):
        delta = jnp.sum(product[:, head_columns(h)], axis=1, keepdims=True)
        delta_ref[h] = jnp.broadcast_to(delta, (rows, 128))
        for i, piece in enumerate(pieces_of(delta)):
            extra = extra + jnp.where(lane == 3 * h + i, piece, 0.0)
        for i, piece in enumerate(pieces_of(stat_ref[h][:, :1])):
            extra = extra + jnp.where(lane == 9 + 3 * h + i, piece, 0.0)
        g_ref[h] = jnp.concatenate([zeros, grad[:, head_columns(h)].astype(BF16)], axis=1)
    sent_ref[...] = jnp.concatenate([grad, extra], axis=1).astype(BF16)


def grad_rows(mixed, w_out, attended, stat, seg):
    rows = mixed.shape[0]
    return pl.pallas_call(
        grad_rows_kernel,
        out_shape=(
            jax.ShapeDtypeStruct((rows, 256), BF16),
            jax.ShapeDtypeStruct((HEADS_DEV, rows, 128), BF16),
            jax.ShapeDtypeStruct((HEADS_DEV, rows, 128), F32),
        ),
        in_specs=vmem_specs(5),
        out_specs=tuple(vmem_specs(3)),
        compiler_params=pltpu.CompilerParams(vmem_limit_bytes=VMEM_LIMIT),
        name="grad_rows",
    )(mixed, w_out, attended, stat, seg)


def send_out(held, out_ref, sem):
    copy = pltpu.make_async_copy(held, out_ref, sem)
    copy.start()
    copy.wait()


def last_rows(x, group):
    parts = x.reshape(64, 16, x.shape[1])[:, 4 * group : 4 * group + 4]
    return jnp.concatenate([jnp.zeros((64, 12, x.shape[1]), F32), parts], axis=1).reshape(x.shape)


def early_grads_kernel(spread_ref, branch_ref, activated_ref, first_ref, up_ref, out_ref, held, sem):
    quarter = held.shape[1] // 3
    made = []
    for left, right in ((first_ref, up_ref), (branch_ref, activated_ref)):
        wide = jnp.dot(left[...], spread_ref[...], preferred_element_type=F32).astype(BF16)
        for half in range(2):
            made.append(dot_tn(wide, right[:, half * quarter : (half + 1) * quarter]))
    for g in range(3):
        held[:, g * quarter : (g + 1) * quarter] = (made[g] + last_rows(made[3], g)).astype(BF16)
    send_out(held, out_ref, sem)


def early_grads(spread, branch, activated, first, up):
    shape = (spread.shape[1], up.shape[1] * 3 // 2)
    return pl.pallas_call(
        early_grads_kernel,
        out_shape=jax.ShapeDtypeStruct(shape, BF16),
        in_specs=vmem_specs(5),
        out_specs=pl.BlockSpec(memory_space=pltpu.HBM),
        scratch_shapes=[pltpu.VMEM(shape, BF16), pltpu.SemaphoreType.DMA],
        compiler_params=pltpu.CompilerParams(vmem_limit_bytes=VMEM_LIMIT),
        name="early_grads",
    )(spread, branch, activated, first, up)


def out_rows_kernel(spread_ref, mixed_ref, attended_ref, out_ref):
    wide = jnp.dot(mixed_ref[...], spread_ref[...], preferred_element_type=F32).astype(BF16)
    made = dot_tn(wide, attended_ref[...].astype(BF16))
    out_ref[...] = jnp.concatenate([last_rows(made, g) for g in range(3)], axis=1).astype(BF16)


def out_rows(spread, mixed, attended):
    return pl.pallas_call(
        out_rows_kernel,
        out_shape=jax.ShapeDtypeStruct((spread.shape[1], 3 * attended.shape[1]), BF16),
        in_specs=vmem_specs(3),
        out_specs=vmem_specs(1)[0],
        compiler_params=pltpu.CompilerParams(vmem_limit_bytes=VMEM_LIMIT),
        name="out_rows",
    )(spread, mixed, attended)


def vector_rows_kernel(
    cot_ref, two_ref, resid_two_ref, first_ref, one_ref, resid_one_ref, up_ref, spread_ref, bias_ref,
    parts_ref, out_ref,
):
    cot, first = cot_ref[...].astype(F32), first_ref[...]
    columns = (
        first * one_ref[...],
        cot * two_ref[...],
        resid_one_ref[...],
        first,
        resid_two_ref[...],
        cot,
    )
    rows = jnp.concatenate([jnp.sum(c, axis=0, keepdims=True) for c in columns], axis=0)
    bias = jnp.sum(up_ref[...].astype(F32), axis=0, keepdims=True) * parts_ref[...]
    made = [
        jnp.dot(rows.astype(BF16), spread_ref[...], preferred_element_type=F32),
        jnp.dot(bias.astype(BF16), bias_ref[...], preferred_element_type=F32),
    ]
    out_ref[...] = jnp.concatenate(made, axis=0)


def vector_rows(spread, *args):
    return pl.pallas_call(
        vector_rows_kernel,
        out_shape=jax.ShapeDtypeStruct((8, spread.shape[1]), F32),
        in_specs=vmem_specs(10),
        out_specs=vmem_specs(1)[0],
        compiler_params=pltpu.CompilerParams(vmem_limit_bytes=VMEM_LIMIT),
        name="vector_rows",
    )(*args)


def late_grads_kernel(
    hid_ref, dkv_ref, dq_ref, rows_ref, q_place_ref, v_place_ref, placed_ref, w_ref, spread_ref,
    out_ref, back_ref, held, sem,
):
    wide = hid_ref.shape[1]
    grads = jnp.concatenate([dkv_ref[...], dq_ref[...]], axis=1)
    cols = grads.shape[1]
    made = dot_tn(hid_ref[...], grads) + placed_ref[...].astype(F32)
    sums = [rows_ref[...]]
    for grad, place in ((dq_ref, q_place_ref), (dkv_ref, v_place_ref)):
        row = jnp.sum(grad[...].astype(F32), axis=0, keepdims=True).astype(BF16)
        sums.append(jnp.dot(row, place[...], preferred_element_type=F32))
    sums.append(jnp.zeros((128 - 10, wide), F32))
    small = jnp.transpose(jnp.concatenate(sums, axis=0))[:, :64]
    held[...] = jnp.concatenate([made, small], axis=1).astype(BF16)
    copy = pltpu.make_async_copy(held, out_ref, sem)
    copy.start()
    back = dot_nt(grads, w_ref[:, :cols]).astype(BF16)
    back_ref[...] = dot_nt(back, spread_ref[...]).astype(BF16)
    copy.wait()


def late_grads(hid, dkv, dq, rows, q_place, v_place, placed, w, spread):
    shape = (hid.shape[1], dkv.shape[1] + dq.shape[1] + 64)
    return pl.pallas_call(
        late_grads_kernel,
        out_shape=(
            jax.ShapeDtypeStruct(shape, BF16),
            jax.ShapeDtypeStruct((hid.shape[0], spread.shape[0]), BF16),
        ),
        in_specs=vmem_specs(9),
        out_specs=(pl.BlockSpec(memory_space=pltpu.HBM), vmem_specs(1)[0]),
        scratch_shapes=[pltpu.VMEM(shape, BF16), pltpu.SemaphoreType.DMA],
        compiler_params=pltpu.CompilerParams(vmem_limit_bytes=VMEM_LIMIT),
        name="late_grads",
    )(hid, dkv, dq, rows, q_place, v_place, placed, w, spread)


def project_kernel(hid_ref, w_ref, bias_ref, scale_ref, sent_ref, q_ref):
    made = jnp.dot(hid_ref[...], w_ref[...], preferred_element_type=F32) + bias_ref[...]
    made = (made.astype(BF16).astype(F32) * scale_ref[...]).astype(BF16)
    sent_ref[...] = made
    zeros = jnp.zeros((made.shape[0], HEAD_DIM), BF16)
    for h in range(HEADS_DEV):
        at = 2 * HEADS_DEV * HEAD_DIM + h * HEAD_DIM
        q_ref[h] = jnp.concatenate([made[:, at : at + HEAD_DIM], zeros], axis=1)


def project(hid, w, bias, scale):
    rows = hid.shape[0]
    return pl.pallas_call(
        project_kernel,
        out_shape=(
            jax.ShapeDtypeStruct((rows, w.shape[1]), BF16),
            jax.ShapeDtypeStruct((HEADS_DEV, rows, 128), BF16),
        ),
        in_specs=vmem_specs(4),
        out_specs=tuple(vmem_specs(2)),
        compiler_params=pltpu.CompilerParams(vmem_limit_bytes=VMEM_LIMIT),
        name="project",
    )(hid, w, bias, scale)


def key_back_blocks(k_ref, v_ref, k_acc, v_acc, q_buffer, g_buffer, q_sems, g_sems):
    def step(j, carry):
        queries = block_of(q_buffer, q_sems, j)
        grads = block_of(g_buffer, g_sems, j)
        lane = lax.broadcasted_iota(jnp.int32, queries.shape, 1)
        queries = jnp.where(lane < HEADS_DEV * HEAD_DIM, queries, grads)
        for h in range(HEADS_DEV):
            scores = lax.dot_general(k_ref[h], queries, NT, preferred_element_type=F32)
            probs = jnp.exp(scores)
            v_acc[h] = v_acc[h] + jnp.dot(probs.astype(BF16), grads, preferred_element_type=F32)
            back = probs * lax.dot_general(v_ref[h], grads, NT, preferred_element_type=F32)
            k_acc[h] = k_acc[h] + jnp.dot(back.astype(BF16), queries, preferred_element_type=F32)
        return carry

    lax.fori_loop(0, q_sems.shape[0], step, 0)


def key_heads(kv_ref, tag_ref, k_heads, v_heads):
    rows = kv_ref.shape[0]
    feat = HEADS_DEV * HEAD_DIM
    lane = lax.broadcasted_iota(jnp.int32, (rows, HEAD_DIM), 1)
    tag = tag_ref[...]
    masks = jnp.where((lane == 21) & (tag < 0), NEG, 0.0)
    for s in range(3):
        masks = masks + jnp.where((lane == 18 + s) & (tag == s), NEG, 0.0)
    for h in range(HEADS_DEV):
        block = kv_ref[:, head_block(h)].astype(F32)
        before = [jnp.zeros((rows, h * HEAD_DIM), F32)] if h else []
        left = feat - (h + 1) * HEAD_DIM
        after = [jnp.zeros((rows, left), F32)] if left else []
        k_extra = masks - jnp.where((lane >= 9 + 3 * h) & (lane < 12 + 3 * h), 1.0, 0.0)
        v_extra = -jnp.where((lane >= 3 * h) & (lane < 3 * h + 3), 1.0, 0.0)
        for heads, part, extra in (
            (k_heads, block[:, :HEAD_DIM], k_extra),
            (v_heads, block[:, HEAD_DIM:], v_extra),
        ):
            heads[h] = jnp.concatenate(before + [part] + after + [extra], axis=1).astype(BF16)


def key_near_kernel(kv_ref, tag_ref, *rest):
    q_blocks, g_blocks = rest[:6], rest[6:12]
    k_acc, v_acc, k_heads, v_heads, q_buffer, q_sems, g_buffer, g_sems = rest[12:]
    copies_in(q_blocks, q_buffer, q_sems, 2 * HEADS_DEV * HEAD_DIM)
    copies_in(g_blocks, g_buffer, g_sems)
    key_heads(kv_ref, tag_ref, k_heads, v_heads)
    k_acc[...] = jnp.zeros_like(k_acc)
    v_acc[...] = jnp.zeros_like(v_acc)
    key_back_blocks(k_heads, v_heads, k_acc, v_acc, q_buffer, g_buffer, q_sems, g_sems)


def key_far_kernel(kv_ref, tag_ref, diag_ref, k_in, v_in, *rest):
    q_blocks, g_blocks = rest[:4], rest[4:8]
    dkv_ref, k_heads, v_heads, k_acc, v_acc, q_buffer, q_sems, g_buffer, g_sems = rest[8:]
    copies_in(q_blocks, q_buffer, q_sems, 2 * HEADS_DEV * HEAD_DIM)
    copies_in(g_blocks, g_buffer, g_sems)
    key_heads(kv_ref, tag_ref, k_heads, v_heads)
    k_acc[...], v_acc[...] = k_in[...], v_in[...]
    key_back_blocks(k_heads, v_heads, k_acc, v_acc, q_buffer, g_buffer, q_sems, g_sems)
    parts = []
    for h in range(HEADS_DEV):
        parts += [k_acc[h][:, head_columns(h)], v_acc[h][:, head_columns(h)]]
    dkv_ref[...] = (jnp.concatenate(parts, axis=1) + diag_ref[...]).astype(BF16)


def key_near(kv_own, tag, q_blocks, g_blocks):
    rows, width = kv_own.shape[0], g_blocks[0].shape[2]
    return pl.pallas_call(
        key_near_kernel,
        out_shape=(head_state(rows, width),) * 2,
        in_specs=vmem_specs(2) + any_specs(12),
        out_specs=tuple(vmem_specs(2)),
        scratch_shapes=[pltpu.VMEM((HEADS_DEV, rows, width), BF16)] * 2
        + buffers(q_blocks, width)
        + buffers(g_blocks, width),
        compiler_params=pltpu.CompilerParams(vmem_limit_bytes=VMEM_LIMIT),
        cost_estimate=cost(rows, q_blocks, 2048),
        name="key_near",
    )(kv_own, tag, *q_blocks, *g_blocks)


def key_far(kv_own, tag, diagonal, state, q_blocks, g_blocks):
    rows, width = kv_own.shape[0], g_blocks[0].shape[2]
    return pl.pallas_call(
        key_far_kernel,
        out_shape=jax.ShapeDtypeStruct(diagonal.shape, BF16),
        in_specs=vmem_specs(5) + any_specs(8),
        out_specs=vmem_specs(1)[0],
        scratch_shapes=[pltpu.VMEM((HEADS_DEV, rows, width), BF16)] * 2
        + [pltpu.VMEM((HEADS_DEV, rows, width), F32)] * 2
        + buffers(q_blocks, width)
        + buffers(g_blocks, width),
        compiler_params=pltpu.CompilerParams(vmem_limit_bytes=VMEM_LIMIT),
        cost_estimate=cost(rows, q_blocks, 2048),
        name="key_far",
    )(kv_own, tag, diagonal, *state, *q_blocks, *g_blocks)


def dot(a, b):
    return jnp.dot(a, b, preferred_element_type=F32)


def dot_nt(a, b):
    return lax.dot_general(a, b, NT, preferred_element_type=F32)


def dot_tn(a, b):
    return lax.dot_general(a, b, (((0,), (0,)), ((), ())), preferred_element_type=F32)


def core_half(x, axis, at):
    size = x.shape[axis] // 2
    return lax.dynamic_slice_in_dim(x, at * size, size, axis)


def interleaved(k, v):
    shape = (*k.shape[:-1], -1, HEAD_DIM)
    return jnp.stack([k.reshape(shape), v.reshape(shape)], axis=-2).reshape(*k.shape[:-1], -1)


def per_device(
    hidden,
    w_qkv,
    w_out,
    b_qv,
    w_up,
    w_down,
    b_up,
    norm_gains,
    norm_shifts,
    segments,
    lengths,
    cotangent,
):
    core = lax.axis_index("core")
    heads_at = lax.axis_index("heads")
    own_ctx = ((lax.axis_index("z") * 4 + lax.axis_index("y")) * 2 + lax.axis_index("xh")) * 2 + core
    tok = hidden.shape[0]
    rows = w_up.shape[0]
    feat = HEADS_DEV * HEAD_DIM
    hidden_units = w_up.shape[1] // 2

    hid = chip_tokens(hidden)
    out_turned, down_turned = w_out.T, w_down.T
    low_tok = segments.astype(BF16).reshape(2, tok // 2)
    kv_cols = 2 * feat

    def halves(x):
        return jnp.swapaxes(x.reshape(rows, 2, -1), 0, 1)

    q_half, k_half, v_half = (halves(w_qkv[i]) for i in range(3))
    tail = jnp.broadcast_to(jnp.pad(low_tok, ((0, rows - 2), (0, 0))), (2, rows, tok // 2))
    urgent = jnp.concatenate([interleaved(k_half, v_half), q_half, tail], axis=2)
    urgent = jnp.pad(urgent, ((0, 0), (0, 16 - rows), (0, 0)))
    urgent = jnp.broadcast_to(urgent[None], (32, *urgent.shape)).reshape(64, 16, -1)
    later = jnp.concatenate([halves(w) for w in (out_turned, w_up, down_turned)], axis=2)
    mine = lax.dynamic_index_in_dim(later, core, 0, keepdims=False)
    theirs = shifted(lax.dynamic_index_in_dim(later, 1 - core, 0, keepdims=False), "core", 1)
    theirs, urgent = lax.optimization_barrier((theirs, urgent))
    later = pair_ordered(mine, theirs, "core").reshape(2 * rows, -1)
    rest = lax.all_gather(later, CHIPS, axis=0, tiled=True)
    w_urgent = lax.all_to_all(urgent, CTX, 0, 0, tiled=True)
    seg_all = w_urgent[:, :2, kv_cols + feat :].reshape(-1, tok).astype(jnp.int32)
    w_urgent = w_urgent.reshape(64 * 16, -1)
    at_wide = jnp.arange(64 * 16, dtype=jnp.int32)
    at_feature = jnp.arange(64 * rows, dtype=jnp.int32)
    spread = (
        (at_feature // rows * 16 + at_feature % rows)[:, None] == at_wide[None, :]
    ).astype(BF16)
    hid_wide = dot(hid, spread).astype(BF16)

    w_out_t = rest[:, :feat]
    w_up_all = rest[:, feat : feat + hidden_units]
    w_down_t = rest[:, feat + hidden_units :]

    bias = b_qv.astype(F32)
    q_bias, v_bias = core_half(bias[0], 0, core), core_half(bias[1], 0, core)
    no_bias = jnp.zeros((tok // 2,), F32)
    bias_row = jnp.concatenate([interleaved(jnp.zeros_like(v_bias), v_bias), q_bias, no_bias])
    column = jnp.arange(bias_row.shape[0], dtype=jnp.int32)
    scale_row = jnp.where(
        column < kv_cols, 1.0, jnp.where(column < kv_cols + feat, HEAD_DIM ** (-0.5), 0.0)
    ).astype(F32)
    sent, q_heads = project(hid_wide, w_urgent, bias_row[None], scale_row[None])
    kv_own = sent[:, :kv_cols]
    starts = [jnp.sum((seg_all < s).astype(jnp.int32)) for s in range(3)]
    places = jnp.arange(seg_all.size, dtype=jnp.int32).reshape(seg_all.shape)
    run_end = jnp.zeros_like(seg_all)
    for s in range(3):
        run_end = jnp.where(seg_all == s, starts[s] + lengths[s], run_end)
    tag_all = jnp.where(places < run_end, seg_all, -1).astype(F32)
    order = jnp.concatenate([relative_order("z", "y", 0), relative_order("y", "z", 1)])
    tags = jnp.take(tag_all, order, axis=0).reshape(8, -1)
    both = jnp.stack([own_ctx, own_ctx + 1 - 2 * core])
    tag_own = jnp.take(tag_all, both, axis=0).reshape(-1, 1)
    seg_own = jnp.take(seg_all, both, axis=0).astype(F32).reshape(-1, 1)

    sent_z, sent_y = lax.optimization_barrier(gather_first(sent))
    blocks = gather_second(sent_z, sent_y)
    near, far = near_blocks(blocks), far_blocks(blocks)
    state = attend_near(q_heads, kv_own, tags, seg_own, tag_own, near)
    attended, stat = attend_far(q_heads, tags, seg_own, state, far)
    attended_low = attended.astype(BF16)

    gain_rows = norm_gains.astype(F32)
    shifts = norm_shifts.astype(F32)
    attn_mixed = team_sum(dot_nt(attended_low, w_out_t))
    first_out, normed_one, inverse_one = layer_norm(
        hidden.astype(F32) + attn_mixed + shifts[0], gain_rows[0], shifts[1]
    )
    first_low = chip_tokens(first_out.astype(BF16))
    up_bias = core_half(b_up, 0, core).astype(F32)
    up_proj = dot(first_low, w_up_all) + up_bias
    activated = exact_gelu(up_proj).astype(BF16)
    second = team_sum(dot_nt(activated, w_down_t))
    output, normed_two, inverse_two = layer_norm(
        first_out + second + shifts[2], gain_rows[1], shifts[3]
    )
    resid_two = norm_back(
        cotangent.astype(F32), normed_two, inverse_two, gain_rows[1]
    )
    branch_low = chip_tokens(resid_two.astype(BF16))
    act_grad = dot(branch_low, w_down_t)
    up_low = jax.vjp(exact_gelu, up_proj)[1](act_grad)[0].astype(BF16)
    first_grad = resid_two + team_sum(dot_nt(up_low, w_up_all))
    resid_one = norm_back(first_grad, normed_one, inverse_one, gain_rows[0])
    mixed_low = chip_tokens(resid_one.astype(BF16))
    g_sent, g_heads, delta = grad_rows(mixed_low, w_out_t, attended, stat, seg_own)
    made = early_grads(spread, branch_low, activated, first_low, up_low)
    (g_z, g_y), g_heads, made = lax.optimization_barrier((gather_first(g_sent), g_heads, made))
    g_blocks = gather_second(g_z, g_y)
    early = to_owners(made)
    out_placed = out_rows(spread, mixed_low, attended_low)
    at_bias = jnp.arange(hidden_units, dtype=jnp.int32)
    at_half = jnp.arange(feat, dtype=jnp.int32)
    at_kv = jnp.arange(kv_cols, dtype=jnp.int32)

    def placed(owner, row):
        return ((owner * 16 + row)[:, None] == at_wide[None, :]).astype(BF16)

    first_owner = 32 * core
    bias_place = placed(first_owner + at_bias // 24, at_bias % 12)
    q_place = placed(first_owner + at_half // 6, at_half % 6)
    at_value = at_kv // 128 * HEAD_DIM + at_kv % 128 - HEAD_DIM
    is_value = at_kv % 128 >= HEAD_DIM
    v_place = placed(jnp.where(is_value, first_owner + at_value // 6, -1), at_value % 6)
    parts = jnp.arange(2, dtype=jnp.int32)[:, None] == (at_bias % 24 // 12)[None, :]
    rows_made = vector_rows(
        spread,
        cotangent,
        normed_two,
        resid_two,
        first_grad,
        normed_one,
        resid_one,
        up_low,
        spread,
        bias_place,
        parts.astype(F32),
    )

    dq, diagonal = query_back(
        q_heads, g_heads, kv_own, tags, seg_own, tag_own, stat, delta, near + far
    )
    key_state = key_near(kv_own, tag_own, near, near_blocks(g_blocks))
    dkv = key_far(kv_own, tag_own, diagonal, key_state, far, far_blocks(g_blocks))
    dkv, early = lax.optimization_barrier((dkv, early))
    late, back = late_grads(
        hid_wide, dkv, dq, rows_made, q_place, v_place, out_placed, w_urgent, spread
    )
    late = to_owners(late)
    hidden_grad = resid_one + team_sum(back.astype(F32))

    early_sums, late_sums = owner_sums(early), owner_sums(late)

    def columns(x, start, size):
        return jnp.concatenate([x[c, :rows, start : start + size] for c in range(2)], axis=1)

    kv_pairs = columns(late_sums, 0, kv_cols).reshape(rows, 2 * HEADS_DEV, 2, HEAD_DIM)
    k_cols = kv_pairs[:, :, 0].reshape(rows, -1)
    v_cols = kv_pairs[:, :, 1].reshape(rows, -1)
    q_cols = columns(late_sums, kv_cols, feat)

    def last(x, size):
        return jnp.concatenate(
            [x[:, rows:, g * size : (g + 1) * size] for g in range(3)], axis=1
        )

    quarter = hidden_units // 2
    up_cols = columns(early_sums, 0, hidden_units)
    down_first, down_last = early_sums[:, :rows, hidden_units:], last(early_sums, quarter)
    down_cols = jnp.concatenate(
        [down_first[0], down_last[0], down_first[1], down_last[1]], axis=1
    )
    out_last = last(late_sums, feat)
    out_cols = jnp.concatenate([out_last[0], out_last[1]], axis=1)
    small = (late_sums[0] + late_sums[1])[:rows, kv_cols + feat :].T
    vec_out = small[:6].reshape(6, 2, 6)
    bias_out = small[6:8].reshape(-1)
    qv_out = small[8:10, :6]
    vec_out = lax.dynamic_index_in_dim(vec_out, heads_at, 1, keepdims=False)
    return (
        output.astype(BF16),
        hidden_grad,
        jnp.stack([q_cols, k_cols, v_cols]),
        out_cols.T,
        qv_out,
        up_cols,
        down_cols.T,
        bias_out,
        vec_out[:2],
        vec_out[2:],
    )


def solution(mesh):
    fine = Mesh(mesh.devices.reshape(4, 4, 2, 2, 2), ("z", "y", "xh", "core", "heads"))
    return jax.shard_map(
        per_device,
        mesh=fine,
        in_specs=(
            P(CTX, None),
            P(None, CTX, "heads"),
            P("heads", CTX),
            P(None, "heads"),
            P(CTX, "heads"),
            P("heads", CTX),
            P("heads"),
            P(),
            P(),
            P(CTX),
            P(),
            P(CTX, None),
        ),
        out_specs=(
            P(CTX, None),
            P(CTX, None),
            P(None, CTX, "heads"),
            P("heads", CTX),
            P(None, ("heads", *CTX)),
            P(CTX, "heads"),
            P("heads", CTX),
            P(("heads", *CTX)),
            P(None, (*CTX, "heads")),
            P(None, (*CTX, "heads")),
        ),
        check_vma=False,
    )
```

```python
import functools

import jax
import jax.numpy as jnp
from jax import lax
from jax.experimental import pallas as pl
from jax.experimental.pallas import tpu as pltpu
from jax.sharding import Mesh, PartitionSpec as P

HEAD_DIM = 64
HEADS_DEV = 3
EPS = 1e-06
NEG = -1e30
CTX = ("z", "y", "xh", "core")
CHIPS = ("z", "y", "xh")
F32 = jnp.float32
BF16 = jnp.bfloat16
NT = (((1,), (1,)), ((), ()))
VMEM_LIMIT = 50 * 1024 * 1024
OFFSETS = (0, -1, 1, 2)


def shifted(x, axis, step):
    n = lax.axis_size(axis)
    return lax.ppermute(x, axis, [(i, (i + step) % n) for i in range(n)])


def ring_halves(x, axis):
    half = x.shape[0] // 2
    before, after = shifted(x, axis, 1), shifted(x, axis, -1)
    return [x, before, after, shifted(before[:half], axis, 1), shifted(after[half:], axis, -1)]


def ring_pairs(low, high, axis):
    low_before, low_after = shifted(low, axis, 1), shifted(low, axis, -1)
    high_before, high_after = shifted(high, axis, 1), shifted(high, axis, -1)
    near = [low, high, low_before, high_before, low_after, high_after]
    return near, [shifted(low_before, axis, 1), shifted(high_after, axis, -1)]


def first_pieces(x):
    half = x.shape[0] // 2
    streams = []
    for part, axis in ((x[:half], "z"), (x[half:], "y")):
        both = jnp.concatenate([part, shifted(part, "xh", 1)], axis=0)
        streams.append(ring_halves(both, axis))
    return streams


def gather_first(x):
    return tuple(jnp.concatenate(pieces, axis=0) for pieces in first_pieces(x))


def gather_first_pairs(x):
    streams = []
    for own, before, after, far_low, far_high in first_pieces(x):
        streams.append(jnp.concatenate([own, before], axis=0))
        streams.append(jnp.concatenate([after, far_low, far_high], axis=0))
    return tuple(streams)


def gather_second(z_stream, y_stream):
    blocks = ring_halves(z_stream, "y") + ring_halves(y_stream, "z")
    blocks = [b.reshape(-1, z_stream.shape[0] // 2, b.shape[1]) for b in blocks]
    return blocks[:3] + blocks[5:8], blocks[3:5] + blocks[8:]


def gather_second_pairs(z_low, z_high, y_low, y_high):
    z_near, z_far = ring_pairs(z_low, z_high, "y")
    y_near, y_far = ring_pairs(y_low, y_high, "z")
    return [b[None] for b in z_near + y_near], [b[None] for b in z_far + y_far]


def relative_order(first, second, core_at):
    place = {a: lax.axis_index(a) for a in CHIPS}
    core = lax.axis_index("core")
    order = []
    for second_step in OFFSETS:
        for first_step in OFFSETS:
            for xh_step in (0, 1):
                at = dict(place)
                at[first] = (at[first] + first_step) % 4
                at[second] = (at[second] + second_step) % 4
                at["xh"] = (at["xh"] + xh_step) % 2
                order.append(((at["z"] * 4 + at["y"]) * 2 + at["xh"]) * 2 + (core + core_at) % 2)
    return jnp.stack(order)


def pair_ordered(own, other, axis):
    first = lax.axis_index(axis) == 0
    return jnp.stack([jnp.where(first, own, other), jnp.where(first, other, own)])


def to_owners(x):
    return lax.all_to_all(x.reshape(64, 16, -1), CTX, 0, 0, tiled=True)


def to_planes(x):
    return lax.all_to_all(x.reshape(64, 16, -1), ("z", "y"), 0, 0, tiled=True)


def planes_to_owners(parts):
    sums = jnp.sum(parts.reshape(16, 4, *parts.shape[1:]).astype(F32), axis=0)
    return lax.all_to_all(sums.astype(BF16), ("xh", "core"), 0, 0, tiled=True)


def owner_sums(parts):
    return jnp.sum(parts.reshape(-1, 2, *parts.shape[1:]).astype(F32), axis=0)


def team_sum(partial):
    rows = partial.shape[0] // 2
    near = partial[:rows] + shifted(partial[rows:].astype(BF16), "core", 1).astype(F32)
    low = lax.optimization_barrier(near.astype(BF16))
    return low.astype(F32) + shifted(low, "heads", 1).astype(F32)


def chip_tokens(x):
    return jnp.concatenate([x, shifted(x, "core", 1)], axis=0)


def layer_norm(residual, gain_row, shift_row):
    centred = residual - jnp.mean(residual, axis=-1, keepdims=True)
    inverse = lax.rsqrt(jnp.mean(centred * centred, axis=-1, keepdims=True) + EPS)
    normed = centred * inverse
    return (normed * gain_row + shift_row, normed, inverse)


def norm_back(incoming, normed, inverse, gain_row):
    scaled = incoming * gain_row
    projected = (
        scaled
        - jnp.mean(scaled, axis=-1, keepdims=True)
        - normed * jnp.mean(scaled * normed, axis=-1, keepdims=True)
    )
    return inverse * projected


def exact_gelu(pre_act):
    return jax.nn.gelu(pre_act, approximate=False)


def pieces_of(column):
    high = column.astype(BF16).astype(F32)
    middle = (column - high).astype(BF16).astype(F32)
    return high, middle, column - high - middle


def head_columns(h):
    return slice(h * HEAD_DIM, (h + 1) * HEAD_DIM)


def head_block(h):
    return slice(h * 128, (h + 1) * 128)


def diagonal_scores(q_ref, kv_ref, h):
    product = q_ref[h].astype(F32) * kv_ref[:, head_block(h)].astype(F32)
    return jnp.sum(product, axis=1, keepdims=True)


def copies_in(sources, buffer, sems, first_lane=0):
    at = 0
    lanes = pl.ds(first_lane, buffer.shape[2])
    for source in sources:
        size = source.shape[0]
        pltpu.make_async_copy(
            source.at[:, :, lanes], buffer.at[pl.ds(at, size)], sems.at[at // 2]
        ).start()
        at += size


def block_of(buffer, sems, j):
    block = buffer.at[pl.ds(2 * j, 2)]
    pltpu.make_async_copy(block, block, sems.at[j]).wait()
    return buffer[pl.ds(2 * j, 2)].reshape(-1, buffer.shape[2])


def attend_blocks(q_ref, tags_ref, seg_ref, top, total, acc, buffer, sems, row_of):
    rows = q_ref.shape[1]
    seg_wide = jnp.broadcast_to(seg_ref[...], (rows, 128))

    def step(j, carry):
        whole = block_of(buffer, sems, j)
        tags = tags_ref[pl.ds(row_of(j), 1), :]
        keys = tags.shape[1]
        allowed = jnp.tile(seg_wide, (1, keys // 128)) == tags
        for h in range(HEADS_DEV):
            kv = whole[:, head_block(h)]
            scores = lax.dot_general(q_ref[h], kv, NT, preferred_element_type=F32)
            scores = jnp.where(allowed, scores, NEG)
            before = top[h]
            now = jnp.maximum(before, jnp.max(scores, axis=1, keepdims=True))
            weights = jnp.exp(scores - jnp.tile(now, (1, keys // 128)))
            fade = jnp.exp(before - now)
            sums = weights[:, :128]
            for k in range(1, keys // 128):
                sums = sums + weights[:, k * 128 : (k + 1) * 128]
            total[h] = total[h] * fade + sums
            acc[h] = acc[h] * fade + jnp.dot(weights.astype(BF16), kv, preferred_element_type=F32)
            top[h] = now
        return carry

    lax.fori_loop(0, sems.shape[0], step, 0)


def near_row(j):
    return j + (j >= 3).astype(jnp.int32)


def far_row(j):
    return 4 * j + 3


def attend_near_kernel(count, q_ref, own_ref, tags_ref, seg_ref, tag_ref, *rest):
    blocks, (top, total, acc, buffer, sems) = rest[:count], rest[count:]
    copies_in(blocks, buffer, sems)
    rows = q_ref.shape[1]
    padded = tag_ref[...] < 0
    for h in range(HEADS_DEV):
        diagonal = diagonal_scores(q_ref, own_ref, h)
        top[h] = jnp.broadcast_to(jnp.where(padded, diagonal, NEG), (rows, 128))
        lane = lax.broadcasted_iota(jnp.int32, (rows, 128), 1)
        total[h] = jnp.where((lane == 0) & padded, 1.0, 0.0)
        acc[h] = jnp.where(padded, own_ref[:, head_block(h)].astype(F32), 0.0)
    attend_blocks(q_ref, tags_ref, seg_ref, top, total, acc, buffer, sems, near_row)


def attend_far_kernel(q_ref, tags_ref, seg_ref, top_in, total_in, acc_in, *rest):
    blocks, (out_ref, stat_ref, top, total, acc, buffer, sems) = rest[:4], rest[4:]
    copies_in(blocks, buffer, sems)
    top[...], total[...], acc[...] = top_in[...], total_in[...], acc_in[...]
    attend_blocks(q_ref, tags_ref, seg_ref, top, total, acc, buffer, sems, far_row)
    outs = []
    for h in range(HEADS_DEV):
        sums = jnp.sum(total[h], axis=1, keepdims=True)
        outs.append((acc[h] / sums)[:, HEAD_DIM:])
        stat_ref[h] = top[h] + jnp.log(sums)
    out_ref[...] = jnp.concatenate(outs, axis=1)


def vmem_specs(n):
    return [pl.BlockSpec(memory_space=pltpu.VMEM)] * n


def any_specs(n):
    return [pl.BlockSpec(memory_space=pl.ANY)] * n


def head_state(rows, lanes=128):
    return jax.ShapeDtypeStruct((HEADS_DEV, rows, lanes), F32)


def cost(rows, blocks, flops):
    keys = sum(b.shape[0] * b.shape[1] for b in blocks)
    pairs = rows * keys * HEADS_DEV
    return pl.CostEstimate(
        flops=pairs * flops, bytes_accessed=keys * 1024, transcendentals=pairs
    )


def buffers(blocks, lanes):
    count = sum(b.shape[0] for b in blocks)
    return [
        pltpu.VMEM((count, blocks[0].shape[1], lanes), BF16),
        pltpu.SemaphoreType.DMA((count // 2,)),
    ]


def attend_near(q_heads, kv_own, tags, seg, tag, blocks):
    rows = kv_own.shape[0]
    return pl.pallas_call(
        functools.partial(attend_near_kernel, len(blocks)),
        out_shape=(head_state(rows),) * 3,
        in_specs=vmem_specs(5) + any_specs(len(blocks)),
        out_specs=tuple(vmem_specs(3)),
        scratch_shapes=buffers(blocks, kv_own.shape[1]),
        compiler_params=pltpu.CompilerParams(vmem_limit_bytes=VMEM_LIMIT),
        cost_estimate=cost(rows, blocks, 512),
        name="attend_near",
    )(q_heads, kv_own, tags, seg, tag, *blocks)


def attend_far(q_heads, tags, seg, state, blocks):
    rows = q_heads.shape[1]
    return pl.pallas_call(
        attend_far_kernel,
        out_shape=(jax.ShapeDtypeStruct((rows, HEADS_DEV * HEAD_DIM), F32), head_state(rows)),
        in_specs=vmem_specs(6) + any_specs(4),
        out_specs=tuple(vmem_specs(2)),
        scratch_shapes=[pltpu.VMEM((HEADS_DEV, rows, 128), F32)] * 3
        + buffers(blocks, HEADS_DEV * 128),
        compiler_params=pltpu.CompilerParams(vmem_limit_bytes=VMEM_LIMIT),
        cost_estimate=cost(rows, blocks, 512),
        name="attend_far",
    )(q_heads, tags, seg, *state, *blocks)


def query_back_kernel(
    count, q_ref, g_ref, own_ref, tags_ref, seg_ref, tag_ref, stat_ref, delta_ref, *rest
):
    blocks, (dq_ref, dkv_ref, buffer, sems, acc) = rest[:count], rest[count:]
    copies_in(blocks, buffer, sems)
    rows = q_ref.shape[1]
    seg_wide = jnp.broadcast_to(seg_ref[...], (rows, 128))
    padded = tag_ref[...] < 0
    for h in range(HEADS_DEV):
        own = own_ref[:, head_block(h)].astype(F32)
        prob = jnp.exp(diagonal_scores(q_ref, own_ref, h) - stat_ref[h][:, :1])
        prob = jnp.where(padded, prob, 0.0)
        grad = diagonal_scores(g_ref, own_ref, h) - delta_ref[h][:, :1]
        score = (prob * grad).astype(BF16).astype(F32)
        acc[h] = score * own
        dkv_ref[:, head_block(h)] = score * q_ref[h].astype(F32) + prob.astype(BF16).astype(
            F32
        ) * g_ref[h].astype(F32)

    def step(j, carry):
        whole = block_of(buffer, sems, j)
        tags = tags_ref[pl.ds(jnp.where(j < 6, near_row(j), far_row(j - 6)), 1), :]
        keys = tags.shape[1]
        allowed = jnp.tile(seg_wide, (1, keys // 128)) == tags
        for h in range(HEADS_DEV):
            kv = whole[:, head_block(h)]
            scores = lax.dot_general(q_ref[h], kv, NT, preferred_element_type=F32)
            scores = jnp.where(allowed, scores, NEG)
            probs = jnp.exp(scores - jnp.tile(stat_ref[h], (1, keys // 128)))
            grads = lax.dot_general(g_ref[h], kv, NT, preferred_element_type=F32)
            back = probs * (grads - jnp.tile(delta_ref[h], (1, keys // 128)))
            acc[h] = acc[h] + jnp.dot(back.astype(BF16), kv, preferred_element_type=F32)
        return carry

    lax.fori_loop(0, 8, step, 0)
    dq_ref[...] = (
        jnp.concatenate([acc[h][:, :HEAD_DIM] for h in range(HEADS_DEV)], axis=1)
        * HEAD_DIM ** (-0.5)
    ).astype(BF16)


def query_back(q_heads, g_heads, kv_own, tags, seg, tag, stat, delta, blocks):
    rows = kv_own.shape[0]
    return pl.pallas_call(
        functools.partial(query_back_kernel, len(blocks)),
        out_shape=(
            jax.ShapeDtypeStruct((rows, HEADS_DEV * HEAD_DIM), BF16),
            jax.ShapeDtypeStruct(kv_own.shape, F32),
        ),
        in_specs=vmem_specs(8) + any_specs(len(blocks)),
        out_specs=tuple(vmem_specs(2)),
        scratch_shapes=buffers(blocks, kv_own.shape[1]) + [pltpu.VMEM((HEADS_DEV, rows, 128), F32)],
        compiler_params=pltpu.CompilerParams(vmem_limit_bytes=VMEM_LIMIT),
        cost_estimate=cost(rows, blocks, 768),
        name="query_back",
    )(q_heads, g_heads, kv_own, tags, seg, tag, stat, delta, *blocks)


def grad_rows_kernel(
    mixed_ref, out_ref, attended_ref, stat_ref, seg_ref, sent_ref, g_ref, delta_ref
):
    rows = mixed_ref.shape[0]
    grad = jnp.dot(mixed_ref[...], out_ref[...], preferred_element_type=F32).astype(BF16)
    grad = grad.astype(F32)
    product = grad * attended_ref[...]
    lane = lax.broadcasted_iota(jnp.int32, (rows, HEAD_DIM), 1)
    seg = seg_ref[...]
    extra = jnp.where(lane == 21, 1.0, 0.0)
    for s in range(3):
        extra = extra + jnp.where((lane == 18 + s) & (seg != s), 1.0, 0.0)
    zeros = jnp.zeros((rows, HEAD_DIM), BF16)
    for h in range(HEADS_DEV):
        delta = jnp.sum(product[:, head_columns(h)], axis=1, keepdims=True)
        delta_ref[h] = jnp.broadcast_to(delta, (rows, 128))
        for i, piece in enumerate(pieces_of(delta)):
            extra = extra + jnp.where(lane == 3 * h + i, piece, 0.0)
        for i, piece in enumerate(pieces_of(stat_ref[h][:, :1])):
            extra = extra + jnp.where(lane == 9 + 3 * h + i, piece, 0.0)
        g_ref[h] = jnp.concatenate([zeros, grad[:, head_columns(h)].astype(BF16)], axis=1)
    sent_ref[...] = jnp.concatenate([grad, extra], axis=1).astype(BF16)


def grad_rows(mixed, w_out, attended, stat, seg):
    rows = mixed.shape[0]
    return pl.pallas_call(
        grad_rows_kernel,
        out_shape=(
            jax.ShapeDtypeStruct((rows, 256), BF16),
            jax.ShapeDtypeStruct((HEADS_DEV, rows, 128), BF16),
            jax.ShapeDtypeStruct((HEADS_DEV, rows, 128), F32),
        ),
        in_specs=vmem_specs(5),
        out_specs=tuple(vmem_specs(3)),
        compiler_params=pltpu.CompilerParams(vmem_limit_bytes=VMEM_LIMIT),
        name="grad_rows",
    )(mixed, w_out, attended, stat, seg)


def send_out(held, out_ref, sem):
    copy = pltpu.make_async_copy(held, out_ref, sem)
    copy.start()
    copy.wait()


def last_rows(x, group):
    parts = x.reshape(64, 16, x.shape[1])[:, 4 * group : 4 * group + 4]
    return jnp.concatenate([jnp.zeros((64, 12, x.shape[1]), F32), parts], axis=1).reshape(x.shape)


def early_grads_kernel(spread_ref, branch_ref, activated_ref, first_ref, up_ref, out_ref, held, sem):
    quarter = held.shape[1] // 3
    made = []
    for left, right in ((first_ref, up_ref), (branch_ref, activated_ref)):
        wide = jnp.dot(left[...], spread_ref[...], preferred_element_type=F32).astype(BF16)
        for half in range(2):
            made.append(dot_tn(wide, right[:, half * quarter : (half + 1) * quarter]))
    for g in range(3):
        held[:, g * quarter : (g + 1) * quarter] = (made[g] + last_rows(made[3], g)).astype(BF16)
    send_out(held, out_ref, sem)


def early_grads(spread, branch, activated, first, up):
    shape = (spread.shape[1], up.shape[1] * 3 // 2)
    return pl.pallas_call(
        early_grads_kernel,
        out_shape=jax.ShapeDtypeStruct(shape, BF16),
        in_specs=vmem_specs(5),
        out_specs=pl.BlockSpec(memory_space=pltpu.HBM),
        scratch_shapes=[pltpu.VMEM(shape, BF16), pltpu.SemaphoreType.DMA],
        compiler_params=pltpu.CompilerParams(vmem_limit_bytes=VMEM_LIMIT),
        name="early_grads",
    )(spread, branch, activated, first, up)


def out_rows_kernel(spread_ref, mixed_ref, attended_ref, out_ref):
    wide = jnp.dot(mixed_ref[...], spread_ref[...], preferred_element_type=F32).astype(BF16)
    made = dot_tn(wide, attended_ref[...].astype(BF16))
    out_ref[...] = jnp.concatenate([last_rows(made, g) for g in range(3)], axis=1).astype(BF16)


def out_rows(spread, mixed, attended):
    return pl.pallas_call(
        out_rows_kernel,
        out_shape=jax.ShapeDtypeStruct((spread.shape[1], 3 * attended.shape[1]), BF16),
        in_specs=vmem_specs(3),
        out_specs=vmem_specs(1)[0],
        compiler_params=pltpu.CompilerParams(vmem_limit_bytes=VMEM_LIMIT),
        name="out_rows",
    )(spread, mixed, attended)


def vector_rows_kernel(
    cot_ref, two_ref, resid_two_ref, first_ref, one_ref, resid_one_ref, up_ref, spread_ref, bias_ref,
    parts_ref, out_ref,
):
    cot, first = cot_ref[...].astype(F32), first_ref[...]
    columns = (
        first * one_ref[...],
        cot * two_ref[...],
        resid_one_ref[...],
        first,
        resid_two_ref[...],
        cot,
    )
    rows = jnp.concatenate([jnp.sum(c, axis=0, keepdims=True) for c in columns], axis=0)
    bias = jnp.sum(up_ref[...].astype(F32), axis=0, keepdims=True) * parts_ref[...]
    made = [
        jnp.dot(rows.astype(BF16), spread_ref[...], preferred_element_type=F32),
        jnp.dot(bias.astype(BF16), bias_ref[...], preferred_element_type=F32),
    ]
    out_ref[...] = jnp.concatenate(made, axis=0)


def vector_rows(spread, *args):
    return pl.pallas_call(
        vector_rows_kernel,
        out_shape=jax.ShapeDtypeStruct((8, spread.shape[1]), F32),
        in_specs=vmem_specs(10),
        out_specs=vmem_specs(1)[0],
        compiler_params=pltpu.CompilerParams(vmem_limit_bytes=VMEM_LIMIT),
        name="vector_rows",
    )(*args)


def late_grads_kernel(
    hid_ref, dkv_ref, dq_ref, rows_ref, q_place_ref, v_place_ref, placed_ref, w_ref, spread_ref,
    out_ref, back_ref, held, sem,
):
    wide = hid_ref.shape[1]
    grads = jnp.concatenate([dkv_ref[...], dq_ref[...]], axis=1)
    cols = grads.shape[1]
    made = dot_tn(hid_ref[...], grads) + placed_ref[...].astype(F32)
    sums = [rows_ref[...]]
    for grad, place in ((dq_ref, q_place_ref), (dkv_ref, v_place_ref)):
        row = jnp.sum(grad[...].astype(F32), axis=0, keepdims=True).astype(BF16)
        sums.append(jnp.dot(row, place[...], preferred_element_type=F32))
    sums.append(jnp.zeros((128 - 10, wide), F32))
    small = jnp.transpose(jnp.concatenate(sums, axis=0))[:, :64]
    held[...] = jnp.concatenate([made, small], axis=1).astype(BF16)
    copy = pltpu.make_async_copy(held, out_ref, sem)
    copy.start()
    back = dot_nt(grads, w_ref[:, :cols]).astype(BF16)
    back_ref[...] = dot_nt(back, spread_ref[...]).astype(BF16)
    copy.wait()


def late_grads(hid, dkv, dq, rows, q_place, v_place, placed, w, spread):
    shape = (hid.shape[1], dkv.shape[1] + dq.shape[1] + 64)
    return pl.pallas_call(
        late_grads_kernel,
        out_shape=(
            jax.ShapeDtypeStruct(shape, BF16),
            jax.ShapeDtypeStruct((hid.shape[0], spread.shape[0]), BF16),
        ),
        in_specs=vmem_specs(9),
        out_specs=(pl.BlockSpec(memory_space=pltpu.HBM), vmem_specs(1)[0]),
        scratch_shapes=[pltpu.VMEM(shape, BF16), pltpu.SemaphoreType.DMA],
        compiler_params=pltpu.CompilerParams(vmem_limit_bytes=VMEM_LIMIT),
        name="late_grads",
    )(hid, dkv, dq, rows, q_place, v_place, placed, w, spread)


def project_kernel(hid_ref, w_ref, bias_ref, scale_ref, sent_ref, q_ref):
    made = jnp.dot(hid_ref[...], w_ref[...], preferred_element_type=F32) + bias_ref[...]
    made = (made.astype(BF16).astype(F32) * scale_ref[...]).astype(BF16)
    sent_ref[...] = made
    zeros = jnp.zeros((made.shape[0], HEAD_DIM), BF16)
    for h in range(HEADS_DEV):
        at = 2 * HEADS_DEV * HEAD_DIM + h * HEAD_DIM
        q_ref[h] = jnp.concatenate([made[:, at : at + HEAD_DIM], zeros], axis=1)


def project(hid, w, bias, scale):
    rows = hid.shape[0]
    return pl.pallas_call(
        project_kernel,
        out_shape=(
            jax.ShapeDtypeStruct((rows, w.shape[1]), BF16),
            jax.ShapeDtypeStruct((HEADS_DEV, rows, 128), BF16),
        ),
        in_specs=vmem_specs(4),
        out_specs=tuple(vmem_specs(2)),
        compiler_params=pltpu.CompilerParams(vmem_limit_bytes=VMEM_LIMIT),
        name="project",
    )(hid, w, bias, scale)


def key_back_blocks(k_ref, v_ref, k_acc, v_acc, q_buffer, g_buffer, q_sems, g_sems):
    def step(j, carry):
        queries = block_of(q_buffer, q_sems, j)
        grads = block_of(g_buffer, g_sems, j)
        lane = lax.broadcasted_iota(jnp.int32, queries.shape, 1)
        queries = jnp.where(lane < HEADS_DEV * HEAD_DIM, queries, grads)
        for h in range(HEADS_DEV):
            scores = lax.dot_general(k_ref[h], queries, NT, preferred_element_type=F32)
            probs = jnp.exp(scores)
            v_acc[h] = v_acc[h] + jnp.dot(probs.astype(BF16), grads, preferred_element_type=F32)
            back = probs * lax.dot_general(v_ref[h], grads, NT, preferred_element_type=F32)
            k_acc[h] = k_acc[h] + jnp.dot(back.astype(BF16), queries, preferred_element_type=F32)
        return carry

    lax.fori_loop(0, q_sems.shape[0], step, 0)


def key_heads(kv_ref, tag_ref, k_heads, v_heads):
    rows = kv_ref.shape[0]
    feat = HEADS_DEV * HEAD_DIM
    lane = lax.broadcasted_iota(jnp.int32, (rows, HEAD_DIM), 1)
    tag = tag_ref[...]
    masks = jnp.where((lane == 21) & (tag < 0), NEG, 0.0)
    for s in range(3):
        masks = masks + jnp.where((lane == 18 + s) & (tag == s), NEG, 0.0)
    for h in range(HEADS_DEV):
        block = kv_ref[:, head_block(h)].astype(F32)
        before = [jnp.zeros((rows, h * HEAD_DIM), F32)] if h else []
        left = feat - (h + 1) * HEAD_DIM
        after = [jnp.zeros((rows, left), F32)] if left else []
        k_extra = masks - jnp.where((lane >= 9 + 3 * h) & (lane < 12 + 3 * h), 1.0, 0.0)
        v_extra = -jnp.where((lane >= 3 * h) & (lane < 3 * h + 3), 1.0, 0.0)
        for heads, part, extra in (
            (k_heads, block[:, :HEAD_DIM], k_extra),
            (v_heads, block[:, HEAD_DIM:], v_extra),
        ):
            heads[h] = jnp.concatenate(before + [part] + after + [extra], axis=1).astype(BF16)


def key_near_kernel(count, kv_ref, tag_ref, *rest):
    q_blocks, g_blocks = rest[:count], rest[count : count + 6]
    k_acc, v_acc, k_heads, v_heads, q_buffer, q_sems, g_buffer, g_sems = rest[count + 6 :]
    copies_in(q_blocks, q_buffer, q_sems, 2 * HEADS_DEV * HEAD_DIM)
    copies_in(g_blocks, g_buffer, g_sems)
    key_heads(kv_ref, tag_ref, k_heads, v_heads)
    k_acc[...] = jnp.zeros_like(k_acc)
    v_acc[...] = jnp.zeros_like(v_acc)
    key_back_blocks(k_heads, v_heads, k_acc, v_acc, q_buffer, g_buffer, q_sems, g_sems)


def key_far_kernel(kv_ref, tag_ref, diag_ref, k_in, v_in, *rest):
    q_blocks, g_blocks = rest[:4], rest[4:8]
    dkv_ref, k_heads, v_heads, k_acc, v_acc, q_buffer, q_sems, g_buffer, g_sems = rest[8:]
    copies_in(q_blocks, q_buffer, q_sems, 2 * HEADS_DEV * HEAD_DIM)
    copies_in(g_blocks, g_buffer, g_sems)
    key_heads(kv_ref, tag_ref, k_heads, v_heads)
    k_acc[...], v_acc[...] = k_in[...], v_in[...]
    key_back_blocks(k_heads, v_heads, k_acc, v_acc, q_buffer, g_buffer, q_sems, g_sems)
    parts = []
    for h in range(HEADS_DEV):
        parts += [k_acc[h][:, head_columns(h)], v_acc[h][:, head_columns(h)]]
    dkv_ref[...] = (jnp.concatenate(parts, axis=1) + diag_ref[...]).astype(BF16)


def key_near(kv_own, tag, q_blocks, g_blocks):
    rows, width = kv_own.shape[0], g_blocks[0].shape[2]
    return pl.pallas_call(
        functools.partial(key_near_kernel, len(q_blocks)),
        out_shape=(head_state(rows, width),) * 2,
        in_specs=vmem_specs(2) + any_specs(len(q_blocks) + len(g_blocks)),
        out_specs=tuple(vmem_specs(2)),
        scratch_shapes=[pltpu.VMEM((HEADS_DEV, rows, width), BF16)] * 2
        + buffers(q_blocks, width)
        + buffers(g_blocks, width),
        compiler_params=pltpu.CompilerParams(vmem_limit_bytes=VMEM_LIMIT),
        cost_estimate=cost(rows, q_blocks, 2048),
        name="key_near",
    )(kv_own, tag, *q_blocks, *g_blocks)


def key_far(kv_own, tag, diagonal, state, q_blocks, g_blocks):
    rows, width = kv_own.shape[0], g_blocks[0].shape[2]
    return pl.pallas_call(
        key_far_kernel,
        out_shape=jax.ShapeDtypeStruct(diagonal.shape, BF16),
        in_specs=vmem_specs(5) + any_specs(8),
        out_specs=vmem_specs(1)[0],
        scratch_shapes=[pltpu.VMEM((HEADS_DEV, rows, width), BF16)] * 2
        + [pltpu.VMEM((HEADS_DEV, rows, width), F32)] * 2
        + buffers(q_blocks, width)
        + buffers(g_blocks, width),
        compiler_params=pltpu.CompilerParams(vmem_limit_bytes=VMEM_LIMIT),
        cost_estimate=cost(rows, q_blocks, 2048),
        name="key_far",
    )(kv_own, tag, diagonal, *state, *q_blocks, *g_blocks)


def dot(a, b):
    return jnp.dot(a, b, preferred_element_type=F32)


def dot_nt(a, b):
    return lax.dot_general(a, b, NT, preferred_element_type=F32)


def dot_tn(a, b):
    return lax.dot_general(a, b, (((0,), (0,)), ((), ())), preferred_element_type=F32)


def core_half(x, axis, at):
    size = x.shape[axis] // 2
    return lax.dynamic_slice_in_dim(x, at * size, size, axis)


def interleaved(k, v):
    shape = (*k.shape[:-1], -1, HEAD_DIM)
    return jnp.stack([k.reshape(shape), v.reshape(shape)], axis=-2).reshape(*k.shape[:-1], -1)


def per_device(
    hidden,
    w_qkv,
    w_out,
    b_qv,
    w_up,
    w_down,
    b_up,
    norm_gains,
    norm_shifts,
    segments,
    lengths,
    cotangent,
):
    core = lax.axis_index("core")
    heads_at = lax.axis_index("heads")
    own_ctx = ((lax.axis_index("z") * 4 + lax.axis_index("y")) * 2 + lax.axis_index("xh")) * 2 + core
    tok = hidden.shape[0]
    rows = w_up.shape[0]
    feat = HEADS_DEV * HEAD_DIM
    hidden_units = w_up.shape[1] // 2

    hid = chip_tokens(hidden)
    out_turned, down_turned = w_out.T, w_down.T
    low_tok = segments.astype(BF16).reshape(2, tok // 2)
    kv_cols = 2 * feat

    def halves(x):
        return jnp.swapaxes(x.reshape(rows, 2, -1), 0, 1)

    q_half, k_half, v_half = (halves(w_qkv[i]) for i in range(3))
    tail = jnp.broadcast_to(jnp.pad(low_tok, ((0, rows - 2), (0, 0))), (2, rows, tok // 2))
    urgent = jnp.concatenate([interleaved(k_half, v_half), q_half, tail], axis=2)
    urgent = jnp.pad(urgent, ((0, 0), (0, 16 - rows), (0, 0)))
    urgent = jnp.broadcast_to(urgent[None], (32, *urgent.shape)).reshape(64, 16, -1)
    urgent, *later = lax.optimization_barrier((urgent, out_turned, w_up, down_turned))
    later = jnp.concatenate([halves(w) for w in later], axis=2)
    mine = lax.dynamic_index_in_dim(later, core, 0, keepdims=False)
    theirs = shifted(lax.dynamic_index_in_dim(later, 1 - core, 0, keepdims=False), "core", 1)
    later = pair_ordered(mine, theirs, "core").reshape(2 * rows, -1)
    rest = lax.all_gather(later, CHIPS, axis=0, tiled=True)
    w_urgent = lax.all_to_all(urgent, CTX, 0, 0, tiled=True)
    seg_all = w_urgent[:, :2, kv_cols + feat :].reshape(-1, tok).astype(jnp.int32)
    w_urgent = w_urgent.reshape(64 * 16, -1)
    at_wide = jnp.arange(64 * 16, dtype=jnp.int32)
    at_feature = jnp.arange(64 * rows, dtype=jnp.int32)
    spread = (
        (at_feature // rows * 16 + at_feature % rows)[:, None] == at_wide[None, :]
    ).astype(BF16)
    hid_wide = dot(hid, spread).astype(BF16)

    w_out_t = rest[:, :feat]
    w_up_all = rest[:, feat : feat + hidden_units]
    w_down_t = rest[:, feat + hidden_units :]

    bias = b_qv.astype(F32)
    q_bias, v_bias = core_half(bias[0], 0, core), core_half(bias[1], 0, core)
    no_bias = jnp.zeros((tok // 2,), F32)
    bias_row = jnp.concatenate([interleaved(jnp.zeros_like(v_bias), v_bias), q_bias, no_bias])
    column = jnp.arange(bias_row.shape[0], dtype=jnp.int32)
    scale_row = jnp.where(
        column < kv_cols, 1.0, jnp.where(column < kv_cols + feat, HEAD_DIM ** (-0.5), 0.0)
    ).astype(F32)
    sent, q_heads = project(hid_wide, w_urgent, bias_row[None], scale_row[None])
    kv_own = sent[:, :kv_cols]
    starts = [jnp.sum((seg_all < s).astype(jnp.int32)) for s in range(3)]
    places = jnp.arange(seg_all.size, dtype=jnp.int32).reshape(seg_all.shape)
    run_end = jnp.zeros_like(seg_all)
    for s in range(3):
        run_end = jnp.where(seg_all == s, starts[s] + lengths[s], run_end)
    tag_all = jnp.where(places < run_end, seg_all, -1).astype(F32)
    order = jnp.concatenate([relative_order("z", "y", 0), relative_order("y", "z", 1)])
    tags = jnp.take(tag_all, order, axis=0).reshape(8, -1)
    both = jnp.stack([own_ctx, own_ctx + 1 - 2 * core])
    tag_own = jnp.take(tag_all, both, axis=0).reshape(-1, 1)
    seg_own = jnp.take(seg_all, both, axis=0).astype(F32).reshape(-1, 1)

    near, far = gather_second_pairs(*lax.optimization_barrier(gather_first_pairs(sent)))
    state = attend_near(q_heads, kv_own, tags, seg_own, tag_own, near)
    attended, stat = attend_far(q_heads, tags, seg_own, state, far)
    attended_low = attended.astype(BF16)

    gain_rows = norm_gains.astype(F32)
    shifts = norm_shifts.astype(F32)
    attn_mixed = team_sum(dot_nt(attended_low, w_out_t))
    first_out, normed_one, inverse_one = layer_norm(
        hidden.astype(F32) + attn_mixed + shifts[0], gain_rows[0], shifts[1]
    )
    first_low = chip_tokens(first_out.astype(BF16))
    up_bias = core_half(b_up, 0, core).astype(F32)
    up_proj = dot(first_low, w_up_all) + up_bias
    activated = exact_gelu(up_proj).astype(BF16)
    second = team_sum(dot_nt(activated, w_down_t))
    output, normed_two, inverse_two = layer_norm(
        first_out + second + shifts[2], gain_rows[1], shifts[3]
    )
    resid_two = norm_back(
        cotangent.astype(F32), normed_two, inverse_two, gain_rows[1]
    )
    branch_low = chip_tokens(resid_two.astype(BF16))
    act_grad = dot(branch_low, w_down_t)
    up_low = jax.vjp(exact_gelu, up_proj)[1](act_grad)[0].astype(BF16)
    first_grad = resid_two + team_sum(dot_nt(up_low, w_up_all))
    resid_one = norm_back(first_grad, normed_one, inverse_one, gain_rows[0])
    mixed_low = chip_tokens(resid_one.astype(BF16))
    g_sent, g_heads, delta = grad_rows(mixed_low, w_out_t, attended, stat, seg_own)
    made = early_grads(spread, branch_low, activated, first_low, up_low)
    (g_z, g_y), g_heads, planes = lax.optimization_barrier(
        (gather_first(g_sent), g_heads, to_planes(made))
    )
    g_near, g_far = gather_second(g_z, g_y)
    early = planes_to_owners(planes)
    out_placed = out_rows(spread, mixed_low, attended_low)
    at_bias = jnp.arange(hidden_units, dtype=jnp.int32)
    at_half = jnp.arange(feat, dtype=jnp.int32)
    at_kv = jnp.arange(kv_cols, dtype=jnp.int32)

    def placed(owner, row):
        return ((owner * 16 + row)[:, None] == at_wide[None, :]).astype(BF16)

    first_owner = 32 * core
    bias_place = placed(first_owner + at_bias // 24, at_bias % 12)
    q_place = placed(first_owner + at_half // 6, at_half % 6)
    at_value = at_kv // 128 * HEAD_DIM + at_kv % 128 - HEAD_DIM
    is_value = at_kv % 128 >= HEAD_DIM
    v_place = placed(jnp.where(is_value, first_owner + at_value // 6, -1), at_value % 6)
    parts = jnp.arange(2, dtype=jnp.int32)[:, None] == (at_bias % 24 // 12)[None, :]
    rows_made = vector_rows(
        spread,
        cotangent,
        normed_two,
        resid_two,
        first_grad,
        normed_one,
        resid_one,
        up_low,
        spread,
        bias_place,
        parts.astype(F32),
    )

    dq, diagonal = query_back(
        q_heads, g_heads, kv_own, tags, seg_own, tag_own, stat, delta, near + far
    )
    key_state = key_near(kv_own, tag_own, near, g_near)
    dkv = key_far(kv_own, tag_own, diagonal, key_state, far, g_far)
    dkv, early = lax.optimization_barrier((dkv, early))
    late, back = late_grads(
        hid_wide, dkv, dq, rows_made, q_place, v_place, out_placed, w_urgent, spread
    )
    late = to_owners(late)
    hidden_grad = resid_one + team_sum(back.astype(F32))

    early_sums, late_sums = owner_sums(early), owner_sums(late)

    def columns(x, start, size):
        return jnp.concatenate([x[c, :rows, start : start + size] for c in range(2)], axis=1)

    kv_pairs = columns(late_sums, 0, kv_cols).reshape(rows, 2 * HEADS_DEV, 2, HEAD_DIM)
    k_cols = kv_pairs[:, :, 0].reshape(rows, -1)
    v_cols = kv_pairs[:, :, 1].reshape(rows, -1)
    q_cols = columns(late_sums, kv_cols, feat)

    def last(x, size):
        return jnp.concatenate(
            [x[:, rows:, g * size : (g + 1) * size] for g in range(3)], axis=1
        )

    quarter = hidden_units // 2
    up_cols = columns(early_sums, 0, hidden_units)
    down_first, down_last = early_sums[:, :rows, hidden_units:], last(early_sums, quarter)
    down_cols = jnp.concatenate(
        [down_first[0], down_last[0], down_first[1], down_last[1]], axis=1
    )
    out_last = last(late_sums, feat)
    out_cols = jnp.concatenate([out_last[0], out_last[1]], axis=1)
    small = (late_sums[0] + late_sums[1])[:rows, kv_cols + feat :].T
    vec_out = small[:6].reshape(6, 2, 6)
    bias_out = small[6:8].reshape(-1)
    qv_out = small[8:10, :6]
    vec_out = lax.dynamic_index_in_dim(vec_out, heads_at, 1, keepdims=False)
    return (
        output.astype(BF16),
        hidden_grad,
        jnp.stack([q_cols, k_cols, v_cols]),
        out_cols.T,
        qv_out,
        up_cols,
        down_cols.T,
        bias_out,
        vec_out[:2],
        vec_out[2:],
    )


def solution(mesh):
    fine = Mesh(mesh.devices.reshape(4, 4, 2, 2, 2), ("z", "y", "xh", "core", "heads"))
    return jax.shard_map(
        per_device,
        mesh=fine,
        in_specs=(
            P(CTX, None),
            P(None, CTX, "heads"),
            P("heads", CTX),
            P(None, "heads"),
            P(CTX, "heads"),
            P("heads", CTX),
            P("heads"),
            P(),
            P(),
            P(CTX),
            P(),
            P(CTX, None),
        ),
        out_specs=(
            P(CTX, None),
            P(CTX, None),
            P(None, CTX, "heads"),
            P("heads", CTX),
            P(None, ("heads", *CTX)),
            P(CTX, "heads"),
            P("heads", CTX),
            P(("heads", *CTX)),
            P(None, (*CTX, "heads")),
            P(None, (*CTX, "heads")),
        ),
        check_vma=False,
    )
```

```python
import jax
import jax.numpy as jnp
from jax import lax
from jax.experimental import pallas as pl
from jax.experimental.pallas import tpu as pltpu
from jax.sharding import Mesh, PartitionSpec as P

HEAD_DIM = 64
HEADS_DEV = 3
EPS = 1e-06
NEG = -1e30
CTX = ("z", "y", "xh", "core")
CHIPS = ("z", "y", "xh")
F32 = jnp.float32
BF16 = jnp.bfloat16
NT = (((1,), (1,)), ((), ()))
VMEM_LIMIT = 50 * 1024 * 1024
OFFSETS = (0, -1, 1, 2)


def shifted(x, axis, step):
    n = lax.axis_size(axis)
    return lax.ppermute(x, axis, [(i, (i + step) % n) for i in range(n)])


def ring_halves(x, axis):
    half = x.shape[0] // 2
    before, after = shifted(x, axis, 1), shifted(x, axis, -1)
    return [x, before, after, shifted(before[:half], axis, 1), shifted(after[half:], axis, -1)]


def gather_first(x):
    half = x.shape[0] // 2
    streams = []
    for part, axis in ((x[:half], "z"), (x[half:], "y")):
        both = jnp.concatenate([part, shifted(part, "xh", 1)], axis=0)
        streams.append(jnp.concatenate(ring_halves(both, axis), axis=0))
    return tuple(streams)


def gather_second(z_stream, y_stream):
    blocks = ring_halves(z_stream, "y") + ring_halves(y_stream, "z")
    return [b.reshape(-1, z_stream.shape[0] // 2, b.shape[1]) for b in blocks]


def near_blocks(blocks):
    return blocks[:3] + blocks[5:8]


def far_blocks(blocks):
    return blocks[3:5] + blocks[8:]


def relative_order(first, second, core_at):
    place = {a: lax.axis_index(a) for a in CHIPS}
    core = lax.axis_index("core")
    order = []
    for second_step in OFFSETS:
        for first_step in OFFSETS:
            for xh_step in (0, 1):
                at = dict(place)
                at[first] = (at[first] + first_step) % 4
                at[second] = (at[second] + second_step) % 4
                at["xh"] = (at["xh"] + xh_step) % 2
                order.append(((at["z"] * 4 + at["y"]) * 2 + at["xh"]) * 2 + (core + core_at) % 2)
    return jnp.stack(order)


def pair_ordered(own, other, axis):
    first = lax.axis_index(axis) == 0
    return jnp.stack([jnp.where(first, own, other), jnp.where(first, other, own)])


def to_owners(x):
    return lax.all_to_all(x.reshape(64, 16, -1), CTX, 0, 0, tiled=True)


def owner_sums(parts):
    return jnp.sum(parts.reshape(-1, 2, *parts.shape[1:]).astype(F32), axis=0)


def team_sum(partial):
    rows = partial.shape[0] // 2
    near = partial[:rows] + shifted(partial[rows:].astype(BF16), "core", 1).astype(F32)
    low = lax.optimization_barrier(near.astype(BF16))
    return low.astype(F32) + shifted(low, "heads", 1).astype(F32)


def chip_tokens(x):
    return jnp.concatenate([x, shifted(x, "core", 1)], axis=0)


def layer_norm(residual, gain_row, shift_row):
    centred = residual - jnp.mean(residual, axis=-1, keepdims=True)
    inverse = lax.rsqrt(jnp.mean(centred * centred, axis=-1, keepdims=True) + EPS)
    normed = centred * inverse
    return (normed * gain_row + shift_row, normed, inverse)


def norm_back(incoming, normed, inverse, gain_row):
    scaled = incoming * gain_row
    projected = (
        scaled
        - jnp.mean(scaled, axis=-1, keepdims=True)
        - normed * jnp.mean(scaled * normed, axis=-1, keepdims=True)
    )
    return inverse * projected


def exact_gelu(pre_act):
    return jax.nn.gelu(pre_act, approximate=False)


def pieces_of(column):
    high = column.astype(BF16).astype(F32)
    middle = (column - high).astype(BF16).astype(F32)
    return high, middle, column - high - middle


def head_columns(h):
    return slice(h * HEAD_DIM, (h + 1) * HEAD_DIM)


def head_block(h):
    return slice(h * 128, (h + 1) * 128)


def diagonal_scores(q_ref, kv_ref, h):
    product = q_ref[h].astype(F32) * kv_ref[:, head_block(h)].astype(F32)
    return jnp.sum(product, axis=1, keepdims=True)


def copies_in(sources, buffer, sems):
    at = 0
    for source in sources:
        size = source.shape[0]
        pltpu.make_async_copy(source, buffer.at[pl.ds(at, size)], sems.at[at // 2]).start()
        at += size


def block_of(buffer, sems, j):
    block = buffer.at[pl.ds(2 * j, 2)]
    pltpu.make_async_copy(block, block, sems.at[j]).wait()
    return buffer[pl.ds(2 * j, 2)].reshape(-1, buffer.shape[2])


def attend_blocks(q_ref, tags_ref, seg_ref, top, total, acc, buffer, sems, row_of):
    rows = q_ref.shape[1]
    seg_wide = jnp.broadcast_to(seg_ref[...], (rows, 128))

    def step(j, carry):
        whole = block_of(buffer, sems, j)
        tags = tags_ref[pl.ds(row_of(j), 1), :]
        keys = tags.shape[1]
        allowed = jnp.tile(seg_wide, (1, keys // 128)) == tags
        for h in range(HEADS_DEV):
            kv = whole[:, head_block(h)]
            scores = lax.dot_general(q_ref[h], kv, NT, preferred_element_type=F32)
            scores = jnp.where(allowed, scores, NEG)
            before = top[h]
            now = jnp.maximum(before, jnp.max(scores, axis=1, keepdims=True))
            weights = jnp.exp(scores - jnp.tile(now, (1, keys // 128)))
            fade = jnp.exp(before - now)
            sums = weights[:, :128]
            for k in range(1, keys // 128):
                sums = sums + weights[:, k * 128 : (k + 1) * 128]
            total[h] = total[h] * fade + sums
            acc[h] = acc[h] * fade + jnp.dot(weights.astype(BF16), kv, preferred_element_type=F32)
            top[h] = now
        return carry

    lax.fori_loop(0, sems.shape[0], step, 0)


def near_row(j):
    return j + (j >= 3).astype(jnp.int32)


def far_row(j):
    return 4 * j + 3


def attend_near_kernel(q_ref, own_ref, tags_ref, seg_ref, tag_ref, *rest):
    blocks, (top, total, acc, buffer, sems) = rest[:6], rest[6:]
    copies_in(blocks, buffer, sems)
    rows = q_ref.shape[1]
    padded = tag_ref[...] < 0
    for h in range(HEADS_DEV):
        diagonal = diagonal_scores(q_ref, own_ref, h)
        top[h] = jnp.broadcast_to(jnp.where(padded, diagonal, NEG), (rows, 128))
        lane = lax.broadcasted_iota(jnp.int32, (rows, 128), 1)
        total[h] = jnp.where((lane == 0) & padded, 1.0, 0.0)
        acc[h] = jnp.where(padded, own_ref[:, head_block(h)].astype(F32), 0.0)
    attend_blocks(q_ref, tags_ref, seg_ref, top, total, acc, buffer, sems, near_row)


def attend_far_kernel(q_ref, tags_ref, seg_ref, top_in, total_in, acc_in, *rest):
    blocks, (out_ref, stat_ref, top, total, acc, buffer, sems) = rest[:4], rest[4:]
    copies_in(blocks, buffer, sems)
    top[...], total[...], acc[...] = top_in[...], total_in[...], acc_in[...]
    attend_blocks(q_ref, tags_ref, seg_ref, top, total, acc, buffer, sems, far_row)
    outs = []
    for h in range(HEADS_DEV):
        sums = jnp.sum(total[h], axis=1, keepdims=True)
        outs.append((acc[h] / sums)[:, HEAD_DIM:])
        stat_ref[h] = top[h] + jnp.log(sums)
    out_ref[...] = jnp.concatenate(outs, axis=1)


def vmem_specs(n):
    return [pl.BlockSpec(memory_space=pltpu.VMEM)] * n


def any_specs(n):
    return [pl.BlockSpec(memory_space=pl.ANY)] * n


def head_state(rows, lanes=128):
    return jax.ShapeDtypeStruct((HEADS_DEV, rows, lanes), F32)


def cost(rows, blocks, flops):
    keys = sum(b.shape[0] * b.shape[1] for b in blocks)
    pairs = rows * keys * HEADS_DEV
    return pl.CostEstimate(
        flops=pairs * flops, bytes_accessed=keys * 1024, transcendentals=pairs
    )


def buffers(blocks, lanes):
    count = sum(b.shape[0] for b in blocks)
    return [
        pltpu.VMEM((count, blocks[0].shape[1], lanes), BF16),
        pltpu.SemaphoreType.DMA((count // 2,)),
    ]


def attend_near(q_heads, kv_own, tags, seg, tag, blocks):
    rows = kv_own.shape[0]
    return pl.pallas_call(
        attend_near_kernel,
        out_shape=(head_state(rows),) * 3,
        in_specs=vmem_specs(5) + any_specs(6),
        out_specs=tuple(vmem_specs(3)),
        scratch_shapes=buffers(blocks, kv_own.shape[1]),
        compiler_params=pltpu.CompilerParams(vmem_limit_bytes=VMEM_LIMIT),
        cost_estimate=cost(rows, blocks, 512),
        name="attend_near",
    )(q_heads, kv_own, tags, seg, tag, *blocks)


def attend_far(q_heads, tags, seg, state, blocks):
    rows = q_heads.shape[1]
    return pl.pallas_call(
        attend_far_kernel,
        out_shape=(jax.ShapeDtypeStruct((rows, HEADS_DEV * HEAD_DIM), F32), head_state(rows)),
        in_specs=vmem_specs(6) + any_specs(4),
        out_specs=tuple(vmem_specs(2)),
        scratch_shapes=[pltpu.VMEM((HEADS_DEV, rows, 128), F32)] * 3
        + buffers(blocks, HEADS_DEV * 128),
        compiler_params=pltpu.CompilerParams(vmem_limit_bytes=VMEM_LIMIT),
        cost_estimate=cost(rows, blocks, 512),
        name="attend_far",
    )(q_heads, tags, seg, *state, *blocks)


def query_back_kernel(q_ref, g_ref, own_ref, tags_ref, seg_ref, tag_ref, stat_ref, delta_ref, *rest):
    blocks, (dq_ref, dkv_ref, buffer, sems, acc) = rest[:10], rest[10:]
    copies_in(blocks, buffer, sems)
    rows = q_ref.shape[1]
    seg_wide = jnp.broadcast_to(seg_ref[...], (rows, 128))
    padded = tag_ref[...] < 0
    for h in range(HEADS_DEV):
        own = own_ref[:, head_block(h)].astype(F32)
        prob = jnp.exp(diagonal_scores(q_ref, own_ref, h) - stat_ref[h][:, :1])
        prob = jnp.where(padded, prob, 0.0)
        grad = diagonal_scores(g_ref, own_ref, h) - delta_ref[h][:, :1]
        score = (prob * grad).astype(BF16).astype(F32)
        acc[h] = score * own
        dkv_ref[:, head_block(h)] = score * q_ref[h].astype(F32) + prob.astype(BF16).astype(
            F32
        ) * g_ref[h].astype(F32)

    def step(j, carry):
        whole = block_of(buffer, sems, j)
        tags = tags_ref[pl.ds(jnp.where(j < 6, near_row(j), far_row(j - 6)), 1), :]
        keys = tags.shape[1]
        allowed = jnp.tile(seg_wide, (1, keys // 128)) == tags
        for h in range(HEADS_DEV):
            kv = whole[:, head_block(h)]
            scores = lax.dot_general(q_ref[h], kv, NT, preferred_element_type=F32)
            scores = jnp.where(allowed, scores, NEG)
            probs = jnp.exp(scores - jnp.tile(stat_ref[h], (1, keys // 128)))
            grads = lax.dot_general(g_ref[h], kv, NT, preferred_element_type=F32)
            back = probs * (grads - jnp.tile(delta_ref[h], (1, keys // 128)))
            acc[h] = acc[h] + jnp.dot(back.astype(BF16), kv, preferred_element_type=F32)
        return carry

    lax.fori_loop(0, 8, step, 0)
    dq_ref[...] = (
        jnp.concatenate([acc[h][:, :HEAD_DIM] for h in range(HEADS_DEV)], axis=1)
        * HEAD_DIM ** (-0.5)
    ).astype(BF16)


def query_back(q_heads, g_heads, kv_own, tags, seg, tag, stat, delta, blocks):
    rows = kv_own.shape[0]
    return pl.pallas_call(
        query_back_kernel,
        out_shape=(
            jax.ShapeDtypeStruct((rows, HEADS_DEV * HEAD_DIM), BF16),
            jax.ShapeDtypeStruct(kv_own.shape, F32),
        ),
        in_specs=vmem_specs(8) + any_specs(10),
        out_specs=tuple(vmem_specs(2)),
        scratch_shapes=buffers(blocks, kv_own.shape[1]) + [pltpu.VMEM((HEADS_DEV, rows, 128), F32)],
        compiler_params=pltpu.CompilerParams(vmem_limit_bytes=VMEM_LIMIT),
        cost_estimate=cost(rows, blocks, 768),
        name="query_back",
    )(q_heads, g_heads, kv_own, tags, seg, tag, stat, delta, *blocks)


def grad_rows_kernel(
    mixed_ref, out_ref, attended_ref, stat_ref, seg_ref, sent_ref, g_ref, delta_ref
):
    rows = mixed_ref.shape[0]
    grad = jnp.dot(mixed_ref[...], out_ref[...], preferred_element_type=F32).astype(BF16)
    grad = grad.astype(F32)
    product = grad * attended_ref[...]
    lane = lax.broadcasted_iota(jnp.int32, (rows, HEAD_DIM), 1)
    seg = seg_ref[...]
    extra = jnp.where(lane == 21, 1.0, 0.0)
    for s in range(3):
        extra = extra + jnp.where((lane == 18 + s) & (seg != s), 1.0, 0.0)
    zeros = jnp.zeros((rows, HEAD_DIM), BF16)
    for h in range(HEADS_DEV):
        delta = jnp.sum(product[:, head_columns(h)], axis=1, keepdims=True)
        delta_ref[h] = jnp.broadcast_to(delta, (rows, 128))
        for i, piece in enumerate(pieces_of(delta)):
            extra = extra + jnp.where(lane == 3 * h + i, piece, 0.0)
        for i, piece in enumerate(pieces_of(stat_ref[h][:, :1])):
            extra = extra + jnp.where(lane == 9 + 3 * h + i, piece, 0.0)
        g_ref[h] = jnp.concatenate([zeros, grad[:, head_columns(h)].astype(BF16)], axis=1)
    sent_ref[...] = jnp.concatenate([grad, extra], axis=1).astype(BF16)


def grad_rows(mixed, w_out, attended, stat, seg):
    rows = mixed.shape[0]
    return pl.pallas_call(
        grad_rows_kernel,
        out_shape=(
            jax.ShapeDtypeStruct((rows, 256), BF16),
            jax.ShapeDtypeStruct((HEADS_DEV, rows, 128), BF16),
            jax.ShapeDtypeStruct((HEADS_DEV, rows, 128), F32),
        ),
        in_specs=vmem_specs(5),
        out_specs=tuple(vmem_specs(3)),
        compiler_params=pltpu.CompilerParams(vmem_limit_bytes=VMEM_LIMIT),
        name="grad_rows",
    )(mixed, w_out, attended, stat, seg)


def send_out(held, out_ref, sem):
    copy = pltpu.make_async_copy(held, out_ref, sem)
    copy.start()
    copy.wait()


def last_rows(x, group):
    parts = x.reshape(64, 16, x.shape[1])[:, 4 * group : 4 * group + 4]
    return jnp.concatenate([jnp.zeros((64, 12, x.shape[1]), F32), parts], axis=1).reshape(x.shape)


def early_grads_kernel(spread_ref, branch_ref, activated_ref, first_ref, up_ref, out_ref, held, sem):
    quarter = held.shape[1] // 3
    made = []
    for left, right in ((first_ref, up_ref), (branch_ref, activated_ref)):
        wide = jnp.dot(left[...], spread_ref[...], preferred_element_type=F32).astype(BF16)
        for half in range(2):
            made.append(dot_tn(wide, right[:, half * quarter : (half + 1) * quarter]))
    for g in range(3):
        held[:, g * quarter : (g + 1) * quarter] = (made[g] + last_rows(made[3], g)).astype(BF16)
    send_out(held, out_ref, sem)


def early_grads(spread, branch, activated, first, up):
    shape = (spread.shape[1], up.shape[1] * 3 // 2)
    return pl.pallas_call(
        early_grads_kernel,
        out_shape=jax.ShapeDtypeStruct(shape, BF16),
        in_specs=vmem_specs(5),
        out_specs=pl.BlockSpec(memory_space=pltpu.HBM),
        scratch_shapes=[pltpu.VMEM(shape, BF16), pltpu.SemaphoreType.DMA],
        compiler_params=pltpu.CompilerParams(vmem_limit_bytes=VMEM_LIMIT),
        name="early_grads",
    )(spread, branch, activated, first, up)


def out_rows_kernel(spread_ref, mixed_ref, attended_ref, out_ref):
    wide = jnp.dot(mixed_ref[...], spread_ref[...], preferred_element_type=F32).astype(BF16)
    made = dot_tn(wide, attended_ref[...].astype(BF16))
    out_ref[...] = jnp.concatenate([last_rows(made, g) for g in range(3)], axis=1).astype(BF16)


def out_rows(spread, mixed, attended):
    return pl.pallas_call(
        out_rows_kernel,
        out_shape=jax.ShapeDtypeStruct((spread.shape[1], 3 * attended.shape[1]), BF16),
        in_specs=vmem_specs(3),
        out_specs=vmem_specs(1)[0],
        compiler_params=pltpu.CompilerParams(vmem_limit_bytes=VMEM_LIMIT),
        name="out_rows",
    )(spread, mixed, attended)


def vector_rows_kernel(
    cot_ref, two_ref, resid_two_ref, first_ref, one_ref, resid_one_ref, up_ref, spread_ref, bias_ref,
    parts_ref, out_ref,
):
    cot, first = cot_ref[...].astype(F32), first_ref[...]
    columns = (
        first * one_ref[...],
        cot * two_ref[...],
        resid_one_ref[...],
        first,
        resid_two_ref[...],
        cot,
    )
    rows = jnp.concatenate([jnp.sum(c, axis=0, keepdims=True) for c in columns], axis=0)
    bias = jnp.sum(up_ref[...].astype(F32), axis=0, keepdims=True) * parts_ref[...]
    made = [
        jnp.dot(rows.astype(BF16), spread_ref[...], preferred_element_type=F32),
        jnp.dot(bias.astype(BF16), bias_ref[...], preferred_element_type=F32),
    ]
    out_ref[...] = jnp.concatenate(made, axis=0)


def vector_rows(spread, *args):
    return pl.pallas_call(
        vector_rows_kernel,
        out_shape=jax.ShapeDtypeStruct((8, spread.shape[1]), F32),
        in_specs=vmem_specs(10),
        out_specs=vmem_specs(1)[0],
        compiler_params=pltpu.CompilerParams(vmem_limit_bytes=VMEM_LIMIT),
        name="vector_rows",
    )(*args)


def late_grads_kernel(
    hid_ref, dkv_ref, dq_ref, rows_ref, q_place_ref, v_place_ref, placed_ref, w_ref, spread_ref,
    out_ref, back_ref, held, sem,
):
    wide = hid_ref.shape[1]
    grads = jnp.concatenate([dkv_ref[...], dq_ref[...]], axis=1)
    cols = grads.shape[1]
    made = dot_tn(hid_ref[...], grads) + placed_ref[...].astype(F32)
    sums = [rows_ref[...]]
    for grad, place in ((dq_ref, q_place_ref), (dkv_ref, v_place_ref)):
        row = jnp.sum(grad[...].astype(F32), axis=0, keepdims=True).astype(BF16)
        sums.append(jnp.dot(row, place[...], preferred_element_type=F32))
    sums.append(jnp.zeros((128 - 10, wide), F32))
    small = jnp.transpose(jnp.concatenate(sums, axis=0))[:, :64]
    held[...] = jnp.concatenate([made, small], axis=1).astype(BF16)
    copy = pltpu.make_async_copy(held, out_ref, sem)
    copy.start()
    back = dot_nt(grads, w_ref[:, :cols]).astype(BF16)
    back_ref[...] = dot_nt(back, spread_ref[...]).astype(BF16)
    copy.wait()


def late_grads(hid, dkv, dq, rows, q_place, v_place, placed, w, spread):
    shape = (hid.shape[1], dkv.shape[1] + dq.shape[1] + 64)
    return pl.pallas_call(
        late_grads_kernel,
        out_shape=(
            jax.ShapeDtypeStruct(shape, BF16),
            jax.ShapeDtypeStruct((hid.shape[0], spread.shape[0]), BF16),
        ),
        in_specs=vmem_specs(9),
        out_specs=(pl.BlockSpec(memory_space=pltpu.HBM), vmem_specs(1)[0]),
        scratch_shapes=[pltpu.VMEM(shape, BF16), pltpu.SemaphoreType.DMA],
        compiler_params=pltpu.CompilerParams(vmem_limit_bytes=VMEM_LIMIT),
        name="late_grads",
    )(hid, dkv, dq, rows, q_place, v_place, placed, w, spread)


def project_kernel(hid_ref, w_ref, bias_ref, scale_ref, kv_ref, wide_ref, q_ref):
    made = jnp.dot(hid_ref[...], w_ref[...], preferred_element_type=F32) + bias_ref[...]
    made = (made.astype(BF16).astype(F32) * scale_ref[...]).astype(BF16)
    kv_cols = kv_ref.shape[1]
    kv_ref[...] = made[:, :kv_cols]
    wide_ref[...] = made[:, kv_cols:]
    zeros = jnp.zeros((made.shape[0], HEAD_DIM), BF16)
    for h in range(HEADS_DEV):
        at = kv_cols + h * HEAD_DIM
        q_ref[h] = jnp.concatenate([made[:, at : at + HEAD_DIM], zeros], axis=1)


def project(hid, w, bias, scale):
    rows = hid.shape[0]
    return pl.pallas_call(
        project_kernel,
        out_shape=(
            jax.ShapeDtypeStruct((rows, HEADS_DEV * 128), BF16),
            jax.ShapeDtypeStruct((rows, w.shape[1] - HEADS_DEV * 128), BF16),
            jax.ShapeDtypeStruct((HEADS_DEV, rows, 128), BF16),
        ),
        in_specs=vmem_specs(4),
        out_specs=tuple(vmem_specs(3)),
        compiler_params=pltpu.CompilerParams(vmem_limit_bytes=VMEM_LIMIT),
        name="project",
    )(hid, w, bias, scale)


def queries_in(order_ref, q_ref, q_buffer, q_sems, rows):
    for i in range(8 * len(rows)):
        source = order_ref[8 * rows[i // 8] + i % 8]
        pltpu.make_async_copy(q_ref.at[source], q_buffer.at[i], q_sems.at[i // 8]).start()


def key_back_blocks(k_ref, v_ref, k_acc, v_acc, q_buffer, g_buffer, q_sems, g_sems):
    def step(j, carry):
        eight = q_buffer.at[pl.ds(8 * j, 8)]
        pltpu.make_async_copy(eight, eight, q_sems.at[j]).wait()
        queries = q_buffer[pl.ds(8 * j, 8)].reshape(-1, q_buffer.shape[2])
        grads = block_of(g_buffer, g_sems, j)
        lane = lax.broadcasted_iota(jnp.int32, queries.shape, 1)
        queries = jnp.where(lane < HEADS_DEV * HEAD_DIM, queries, grads)
        for h in range(HEADS_DEV):
            scores = lax.dot_general(k_ref[h], queries, NT, preferred_element_type=F32)
            probs = jnp.exp(scores)
            v_acc[h] = v_acc[h] + jnp.dot(probs.astype(BF16), grads, preferred_element_type=F32)
            back = probs * lax.dot_general(v_ref[h], grads, NT, preferred_element_type=F32)
            k_acc[h] = k_acc[h] + jnp.dot(back.astype(BF16), queries, preferred_element_type=F32)
        return carry

    lax.fori_loop(0, q_sems.shape[0], step, 0)


def key_heads(kv_ref, tag_ref, k_heads, v_heads):
    rows = kv_ref.shape[0]
    feat = HEADS_DEV * HEAD_DIM
    lane = lax.broadcasted_iota(jnp.int32, (rows, HEAD_DIM), 1)
    tag = tag_ref[...]
    masks = jnp.where((lane == 21) & (tag < 0), NEG, 0.0)
    for s in range(3):
        masks = masks + jnp.where((lane == 18 + s) & (tag == s), NEG, 0.0)
    for h in range(HEADS_DEV):
        block = kv_ref[:, head_block(h)].astype(F32)
        before = [jnp.zeros((rows, h * HEAD_DIM), F32)] if h else []
        left = feat - (h + 1) * HEAD_DIM
        after = [jnp.zeros((rows, left), F32)] if left else []
        k_extra = masks - jnp.where((lane >= 9 + 3 * h) & (lane < 12 + 3 * h), 1.0, 0.0)
        v_extra = -jnp.where((lane >= 3 * h) & (lane < 3 * h + 3), 1.0, 0.0)
        for heads, part, extra in (
            (k_heads, block[:, :HEAD_DIM], k_extra),
            (v_heads, block[:, HEAD_DIM:], v_extra),
        ):
            heads[h] = jnp.concatenate(before + [part] + after + [extra], axis=1).astype(BF16)


def key_near_kernel(order_ref, kv_ref, tag_ref, q_ref, *rest):
    g_blocks = rest[:6]
    k_acc, v_acc, k_heads, v_heads, q_buffer, q_sems, g_buffer, g_sems = rest[6:]
    queries_in(order_ref, q_ref, q_buffer, q_sems, (0, 1, 2, 4, 5, 6))
    copies_in(g_blocks, g_buffer, g_sems)
    key_heads(kv_ref, tag_ref, k_heads, v_heads)
    k_acc[...] = jnp.zeros_like(k_acc)
    v_acc[...] = jnp.zeros_like(v_acc)
    key_back_blocks(k_heads, v_heads, k_acc, v_acc, q_buffer, g_buffer, q_sems, g_sems)


def key_far_kernel(order_ref, kv_ref, tag_ref, diag_ref, k_in, v_in, q_ref, *rest):
    g_blocks = rest[:4]
    dkv_ref, k_heads, v_heads, k_acc, v_acc, q_buffer, q_sems, g_buffer, g_sems = rest[4:]
    queries_in(order_ref, q_ref, q_buffer, q_sems, (3, 7))
    copies_in(g_blocks, g_buffer, g_sems)
    key_heads(kv_ref, tag_ref, k_heads, v_heads)
    k_acc[...], v_acc[...] = k_in[...], v_in[...]
    key_back_blocks(k_heads, v_heads, k_acc, v_acc, q_buffer, g_buffer, q_sems, g_sems)
    parts = []
    for h in range(HEADS_DEV):
        parts += [k_acc[h][:, head_columns(h)], v_acc[h][:, head_columns(h)]]
    dkv_ref[...] = (jnp.concatenate(parts, axis=1) + diag_ref[...]).astype(BF16)


def query_buffers(count, q_all):
    return [
        pltpu.VMEM((8 * count, *q_all.shape[1:]), BF16),
        pltpu.SemaphoreType.DMA((count,)),
    ]


def smem_spec():
    return [pl.BlockSpec(memory_space=pltpu.SMEM)]


def key_near(order, kv_own, tag, q_all, g_blocks):
    rows, width = kv_own.shape[0], g_blocks[0].shape[2]
    return pl.pallas_call(
        key_near_kernel,
        out_shape=(head_state(rows, width),) * 2,
        in_specs=smem_spec() + vmem_specs(2) + any_specs(7),
        out_specs=tuple(vmem_specs(2)),
        scratch_shapes=[pltpu.VMEM((HEADS_DEV, rows, width), BF16)] * 2
        + query_buffers(6, q_all)
        + buffers(g_blocks, width),
        compiler_params=pltpu.CompilerParams(vmem_limit_bytes=VMEM_LIMIT),
        cost_estimate=cost(rows, g_blocks, 2048),
        name="key_near",
    )(order, kv_own, tag, q_all, *g_blocks)


def key_far(order, kv_own, tag, diagonal, state, q_all, g_blocks):
    rows, width = kv_own.shape[0], g_blocks[0].shape[2]
    return pl.pallas_call(
        key_far_kernel,
        out_shape=jax.ShapeDtypeStruct(diagonal.shape, BF16),
        in_specs=smem_spec() + vmem_specs(5) + any_specs(5),
        out_specs=vmem_specs(1)[0],
        scratch_shapes=[pltpu.VMEM((HEADS_DEV, rows, width), BF16)] * 2
        + [pltpu.VMEM((HEADS_DEV, rows, width), F32)] * 2
        + query_buffers(2, q_all)
        + buffers(g_blocks, width),
        compiler_params=pltpu.CompilerParams(vmem_limit_bytes=VMEM_LIMIT),
        cost_estimate=cost(rows, g_blocks, 2048),
        name="key_far",
    )(order, kv_own, tag, diagonal, *state, q_all, *g_blocks)


def dot(a, b):
    return jnp.dot(a, b, preferred_element_type=F32)


def dot_nt(a, b):
    return lax.dot_general(a, b, NT, preferred_element_type=F32)


def dot_tn(a, b):
    return lax.dot_general(a, b, (((0,), (0,)), ((), ())), preferred_element_type=F32)


def core_half(x, axis, at):
    size = x.shape[axis] // 2
    return lax.dynamic_slice_in_dim(x, at * size, size, axis)


def interleaved(k, v):
    shape = (*k.shape[:-1], -1, HEAD_DIM)
    return jnp.stack([k.reshape(shape), v.reshape(shape)], axis=-2).reshape(*k.shape[:-1], -1)


def per_device(
    hidden,
    w_qkv,
    w_out,
    b_qv,
    w_up,
    w_down,
    b_up,
    norm_gains,
    norm_shifts,
    segments,
    lengths,
    cotangent,
):
    core = lax.axis_index("core")
    heads_at = lax.axis_index("heads")
    own_ctx = ((lax.axis_index("z") * 4 + lax.axis_index("y")) * 2 + lax.axis_index("xh")) * 2 + core
    tok = hidden.shape[0]
    rows = w_up.shape[0]
    feat = HEADS_DEV * HEAD_DIM
    hidden_units = w_up.shape[1] // 2

    hid = chip_tokens(hidden)
    out_turned, down_turned = w_out.T, w_down.T
    low_tok = segments.astype(BF16).reshape(2, tok // 2)
    kv_cols = 2 * feat

    def halves(x):
        return jnp.swapaxes(x.reshape(rows, 2, -1), 0, 1)

    q_half, k_half, v_half = (halves(w_qkv[i]) for i in range(3))
    tail = jnp.broadcast_to(jnp.pad(low_tok, ((0, rows - 2), (0, 0))), (2, rows, tok // 2))
    urgent = jnp.concatenate([interleaved(k_half, v_half), q_half, tail], axis=2)
    urgent = jnp.pad(urgent, ((0, 0), (0, 16 - rows), (0, 0)))
    urgent = jnp.broadcast_to(urgent[None], (32, *urgent.shape)).reshape(64, 16, -1)
    urgent, *later = lax.optimization_barrier((urgent, out_turned, w_up, down_turned))
    later = jnp.concatenate([halves(w) for w in later], axis=2)
    mine = lax.dynamic_index_in_dim(later, core, 0, keepdims=False)
    theirs = shifted(lax.dynamic_index_in_dim(later, 1 - core, 0, keepdims=False), "core", 1)
    later = pair_ordered(mine, theirs, "core").reshape(2 * rows, -1)
    rest = lax.all_gather(later, CHIPS, axis=0, tiled=True)
    w_urgent = lax.all_to_all(urgent, CTX, 0, 0, tiled=True)
    seg_all = w_urgent[:, :2, kv_cols + feat :].reshape(-1, tok).astype(jnp.int32)
    w_urgent = w_urgent.reshape(64 * 16, -1)
    at_wide = jnp.arange(64 * 16, dtype=jnp.int32)
    at_feature = jnp.arange(64 * rows, dtype=jnp.int32)
    spread = (
        (at_feature // rows * 16 + at_feature % rows)[:, None] == at_wide[None, :]
    ).astype(BF16)
    hid_wide = dot(hid, spread).astype(BF16)

    w_out_t = rest[:, :feat]
    w_up_all = rest[:, feat : feat + hidden_units]
    w_down_t = rest[:, feat + hidden_units :]

    bias = b_qv.astype(F32)
    q_bias, v_bias = core_half(bias[0], 0, core), core_half(bias[1], 0, core)
    no_bias = jnp.zeros((tok // 2,), F32)
    bias_row = jnp.concatenate([interleaved(jnp.zeros_like(v_bias), v_bias), q_bias, no_bias])
    column = jnp.arange(bias_row.shape[0], dtype=jnp.int32)
    scale_row = jnp.where(
        column < kv_cols, 1.0, jnp.where(column < kv_cols + feat, HEAD_DIM ** (-0.5), 0.0)
    ).astype(F32)
    kv_own, q_wide, q_heads = project(hid_wide, w_urgent, bias_row[None], scale_row[None])
    q_all = lax.all_gather(q_wide, CHIPS, axis=0, tiled=True).reshape(64, tok, -1)
    starts = [jnp.sum((seg_all < s).astype(jnp.int32)) for s in range(3)]
    places = jnp.arange(seg_all.size, dtype=jnp.int32).reshape(seg_all.shape)
    run_end = jnp.zeros_like(seg_all)
    for s in range(3):
        run_end = jnp.where(seg_all == s, starts[s] + lengths[s], run_end)
    tag_all = jnp.where(places < run_end, seg_all, -1).astype(F32)
    order = jnp.concatenate([relative_order("z", "y", 0), relative_order("y", "z", 1)])
    q_order = jnp.where(core == 0, order, order + 1 - 2 * (order % 2))
    tags = jnp.take(tag_all, order, axis=0).reshape(8, -1)
    both = jnp.stack([own_ctx, own_ctx + 1 - 2 * core])
    tag_own = jnp.take(tag_all, both, axis=0).reshape(-1, 1)
    seg_own = jnp.take(seg_all, both, axis=0).astype(F32).reshape(-1, 1)

    sent_z, sent_y = lax.optimization_barrier(gather_first(kv_own))
    blocks = gather_second(sent_z, sent_y)
    near, far = near_blocks(blocks), far_blocks(blocks)
    state = attend_near(q_heads, kv_own, tags, seg_own, tag_own, near)
    attended, stat = attend_far(q_heads, tags, seg_own, state, far)
    attended_low = attended.astype(BF16)

    gain_rows = norm_gains.astype(F32)
    shifts = norm_shifts.astype(F32)
    attn_mixed = team_sum(dot_nt(attended_low, w_out_t))
    first_out, normed_one, inverse_one = layer_norm(
        hidden.astype(F32) + attn_mixed + shifts[0], gain_rows[0], shifts[1]
    )
    first_low = chip_tokens(first_out.astype(BF16))
    up_bias = core_half(b_up, 0, core).astype(F32)
    up_proj = dot(first_low, w_up_all) + up_bias
    activated = exact_gelu(up_proj).astype(BF16)
    second = team_sum(dot_nt(activated, w_down_t))
    output, normed_two, inverse_two = layer_norm(
        first_out + second + shifts[2], gain_rows[1], shifts[3]
    )
    resid_two = norm_back(
        cotangent.astype(F32), normed_two, inverse_two, gain_rows[1]
    )
    branch_low = chip_tokens(resid_two.astype(BF16))
    act_grad = dot(branch_low, w_down_t)
    up_low = jax.vjp(exact_gelu, up_proj)[1](act_grad)[0].astype(BF16)
    first_grad = resid_two + team_sum(dot_nt(up_low, w_up_all))
    resid_one = norm_back(first_grad, normed_one, inverse_one, gain_rows[0])
    mixed_low = chip_tokens(resid_one.astype(BF16))
    g_sent, g_heads, delta = grad_rows(mixed_low, w_out_t, attended, stat, seg_own)
    made = early_grads(spread, branch_low, activated, first_low, up_low)
    (g_z, g_y), g_heads = lax.optimization_barrier((gather_first(g_sent), g_heads))
    g_blocks = gather_second(g_z, g_y)
    g_near, g_far = near_blocks(g_blocks), far_blocks(g_blocks)
    g_near, made = lax.optimization_barrier((g_near, made))
    early = to_owners(made)
    out_placed = out_rows(spread, mixed_low, attended_low)
    at_bias = jnp.arange(hidden_units, dtype=jnp.int32)
    at_half = jnp.arange(feat, dtype=jnp.int32)
    at_kv = jnp.arange(kv_cols, dtype=jnp.int32)

    def placed(owner, row):
        return ((owner * 16 + row)[:, None] == at_wide[None, :]).astype(BF16)

    first_owner = 32 * core
    bias_place = placed(first_owner + at_bias // 24, at_bias % 12)
    q_place = placed(first_owner + at_half // 6, at_half % 6)
    at_value = at_kv // 128 * HEAD_DIM + at_kv % 128 - HEAD_DIM
    is_value = at_kv % 128 >= HEAD_DIM
    v_place = placed(jnp.where(is_value, first_owner + at_value // 6, -1), at_value % 6)
    parts = jnp.arange(2, dtype=jnp.int32)[:, None] == (at_bias % 24 // 12)[None, :]
    rows_made = vector_rows(
        spread,
        cotangent,
        normed_two,
        resid_two,
        first_grad,
        normed_one,
        resid_one,
        up_low,
        spread,
        bias_place,
        parts.astype(F32),
    )

    dq, diagonal = query_back(
        q_heads, g_heads, kv_own, tags, seg_own, tag_own, stat, delta, near + far
    )
    key_state = key_near(q_order, kv_own, tag_own, q_all, g_near)
    dkv = key_far(q_order, kv_own, tag_own, diagonal, key_state, q_all, g_far)
    dkv, early = lax.optimization_barrier((dkv, early))
    late, back = late_grads(
        hid_wide, dkv, dq, rows_made, q_place, v_place, out_placed, w_urgent, spread
    )
    late = to_owners(late)
    hidden_grad = resid_one + team_sum(back.astype(F32))

    early_sums, late_sums = owner_sums(early), owner_sums(late)

    def columns(x, start, size):
        return jnp.concatenate([x[c, :rows, start : start + size] for c in range(2)], axis=1)

    kv_pairs = columns(late_sums, 0, kv_cols).reshape(rows, 2 * HEADS_DEV, 2, HEAD_DIM)
    k_cols = kv_pairs[:, :, 0].reshape(rows, -1)
    v_cols = kv_pairs[:, :, 1].reshape(rows, -1)
    q_cols = columns(late_sums, kv_cols, feat)

    def last(x, size):
        return jnp.concatenate(
            [x[:, rows:, g * size : (g + 1) * size] for g in range(3)], axis=1
        )

    quarter = hidden_units // 2
    up_cols = columns(early_sums, 0, hidden_units)
    down_first, down_last = early_sums[:, :rows, hidden_units:], last(early_sums, quarter)
    down_cols = jnp.concatenate(
        [down_first[0], down_last[0], down_first[1], down_last[1]], axis=1
    )
    out_last = last(late_sums, feat)
    out_cols = jnp.concatenate([out_last[0], out_last[1]], axis=1)
    small = (late_sums[0] + late_sums[1])[:rows, kv_cols + feat :].T
    vec_out = small[:6].reshape(6, 2, 6)
    bias_out = small[6:8].reshape(-1)
    qv_out = small[8:10, :6]
    vec_out = lax.dynamic_index_in_dim(vec_out, heads_at, 1, keepdims=False)
    return (
        output.astype(BF16),
        hidden_grad,
        jnp.stack([q_cols, k_cols, v_cols]),
        out_cols.T,
        qv_out,
        up_cols,
        down_cols.T,
        bias_out,
        vec_out[:2],
        vec_out[2:],
    )


def solution(mesh):
    fine = Mesh(mesh.devices.reshape(4, 4, 2, 2, 2), ("z", "y", "xh", "core", "heads"))
    return jax.shard_map(
        per_device,
        mesh=fine,
        in_specs=(
            P(CTX, None),
            P(None, CTX, "heads"),
            P("heads", CTX),
            P(None, "heads"),
            P(CTX, "heads"),
            P("heads", CTX),
            P("heads"),
            P(),
            P(),
            P(CTX),
            P(),
            P(CTX, None),
        ),
        out_specs=(
            P(CTX, None),
            P(CTX, None),
            P(None, CTX, "heads"),
            P("heads", CTX),
            P(None, ("heads", *CTX)),
            P(CTX, "heads"),
            P("heads", CTX),
            P(("heads", *CTX)),
            P(None, (*CTX, "heads")),
            P(None, (*CTX, "heads")),
        ),
        check_vma=False,
    )
```

```python
import jax
import jax.numpy as jnp
from jax import lax
from jax.experimental import pallas as pl
from jax.experimental.pallas import tpu as pltpu
from jax.sharding import Mesh, PartitionSpec as P

HEAD_DIM = 64
HEADS_DEV = 3
EPS = 1e-06
NEG = -1e30
CTX = ("z", "y", "xh", "core")
CHIPS = ("z", "y", "xh")
F32 = jnp.float32
BF16 = jnp.bfloat16
NT = (((1,), (1,)), ((), ()))
VMEM_LIMIT = 50 * 1024 * 1024
OFFSETS = (0, -1, 1, 2)


def shifted(x, axis, step):
    n = lax.axis_size(axis)
    return lax.ppermute(x, axis, [(i, (i + step) % n) for i in range(n)])


def ring_halves(x, axis):
    half = x.shape[0] // 2
    before, after = shifted(x, axis, 1), shifted(x, axis, -1)
    return [x, before, after, shifted(before[:half], axis, 1), shifted(after[half:], axis, -1)]


def gather_first(x):
    half = x.shape[0] // 2
    streams = []
    for part, axis in ((x[:half], "z"), (x[half:], "y")):
        both = jnp.concatenate([part, shifted(part, "xh", 1)], axis=0)
        streams.append(jnp.concatenate(ring_halves(both, axis), axis=0))
    return tuple(streams)


def gather_second(z_stream, y_stream):
    blocks = ring_halves(z_stream, "y") + ring_halves(y_stream, "z")
    return [b.reshape(-1, z_stream.shape[0] // 2, b.shape[1]) for b in blocks]


def near_blocks(blocks):
    return blocks[:3] + blocks[5:8]


def far_blocks(blocks):
    return blocks[3:5] + blocks[8:]


def relative_order(first, second, core_at):
    place = {a: lax.axis_index(a) for a in CHIPS}
    core = lax.axis_index("core")
    order = []
    for second_step in OFFSETS:
        for first_step in OFFSETS:
            for xh_step in (0, 1):
                at = dict(place)
                at[first] = (at[first] + first_step) % 4
                at[second] = (at[second] + second_step) % 4
                at["xh"] = (at["xh"] + xh_step) % 2
                order.append(((at["z"] * 4 + at["y"]) * 2 + at["xh"]) * 2 + (core + core_at) % 2)
    return jnp.stack(order)


def pair_ordered(own, other, axis):
    first = lax.axis_index(axis) == 0
    return jnp.stack([jnp.where(first, own, other), jnp.where(first, other, own)])


def to_owners(x):
    return lax.all_to_all(x.reshape(64, 16, -1), CTX, 0, 0, tiled=True)


def owner_sums(parts):
    return jnp.sum(parts.reshape(-1, 2, *parts.shape[1:]).astype(F32), axis=0)


def team_sum(partial):
    rows = partial.shape[0] // 2
    near = partial[:rows] + shifted(partial[rows:].astype(BF16), "core", 1).astype(F32)
    low = lax.optimization_barrier(near.astype(BF16))
    return low.astype(F32) + shifted(low, "heads", 1).astype(F32)


def chip_tokens(x):
    return jnp.concatenate([x, shifted(x, "core", 1)], axis=0)


def layer_norm(residual, gain_row, shift_row):
    centred = residual - jnp.mean(residual, axis=-1, keepdims=True)
    inverse = lax.rsqrt(jnp.mean(centred * centred, axis=-1, keepdims=True) + EPS)
    normed = centred * inverse
    return (normed * gain_row + shift_row, normed, inverse)


def norm_back(incoming, normed, inverse, gain_row):
    scaled = incoming * gain_row
    projected = (
        scaled
        - jnp.mean(scaled, axis=-1, keepdims=True)
        - normed * jnp.mean(scaled * normed, axis=-1, keepdims=True)
    )
    return inverse * projected


def exact_gelu(pre_act):
    return jax.nn.gelu(pre_act, approximate=False)


def pieces_of(column):
    high = column.astype(BF16).astype(F32)
    middle = (column - high).astype(BF16).astype(F32)
    return high, middle, column - high - middle


def head_columns(h):
    return slice(h * HEAD_DIM, (h + 1) * HEAD_DIM)


def head_block(h):
    return slice(h * 128, (h + 1) * 128)


def diagonal_scores(q_ref, kv_ref, h):
    product = q_ref[h].astype(F32) * kv_ref[:, head_block(h)].astype(F32)
    return jnp.sum(product, axis=1, keepdims=True)


def copies_in(sources, buffer, sems):
    at = 0
    for source in sources:
        size = source.shape[0]
        pltpu.make_async_copy(source, buffer.at[pl.ds(at, size)], sems.at[at // 2]).start()
        at += size


def block_of(buffer, sems, j):
    block = buffer.at[pl.ds(2 * j, 2)]
    pltpu.make_async_copy(block, block, sems.at[j]).wait()
    return buffer[pl.ds(2 * j, 2)].reshape(-1, buffer.shape[2])


def attend_blocks(q_ref, tags_ref, seg_ref, top, total, acc, buffer, sems, row_of):
    rows = q_ref.shape[1]
    seg_wide = jnp.broadcast_to(seg_ref[...], (rows, 128))

    def step(j, carry):
        whole = block_of(buffer, sems, j)
        tags = tags_ref[pl.ds(row_of(j), 1), :]
        keys = tags.shape[1]
        allowed = jnp.tile(seg_wide, (1, keys // 128)) == tags
        for h in range(HEADS_DEV):
            kv = whole[:, head_block(h)]
            scores = lax.dot_general(q_ref[h], kv, NT, preferred_element_type=F32)
            scores = jnp.where(allowed, scores, NEG)
            before = top[h]
            now = jnp.maximum(before, jnp.max(scores, axis=1, keepdims=True))
            weights = jnp.exp(scores - jnp.tile(now, (1, keys // 128)))
            fade = jnp.exp(before - now)
            sums = weights[:, :128]
            for k in range(1, keys // 128):
                sums = sums + weights[:, k * 128 : (k + 1) * 128]
            total[h] = total[h] * fade + sums
            acc[h] = acc[h] * fade + jnp.dot(weights.astype(BF16), kv, preferred_element_type=F32)
            top[h] = now
        return carry

    lax.fori_loop(0, sems.shape[0], step, 0)


def near_row(j):
    return j + (j >= 3).astype(jnp.int32)


def far_row(j):
    return 4 * j + 3


def attend_near_kernel(q_ref, own_ref, tags_ref, seg_ref, tag_ref, *rest):
    blocks, (top, total, acc, buffer, sems) = rest[:6], rest[6:]
    copies_in(blocks, buffer, sems)
    rows = q_ref.shape[1]
    padded = tag_ref[...] < 0
    for h in range(HEADS_DEV):
        diagonal = diagonal_scores(q_ref, own_ref, h)
        top[h] = jnp.broadcast_to(jnp.where(padded, diagonal, NEG), (rows, 128))
        lane = lax.broadcasted_iota(jnp.int32, (rows, 128), 1)
        total[h] = jnp.where((lane == 0) & padded, 1.0, 0.0)
        acc[h] = jnp.where(padded, own_ref[:, head_block(h)].astype(F32), 0.0)
    attend_blocks(q_ref, tags_ref, seg_ref, top, total, acc, buffer, sems, near_row)


def attend_far_kernel(q_ref, tags_ref, seg_ref, top_in, total_in, acc_in, *rest):
    blocks, (out_ref, stat_ref, top, total, acc, buffer, sems) = rest[:4], rest[4:]
    copies_in(blocks, buffer, sems)
    top[...], total[...], acc[...] = top_in[...], total_in[...], acc_in[...]
    attend_blocks(q_ref, tags_ref, seg_ref, top, total, acc, buffer, sems, far_row)
    outs = []
    for h in range(HEADS_DEV):
        sums = jnp.sum(total[h], axis=1, keepdims=True)
        outs.append((acc[h] / sums)[:, HEAD_DIM:])
        stat_ref[h] = top[h] + jnp.log(sums)
    out_ref[...] = jnp.concatenate(outs, axis=1)


def vmem_specs(n):
    return [pl.BlockSpec(memory_space=pltpu.VMEM)] * n


def any_specs(n):
    return [pl.BlockSpec(memory_space=pl.ANY)] * n


def head_state(rows, lanes=128):
    return jax.ShapeDtypeStruct((HEADS_DEV, rows, lanes), F32)


def cost(rows, blocks, flops):
    keys = sum(b.shape[0] * b.shape[1] for b in blocks)
    pairs = rows * keys * HEADS_DEV
    return pl.CostEstimate(
        flops=pairs * flops, bytes_accessed=keys * 1024, transcendentals=pairs
    )


def buffers(blocks, lanes):
    count = sum(b.shape[0] for b in blocks)
    return [
        pltpu.VMEM((count, blocks[0].shape[1], lanes), BF16),
        pltpu.SemaphoreType.DMA((count // 2,)),
    ]


def attend_near(q_heads, kv_own, tags, seg, tag, blocks):
    rows = kv_own.shape[0]
    return pl.pallas_call(
        attend_near_kernel,
        out_shape=(head_state(rows),) * 3,
        in_specs=vmem_specs(5) + any_specs(6),
        out_specs=tuple(vmem_specs(3)),
        scratch_shapes=buffers(blocks, kv_own.shape[1]),
        compiler_params=pltpu.CompilerParams(vmem_limit_bytes=VMEM_LIMIT),
        cost_estimate=cost(rows, blocks, 512),
        name="attend_near",
    )(q_heads, kv_own, tags, seg, tag, *blocks)


def attend_far(q_heads, tags, seg, state, blocks):
    rows = q_heads.shape[1]
    return pl.pallas_call(
        attend_far_kernel,
        out_shape=(jax.ShapeDtypeStruct((rows, HEADS_DEV * HEAD_DIM), F32), head_state(rows)),
        in_specs=vmem_specs(6) + any_specs(4),
        out_specs=tuple(vmem_specs(2)),
        scratch_shapes=[pltpu.VMEM((HEADS_DEV, rows, 128), F32)] * 3
        + buffers(blocks, HEADS_DEV * 128),
        compiler_params=pltpu.CompilerParams(vmem_limit_bytes=VMEM_LIMIT),
        cost_estimate=cost(rows, blocks, 512),
        name="attend_far",
    )(q_heads, tags, seg, *state, *blocks)


def query_back_kernel(q_ref, g_ref, own_ref, tags_ref, seg_ref, tag_ref, stat_ref, delta_ref, *rest):
    blocks, (dq_ref, dkv_ref, buffer, sems, acc) = rest[:10], rest[10:]
    copies_in(blocks, buffer, sems)
    rows = q_ref.shape[1]
    seg_wide = jnp.broadcast_to(seg_ref[...], (rows, 128))
    padded = tag_ref[...] < 0
    for h in range(HEADS_DEV):
        own = own_ref[:, head_block(h)].astype(F32)
        prob = jnp.exp(diagonal_scores(q_ref, own_ref, h) - stat_ref[h][:, :1])
        prob = jnp.where(padded, prob, 0.0)
        grad = diagonal_scores(g_ref, own_ref, h) - delta_ref[h][:, :1]
        score = (prob * grad).astype(BF16).astype(F32)
        acc[h] = score * own
        dkv_ref[:, head_block(h)] = score * q_ref[h].astype(F32) + prob.astype(BF16).astype(
            F32
        ) * g_ref[h].astype(F32)

    def step(j, carry):
        whole = block_of(buffer, sems, j)
        tags = tags_ref[pl.ds(jnp.where(j < 6, near_row(j), far_row(j - 6)), 1), :]
        keys = tags.shape[1]
        allowed = jnp.tile(seg_wide, (1, keys // 128)) == tags
        for h in range(HEADS_DEV):
            kv = whole[:, head_block(h)]
            scores = lax.dot_general(q_ref[h], kv, NT, preferred_element_type=F32)
            scores = jnp.where(allowed, scores, NEG)
            probs = jnp.exp(scores - jnp.tile(stat_ref[h], (1, keys // 128)))
            grads = lax.dot_general(g_ref[h], kv, NT, preferred_element_type=F32)
            back = probs * (grads - jnp.tile(delta_ref[h], (1, keys // 128)))
            acc[h] = acc[h] + jnp.dot(back.astype(BF16), kv, preferred_element_type=F32)
        return carry

    lax.fori_loop(0, 8, step, 0)
    dq_ref[...] = (
        jnp.concatenate([acc[h][:, :HEAD_DIM] for h in range(HEADS_DEV)], axis=1)
        * HEAD_DIM ** (-0.5)
    ).astype(BF16)


def query_back(q_heads, g_heads, kv_own, tags, seg, tag, stat, delta, blocks):
    rows = kv_own.shape[0]
    return pl.pallas_call(
        query_back_kernel,
        out_shape=(
            jax.ShapeDtypeStruct((rows, HEADS_DEV * HEAD_DIM), BF16),
            jax.ShapeDtypeStruct(kv_own.shape, F32),
        ),
        in_specs=vmem_specs(8) + any_specs(10),
        out_specs=tuple(vmem_specs(2)),
        scratch_shapes=buffers(blocks, kv_own.shape[1]) + [pltpu.VMEM((HEADS_DEV, rows, 128), F32)],
        compiler_params=pltpu.CompilerParams(vmem_limit_bytes=VMEM_LIMIT),
        cost_estimate=cost(rows, blocks, 768),
        name="query_back",
    )(q_heads, g_heads, kv_own, tags, seg, tag, stat, delta, *blocks)


def grad_rows_kernel(
    mixed_ref, out_ref, attended_ref, stat_ref, seg_ref, sent_ref, g_ref, delta_ref
):
    rows = mixed_ref.shape[0]
    grad = jnp.dot(mixed_ref[...], out_ref[...], preferred_element_type=F32).astype(BF16)
    grad = grad.astype(F32)
    product = grad * attended_ref[...]
    lane = lax.broadcasted_iota(jnp.int32, (rows, HEAD_DIM), 1)
    seg = seg_ref[...]
    extra = jnp.where(lane == 21, 1.0, 0.0)
    for s in range(3):
        extra = extra + jnp.where((lane == 18 + s) & (seg != s), 1.0, 0.0)
    zeros = jnp.zeros((rows, HEAD_DIM), BF16)
    for h in range(HEADS_DEV):
        delta = jnp.sum(product[:, head_columns(h)], axis=1, keepdims=True)
        delta_ref[h] = jnp.broadcast_to(delta, (rows, 128))
        for i, piece in enumerate(pieces_of(delta)):
            extra = extra + jnp.where(lane == 3 * h + i, piece, 0.0)
        for i, piece in enumerate(pieces_of(stat_ref[h][:, :1])):
            extra = extra + jnp.where(lane == 9 + 3 * h + i, piece, 0.0)
        g_ref[h] = jnp.concatenate([zeros, grad[:, head_columns(h)].astype(BF16)], axis=1)
    sent_ref[...] = jnp.concatenate([grad, extra], axis=1).astype(BF16)


def grad_rows(mixed, w_out, attended, stat, seg):
    rows = mixed.shape[0]
    return pl.pallas_call(
        grad_rows_kernel,
        out_shape=(
            jax.ShapeDtypeStruct((rows, 256), BF16),
            jax.ShapeDtypeStruct((HEADS_DEV, rows, 128), BF16),
            jax.ShapeDtypeStruct((HEADS_DEV, rows, 128), F32),
        ),
        in_specs=vmem_specs(5),
        out_specs=tuple(vmem_specs(3)),
        compiler_params=pltpu.CompilerParams(vmem_limit_bytes=VMEM_LIMIT),
        name="grad_rows",
    )(mixed, w_out, attended, stat, seg)


def send_out(held, out_ref, sem):
    copy = pltpu.make_async_copy(held, out_ref, sem)
    copy.start()
    copy.wait()


def last_rows(x, group):
    parts = x.reshape(64, 16, x.shape[1])[:, 4 * group : 4 * group + 4]
    return jnp.concatenate([jnp.zeros((64, 12, x.shape[1]), F32), parts], axis=1).reshape(x.shape)


def early_grads_kernel(spread_ref, branch_ref, activated_ref, first_ref, up_ref, out_ref, held, sem):
    quarter = held.shape[1] // 3
    made = []
    for left, right in ((first_ref, up_ref), (branch_ref, activated_ref)):
        wide = jnp.dot(left[...], spread_ref[...], preferred_element_type=F32).astype(BF16)
        for half in range(2):
            made.append(dot_tn(wide, right[:, half * quarter : (half + 1) * quarter]))
    for g in range(3):
        held[:, g * quarter : (g + 1) * quarter] = (made[g] + last_rows(made[3], g)).astype(BF16)
    send_out(held, out_ref, sem)


def early_grads(spread, branch, activated, first, up):
    shape = (spread.shape[1], up.shape[1] * 3 // 2)
    return pl.pallas_call(
        early_grads_kernel,
        out_shape=jax.ShapeDtypeStruct(shape, BF16),
        in_specs=vmem_specs(5),
        out_specs=pl.BlockSpec(memory_space=pltpu.HBM),
        scratch_shapes=[pltpu.VMEM(shape, BF16), pltpu.SemaphoreType.DMA],
        compiler_params=pltpu.CompilerParams(vmem_limit_bytes=VMEM_LIMIT),
        name="early_grads",
    )(spread, branch, activated, first, up)


def out_rows_kernel(spread_ref, mixed_ref, attended_ref, out_ref):
    wide = jnp.dot(mixed_ref[...], spread_ref[...], preferred_element_type=F32).astype(BF16)
    made = dot_tn(wide, attended_ref[...].astype(BF16))
    out_ref[...] = jnp.concatenate([last_rows(made, g) for g in range(3)], axis=1).astype(BF16)


def out_rows(spread, mixed, attended):
    return pl.pallas_call(
        out_rows_kernel,
        out_shape=jax.ShapeDtypeStruct((spread.shape[1], 3 * attended.shape[1]), BF16),
        in_specs=vmem_specs(3),
        out_specs=vmem_specs(1)[0],
        compiler_params=pltpu.CompilerParams(vmem_limit_bytes=VMEM_LIMIT),
        name="out_rows",
    )(spread, mixed, attended)


def vector_rows_kernel(
    cot_ref, two_ref, resid_two_ref, first_ref, one_ref, resid_one_ref, up_ref, spread_ref, bias_ref,
    parts_ref, out_ref,
):
    cot, first = cot_ref[...].astype(F32), first_ref[...]
    columns = (
        first * one_ref[...],
        cot * two_ref[...],
        resid_one_ref[...],
        first,
        resid_two_ref[...],
        cot,
    )
    rows = jnp.concatenate([jnp.sum(c, axis=0, keepdims=True) for c in columns], axis=0)
    bias = jnp.sum(up_ref[...].astype(F32), axis=0, keepdims=True) * parts_ref[...]
    made = [
        jnp.dot(rows.astype(BF16), spread_ref[...], preferred_element_type=F32),
        jnp.dot(bias.astype(BF16), bias_ref[...], preferred_element_type=F32),
    ]
    out_ref[...] = jnp.concatenate(made, axis=0)


def vector_rows(spread, *args):
    return pl.pallas_call(
        vector_rows_kernel,
        out_shape=jax.ShapeDtypeStruct((8, spread.shape[1]), F32),
        in_specs=vmem_specs(10),
        out_specs=vmem_specs(1)[0],
        compiler_params=pltpu.CompilerParams(vmem_limit_bytes=VMEM_LIMIT),
        name="vector_rows",
    )(*args)


def late_grads_kernel(
    hid_ref, dkv_ref, dq_ref, rows_ref, q_place_ref, v_place_ref, placed_ref, w_ref, spread_ref,
    out_ref, back_ref, held, sem,
):
    wide = hid_ref.shape[1]
    grads = jnp.concatenate([dkv_ref[...], dq_ref[...]], axis=1)
    cols = grads.shape[1]
    made = dot_tn(hid_ref[...], grads) + placed_ref[...].astype(F32)
    sums = [rows_ref[...]]
    for grad, place in ((dq_ref, q_place_ref), (dkv_ref, v_place_ref)):
        row = jnp.sum(grad[...].astype(F32), axis=0, keepdims=True).astype(BF16)
        sums.append(jnp.dot(row, place[...], preferred_element_type=F32))
    sums.append(jnp.zeros((128 - 10, wide), F32))
    small = jnp.transpose(jnp.concatenate(sums, axis=0))[:, :64]
    held[...] = jnp.concatenate([made, small], axis=1).astype(BF16)
    copy = pltpu.make_async_copy(held, out_ref, sem)
    copy.start()
    back = dot_nt(grads, w_ref[:, :cols]).astype(BF16)
    back_ref[...] = dot_nt(back, spread_ref[...]).astype(BF16)
    copy.wait()


def late_grads(hid, dkv, dq, rows, q_place, v_place, placed, w, spread):
    shape = (hid.shape[1], dkv.shape[1] + dq.shape[1] + 64)
    return pl.pallas_call(
        late_grads_kernel,
        out_shape=(
            jax.ShapeDtypeStruct(shape, BF16),
            jax.ShapeDtypeStruct((hid.shape[0], spread.shape[0]), BF16),
        ),
        in_specs=vmem_specs(9),
        out_specs=(pl.BlockSpec(memory_space=pltpu.HBM), vmem_specs(1)[0]),
        scratch_shapes=[pltpu.VMEM(shape, BF16), pltpu.SemaphoreType.DMA],
        compiler_params=pltpu.CompilerParams(vmem_limit_bytes=VMEM_LIMIT),
        name="late_grads",
    )(hid, dkv, dq, rows, q_place, v_place, placed, w, spread)


def project_kernel(hid_ref, w_ref, bias_ref, scale_ref, kv_ref, wide_ref, q_ref):
    made = jnp.dot(hid_ref[...], w_ref[...], preferred_element_type=F32) + bias_ref[...]
    made = (made.astype(BF16).astype(F32) * scale_ref[...]).astype(BF16)
    kv_cols = kv_ref.shape[1]
    kv_ref[...] = made[:, :kv_cols]
    wide_ref[...] = made[:, kv_cols:]
    zeros = jnp.zeros((made.shape[0], HEAD_DIM), BF16)
    for h in range(HEADS_DEV):
        at = kv_cols + h * HEAD_DIM
        q_ref[h] = jnp.concatenate([made[:, at : at + HEAD_DIM], zeros], axis=1)


def project(hid, w, bias, scale):
    rows = hid.shape[0]
    return pl.pallas_call(
        project_kernel,
        out_shape=(
            jax.ShapeDtypeStruct((rows, HEADS_DEV * 128), BF16),
            jax.ShapeDtypeStruct((rows, w.shape[1] - HEADS_DEV * 128), BF16),
            jax.ShapeDtypeStruct((HEADS_DEV, rows, 128), BF16),
        ),
        in_specs=vmem_specs(4),
        out_specs=tuple(vmem_specs(3)),
        compiler_params=pltpu.CompilerParams(vmem_limit_bytes=VMEM_LIMIT),
        name="project",
    )(hid, w, bias, scale)


def queries_in(order_ref, q_ref, q_buffer, q_sems, rows):
    for i in range(8 * len(rows)):
        source = order_ref[8 * rows[i // 8] + i % 8]
        pltpu.make_async_copy(q_ref.at[source], q_buffer.at[i], q_sems.at[i // 8]).start()


def key_back_blocks(k_ref, v_ref, k_acc, v_acc, q_buffer, g_buffer, q_sems, g_sems):
    def step(j, carry):
        eight = q_buffer.at[pl.ds(8 * j, 8)]
        pltpu.make_async_copy(eight, eight, q_sems.at[j]).wait()
        queries = q_buffer[pl.ds(8 * j, 8)].reshape(-1, q_buffer.shape[2])
        grads = block_of(g_buffer, g_sems, j)
        lane = lax.broadcasted_iota(jnp.int32, queries.shape, 1)
        queries = jnp.where(lane < HEADS_DEV * HEAD_DIM, queries, grads)
        for h in range(HEADS_DEV):
            scores = lax.dot_general(k_ref[h], queries, NT, preferred_element_type=F32)
            probs = jnp.exp(scores)
            v_acc[h] = v_acc[h] + jnp.dot(probs.astype(BF16), grads, preferred_element_type=F32)
            back = probs * lax.dot_general(v_ref[h], grads, NT, preferred_element_type=F32)
            k_acc[h] = k_acc[h] + jnp.dot(back.astype(BF16), queries, preferred_element_type=F32)
        return carry

    lax.fori_loop(0, q_sems.shape[0], step, 0)


def key_heads(kv_ref, tag_ref, k_heads, v_heads):
    rows = kv_ref.shape[0]
    feat = HEADS_DEV * HEAD_DIM
    lane = lax.broadcasted_iota(jnp.int32, (rows, HEAD_DIM), 1)
    tag = tag_ref[...]
    masks = jnp.where((lane == 21) & (tag < 0), NEG, 0.0)
    for s in range(3):
        masks = masks + jnp.where((lane == 18 + s) & (tag == s), NEG, 0.0)
    for h in range(HEADS_DEV):
        block = kv_ref[:, head_block(h)].astype(F32)
        before = [jnp.zeros((rows, h * HEAD_DIM), F32)] if h else []
        left = feat - (h + 1) * HEAD_DIM
        after = [jnp.zeros((rows, left), F32)] if left else []
        k_extra = masks - jnp.where((lane >= 9 + 3 * h) & (lane < 12 + 3 * h), 1.0, 0.0)
        v_extra = -jnp.where((lane >= 3 * h) & (lane < 3 * h + 3), 1.0, 0.0)
        for heads, part, extra in (
            (k_heads, block[:, :HEAD_DIM], k_extra),
            (v_heads, block[:, HEAD_DIM:], v_extra),
        ):
            heads[h] = jnp.concatenate(before + [part] + after + [extra], axis=1).astype(BF16)


def key_near_kernel(order_ref, kv_ref, tag_ref, q_ref, *rest):
    g_blocks = rest[:6]
    k_acc, v_acc, k_heads, v_heads, q_buffer, q_sems, g_buffer, g_sems = rest[6:]
    queries_in(order_ref, q_ref, q_buffer, q_sems, (0, 1, 2, 4, 5, 6))
    copies_in(g_blocks, g_buffer, g_sems)
    key_heads(kv_ref, tag_ref, k_heads, v_heads)
    k_acc[...] = jnp.zeros_like(k_acc)
    v_acc[...] = jnp.zeros_like(v_acc)
    key_back_blocks(k_heads, v_heads, k_acc, v_acc, q_buffer, g_buffer, q_sems, g_sems)


def key_far_kernel(order_ref, kv_ref, tag_ref, diag_ref, k_in, v_in, q_ref, *rest):
    g_blocks = rest[:4]
    dkv_ref, k_heads, v_heads, k_acc, v_acc, q_buffer, q_sems, g_buffer, g_sems = rest[4:]
    queries_in(order_ref, q_ref, q_buffer, q_sems, (3, 7))
    copies_in(g_blocks, g_buffer, g_sems)
    key_heads(kv_ref, tag_ref, k_heads, v_heads)
    k_acc[...], v_acc[...] = k_in[...], v_in[...]
    key_back_blocks(k_heads, v_heads, k_acc, v_acc, q_buffer, g_buffer, q_sems, g_sems)
    parts = []
    for h in range(HEADS_DEV):
        parts += [k_acc[h][:, head_columns(h)], v_acc[h][:, head_columns(h)]]
    dkv_ref[...] = (jnp.concatenate(parts, axis=1) + diag_ref[...]).astype(BF16)


def query_buffers(count, q_all):
    return [
        pltpu.VMEM((8 * count, *q_all.shape[1:]), BF16),
        pltpu.SemaphoreType.DMA((count,)),
    ]


def smem_spec():
    return [pl.BlockSpec(memory_space=pltpu.SMEM)]


def key_near(order, kv_own, tag, q_all, g_blocks):
    rows, width = kv_own.shape[0], g_blocks[0].shape[2]
    return pl.pallas_call(
        key_near_kernel,
        out_shape=(head_state(rows, width),) * 2,
        in_specs=smem_spec() + vmem_specs(2) + any_specs(7),
        out_specs=tuple(vmem_specs(2)),
        scratch_shapes=[pltpu.VMEM((HEADS_DEV, rows, width), BF16)] * 2
        + query_buffers(6, q_all)
        + buffers(g_blocks, width),
        compiler_params=pltpu.CompilerParams(vmem_limit_bytes=VMEM_LIMIT),
        cost_estimate=cost(rows, g_blocks, 2048),
        name="key_near",
    )(order, kv_own, tag, q_all, *g_blocks)


def key_far(order, kv_own, tag, diagonal, state, q_all, g_blocks):
    rows, width = kv_own.shape[0], g_blocks[0].shape[2]
    return pl.pallas_call(
        key_far_kernel,
        out_shape=jax.ShapeDtypeStruct(diagonal.shape, BF16),
        in_specs=smem_spec() + vmem_specs(5) + any_specs(5),
        out_specs=vmem_specs(1)[0],
        scratch_shapes=[pltpu.VMEM((HEADS_DEV, rows, width), BF16)] * 2
        + [pltpu.VMEM((HEADS_DEV, rows, width), F32)] * 2
        + query_buffers(2, q_all)
        + buffers(g_blocks, width),
        compiler_params=pltpu.CompilerParams(vmem_limit_bytes=VMEM_LIMIT),
        cost_estimate=cost(rows, g_blocks, 2048),
        name="key_far",
    )(order, kv_own, tag, diagonal, *state, q_all, *g_blocks)


def dot(a, b):
    return jnp.dot(a, b, preferred_element_type=F32)


def dot_nt(a, b):
    return lax.dot_general(a, b, NT, preferred_element_type=F32)


def dot_tn(a, b):
    return lax.dot_general(a, b, (((0,), (0,)), ((), ())), preferred_element_type=F32)


def core_half(x, axis, at):
    size = x.shape[axis] // 2
    return lax.dynamic_slice_in_dim(x, at * size, size, axis)


def interleaved(k, v):
    shape = (*k.shape[:-1], -1, HEAD_DIM)
    return jnp.stack([k.reshape(shape), v.reshape(shape)], axis=-2).reshape(*k.shape[:-1], -1)


def per_device(
    hidden,
    w_qkv,
    w_out,
    b_qv,
    w_up,
    w_down,
    b_up,
    norm_gains,
    norm_shifts,
    segments,
    lengths,
    cotangent,
):
    core = lax.axis_index("core")
    heads_at = lax.axis_index("heads")
    own_ctx = ((lax.axis_index("z") * 4 + lax.axis_index("y")) * 2 + lax.axis_index("xh")) * 2 + core
    tok = hidden.shape[0]
    rows = w_up.shape[0]
    feat = HEADS_DEV * HEAD_DIM
    hidden_units = w_up.shape[1] // 2

    hid = chip_tokens(hidden)
    out_turned, down_turned = w_out.T, w_down.T
    low_tok = segments.astype(BF16).reshape(2, tok // 2)
    kv_cols = 2 * feat

    def halves(x):
        return jnp.swapaxes(x.reshape(rows, 2, -1), 0, 1)

    q_half, k_half, v_half = (halves(w_qkv[i]) for i in range(3))
    tail = jnp.broadcast_to(jnp.pad(low_tok, ((0, rows - 2), (0, 0))), (2, rows, tok // 2))
    urgent = jnp.concatenate([interleaved(k_half, v_half), q_half, tail], axis=2)
    urgent = jnp.pad(urgent, ((0, 0), (0, 16 - rows), (0, 0)))
    urgent = jnp.broadcast_to(urgent[None], (32, *urgent.shape)).reshape(64, 16, -1)
    urgent, *later = lax.optimization_barrier((urgent, out_turned, w_up, down_turned))
    later = jnp.concatenate([halves(w) for w in later], axis=2)
    mine = lax.dynamic_index_in_dim(later, core, 0, keepdims=False)
    theirs = shifted(lax.dynamic_index_in_dim(later, 1 - core, 0, keepdims=False), "core", 1)
    later = pair_ordered(mine, theirs, "core").reshape(2 * rows, -1)
    rest = lax.all_gather(later, CHIPS, axis=0, tiled=True)
    w_urgent = lax.all_to_all(urgent, CTX, 0, 0, tiled=True)
    seg_all = w_urgent[:, :2, kv_cols + feat :].reshape(-1, tok).astype(jnp.int32)
    w_urgent = w_urgent.reshape(64 * 16, -1)
    at_wide = jnp.arange(64 * 16, dtype=jnp.int32)
    at_feature = jnp.arange(64 * rows, dtype=jnp.int32)
    spread = (
        (at_feature // rows * 16 + at_feature % rows)[:, None] == at_wide[None, :]
    ).astype(BF16)
    hid_wide = dot(hid, spread).astype(BF16)

    w_out_t = rest[:, :feat]
    w_up_all = rest[:, feat : feat + hidden_units]
    w_down_t = rest[:, feat + hidden_units :]

    bias = b_qv.astype(F32)
    q_bias, v_bias = core_half(bias[0], 0, core), core_half(bias[1], 0, core)
    no_bias = jnp.zeros((tok // 2,), F32)
    bias_row = jnp.concatenate([interleaved(jnp.zeros_like(v_bias), v_bias), q_bias, no_bias])
    column = jnp.arange(bias_row.shape[0], dtype=jnp.int32)
    scale_row = jnp.where(
        column < kv_cols, 1.0, jnp.where(column < kv_cols + feat, HEAD_DIM ** (-0.5), 0.0)
    ).astype(F32)
    kv_own, q_wide, q_heads = project(hid_wide, w_urgent, bias_row[None], scale_row[None])
    q_all = lax.all_gather(q_wide, CHIPS, axis=0, tiled=True).reshape(64, tok, -1)
    starts = [jnp.sum((seg_all < s).astype(jnp.int32)) for s in range(3)]
    places = jnp.arange(seg_all.size, dtype=jnp.int32).reshape(seg_all.shape)
    run_end = jnp.zeros_like(seg_all)
    for s in range(3):
        run_end = jnp.where(seg_all == s, starts[s] + lengths[s], run_end)
    tag_all = jnp.where(places < run_end, seg_all, -1).astype(F32)
    order = jnp.concatenate([relative_order("z", "y", 0), relative_order("y", "z", 1)])
    q_order = jnp.where(core == 0, order, order + 1 - 2 * (order % 2))
    tags = jnp.take(tag_all, order, axis=0).reshape(8, -1)
    both = jnp.stack([own_ctx, own_ctx + 1 - 2 * core])
    tag_own = jnp.take(tag_all, both, axis=0).reshape(-1, 1)
    seg_own = jnp.take(seg_all, both, axis=0).astype(F32).reshape(-1, 1)

    sent_z, sent_y = lax.optimization_barrier(gather_first(kv_own))
    blocks = gather_second(sent_z, sent_y)
    near, far = near_blocks(blocks), far_blocks(blocks)
    state = attend_near(q_heads, kv_own, tags, seg_own, tag_own, near)
    attended, stat = attend_far(q_heads, tags, seg_own, state, far)
    attended_low = attended.astype(BF16)

    gain_rows = norm_gains.astype(F32)
    shifts = norm_shifts.astype(F32)
    attn_mixed = team_sum(dot_nt(attended_low, w_out_t))
    first_out, normed_one, inverse_one = layer_norm(
        hidden.astype(F32) + attn_mixed + shifts[0], gain_rows[0], shifts[1]
    )
    first_low = chip_tokens(first_out.astype(BF16))
    up_bias = core_half(b_up, 0, core).astype(F32)
    up_proj = dot(first_low, w_up_all) + up_bias
    activated = exact_gelu(up_proj).astype(BF16)
    second = team_sum(dot_nt(activated, w_down_t))
    output, normed_two, inverse_two = layer_norm(
        first_out + second + shifts[2], gain_rows[1], shifts[3]
    )
    resid_two = norm_back(
        cotangent.astype(F32), normed_two, inverse_two, gain_rows[1]
    )
    branch_low = chip_tokens(resid_two.astype(BF16))
    act_grad = dot(branch_low, w_down_t)
    up_low = jax.vjp(exact_gelu, up_proj)[1](act_grad)[0].astype(BF16)
    first_grad = resid_two + team_sum(dot_nt(up_low, w_up_all))
    resid_one = norm_back(first_grad, normed_one, inverse_one, gain_rows[0])
    mixed_low = chip_tokens(resid_one.astype(BF16))
    g_sent, g_heads, delta = grad_rows(mixed_low, w_out_t, attended, stat, seg_own)
    made = early_grads(spread, branch_low, activated, first_low, up_low)
    (g_z, g_y), g_heads, made = lax.optimization_barrier((gather_first(g_sent), g_heads, made))
    g_blocks = gather_second(g_z, g_y)
    g_near, g_far = near_blocks(g_blocks), far_blocks(g_blocks)
    at_bias = jnp.arange(hidden_units, dtype=jnp.int32)
    at_half = jnp.arange(feat, dtype=jnp.int32)
    at_kv = jnp.arange(kv_cols, dtype=jnp.int32)

    def placed(owner, row):
        return ((owner * 16 + row)[:, None] == at_wide[None, :]).astype(BF16)

    first_owner = 32 * core
    bias_place = placed(first_owner + at_bias // 24, at_bias % 12)
    q_place = placed(first_owner + at_half // 6, at_half % 6)
    at_value = at_kv // 128 * HEAD_DIM + at_kv % 128 - HEAD_DIM
    is_value = at_kv % 128 >= HEAD_DIM
    v_place = placed(jnp.where(is_value, first_owner + at_value // 6, -1), at_value % 6)
    parts = jnp.arange(2, dtype=jnp.int32)[:, None] == (at_bias % 24 // 12)[None, :]
    dq, diagonal = query_back(
        q_heads, g_heads, kv_own, tags, seg_own, tag_own, stat, delta, near + far
    )
    g_near, made, dq, spread = lax.optimization_barrier((g_near, made, dq, spread))
    early = to_owners(made)
    out_placed = out_rows(spread, mixed_low, attended_low)
    rows_made = vector_rows(
        spread,
        cotangent,
        normed_two,
        resid_two,
        first_grad,
        normed_one,
        resid_one,
        up_low,
        spread,
        bias_place,
        parts.astype(F32),
    )

    key_state = key_near(q_order, kv_own, tag_own, q_all, g_near)
    dkv = key_far(q_order, kv_own, tag_own, diagonal, key_state, q_all, g_far)
    dkv, early = lax.optimization_barrier((dkv, early))
    late, back = late_grads(
        hid_wide, dkv, dq, rows_made, q_place, v_place, out_placed, w_urgent, spread
    )
    late = to_owners(late)
    hidden_grad = resid_one + team_sum(back.astype(F32))

    early_sums, late_sums = owner_sums(early), owner_sums(late)

    def columns(x, start, size):
        return jnp.concatenate([x[c, :rows, start : start + size] for c in range(2)], axis=1)

    kv_pairs = columns(late_sums, 0, kv_cols).reshape(rows, 2 * HEADS_DEV, 2, HEAD_DIM)
    k_cols = kv_pairs[:, :, 0].reshape(rows, -1)
    v_cols = kv_pairs[:, :, 1].reshape(rows, -1)
    q_cols = columns(late_sums, kv_cols, feat)

    def last(x, size):
        return jnp.concatenate(
            [x[:, rows:, g * size : (g + 1) * size] for g in range(3)], axis=1
        )

    quarter = hidden_units // 2
    up_cols = columns(early_sums, 0, hidden_units)
    down_first, down_last = early_sums[:, :rows, hidden_units:], last(early_sums, quarter)
    down_cols = jnp.concatenate(
        [down_first[0], down_last[0], down_first[1], down_last[1]], axis=1
    )
    out_last = last(late_sums, feat)
    out_cols = jnp.concatenate([out_last[0], out_last[1]], axis=1)
    small = (late_sums[0] + late_sums[1])[:rows, kv_cols + feat :].T
    vec_out = small[:6].reshape(6, 2, 6)
    bias_out = small[6:8].reshape(-1)
    qv_out = small[8:10, :6]
    vec_out = lax.dynamic_index_in_dim(vec_out, heads_at, 1, keepdims=False)
    return (
        output.astype(BF16),
        hidden_grad,
        jnp.stack([q_cols, k_cols, v_cols]),
        out_cols.T,
        qv_out,
        up_cols,
        down_cols.T,
        bias_out,
        vec_out[:2],
        vec_out[2:],
    )


def solution(mesh):
    fine = Mesh(mesh.devices.reshape(4, 4, 2, 2, 2), ("z", "y", "xh", "core", "heads"))
    return jax.shard_map(
        per_device,
        mesh=fine,
        in_specs=(
            P(CTX, None),
            P(None, CTX, "heads"),
            P("heads", CTX),
            P(None, "heads"),
            P(CTX, "heads"),
            P("heads", CTX),
            P("heads"),
            P(),
            P(),
            P(CTX),
            P(),
            P(CTX, None),
        ),
        out_specs=(
            P(CTX, None),
            P(CTX, None),
            P(None, CTX, "heads"),
            P("heads", CTX),
            P(None, ("heads", *CTX)),
            P(CTX, "heads"),
            P("heads", CTX),
            P(("heads", *CTX)),
            P(None, (*CTX, "heads")),
            P(None, (*CTX, "heads")),
        ),
        check_vma=False,
    )
```

```python
import jax
import jax.numpy as jnp
from jax import lax
from jax.experimental import pallas as pl
from jax.experimental.pallas import tpu as pltpu
from jax.sharding import Mesh, PartitionSpec as P

HEAD_DIM = 64
HEADS_DEV = 3
EPS = 1e-06
NEG = -1e30
CTX = ("z", "y", "xh", "core")
CHIPS = ("z", "y", "xh")
F32 = jnp.float32
BF16 = jnp.bfloat16
NT = (((1,), (1,)), ((), ()))
VMEM_LIMIT = 50 * 1024 * 1024
OFFSETS = (0, -1, 1, 2)


def shifted(x, axis, step):
    n = lax.axis_size(axis)
    return lax.ppermute(x, axis, [(i, (i + step) % n) for i in range(n)])


def ring_halves(x, axis):
    half = x.shape[0] // 2
    before, after = shifted(x, axis, 1), shifted(x, axis, -1)
    return [x, before, after, shifted(before[:half], axis, 1), shifted(after[half:], axis, -1)]


def ring_near(x, axis):
    return [paired(b) for b in (x, shifted(x, axis, 1), shifted(x, axis, -1))]


def paired(x):
    return x.reshape(2, x.shape[0] // 2, x.shape[1])


def gather_first(x):
    half = x.shape[0] // 2
    streams = []
    for part, axis in ((x[:half], "z"), (x[half:], "y")):
        both = jnp.concatenate([part, shifted(part, "xh", 1)], axis=0)
        streams.append(jnp.concatenate(ring_halves(both, axis), axis=0))
    return tuple(streams)


def gather_second(z_stream, y_stream):
    blocks = ring_halves(z_stream, "y") + ring_halves(y_stream, "z")
    return [b.reshape(-1, z_stream.shape[0] // 2, b.shape[1]) for b in blocks]


def near_blocks(blocks):
    return blocks[:3] + blocks[5:8]


def far_blocks(blocks):
    return blocks[3:5] + blocks[8:]


def relative_order(first, second, core_at):
    place = {a: lax.axis_index(a) for a in CHIPS}
    core = lax.axis_index("core")
    order = []
    for second_step in OFFSETS:
        for first_step in OFFSETS:
            for xh_step in (0, 1):
                at = dict(place)
                at[first] = (at[first] + first_step) % 4
                at[second] = (at[second] + second_step) % 4
                at["xh"] = (at["xh"] + xh_step) % 2
                order.append(((at["z"] * 4 + at["y"]) * 2 + at["xh"]) * 2 + (core + core_at) % 2)
    return jnp.stack(order)


def pair_ordered(own, other, axis):
    first = lax.axis_index(axis) == 0
    return jnp.stack([jnp.where(first, own, other), jnp.where(first, other, own)])


def to_owners(x):
    return lax.all_to_all(x.reshape(64, 16, -1), CTX, 0, 0, tiled=True)


def owner_sums(parts):
    return jnp.sum(parts.reshape(-1, 2, *parts.shape[1:]).astype(F32), axis=0)


def team_sum(partial, beside=()):
    rows = partial.shape[0] // 2
    near = partial[:rows] + shifted(partial[rows:].astype(BF16), "core", 1).astype(F32)
    low = lax.optimization_barrier(near.astype(BF16))
    got, beside = lax.optimization_barrier((shifted(low, "heads", 1), beside))
    return low.astype(F32) + got.astype(F32), beside


def chip_tokens(x):
    return jnp.concatenate([x, shifted(x, "core", 1)], axis=0)


def layer_norm(residual, gain_row, shift_row):
    centred = residual - jnp.mean(residual, axis=-1, keepdims=True)
    inverse = lax.rsqrt(jnp.mean(centred * centred, axis=-1, keepdims=True) + EPS)
    normed = centred * inverse
    return (normed * gain_row + shift_row, normed, inverse)


def norm_back(incoming, normed, inverse, gain_row):
    scaled = incoming * gain_row
    projected = (
        scaled
        - jnp.mean(scaled, axis=-1, keepdims=True)
        - normed * jnp.mean(scaled * normed, axis=-1, keepdims=True)
    )
    return inverse * projected


def exact_gelu(pre_act):
    return jax.nn.gelu(pre_act, approximate=False)


def pieces_of(column):
    high = column.astype(BF16).astype(F32)
    middle = (column - high).astype(BF16).astype(F32)
    return high, middle, column - high - middle


def head_columns(h):
    return slice(h * HEAD_DIM, (h + 1) * HEAD_DIM)


def head_block(h):
    return slice(h * 128, (h + 1) * 128)


def diagonal_scores(q_ref, kv_ref, h):
    product = q_ref[h].astype(F32) * kv_ref[:, head_block(h)].astype(F32)
    return jnp.sum(product, axis=1, keepdims=True)


def copies_in(sources, buffer, sems):
    at = 0
    for source in sources:
        size = source.shape[0]
        pltpu.make_async_copy(source, buffer.at[pl.ds(at, size)], sems.at[at // 2]).start()
        at += size


def block_of(buffer, sems, j):
    block = buffer.at[pl.ds(2 * j, 2)]
    pltpu.make_async_copy(block, block, sems.at[j]).wait()
    return buffer[pl.ds(2 * j, 2)].reshape(-1, buffer.shape[2])


def attend_blocks(q_ref, tags_ref, seg_ref, top, total, acc, buffer, sems, row_of):
    rows = q_ref.shape[1]
    seg_wide = jnp.broadcast_to(seg_ref[...], (rows, 128))

    def step(j, carry):
        whole = block_of(buffer, sems, j)
        tags = tags_ref[pl.ds(row_of(j), 1), :]
        keys = tags.shape[1]
        allowed = jnp.tile(seg_wide, (1, keys // 128)) == tags
        for h in range(HEADS_DEV):
            kv = whole[:, head_block(h)]
            scores = lax.dot_general(q_ref[h], kv, NT, preferred_element_type=F32)
            scores = jnp.where(allowed, scores, NEG)
            before = top[h]
            now = jnp.maximum(before, jnp.max(scores, axis=1, keepdims=True))
            weights = jnp.exp(scores - jnp.tile(now, (1, keys // 128)))
            fade = jnp.exp(before - now)
            sums = weights[:, :128]
            for k in range(1, keys // 128):
                sums = sums + weights[:, k * 128 : (k + 1) * 128]
            total[h] = total[h] * fade + sums
            acc[h] = acc[h] * fade + jnp.dot(weights.astype(BF16), kv, preferred_element_type=F32)
            top[h] = now
        return carry

    lax.fori_loop(0, sems.shape[0], step, 0)


def near_row(j):
    return j + (j >= 3).astype(jnp.int32)


def far_row(j):
    return 4 * j + 3


def attend_near_kernel(q_ref, own_ref, tags_ref, seg_ref, tag_ref, *rest):
    blocks, (top, total, acc, buffer, sems) = rest[:6], rest[6:]
    copies_in(blocks, buffer, sems)
    rows = q_ref.shape[1]
    padded = tag_ref[...] < 0
    for h in range(HEADS_DEV):
        diagonal = diagonal_scores(q_ref, own_ref, h)
        top[h] = jnp.broadcast_to(jnp.where(padded, diagonal, NEG), (rows, 128))
        lane = lax.broadcasted_iota(jnp.int32, (rows, 128), 1)
        total[h] = jnp.where((lane == 0) & padded, 1.0, 0.0)
        acc[h] = jnp.where(padded, own_ref[:, head_block(h)].astype(F32), 0.0)
    attend_blocks(q_ref, tags_ref, seg_ref, top, total, acc, buffer, sems, near_row)


def attend_far_kernel(q_ref, tags_ref, seg_ref, top_in, total_in, acc_in, *rest):
    blocks, (out_ref, stat_ref, top, total, acc, buffer, sems) = rest[:4], rest[4:]
    copies_in(blocks, buffer, sems)
    top[...], total[...], acc[...] = top_in[...], total_in[...], acc_in[...]
    attend_blocks(q_ref, tags_ref, seg_ref, top, total, acc, buffer, sems, far_row)
    outs = []
    for h in range(HEADS_DEV):
        sums = jnp.sum(total[h], axis=1, keepdims=True)
        outs.append((acc[h] / sums)[:, HEAD_DIM:])
        stat_ref[h] = top[h] + jnp.log(sums)
    out_ref[...] = jnp.concatenate(outs, axis=1)


def vmem_specs(n):
    return [pl.BlockSpec(memory_space=pltpu.VMEM)] * n


def any_specs(n):
    return [pl.BlockSpec(memory_space=pl.ANY)] * n


def head_state(rows, lanes=128):
    return jax.ShapeDtypeStruct((HEADS_DEV, rows, lanes), F32)


def cost(rows, blocks, flops):
    keys = sum(b.shape[0] * b.shape[1] for b in blocks)
    pairs = rows * keys * HEADS_DEV
    return pl.CostEstimate(
        flops=pairs * flops, bytes_accessed=keys * 1024, transcendentals=pairs
    )


def buffers(blocks, lanes):
    count = sum(b.shape[0] for b in blocks)
    return [
        pltpu.VMEM((count, blocks[0].shape[1], lanes), BF16),
        pltpu.SemaphoreType.DMA((count // 2,)),
    ]


def attend_near(q_heads, kv_own, tags, seg, tag, blocks):
    rows = kv_own.shape[0]
    return pl.pallas_call(
        attend_near_kernel,
        out_shape=(head_state(rows),) * 3,
        in_specs=vmem_specs(5) + any_specs(6),
        out_specs=tuple(vmem_specs(3)),
        scratch_shapes=buffers(blocks, kv_own.shape[1]),
        compiler_params=pltpu.CompilerParams(vmem_limit_bytes=VMEM_LIMIT),
        cost_estimate=cost(rows, blocks, 512),
        name="attend_near",
    )(q_heads, kv_own, tags, seg, tag, *blocks)


def attend_far(q_heads, tags, seg, state, blocks):
    rows = q_heads.shape[1]
    return pl.pallas_call(
        attend_far_kernel,
        out_shape=(jax.ShapeDtypeStruct((rows, HEADS_DEV * HEAD_DIM), F32), head_state(rows)),
        in_specs=vmem_specs(6) + any_specs(4),
        out_specs=tuple(vmem_specs(2)),
        scratch_shapes=[pltpu.VMEM((HEADS_DEV, rows, 128), F32)] * 3
        + buffers(blocks, HEADS_DEV * 128),
        compiler_params=pltpu.CompilerParams(vmem_limit_bytes=VMEM_LIMIT),
        cost_estimate=cost(rows, blocks, 512),
        name="attend_far",
    )(q_heads, tags, seg, *state, *blocks)


def query_back_kernel(q_ref, g_ref, own_ref, tags_ref, seg_ref, tag_ref, stat_ref, delta_ref, *rest):
    blocks, (dq_ref, dkv_ref, buffer, sems, acc) = rest[:10], rest[10:]
    copies_in(blocks, buffer, sems)
    rows = q_ref.shape[1]
    seg_wide = jnp.broadcast_to(seg_ref[...], (rows, 128))
    padded = tag_ref[...] < 0
    for h in range(HEADS_DEV):
        own = own_ref[:, head_block(h)].astype(F32)
        prob = jnp.exp(diagonal_scores(q_ref, own_ref, h) - stat_ref[h][:, :1])
        prob = jnp.where(padded, prob, 0.0)
        grad = diagonal_scores(g_ref, own_ref, h) - delta_ref[h][:, :1]
        score = (prob * grad).astype(BF16).astype(F32)
        acc[h] = score * own
        dkv_ref[:, head_block(h)] = score * q_ref[h].astype(F32) + prob.astype(BF16).astype(
            F32
        ) * g_ref[h].astype(F32)

    def step(j, carry):
        whole = block_of(buffer, sems, j)
        tags = tags_ref[pl.ds(jnp.where(j < 6, near_row(j), far_row(j - 6)), 1), :]
        keys = tags.shape[1]
        allowed = jnp.tile(seg_wide, (1, keys // 128)) == tags
        for h in range(HEADS_DEV):
            kv = whole[:, head_block(h)]
            scores = lax.dot_general(q_ref[h], kv, NT, preferred_element_type=F32)
            scores = jnp.where(allowed, scores, NEG)
            probs = jnp.exp(scores - jnp.tile(stat_ref[h], (1, keys // 128)))
            grads = lax.dot_general(g_ref[h], kv, NT, preferred_element_type=F32)
            back = probs * (grads - jnp.tile(delta_ref[h], (1, keys // 128)))
            acc[h] = acc[h] + jnp.dot(back.astype(BF16), kv, preferred_element_type=F32)
        return carry

    lax.fori_loop(0, 8, step, 0)
    dq_ref[...] = (
        jnp.concatenate([acc[h][:, :HEAD_DIM] for h in range(HEADS_DEV)], axis=1)
        * HEAD_DIM ** (-0.5)
    ).astype(BF16)


def query_back(q_heads, g_heads, kv_own, tags, seg, tag, stat, delta, blocks):
    rows = kv_own.shape[0]
    return pl.pallas_call(
        query_back_kernel,
        out_shape=(
            jax.ShapeDtypeStruct((rows, HEADS_DEV * HEAD_DIM), BF16),
            jax.ShapeDtypeStruct(kv_own.shape, F32),
        ),
        in_specs=vmem_specs(8) + any_specs(10),
        out_specs=tuple(vmem_specs(2)),
        scratch_shapes=buffers(blocks, kv_own.shape[1]) + [pltpu.VMEM((HEADS_DEV, rows, 128), F32)],
        compiler_params=pltpu.CompilerParams(vmem_limit_bytes=VMEM_LIMIT),
        cost_estimate=cost(rows, blocks, 768),
        name="query_back",
    )(q_heads, g_heads, kv_own, tags, seg, tag, stat, delta, *blocks)


def grad_rows_kernel(
    mixed_ref, out_ref, attended_ref, stat_ref, seg_ref, sent_ref, g_ref, delta_ref
):
    rows = mixed_ref.shape[0]
    grad = jnp.dot(mixed_ref[...], out_ref[...], preferred_element_type=F32).astype(BF16)
    grad = grad.astype(F32)
    product = grad * attended_ref[...]
    lane = lax.broadcasted_iota(jnp.int32, (rows, HEAD_DIM), 1)
    seg = seg_ref[...]
    extra = jnp.where(lane == 21, 1.0, 0.0)
    for s in range(3):
        extra = extra + jnp.where((lane == 18 + s) & (seg != s), 1.0, 0.0)
    zeros = jnp.zeros((rows, HEAD_DIM), BF16)
    for h in range(HEADS_DEV):
        delta = jnp.sum(product[:, head_columns(h)], axis=1, keepdims=True)
        delta_ref[h] = jnp.broadcast_to(delta, (rows, 128))
        for i, piece in enumerate(pieces_of(delta)):
            extra = extra + jnp.where(lane == 3 * h + i, piece, 0.0)
        for i, piece in enumerate(pieces_of(stat_ref[h][:, :1])):
            extra = extra + jnp.where(lane == 9 + 3 * h + i, piece, 0.0)
        g_ref[h] = jnp.concatenate([zeros, grad[:, head_columns(h)].astype(BF16)], axis=1)
    sent_ref[...] = jnp.concatenate([grad, extra], axis=1).astype(BF16)


def grad_rows(mixed, w_out, attended, stat, seg):
    rows = mixed.shape[0]
    return pl.pallas_call(
        grad_rows_kernel,
        out_shape=(
            jax.ShapeDtypeStruct((rows, 256), BF16),
            jax.ShapeDtypeStruct((HEADS_DEV, rows, 128), BF16),
            jax.ShapeDtypeStruct((HEADS_DEV, rows, 128), F32),
        ),
        in_specs=vmem_specs(5),
        out_specs=tuple(vmem_specs(3)),
        compiler_params=pltpu.CompilerParams(vmem_limit_bytes=VMEM_LIMIT),
        name="grad_rows",
    )(mixed, w_out, attended, stat, seg)


def send_out(held, out_ref, sem):
    copy = pltpu.make_async_copy(held, out_ref, sem)
    copy.start()
    copy.wait()


def last_rows(x, group):
    parts = x.reshape(64, 16, x.shape[1])[:, 4 * group : 4 * group + 4]
    return jnp.concatenate([jnp.zeros((64, 12, x.shape[1]), F32), parts], axis=1).reshape(x.shape)


def early_grads_kernel(spread_ref, branch_ref, activated_ref, first_ref, up_ref, out_ref, held, sem):
    quarter = held.shape[1] // 3
    made = []
    for left, right in ((first_ref, up_ref), (branch_ref, activated_ref)):
        wide = jnp.dot(left[...], spread_ref[...], preferred_element_type=F32).astype(BF16)
        for half in range(2):
            made.append(dot_tn(wide, right[:, half * quarter : (half + 1) * quarter]))
    for g in range(3):
        held[:, g * quarter : (g + 1) * quarter] = (made[g] + last_rows(made[3], g)).astype(BF16)
    send_out(held, out_ref, sem)


def early_grads(spread, branch, activated, first, up):
    shape = (spread.shape[1], up.shape[1] * 3 // 2)
    return pl.pallas_call(
        early_grads_kernel,
        out_shape=jax.ShapeDtypeStruct(shape, BF16),
        in_specs=vmem_specs(5),
        out_specs=pl.BlockSpec(memory_space=pltpu.HBM),
        scratch_shapes=[pltpu.VMEM(shape, BF16), pltpu.SemaphoreType.DMA],
        compiler_params=pltpu.CompilerParams(vmem_limit_bytes=VMEM_LIMIT),
        name="early_grads",
    )(spread, branch, activated, first, up)


def out_rows_kernel(spread_ref, mixed_ref, attended_ref, out_ref):
    wide = jnp.dot(mixed_ref[...], spread_ref[...], preferred_element_type=F32).astype(BF16)
    made = dot_tn(wide, attended_ref[...].astype(BF16))
    out_ref[...] = jnp.concatenate([last_rows(made, g) for g in range(3)], axis=1).astype(BF16)


def out_rows(spread, mixed, attended):
    return pl.pallas_call(
        out_rows_kernel,
        out_shape=jax.ShapeDtypeStruct((spread.shape[1], 3 * attended.shape[1]), BF16),
        in_specs=vmem_specs(3),
        out_specs=vmem_specs(1)[0],
        compiler_params=pltpu.CompilerParams(vmem_limit_bytes=VMEM_LIMIT),
        name="out_rows",
    )(spread, mixed, attended)


def vector_rows_kernel(
    cot_ref, two_ref, resid_two_ref, first_ref, one_ref, resid_one_ref, up_ref, spread_ref, bias_ref,
    parts_ref, out_ref,
):
    cot, first = cot_ref[...].astype(F32), first_ref[...]
    columns = (
        first * one_ref[...],
        cot * two_ref[...],
        resid_one_ref[...],
        first,
        resid_two_ref[...],
        cot,
    )
    rows = jnp.concatenate([jnp.sum(c, axis=0, keepdims=True) for c in columns], axis=0)
    bias = jnp.sum(up_ref[...].astype(F32), axis=0, keepdims=True) * parts_ref[...]
    made = [
        jnp.dot(rows.astype(BF16), spread_ref[...], preferred_element_type=F32),
        jnp.dot(bias.astype(BF16), bias_ref[...], preferred_element_type=F32),
    ]
    out_ref[...] = jnp.concatenate(made, axis=0)


def vector_rows(spread, *args):
    return pl.pallas_call(
        vector_rows_kernel,
        out_shape=jax.ShapeDtypeStruct((8, spread.shape[1]), F32),
        in_specs=vmem_specs(10),
        out_specs=vmem_specs(1)[0],
        compiler_params=pltpu.CompilerParams(vmem_limit_bytes=VMEM_LIMIT),
        name="vector_rows",
    )(*args)


def late_grads_kernel(
    hid_ref, dkv_ref, dq_ref, rows_ref, q_place_ref, v_place_ref, placed_ref, w_ref, spread_ref,
    out_ref, back_ref, held, sem,
):
    wide = hid_ref.shape[1]
    grads = jnp.concatenate([dkv_ref[...], dq_ref[...]], axis=1)
    cols = grads.shape[1]
    made = dot_tn(hid_ref[...], grads) + placed_ref[...].astype(F32)
    sums = [rows_ref[...]]
    for grad, place in ((dq_ref, q_place_ref), (dkv_ref, v_place_ref)):
        row = jnp.sum(grad[...].astype(F32), axis=0, keepdims=True).astype(BF16)
        sums.append(jnp.dot(row, place[...], preferred_element_type=F32))
    sums.append(jnp.zeros((128 - 10, wide), F32))
    small = jnp.transpose(jnp.concatenate(sums, axis=0))[:, :64]
    held[...] = jnp.concatenate([made, small], axis=1).astype(BF16)
    copy = pltpu.make_async_copy(held, out_ref, sem)
    copy.start()
    back = dot_nt(grads, w_ref[:, :cols]).astype(BF16)
    back_ref[...] = dot_nt(back, spread_ref[...]).astype(BF16)
    copy.wait()


def late_grads(hid, dkv, dq, rows, q_place, v_place, placed, w, spread):
    shape = (hid.shape[1], dkv.shape[1] + dq.shape[1] + 64)
    return pl.pallas_call(
        late_grads_kernel,
        out_shape=(
            jax.ShapeDtypeStruct(shape, BF16),
            jax.ShapeDtypeStruct((hid.shape[0], spread.shape[0]), BF16),
        ),
        in_specs=vmem_specs(9),
        out_specs=(pl.BlockSpec(memory_space=pltpu.HBM), vmem_specs(1)[0]),
        scratch_shapes=[pltpu.VMEM(shape, BF16), pltpu.SemaphoreType.DMA],
        compiler_params=pltpu.CompilerParams(vmem_limit_bytes=VMEM_LIMIT),
        name="late_grads",
    )(hid, dkv, dq, rows, q_place, v_place, placed, w, spread)


def project_kernel(hid_ref, w_ref, bias_ref, scale_ref, kv_ref, wide_ref, q_ref):
    made = jnp.dot(hid_ref[...], w_ref[...], preferred_element_type=F32) + bias_ref[...]
    made = (made.astype(BF16).astype(F32) * scale_ref[...]).astype(BF16)
    kv_cols = kv_ref.shape[1]
    kv_ref[...] = made[:, :kv_cols]
    wide_ref[...] = made[:, kv_cols:]
    zeros = jnp.zeros((made.shape[0], HEAD_DIM), BF16)
    for h in range(HEADS_DEV):
        at = kv_cols + h * HEAD_DIM
        q_ref[h] = jnp.concatenate([made[:, at : at + HEAD_DIM], zeros], axis=1)


def project(hid, w, bias, scale):
    rows = hid.shape[0]
    return pl.pallas_call(
        project_kernel,
        out_shape=(
            jax.ShapeDtypeStruct((rows, HEADS_DEV * 128), BF16),
            jax.ShapeDtypeStruct((rows, w.shape[1] - HEADS_DEV * 128), BF16),
            jax.ShapeDtypeStruct((HEADS_DEV, rows, 128), BF16),
        ),
        in_specs=vmem_specs(4),
        out_specs=tuple(vmem_specs(3)),
        compiler_params=pltpu.CompilerParams(vmem_limit_bytes=VMEM_LIMIT),
        name="project",
    )(hid, w, bias, scale)


def queries_in(order_ref, q_ref, q_buffer, q_sems, rows):
    for i in range(8 * len(rows)):
        source = order_ref[8 * rows[i // 8] + i % 8]
        pltpu.make_async_copy(q_ref.at[source], q_buffer.at[i], q_sems.at[i // 8]).start()


def key_back_blocks(k_ref, v_ref, k_acc, v_acc, q_buffer, g_buffer, q_sems, g_sems):
    def step(j, carry):
        eight = q_buffer.at[pl.ds(8 * j, 8)]
        pltpu.make_async_copy(eight, eight, q_sems.at[j]).wait()
        queries = q_buffer[pl.ds(8 * j, 8)].reshape(-1, q_buffer.shape[2])
        grads = block_of(g_buffer, g_sems, j)
        lane = lax.broadcasted_iota(jnp.int32, queries.shape, 1)
        queries = jnp.where(lane < HEADS_DEV * HEAD_DIM, queries, grads)
        for h in range(HEADS_DEV):
            scores = lax.dot_general(k_ref[h], queries, NT, preferred_element_type=F32)
            probs = jnp.exp(scores)
            v_acc[h] = v_acc[h] + jnp.dot(probs.astype(BF16), grads, preferred_element_type=F32)
            back = probs * lax.dot_general(v_ref[h], grads, NT, preferred_element_type=F32)
            k_acc[h] = k_acc[h] + jnp.dot(back.astype(BF16), queries, preferred_element_type=F32)
        return carry

    lax.fori_loop(0, q_sems.shape[0], step, 0)


def key_heads(kv_ref, tag_ref, k_heads, v_heads):
    rows = kv_ref.shape[0]
    feat = HEADS_DEV * HEAD_DIM
    lane = lax.broadcasted_iota(jnp.int32, (rows, HEAD_DIM), 1)
    tag = tag_ref[...]
    masks = jnp.where((lane == 21) & (tag < 0), NEG, 0.0)
    for s in range(3):
        masks = masks + jnp.where((lane == 18 + s) & (tag == s), NEG, 0.0)
    for h in range(HEADS_DEV):
        block = kv_ref[:, head_block(h)].astype(F32)
        before = [jnp.zeros((rows, h * HEAD_DIM), F32)] if h else []
        left = feat - (h + 1) * HEAD_DIM
        after = [jnp.zeros((rows, left), F32)] if left else []
        k_extra = masks - jnp.where((lane >= 9 + 3 * h) & (lane < 12 + 3 * h), 1.0, 0.0)
        v_extra = -jnp.where((lane >= 3 * h) & (lane < 3 * h + 3), 1.0, 0.0)
        for heads, part, extra in (
            (k_heads, block[:, :HEAD_DIM], k_extra),
            (v_heads, block[:, HEAD_DIM:], v_extra),
        ):
            heads[h] = jnp.concatenate(before + [part] + after + [extra], axis=1).astype(BF16)


def key_near_kernel(order_ref, kv_ref, tag_ref, q_ref, *rest):
    g_blocks = rest[:6]
    k_acc, v_acc, k_heads, v_heads, q_buffer, q_sems, g_buffer, g_sems = rest[6:]
    queries_in(order_ref, q_ref, q_buffer, q_sems, (0, 1, 2, 4, 5, 6))
    copies_in(g_blocks, g_buffer, g_sems)
    key_heads(kv_ref, tag_ref, k_heads, v_heads)
    k_acc[...] = jnp.zeros_like(k_acc)
    v_acc[...] = jnp.zeros_like(v_acc)
    key_back_blocks(k_heads, v_heads, k_acc, v_acc, q_buffer, g_buffer, q_sems, g_sems)


def key_far_kernel(order_ref, kv_ref, tag_ref, diag_ref, k_in, v_in, q_ref, *rest):
    g_blocks = rest[:2]
    dkv_ref, k_heads, v_heads, k_acc, v_acc, q_buffer, q_sems, g_buffer, g_sems = rest[2:]
    queries_in(order_ref, q_ref, q_buffer, q_sems, (3, 7))
    copies_in(g_blocks, g_buffer, g_sems)
    key_heads(kv_ref, tag_ref, k_heads, v_heads)
    k_acc[...], v_acc[...] = k_in[...], v_in[...]
    key_back_blocks(k_heads, v_heads, k_acc, v_acc, q_buffer, g_buffer, q_sems, g_sems)
    parts = []
    for h in range(HEADS_DEV):
        parts += [k_acc[h][:, head_columns(h)], v_acc[h][:, head_columns(h)]]
    dkv_ref[...] = (jnp.concatenate(parts, axis=1) + diag_ref[...]).astype(BF16)


def query_buffers(count, q_all):
    return [
        pltpu.VMEM((8 * count, *q_all.shape[1:]), BF16),
        pltpu.SemaphoreType.DMA((count,)),
    ]


def smem_spec():
    return [pl.BlockSpec(memory_space=pltpu.SMEM)]


def key_near(order, kv_own, tag, q_all, g_blocks):
    rows, width = kv_own.shape[0], g_blocks[0].shape[2]
    return pl.pallas_call(
        key_near_kernel,
        out_shape=(head_state(rows, width),) * 2,
        in_specs=smem_spec() + vmem_specs(2) + any_specs(7),
        out_specs=tuple(vmem_specs(2)),
        scratch_shapes=[pltpu.VMEM((HEADS_DEV, rows, width), BF16)] * 2
        + query_buffers(6, q_all)
        + buffers(g_blocks, width),
        compiler_params=pltpu.CompilerParams(vmem_limit_bytes=VMEM_LIMIT),
        cost_estimate=cost(rows, g_blocks, 2048),
        name="key_near",
    )(order, kv_own, tag, q_all, *g_blocks)


def key_far(order, kv_own, tag, diagonal, state, q_all, g_blocks):
    rows, width = kv_own.shape[0], g_blocks[0].shape[2]
    return pl.pallas_call(
        key_far_kernel,
        out_shape=jax.ShapeDtypeStruct(diagonal.shape, BF16),
        in_specs=smem_spec() + vmem_specs(5) + any_specs(3),
        out_specs=vmem_specs(1)[0],
        scratch_shapes=[pltpu.VMEM((HEADS_DEV, rows, width), BF16)] * 2
        + [pltpu.VMEM((HEADS_DEV, rows, width), F32)] * 2
        + query_buffers(2, q_all)
        + buffers(g_blocks, width),
        compiler_params=pltpu.CompilerParams(vmem_limit_bytes=VMEM_LIMIT),
        cost_estimate=cost(rows, g_blocks, 2048),
        name="key_far",
    )(order, kv_own, tag, diagonal, *state, q_all, *g_blocks)


def dot(a, b):
    return jnp.dot(a, b, preferred_element_type=F32)


def dot_nt(a, b):
    return lax.dot_general(a, b, NT, preferred_element_type=F32)


def dot_tn(a, b):
    return lax.dot_general(a, b, (((0,), (0,)), ((), ())), preferred_element_type=F32)


def core_half(x, axis, at):
    size = x.shape[axis] // 2
    return lax.dynamic_slice_in_dim(x, at * size, size, axis)


def interleaved(k, v):
    shape = (*k.shape[:-1], -1, HEAD_DIM)
    return jnp.stack([k.reshape(shape), v.reshape(shape)], axis=-2).reshape(*k.shape[:-1], -1)


def per_device(
    hidden,
    w_qkv,
    w_out,
    b_qv,
    w_up,
    w_down,
    b_up,
    norm_gains,
    norm_shifts,
    segments,
    lengths,
    cotangent,
):
    core = lax.axis_index("core")
    heads_at = lax.axis_index("heads")
    own_ctx = ((lax.axis_index("z") * 4 + lax.axis_index("y")) * 2 + lax.axis_index("xh")) * 2 + core
    tok = hidden.shape[0]
    rows = w_up.shape[0]
    feat = HEADS_DEV * HEAD_DIM
    hidden_units = w_up.shape[1] // 2

    hid = chip_tokens(hidden)
    out_turned, down_turned = w_out.T, w_down.T
    low_tok = segments.astype(BF16).reshape(2, tok // 2)
    kv_cols = 2 * feat

    def halves(x):
        return jnp.swapaxes(x.reshape(rows, 2, -1), 0, 1)

    q_half, k_half, v_half = (halves(w_qkv[i]) for i in range(3))
    tail = jnp.broadcast_to(jnp.pad(low_tok, ((0, rows - 2), (0, 0))), (2, rows, tok // 2))
    urgent = jnp.concatenate([interleaved(k_half, v_half), q_half, tail], axis=2)
    urgent = jnp.pad(urgent, ((0, 0), (0, 16 - rows), (0, 0)))
    urgent = jnp.broadcast_to(urgent[None], (32, *urgent.shape)).reshape(64, 16, -1)
    urgent, *later = lax.optimization_barrier((urgent, out_turned, w_up, down_turned))
    later = jnp.concatenate([halves(w) for w in later], axis=2)
    mine = lax.dynamic_index_in_dim(later, core, 0, keepdims=False)
    theirs = shifted(lax.dynamic_index_in_dim(later, 1 - core, 0, keepdims=False), "core", 1)
    later = pair_ordered(mine, theirs, "core").reshape(2 * rows, -1)
    rest = lax.all_gather(later, CHIPS, axis=0, tiled=True)
    w_urgent = lax.all_to_all(urgent, CTX, 0, 0, tiled=True)
    seg_all = w_urgent[:, :2, kv_cols + feat :].reshape(-1, tok).astype(jnp.int32)
    w_urgent = w_urgent.reshape(64 * 16, -1)
    at_wide = jnp.arange(64 * 16, dtype=jnp.int32)
    at_feature = jnp.arange(64 * rows, dtype=jnp.int32)
    spread = (
        (at_feature // rows * 16 + at_feature % rows)[:, None] == at_wide[None, :]
    ).astype(BF16)
    hid_wide = dot(hid, spread).astype(BF16)
    at_bias = jnp.arange(hidden_units, dtype=jnp.int32)
    at_half = jnp.arange(feat, dtype=jnp.int32)
    at_kv = jnp.arange(kv_cols, dtype=jnp.int32)

    def placed(owner, row):
        return ((owner * 16 + row)[:, None] == at_wide[None, :]).astype(BF16)

    first_owner = 32 * core
    bias_place = placed(first_owner + at_bias // 24, at_bias % 12)
    q_place = placed(first_owner + at_half // 6, at_half % 6)
    at_value = at_kv // 128 * HEAD_DIM + at_kv % 128 - HEAD_DIM
    is_value = at_kv % 128 >= HEAD_DIM
    v_place = placed(jnp.where(is_value, first_owner + at_value // 6, -1), at_value % 6)
    parts = jnp.arange(2, dtype=jnp.int32)[:, None] == (at_bias % 24 // 12)[None, :]
    hid_wide, q_place, v_place, bias_place = lax.optimization_barrier(
        (hid_wide, q_place, v_place, bias_place)
    )

    w_out_t = rest[:, :feat]
    w_up_all = rest[:, feat : feat + hidden_units]
    w_down_t = rest[:, feat + hidden_units :]

    bias = b_qv.astype(F32)
    q_bias, v_bias = core_half(bias[0], 0, core), core_half(bias[1], 0, core)
    no_bias = jnp.zeros((tok // 2,), F32)
    bias_row = jnp.concatenate([interleaved(jnp.zeros_like(v_bias), v_bias), q_bias, no_bias])
    column = jnp.arange(bias_row.shape[0], dtype=jnp.int32)
    scale_row = jnp.where(
        column < kv_cols, 1.0, jnp.where(column < kv_cols + feat, HEAD_DIM ** (-0.5), 0.0)
    ).astype(F32)
    kv_own, q_wide, q_heads = project(hid_wide, w_urgent, bias_row[None], scale_row[None])
    q_all = lax.all_gather(q_wide, CHIPS, axis=0, tiled=True).reshape(64, tok, -1)
    starts = [jnp.sum((seg_all < s).astype(jnp.int32)) for s in range(3)]
    places = jnp.arange(seg_all.size, dtype=jnp.int32).reshape(seg_all.shape)
    run_end = jnp.zeros_like(seg_all)
    for s in range(3):
        run_end = jnp.where(seg_all == s, starts[s] + lengths[s], run_end)
    tag_all = jnp.where(places < run_end, seg_all, -1).astype(F32)
    order = jnp.concatenate([relative_order("z", "y", 0), relative_order("y", "z", 1)])
    q_order = jnp.where(core == 0, order, order + 1 - 2 * (order % 2))
    tags = jnp.take(tag_all, order, axis=0).reshape(8, -1)
    both = jnp.stack([own_ctx, own_ctx + 1 - 2 * core])
    tag_own = jnp.take(tag_all, both, axis=0).reshape(-1, 1)
    seg_own = jnp.take(seg_all, both, axis=0).astype(F32).reshape(-1, 1)

    sent_z, sent_y = lax.optimization_barrier(gather_first(kv_own))
    blocks = gather_second(sent_z, sent_y)
    near, far = near_blocks(blocks), far_blocks(blocks)
    state = attend_near(q_heads, kv_own, tags, seg_own, tag_own, near)
    attended, stat = attend_far(q_heads, tags, seg_own, state, far)
    attended_low = attended.astype(BF16)

    gain_rows = norm_gains.astype(F32)
    shifts = norm_shifts.astype(F32)
    attn_mixed, _ = team_sum(dot_nt(attended_low, w_out_t))
    first_out, normed_one, inverse_one = layer_norm(
        hidden.astype(F32) + attn_mixed + shifts[0], gain_rows[0], shifts[1]
    )
    first_low = chip_tokens(first_out.astype(BF16))
    up_bias = core_half(b_up, 0, core).astype(F32)
    up_proj = dot(first_low, w_up_all) + up_bias
    activated = exact_gelu(up_proj).astype(BF16)
    second, _ = team_sum(dot_nt(activated, w_down_t))
    output, normed_two, inverse_two = layer_norm(
        first_out + second + shifts[2], gain_rows[1], shifts[3]
    )
    resid_two = norm_back(
        cotangent.astype(F32), normed_two, inverse_two, gain_rows[1]
    )
    branch_low = chip_tokens(resid_two.astype(BF16))
    act_grad = dot(branch_low, w_down_t)
    up_low = jax.vjp(exact_gelu, up_proj)[1](act_grad)[0].astype(BF16)
    made = early_grads(spread, branch_low, activated, first_low, up_low)
    first_sum, made = team_sum(dot_nt(up_low, w_up_all), made)
    first_grad = resid_two + first_sum
    resid_one = norm_back(first_grad, normed_one, inverse_one, gain_rows[0])
    mixed_low = chip_tokens(resid_one.astype(BF16))
    g_sent, g_heads, delta = grad_rows(mixed_low, w_out_t, attended, stat, seg_own)
    (g_z, g_y), g_heads = lax.optimization_barrier((gather_first(g_sent), g_heads))
    g_near = ring_near(g_z, "y") + ring_near(g_y, "z")
    dq, diagonal = query_back(
        q_heads, g_heads, kv_own, tags, seg_own, tag_own, stat, delta, near + far
    )
    g_near, g_z, g_y, made, dq, spread = lax.optimization_barrier(
        (g_near, g_z, g_y, made, dq, spread)
    )
    g_far = [paired(shifted(g_z, "y", 2)), paired(shifted(g_y, "z", 2))]
    early = to_owners(made)
    out_placed = out_rows(spread, mixed_low, attended_low)
    rows_made = vector_rows(
        spread,
        cotangent,
        normed_two,
        resid_two,
        first_grad,
        normed_one,
        resid_one,
        up_low,
        spread,
        bias_place,
        parts.astype(F32),
    )

    key_state = key_near(q_order, kv_own, tag_own, q_all, g_near)
    dkv = key_far(q_order, kv_own, tag_own, diagonal, key_state, q_all, g_far)
    late, back = late_grads(
        hid_wide, dkv, dq, rows_made, q_place, v_place, out_placed, w_urgent, spread
    )
    late, early = lax.optimization_barrier((late, early))
    late = to_owners(late)
    hidden_grad = resid_one + team_sum(back.astype(F32))[0]

    early_sums, late_sums = owner_sums(early), owner_sums(late)

    def columns(x, start, size):
        return jnp.concatenate([x[c, :rows, start : start + size] for c in range(2)], axis=1)

    kv_pairs = columns(late_sums, 0, kv_cols).reshape(rows, 2 * HEADS_DEV, 2, HEAD_DIM)
    k_cols = kv_pairs[:, :, 0].reshape(rows, -1)
    v_cols = kv_pairs[:, :, 1].reshape(rows, -1)
    q_cols = columns(late_sums, kv_cols, feat)

    def last(x, size):
        return jnp.concatenate(
            [x[:, rows:, g * size : (g + 1) * size] for g in range(3)], axis=1
        )

    quarter = hidden_units // 2
    up_cols = columns(early_sums, 0, hidden_units)
    down_first, down_last = early_sums[:, :rows, hidden_units:], last(early_sums, quarter)
    down_cols = jnp.concatenate(
        [down_first[0], down_last[0], down_first[1], down_last[1]], axis=1
    )
    out_last = last(late_sums, feat)
    out_cols = jnp.concatenate([out_last[0], out_last[1]], axis=1)
    small = (late_sums[0] + late_sums[1])[:rows, kv_cols + feat :].T
    vec_out = small[:6].reshape(6, 2, 6)
    bias_out = small[6:8].reshape(-1)
    qv_out = small[8:10, :6]
    vec_out = lax.dynamic_index_in_dim(vec_out, heads_at, 1, keepdims=False)
    return (
        output.astype(BF16),
        hidden_grad,
        jnp.stack([q_cols, k_cols, v_cols]),
        out_cols.T,
        qv_out,
        up_cols,
        down_cols.T,
        bias_out,
        vec_out[:2],
        vec_out[2:],
    )


def solution(mesh):
    fine = Mesh(mesh.devices.reshape(4, 4, 2, 2, 2), ("z", "y", "xh", "core", "heads"))
    return jax.shard_map(
        per_device,
        mesh=fine,
        in_specs=(
            P(CTX, None),
            P(None, CTX, "heads"),
            P("heads", CTX),
            P(None, "heads"),
            P(CTX, "heads"),
            P("heads", CTX),
            P("heads"),
            P(),
            P(),
            P(CTX),
            P(),
            P(CTX, None),
        ),
        out_specs=(
            P(CTX, None),
            P(CTX, None),
            P(None, CTX, "heads"),
            P("heads", CTX),
            P(None, ("heads", *CTX)),
            P(CTX, "heads"),
            P("heads", CTX),
            P(("heads", *CTX)),
            P(None, (*CTX, "heads")),
            P(None, (*CTX, "heads")),
        ),
        check_vma=False,
    )
```

```python
import jax
import jax.numpy as jnp
from jax import lax
from jax.experimental import pallas as pl
from jax.experimental.pallas import tpu as pltpu
from jax.sharding import Mesh, PartitionSpec as P

HEAD_DIM = 64
HEADS_DEV = 3
EPS = 1e-06
NEG = -1e30
CTX = ("z", "y", "xh", "core")
CHIPS = ("z", "y", "xh")
F32 = jnp.float32
BF16 = jnp.bfloat16
NT = (((1,), (1,)), ((), ()))
VMEM_LIMIT = 50 * 1024 * 1024
OFFSETS = (0, -1, 1, 2)


def shifted(x, axis, step):
    n = lax.axis_size(axis)
    return lax.ppermute(x, axis, [(i, (i + step) % n) for i in range(n)])


def ring_halves(x, axis):
    half = x.shape[0] // 2
    before, after = shifted(x, axis, 1), shifted(x, axis, -1)
    return [x, before, after, shifted(before[:half], axis, 1), shifted(after[half:], axis, -1)]


def ring_near(x, axis):
    return [paired(b) for b in (x, shifted(x, axis, 1), shifted(x, axis, -1))]


def paired(x):
    return x.reshape(2, x.shape[0] // 2, x.shape[1])


def gather_first(x):
    half = x.shape[0] // 2
    streams = []
    for part, axis in ((x[:half], "z"), (x[half:], "y")):
        both = jnp.concatenate([part, shifted(part, "xh", 1)], axis=0)
        streams.append(jnp.concatenate(ring_halves(both, axis), axis=0))
    return tuple(streams)


def gather_second(z_stream, y_stream):
    blocks = ring_halves(z_stream, "y") + ring_halves(y_stream, "z")
    return [b.reshape(-1, z_stream.shape[0] // 2, b.shape[1]) for b in blocks]


def near_blocks(blocks):
    return blocks[:3] + blocks[5:8]


def far_blocks(blocks):
    return blocks[3:5] + blocks[8:]


def relative_order(first, second, core_at):
    place = {a: lax.axis_index(a) for a in CHIPS}
    core = lax.axis_index("core")
    order = []
    for second_step in OFFSETS:
        for first_step in OFFSETS:
            for xh_step in (0, 1):
                at = dict(place)
                at[first] = (at[first] + first_step) % 4
                at[second] = (at[second] + second_step) % 4
                at["xh"] = (at["xh"] + xh_step) % 2
                order.append(((at["z"] * 4 + at["y"]) * 2 + at["xh"]) * 2 + (core + core_at) % 2)
    return jnp.stack(order)


def pair_ordered(own, other, axis):
    first = lax.axis_index(axis) == 0
    return jnp.stack([jnp.where(first, own, other), jnp.where(first, other, own)])


def to_owners(x):
    return lax.all_to_all(x.reshape(64, 16, -1), CTX, 0, 0, tiled=True)


def owner_sums(parts):
    return jnp.sum(parts.reshape(-1, 2, *parts.shape[1:]).astype(F32), axis=0)


def team_sum(partial, beside=()):
    rows = partial.shape[0] // 2
    near = partial[:rows] + shifted(partial[rows:].astype(BF16), "core", 1).astype(F32)
    low = lax.optimization_barrier(near.astype(BF16))
    got, beside = lax.optimization_barrier((shifted(low, "heads", 1), beside))
    return low.astype(F32) + got.astype(F32), beside


def chip_tokens(x):
    return jnp.concatenate([x, shifted(x, "core", 1)], axis=0)


def layer_norm(residual, gain_row, shift_row):
    centred = residual - jnp.mean(residual, axis=-1, keepdims=True)
    inverse = lax.rsqrt(jnp.mean(centred * centred, axis=-1, keepdims=True) + EPS)
    normed = centred * inverse
    return (normed * gain_row + shift_row, normed, inverse)


def norm_back(incoming, normed, inverse, gain_row):
    scaled = incoming * gain_row
    projected = (
        scaled
        - jnp.mean(scaled, axis=-1, keepdims=True)
        - normed * jnp.mean(scaled * normed, axis=-1, keepdims=True)
    )
    return inverse * projected


def exact_gelu(pre_act):
    return jax.nn.gelu(pre_act, approximate=False)


def pieces_of(column):
    high = column.astype(BF16).astype(F32)
    middle = (column - high).astype(BF16).astype(F32)
    return high, middle, column - high - middle


def head_columns(h):
    return slice(h * HEAD_DIM, (h + 1) * HEAD_DIM)


def head_block(h):
    return slice(h * 128, (h + 1) * 128)


def diagonal_scores(q_ref, kv_ref, h):
    product = q_ref[h].astype(F32) * kv_ref[:, head_block(h)].astype(F32)
    return jnp.sum(product, axis=1, keepdims=True)


def copies_in(sources, buffer, sems):
    at = 0
    for source in sources:
        size = source.shape[0]
        pltpu.make_async_copy(source, buffer.at[pl.ds(at, size)], sems.at[at // 2]).start()
        at += size


def block_of(buffer, sems, j):
    block = buffer.at[pl.ds(2 * j, 2)]
    pltpu.make_async_copy(block, block, sems.at[j]).wait()
    return buffer[pl.ds(2 * j, 2)].reshape(-1, buffer.shape[2])


def attend_blocks(q_ref, tags_ref, seg_ref, top, total, acc, buffer, sems, row_of):
    rows = q_ref.shape[1]
    seg_wide = jnp.broadcast_to(seg_ref[...], (rows, 128))

    def step(j, carry):
        whole = block_of(buffer, sems, j)
        tags = tags_ref[pl.ds(row_of(j), 1), :]
        keys = tags.shape[1]
        allowed = jnp.tile(seg_wide, (1, keys // 128)) == tags
        for h in range(HEADS_DEV):
            kv = whole[:, head_block(h)]
            scores = lax.dot_general(q_ref[h], kv, NT, preferred_element_type=F32)
            scores = jnp.where(allowed, scores, NEG)
            before = top[h]
            now = jnp.maximum(before, jnp.max(scores, axis=1, keepdims=True))
            weights = jnp.exp(scores - jnp.tile(now, (1, keys // 128)))
            fade = jnp.exp(before - now)
            sums = weights[:, :128]
            for k in range(1, keys // 128):
                sums = sums + weights[:, k * 128 : (k + 1) * 128]
            total[h] = total[h] * fade + sums
            acc[h] = acc[h] * fade + jnp.dot(weights.astype(BF16), kv, preferred_element_type=F32)
            top[h] = now
        return carry

    lax.fori_loop(0, sems.shape[0], step, 0)


def near_row(j):
    return j + (j >= 3).astype(jnp.int32)


def far_row(j):
    return 4 * j + 3


def attend_near_kernel(q_ref, own_ref, tags_ref, seg_ref, tag_ref, *rest):
    blocks, (top, total, acc, buffer, sems) = rest[:6], rest[6:]
    copies_in(blocks, buffer, sems)
    rows = q_ref.shape[1]
    padded = tag_ref[...] < 0
    for h in range(HEADS_DEV):
        diagonal = diagonal_scores(q_ref, own_ref, h)
        top[h] = jnp.broadcast_to(jnp.where(padded, diagonal, NEG), (rows, 128))
        lane = lax.broadcasted_iota(jnp.int32, (rows, 128), 1)
        total[h] = jnp.where((lane == 0) & padded, 1.0, 0.0)
        acc[h] = jnp.where(padded, own_ref[:, head_block(h)].astype(F32), 0.0)
    attend_blocks(q_ref, tags_ref, seg_ref, top, total, acc, buffer, sems, near_row)


def attend_far_kernel(q_ref, tags_ref, seg_ref, top_in, total_in, acc_in, *rest):
    blocks, (out_ref, stat_ref, top, total, acc, buffer, sems) = rest[:4], rest[4:]
    copies_in(blocks, buffer, sems)
    top[...], total[...], acc[...] = top_in[...], total_in[...], acc_in[...]
    attend_blocks(q_ref, tags_ref, seg_ref, top, total, acc, buffer, sems, far_row)
    outs = []
    for h in range(HEADS_DEV):
        sums = jnp.sum(total[h], axis=1, keepdims=True)
        outs.append((acc[h] / sums)[:, HEAD_DIM:])
        stat_ref[h] = top[h] + jnp.log(sums)
    out_ref[...] = jnp.concatenate(outs, axis=1)


def vmem_specs(n):
    return [pl.BlockSpec(memory_space=pltpu.VMEM)] * n


def any_specs(n):
    return [pl.BlockSpec(memory_space=pl.ANY)] * n


def head_state(rows, lanes=128):
    return jax.ShapeDtypeStruct((HEADS_DEV, rows, lanes), F32)


def cost(rows, blocks, flops):
    keys = sum(b.shape[0] * b.shape[1] for b in blocks)
    pairs = rows * keys * HEADS_DEV
    return pl.CostEstimate(
        flops=pairs * flops, bytes_accessed=keys * 1024, transcendentals=pairs
    )


def buffers(blocks, lanes):
    count = sum(b.shape[0] for b in blocks)
    return [
        pltpu.VMEM((count, blocks[0].shape[1], lanes), BF16),
        pltpu.SemaphoreType.DMA((count // 2,)),
    ]


def attend_near(q_heads, kv_own, tags, seg, tag, blocks):
    rows = kv_own.shape[0]
    return pl.pallas_call(
        attend_near_kernel,
        out_shape=(head_state(rows),) * 3,
        in_specs=vmem_specs(5) + any_specs(6),
        out_specs=tuple(vmem_specs(3)),
        scratch_shapes=buffers(blocks, kv_own.shape[1]),
        compiler_params=pltpu.CompilerParams(vmem_limit_bytes=VMEM_LIMIT),
        cost_estimate=cost(rows, blocks, 512),
        name="attend_near",
    )(q_heads, kv_own, tags, seg, tag, *blocks)


def attend_far(q_heads, tags, seg, state, blocks):
    rows = q_heads.shape[1]
    return pl.pallas_call(
        attend_far_kernel,
        out_shape=(jax.ShapeDtypeStruct((rows, HEADS_DEV * HEAD_DIM), F32), head_state(rows)),
        in_specs=vmem_specs(6) + any_specs(4),
        out_specs=tuple(vmem_specs(2)),
        scratch_shapes=[pltpu.VMEM((HEADS_DEV, rows, 128), F32)] * 3
        + buffers(blocks, HEADS_DEV * 128),
        compiler_params=pltpu.CompilerParams(vmem_limit_bytes=VMEM_LIMIT),
        cost_estimate=cost(rows, blocks, 512),
        name="attend_far",
    )(q_heads, tags, seg, *state, *blocks)


def query_back_kernel(q_ref, g_ref, own_ref, tags_ref, seg_ref, tag_ref, stat_ref, delta_ref, *rest):
    blocks, (dq_ref, dkv_ref, buffer, sems, acc) = rest[:10], rest[10:]
    copies_in(blocks, buffer, sems)
    rows = q_ref.shape[1]
    seg_wide = jnp.broadcast_to(seg_ref[...], (rows, 128))
    padded = tag_ref[...] < 0
    for h in range(HEADS_DEV):
        own = own_ref[:, head_block(h)].astype(F32)
        prob = jnp.exp(diagonal_scores(q_ref, own_ref, h) - stat_ref[h][:, :1])
        prob = jnp.where(padded, prob, 0.0)
        grad = diagonal_scores(g_ref, own_ref, h) - delta_ref[h][:, :1]
        score = (prob * grad).astype(BF16).astype(F32)
        acc[h] = score * own
        dkv_ref[:, head_block(h)] = score * q_ref[h].astype(F32) + prob.astype(BF16).astype(
            F32
        ) * g_ref[h].astype(F32)

    def step(j, carry):
        whole = block_of(buffer, sems, j)
        tags = tags_ref[pl.ds(jnp.where(j < 6, near_row(j), far_row(j - 6)), 1), :]
        keys = tags.shape[1]
        allowed = jnp.tile(seg_wide, (1, keys // 128)) == tags
        for h in range(HEADS_DEV):
            kv = whole[:, head_block(h)]
            scores = lax.dot_general(q_ref[h], kv, NT, preferred_element_type=F32)
            scores = jnp.where(allowed, scores, NEG)
            probs = jnp.exp(scores - jnp.tile(stat_ref[h], (1, keys // 128)))
            grads = lax.dot_general(g_ref[h], kv, NT, preferred_element_type=F32)
            back = probs * (grads - jnp.tile(delta_ref[h], (1, keys // 128)))
            acc[h] = acc[h] + jnp.dot(back.astype(BF16), kv, preferred_element_type=F32)
        return carry

    lax.fori_loop(0, 8, step, 0)
    dq_ref[...] = (
        jnp.concatenate([acc[h][:, :HEAD_DIM] for h in range(HEADS_DEV)], axis=1)
        * HEAD_DIM ** (-0.5)
    ).astype(BF16)


def query_back(q_heads, g_heads, kv_own, tags, seg, tag, stat, delta, blocks):
    rows = kv_own.shape[0]
    return pl.pallas_call(
        query_back_kernel,
        out_shape=(
            jax.ShapeDtypeStruct((rows, HEADS_DEV * HEAD_DIM), BF16),
            jax.ShapeDtypeStruct(kv_own.shape, F32),
        ),
        in_specs=vmem_specs(8) + any_specs(10),
        out_specs=tuple(vmem_specs(2)),
        scratch_shapes=buffers(blocks, kv_own.shape[1]) + [pltpu.VMEM((HEADS_DEV, rows, 128), F32)],
        compiler_params=pltpu.CompilerParams(vmem_limit_bytes=VMEM_LIMIT),
        cost_estimate=cost(rows, blocks, 768),
        name="query_back",
    )(q_heads, g_heads, kv_own, tags, seg, tag, stat, delta, *blocks)


def grad_rows_kernel(
    mixed_ref, out_ref, attended_ref, stat_ref, seg_ref, sent_ref, g_ref, delta_ref
):
    rows = mixed_ref.shape[0]
    grad = jnp.dot(mixed_ref[...], out_ref[...], preferred_element_type=F32).astype(BF16)
    grad = grad.astype(F32)
    product = grad * attended_ref[...]
    lane = lax.broadcasted_iota(jnp.int32, (rows, HEAD_DIM), 1)
    seg = seg_ref[...]
    extra = jnp.where(lane == 21, 1.0, 0.0)
    for s in range(3):
        extra = extra + jnp.where((lane == 18 + s) & (seg != s), 1.0, 0.0)
    zeros = jnp.zeros((rows, HEAD_DIM), BF16)
    for h in range(HEADS_DEV):
        delta = jnp.sum(product[:, head_columns(h)], axis=1, keepdims=True)
        delta_ref[h] = jnp.broadcast_to(delta, (rows, 128))
        for i, piece in enumerate(pieces_of(delta)):
            extra = extra + jnp.where(lane == 3 * h + i, piece, 0.0)
        for i, piece in enumerate(pieces_of(stat_ref[h][:, :1])):
            extra = extra + jnp.where(lane == 9 + 3 * h + i, piece, 0.0)
        g_ref[h] = jnp.concatenate([zeros, grad[:, head_columns(h)].astype(BF16)], axis=1)
    sent_ref[...] = jnp.concatenate([grad, extra], axis=1).astype(BF16)


def grad_rows(mixed, w_out, attended, stat, seg):
    rows = mixed.shape[0]
    return pl.pallas_call(
        grad_rows_kernel,
        out_shape=(
            jax.ShapeDtypeStruct((rows, 256), BF16),
            jax.ShapeDtypeStruct((HEADS_DEV, rows, 128), BF16),
            jax.ShapeDtypeStruct((HEADS_DEV, rows, 128), F32),
        ),
        in_specs=vmem_specs(5),
        out_specs=tuple(vmem_specs(3)),
        compiler_params=pltpu.CompilerParams(vmem_limit_bytes=VMEM_LIMIT),
        name="grad_rows",
    )(mixed, w_out, attended, stat, seg)


def send_out(held, out_ref, sem):
    copy = pltpu.make_async_copy(held, out_ref, sem)
    copy.start()
    copy.wait()


def last_rows(x, group):
    parts = x.reshape(64, 16, x.shape[1])[:, 4 * group : 4 * group + 4]
    return jnp.concatenate([jnp.zeros((64, 12, x.shape[1]), F32), parts], axis=1).reshape(x.shape)


def early_grads_kernel(spread_ref, branch_ref, activated_ref, first_ref, up_ref, out_ref, held, sem):
    quarter = held.shape[1] // 3
    made = []
    for left, right in ((first_ref, up_ref), (branch_ref, activated_ref)):
        wide = jnp.dot(left[...], spread_ref[...], preferred_element_type=F32).astype(BF16)
        for half in range(2):
            made.append(dot_tn(wide, right[:, half * quarter : (half + 1) * quarter]))
    for g in range(3):
        held[:, g * quarter : (g + 1) * quarter] = (made[g] + last_rows(made[3], g)).astype(BF16)
    send_out(held, out_ref, sem)


def early_grads(spread, branch, activated, first, up):
    shape = (spread.shape[1], up.shape[1] * 3 // 2)
    return pl.pallas_call(
        early_grads_kernel,
        out_shape=jax.ShapeDtypeStruct(shape, BF16),
        in_specs=vmem_specs(5),
        out_specs=pl.BlockSpec(memory_space=pltpu.HBM),
        scratch_shapes=[pltpu.VMEM(shape, BF16), pltpu.SemaphoreType.DMA],
        compiler_params=pltpu.CompilerParams(vmem_limit_bytes=VMEM_LIMIT),
        name="early_grads",
    )(spread, branch, activated, first, up)


def out_rows_kernel(spread_ref, mixed_ref, attended_ref, out_ref):
    wide = jnp.dot(mixed_ref[...], spread_ref[...], preferred_element_type=F32).astype(BF16)
    made = dot_tn(wide, attended_ref[...].astype(BF16))
    out_ref[...] = jnp.concatenate([last_rows(made, g) for g in range(3)], axis=1).astype(BF16)


def out_rows(spread, mixed, attended):
    return pl.pallas_call(
        out_rows_kernel,
        out_shape=jax.ShapeDtypeStruct((spread.shape[1], 3 * attended.shape[1]), BF16),
        in_specs=vmem_specs(3),
        out_specs=vmem_specs(1)[0],
        compiler_params=pltpu.CompilerParams(vmem_limit_bytes=VMEM_LIMIT),
        name="out_rows",
    )(spread, mixed, attended)


def vector_rows_kernel(
    cot_ref, two_ref, resid_two_ref, first_ref, one_ref, resid_one_ref, up_ref, spread_ref, bias_ref,
    parts_ref, out_ref,
):
    cot, first = cot_ref[...].astype(F32), first_ref[...]
    columns = (
        first * one_ref[...],
        cot * two_ref[...],
        resid_one_ref[...],
        first,
        resid_two_ref[...],
        cot,
    )
    rows = jnp.concatenate([jnp.sum(c, axis=0, keepdims=True) for c in columns], axis=0)
    bias = jnp.sum(up_ref[...].astype(F32), axis=0, keepdims=True) * parts_ref[...]
    made = [
        jnp.dot(rows.astype(BF16), spread_ref[...], preferred_element_type=F32),
        jnp.dot(bias.astype(BF16), bias_ref[...], preferred_element_type=F32),
    ]
    out_ref[...] = jnp.concatenate(made, axis=0)


def vector_rows(spread, *args):
    return pl.pallas_call(
        vector_rows_kernel,
        out_shape=jax.ShapeDtypeStruct((8, spread.shape[1]), F32),
        in_specs=vmem_specs(10),
        out_specs=vmem_specs(1)[0],
        compiler_params=pltpu.CompilerParams(vmem_limit_bytes=VMEM_LIMIT),
        name="vector_rows",
    )(*args)


def late_grads_kernel(
    hid_ref, dkv_ref, dq_ref, rows_ref, q_place_ref, v_place_ref, placed_ref, w_ref, spread_ref,
    out_ref, back_ref, held, sem,
):
    wide = hid_ref.shape[1]
    grads = jnp.concatenate([dkv_ref[...], dq_ref[...]], axis=1)
    cols = grads.shape[1]
    made = dot_tn(hid_ref[...], grads) + placed_ref[...].astype(F32)
    sums = [rows_ref[...]]
    for grad, place in ((dq_ref, q_place_ref), (dkv_ref, v_place_ref)):
        row = jnp.sum(grad[...].astype(F32), axis=0, keepdims=True).astype(BF16)
        sums.append(jnp.dot(row, place[...], preferred_element_type=F32))
    sums.append(jnp.zeros((128 - 10, wide), F32))
    small = jnp.transpose(jnp.concatenate(sums, axis=0))[:, :64]
    held[...] = jnp.concatenate([made, small], axis=1).astype(BF16)
    copy = pltpu.make_async_copy(held, out_ref, sem)
    copy.start()
    back = dot_nt(grads, w_ref[:, :cols]).astype(BF16)
    back_ref[...] = dot_nt(back, spread_ref[...]).astype(BF16)
    copy.wait()


def late_grads(hid, dkv, dq, rows, q_place, v_place, placed, w, spread):
    shape = (hid.shape[1], dkv.shape[1] + dq.shape[1] + 64)
    return pl.pallas_call(
        late_grads_kernel,
        out_shape=(
            jax.ShapeDtypeStruct(shape, BF16),
            jax.ShapeDtypeStruct((hid.shape[0], spread.shape[0]), BF16),
        ),
        in_specs=vmem_specs(9),
        out_specs=(pl.BlockSpec(memory_space=pltpu.HBM), vmem_specs(1)[0]),
        scratch_shapes=[pltpu.VMEM(shape, BF16), pltpu.SemaphoreType.DMA],
        compiler_params=pltpu.CompilerParams(vmem_limit_bytes=VMEM_LIMIT),
        name="late_grads",
    )(hid, dkv, dq, rows, q_place, v_place, placed, w, spread)


def project_kernel(hid_ref, w_ref, bias_ref, scale_ref, kv_ref, wide_ref, q_ref):
    made = jnp.dot(hid_ref[...], w_ref[...], preferred_element_type=F32) + bias_ref[...]
    made = (made.astype(BF16).astype(F32) * scale_ref[...]).astype(BF16)
    kv_cols = kv_ref.shape[1]
    kv_ref[...] = made[:, :kv_cols]
    wide_ref[...] = made[:, kv_cols:]
    zeros = jnp.zeros((made.shape[0], HEAD_DIM), BF16)
    for h in range(HEADS_DEV):
        at = kv_cols + h * HEAD_DIM
        q_ref[h] = jnp.concatenate([made[:, at : at + HEAD_DIM], zeros], axis=1)


def project(hid, w, bias, scale):
    rows = hid.shape[0]
    return pl.pallas_call(
        project_kernel,
        out_shape=(
            jax.ShapeDtypeStruct((rows, HEADS_DEV * 128), BF16),
            jax.ShapeDtypeStruct((rows, w.shape[1] - HEADS_DEV * 128), BF16),
            jax.ShapeDtypeStruct((HEADS_DEV, rows, 128), BF16),
        ),
        in_specs=vmem_specs(4),
        out_specs=tuple(vmem_specs(3)),
        compiler_params=pltpu.CompilerParams(vmem_limit_bytes=VMEM_LIMIT),
        name="project",
    )(hid, w, bias, scale)


def queries_in(order_ref, q_ref, q_buffer, q_sems):
    for i in range(64):
        source = q_ref.at[order_ref[i]]
        pltpu.make_async_copy(source, q_buffer.at[i], q_sems.at[i // 8]).start()


def key_back_blocks(k_ref, v_ref, k_acc, v_acc, q_buffer, g_buffer, q_sems, g_sems):
    def step(j, carry):
        eight = q_buffer.at[pl.ds(8 * j, 8)]
        pltpu.make_async_copy(eight, eight, q_sems.at[j]).wait()
        queries = q_buffer[pl.ds(8 * j, 8)].reshape(-1, q_buffer.shape[2])
        grads = block_of(g_buffer, g_sems, j)
        lane = lax.broadcasted_iota(jnp.int32, queries.shape, 1)
        queries = jnp.where(lane < HEADS_DEV * HEAD_DIM, queries, grads)
        for h in range(HEADS_DEV):
            scores = lax.dot_general(k_ref[h], queries, NT, preferred_element_type=F32)
            probs = jnp.exp(scores)
            v_acc[h] = v_acc[h] + jnp.dot(probs.astype(BF16), grads, preferred_element_type=F32)
            back = probs * lax.dot_general(v_ref[h], grads, NT, preferred_element_type=F32)
            k_acc[h] = k_acc[h] + jnp.dot(back.astype(BF16), queries, preferred_element_type=F32)
        return carry

    lax.fori_loop(0, q_sems.shape[0], step, 0)


def key_heads(kv_ref, tag_ref, k_heads, v_heads):
    rows = kv_ref.shape[0]
    feat = HEADS_DEV * HEAD_DIM
    lane = lax.broadcasted_iota(jnp.int32, (rows, HEAD_DIM), 1)
    tag = tag_ref[...]
    masks = jnp.where((lane == 21) & (tag < 0), NEG, 0.0)
    for s in range(3):
        masks = masks + jnp.where((lane == 18 + s) & (tag == s), NEG, 0.0)
    for h in range(HEADS_DEV):
        block = kv_ref[:, head_block(h)].astype(F32)
        before = [jnp.zeros((rows, h * HEAD_DIM), F32)] if h else []
        left = feat - (h + 1) * HEAD_DIM
        after = [jnp.zeros((rows, left), F32)] if left else []
        k_extra = masks - jnp.where((lane >= 9 + 3 * h) & (lane < 12 + 3 * h), 1.0, 0.0)
        v_extra = -jnp.where((lane >= 3 * h) & (lane < 3 * h + 3), 1.0, 0.0)
        for heads, part, extra in (
            (k_heads, block[:, :HEAD_DIM], k_extra),
            (v_heads, block[:, HEAD_DIM:], v_extra),
        ):
            heads[h] = jnp.concatenate(before + [part] + after + [extra], axis=1).astype(BF16)


def key_back_kernel(order_ref, kv_ref, tag_ref, diag_ref, q_ref, *rest):
    g_blocks = rest[:8]
    dkv_ref, k_heads, v_heads, k_acc, v_acc, q_buffer, q_sems, g_buffer, g_sems = rest[8:]
    queries_in(order_ref, q_ref, q_buffer, q_sems)
    copies_in(g_blocks, g_buffer, g_sems)
    key_heads(kv_ref, tag_ref, k_heads, v_heads)
    k_acc[...] = jnp.zeros_like(k_acc)
    v_acc[...] = jnp.zeros_like(v_acc)
    key_back_blocks(k_heads, v_heads, k_acc, v_acc, q_buffer, g_buffer, q_sems, g_sems)
    parts = []
    for h in range(HEADS_DEV):
        parts += [k_acc[h][:, head_columns(h)], v_acc[h][:, head_columns(h)]]
    dkv_ref[...] = (jnp.concatenate(parts, axis=1) + diag_ref[...]).astype(BF16)


def query_buffers(q_all):
    return [pltpu.VMEM(q_all.shape, BF16), pltpu.SemaphoreType.DMA((8,))]


def smem_spec():
    return [pl.BlockSpec(memory_space=pltpu.SMEM)]


def key_back(order, kv_own, tag, diagonal, q_all, g_blocks):
    rows, width = kv_own.shape[0], g_blocks[0].shape[2]
    return pl.pallas_call(
        key_back_kernel,
        out_shape=jax.ShapeDtypeStruct(diagonal.shape, BF16),
        in_specs=smem_spec() + vmem_specs(3) + any_specs(9),
        out_specs=vmem_specs(1)[0],
        scratch_shapes=[pltpu.VMEM((HEADS_DEV, rows, width), BF16)] * 2
        + [pltpu.VMEM((HEADS_DEV, rows, width), F32)] * 2
        + query_buffers(q_all)
        + buffers(g_blocks, width),
        compiler_params=pltpu.CompilerParams(vmem_limit_bytes=VMEM_LIMIT),
        cost_estimate=cost(rows, g_blocks, 2048),
        name="key_back",
    )(order, kv_own, tag, diagonal, q_all, *g_blocks)


def dot(a, b):
    return jnp.dot(a, b, preferred_element_type=F32)


def dot_nt(a, b):
    return lax.dot_general(a, b, NT, preferred_element_type=F32)


def dot_tn(a, b):
    return lax.dot_general(a, b, (((0,), (0,)), ((), ())), preferred_element_type=F32)


def core_half(x, axis, at):
    size = x.shape[axis] // 2
    return lax.dynamic_slice_in_dim(x, at * size, size, axis)


def interleaved(k, v):
    shape = (*k.shape[:-1], -1, HEAD_DIM)
    return jnp.stack([k.reshape(shape), v.reshape(shape)], axis=-2).reshape(*k.shape[:-1], -1)


def per_device(
    hidden,
    w_qkv,
    w_out,
    b_qv,
    w_up,
    w_down,
    b_up,
    norm_gains,
    norm_shifts,
    segments,
    lengths,
    cotangent,
):
    core = lax.axis_index("core")
    heads_at = lax.axis_index("heads")
    own_ctx = ((lax.axis_index("z") * 4 + lax.axis_index("y")) * 2 + lax.axis_index("xh")) * 2 + core
    tok = hidden.shape[0]
    rows = w_up.shape[0]
    feat = HEADS_DEV * HEAD_DIM
    hidden_units = w_up.shape[1] // 2

    hid = chip_tokens(hidden)
    out_turned, down_turned = w_out.T, w_down.T
    low_tok = segments.astype(BF16).reshape(2, tok // 2)
    kv_cols = 2 * feat

    def halves(x):
        return jnp.swapaxes(x.reshape(rows, 2, -1), 0, 1)

    q_half, k_half, v_half = (halves(w_qkv[i]) for i in range(3))
    tail = jnp.broadcast_to(jnp.pad(low_tok, ((0, rows - 2), (0, 0))), (2, rows, tok // 2))
    urgent = jnp.concatenate([interleaved(k_half, v_half), q_half, tail], axis=2)
    urgent = jnp.pad(urgent, ((0, 0), (0, 16 - rows), (0, 0)))
    urgent = jnp.broadcast_to(urgent[None], (32, *urgent.shape)).reshape(64, 16, -1)
    urgent, *later = lax.optimization_barrier((urgent, out_turned, w_up, down_turned))
    later = jnp.concatenate([halves(w) for w in later], axis=2)
    mine = lax.dynamic_index_in_dim(later, core, 0, keepdims=False)
    theirs = shifted(lax.dynamic_index_in_dim(later, 1 - core, 0, keepdims=False), "core", 1)
    later = pair_ordered(mine, theirs, "core").reshape(2 * rows, -1)
    rest = lax.all_gather(later, CHIPS, axis=0, tiled=True)
    w_urgent = lax.all_to_all(urgent, CTX, 0, 0, tiled=True)
    seg_all = w_urgent[:, :2, kv_cols + feat :].reshape(-1, tok).astype(jnp.int32)
    w_urgent = w_urgent.reshape(64 * 16, -1)
    at_wide = jnp.arange(64 * 16, dtype=jnp.int32)
    at_feature = jnp.arange(64 * rows, dtype=jnp.int32)
    spread = (
        (at_feature // rows * 16 + at_feature % rows)[:, None] == at_wide[None, :]
    ).astype(BF16)
    hid_wide = dot(hid, spread).astype(BF16)
    at_bias = jnp.arange(hidden_units, dtype=jnp.int32)
    at_half = jnp.arange(feat, dtype=jnp.int32)
    at_kv = jnp.arange(kv_cols, dtype=jnp.int32)

    def placed(owner, row):
        return ((owner * 16 + row)[:, None] == at_wide[None, :]).astype(BF16)

    first_owner = 32 * core
    bias_place = placed(first_owner + at_bias // 24, at_bias % 12)
    q_place = placed(first_owner + at_half // 6, at_half % 6)
    at_value = at_kv // 128 * HEAD_DIM + at_kv % 128 - HEAD_DIM
    is_value = at_kv % 128 >= HEAD_DIM
    v_place = placed(jnp.where(is_value, first_owner + at_value // 6, -1), at_value % 6)
    parts = jnp.arange(2, dtype=jnp.int32)[:, None] == (at_bias % 24 // 12)[None, :]
    hid_wide, q_place, v_place, bias_place = lax.optimization_barrier(
        (hid_wide, q_place, v_place, bias_place)
    )

    w_out_t = rest[:, :feat]
    w_up_all = rest[:, feat : feat + hidden_units]
    w_down_t = rest[:, feat + hidden_units :]

    bias = b_qv.astype(F32)
    q_bias, v_bias = core_half(bias[0], 0, core), core_half(bias[1], 0, core)
    no_bias = jnp.zeros((tok // 2,), F32)
    bias_row = jnp.concatenate([interleaved(jnp.zeros_like(v_bias), v_bias), q_bias, no_bias])
    column = jnp.arange(bias_row.shape[0], dtype=jnp.int32)
    scale_row = jnp.where(
        column < kv_cols, 1.0, jnp.where(column < kv_cols + feat, HEAD_DIM ** (-0.5), 0.0)
    ).astype(F32)
    kv_own, q_wide, q_heads = project(hid_wide, w_urgent, bias_row[None], scale_row[None])
    q_all = lax.all_gather(q_wide, CHIPS, axis=0, tiled=True).reshape(64, tok, -1)
    starts = [jnp.sum((seg_all < s).astype(jnp.int32)) for s in range(3)]
    places = jnp.arange(seg_all.size, dtype=jnp.int32).reshape(seg_all.shape)
    run_end = jnp.zeros_like(seg_all)
    for s in range(3):
        run_end = jnp.where(seg_all == s, starts[s] + lengths[s], run_end)
    tag_all = jnp.where(places < run_end, seg_all, -1).astype(F32)
    order = jnp.concatenate([relative_order("z", "y", 0), relative_order("y", "z", 1)])
    q_order = jnp.where(core == 0, order, order + 1 - 2 * (order % 2))
    tags = jnp.take(tag_all, order, axis=0).reshape(8, -1)
    both = jnp.stack([own_ctx, own_ctx + 1 - 2 * core])
    tag_own = jnp.take(tag_all, both, axis=0).reshape(-1, 1)
    seg_own = jnp.take(seg_all, both, axis=0).astype(F32).reshape(-1, 1)

    sent_z, sent_y = lax.optimization_barrier(gather_first(kv_own))
    blocks = gather_second(sent_z, sent_y)
    near, far = near_blocks(blocks), far_blocks(blocks)
    state = attend_near(q_heads, kv_own, tags, seg_own, tag_own, near)
    attended, stat = attend_far(q_heads, tags, seg_own, state, far)
    attended_low = attended.astype(BF16)

    gain_rows = norm_gains.astype(F32)
    shifts = norm_shifts.astype(F32)
    attn_mixed, _ = team_sum(dot_nt(attended_low, w_out_t))
    first_out, normed_one, inverse_one = layer_norm(
        hidden.astype(F32) + attn_mixed + shifts[0], gain_rows[0], shifts[1]
    )
    first_low = chip_tokens(first_out.astype(BF16))
    up_bias = core_half(b_up, 0, core).astype(F32)
    up_proj = dot(first_low, w_up_all) + up_bias
    activated = exact_gelu(up_proj).astype(BF16)
    second, _ = team_sum(dot_nt(activated, w_down_t))
    output, normed_two, inverse_two = layer_norm(
        first_out + second + shifts[2], gain_rows[1], shifts[3]
    )
    resid_two = norm_back(
        cotangent.astype(F32), normed_two, inverse_two, gain_rows[1]
    )
    branch_low = chip_tokens(resid_two.astype(BF16))
    act_grad = dot(branch_low, w_down_t)
    up_low = jax.vjp(exact_gelu, up_proj)[1](act_grad)[0].astype(BF16)
    made = early_grads(spread, branch_low, activated, first_low, up_low)
    first_sum, made = team_sum(dot_nt(up_low, w_up_all), made)
    first_grad = resid_two + first_sum
    resid_one = norm_back(first_grad, normed_one, inverse_one, gain_rows[0])
    mixed_low = chip_tokens(resid_one.astype(BF16))
    g_sent, g_heads, delta = grad_rows(mixed_low, w_out_t, attended, stat, seg_own)
    (g_z, g_y), g_heads = lax.optimization_barrier((gather_first(g_sent), g_heads))
    g_near = ring_near(g_z, "y") + ring_near(g_y, "z")
    g_far = [paired(shifted(g_z, "y", 2)), paired(shifted(g_y, "z", 2))]
    dq, diagonal = query_back(
        q_heads, g_heads, kv_own, tags, seg_own, tag_own, stat, delta, near + far
    )
    g_near, made, dq, spread = lax.optimization_barrier((g_near, made, dq, spread))
    g_blocks = [*g_near[:3], g_far[0], *g_near[3:], g_far[1]]
    early = to_owners(made)
    out_placed = out_rows(spread, mixed_low, attended_low)
    rows_made = vector_rows(
        spread,
        cotangent,
        normed_two,
        resid_two,
        first_grad,
        normed_one,
        resid_one,
        up_low,
        spread,
        bias_place,
        parts.astype(F32),
    )

    dkv = key_back(q_order, kv_own, tag_own, diagonal, q_all, g_blocks)
    dkv, early = lax.optimization_barrier((dkv, early))
    late, back = late_grads(
        hid_wide, dkv, dq, rows_made, q_place, v_place, out_placed, w_urgent, spread
    )
    late, early = lax.optimization_barrier((late, early))
    late = to_owners(late)
    hidden_grad = resid_one + team_sum(back.astype(F32))[0]

    early_sums, late_sums = owner_sums(early), owner_sums(late)

    def columns(x, start, size):
        return jnp.concatenate([x[c, :rows, start : start + size] for c in range(2)], axis=1)

    kv_pairs = columns(late_sums, 0, kv_cols).reshape(rows, 2 * HEADS_DEV, 2, HEAD_DIM)
    k_cols = kv_pairs[:, :, 0].reshape(rows, -1)
    v_cols = kv_pairs[:, :, 1].reshape(rows, -1)
    q_cols = columns(late_sums, kv_cols, feat)

    def last(x, size):
        return jnp.concatenate(
            [x[:, rows:, g * size : (g + 1) * size] for g in range(3)], axis=1
        )

    quarter = hidden_units // 2
    up_cols = columns(early_sums, 0, hidden_units)
    down_first, down_last = early_sums[:, :rows, hidden_units:], last(early_sums, quarter)
    down_cols = jnp.concatenate(
        [down_first[0], down_last[0], down_first[1], down_last[1]], axis=1
    )
    out_last = last(late_sums, feat)
    out_cols = jnp.concatenate([out_last[0], out_last[1]], axis=1)
    small = (late_sums[0] + late_sums[1])[:rows, kv_cols + feat :].T
    vec_out = small[:6].reshape(6, 2, 6)
    bias_out = small[6:8].reshape(-1)
    qv_out = small[8:10, :6]
    vec_out = lax.dynamic_index_in_dim(vec_out, heads_at, 1, keepdims=False)
    return (
        output.astype(BF16),
        hidden_grad,
        jnp.stack([q_cols, k_cols, v_cols]),
        out_cols.T,
        qv_out,
        up_cols,
        down_cols.T,
        bias_out,
        vec_out[:2],
        vec_out[2:],
    )


def solution(mesh):
    fine = Mesh(mesh.devices.reshape(4, 4, 2, 2, 2), ("z", "y", "xh", "core", "heads"))
    return jax.shard_map(
        per_device,
        mesh=fine,
        in_specs=(
            P(CTX, None),
            P(None, CTX, "heads"),
            P("heads", CTX),
            P(None, "heads"),
            P(CTX, "heads"),
            P("heads", CTX),
            P("heads"),
            P(),
            P(),
            P(CTX),
            P(),
            P(CTX, None),
        ),
        out_specs=(
            P(CTX, None),
            P(CTX, None),
            P(None, CTX, "heads"),
            P("heads", CTX),
            P(None, ("heads", *CTX)),
            P(CTX, "heads"),
            P("heads", CTX),
            P(("heads", *CTX)),
            P(None, (*CTX, "heads")),
            P(None, (*CTX, "heads")),
        ),
        check_vma=False,
    )
```

```python
import jax
import jax.numpy as jnp
from jax import lax
from jax.experimental import pallas as pl
from jax.experimental.pallas import tpu as pltpu
from jax.sharding import Mesh, PartitionSpec as P

HEAD_DIM = 64
HEADS_DEV = 3
EPS = 1e-06
NEG = -1e30
CTX = ("z", "y", "xh", "core")
CHIPS = ("z", "y", "xh")
F32 = jnp.float32
BF16 = jnp.bfloat16
NT = (((1,), (1,)), ((), ()))
VMEM_LIMIT = 50 * 1024 * 1024
OFFSETS = (0, -1, 1, 2)


def shifted(x, axis, step):
    n = lax.axis_size(axis)
    return lax.ppermute(x, axis, [(i, (i + step) % n) for i in range(n)])


def ring_halves(x, axis):
    half = x.shape[0] // 2
    before, after = shifted(x, axis, 1), shifted(x, axis, -1)
    return [x, before, after, shifted(before[:half], axis, 1), shifted(after[half:], axis, -1)]


def ring_near(x, axis):
    return [paired(b) for b in (x, shifted(x, axis, 1), shifted(x, axis, -1))]


def paired(x):
    return x.reshape(2, x.shape[0] // 2, x.shape[1])


def gather_first(x):
    half = x.shape[0] // 2
    streams = []
    for part, axis in ((x[:half], "z"), (x[half:], "y")):
        both = jnp.concatenate([part, shifted(part, "xh", 1)], axis=0)
        streams.append(jnp.concatenate(ring_halves(both, axis), axis=0))
    return tuple(streams)


def gather_second(z_stream, y_stream):
    blocks = ring_halves(z_stream, "y") + ring_halves(y_stream, "z")
    return [b.reshape(-1, z_stream.shape[0] // 2, b.shape[1]) for b in blocks]


def near_blocks(blocks):
    return blocks[:3] + blocks[5:8]


def far_blocks(blocks):
    return blocks[3:5] + blocks[8:]


def relative_order(first, second, core_at):
    place = {a: lax.axis_index(a) for a in CHIPS}
    core = lax.axis_index("core")
    order = []
    for second_step in OFFSETS:
        for first_step in OFFSETS:
            for xh_step in (0, 1):
                at = dict(place)
                at[first] = (at[first] + first_step) % 4
                at[second] = (at[second] + second_step) % 4
                at["xh"] = (at["xh"] + xh_step) % 2
                order.append(((at["z"] * 4 + at["y"]) * 2 + at["xh"]) * 2 + (core + core_at) % 2)
    return jnp.stack(order)


def pair_ordered(own, other, axis):
    first = lax.axis_index(axis) == 0
    return jnp.stack([jnp.where(first, own, other), jnp.where(first, other, own)])


def to_owners(x):
    return lax.all_to_all(x.reshape(64, 16, -1), CTX, 0, 0, tiled=True)


def owner_sums(parts):
    return jnp.sum(parts.reshape(-1, 2, *parts.shape[1:]).astype(F32), axis=0)


def team_sum(partial, beside=()):
    rows = partial.shape[0] // 2
    near = partial[:rows] + shifted(partial[rows:].astype(BF16), "core", 1).astype(F32)
    low = lax.optimization_barrier(near.astype(BF16))
    got, beside = lax.optimization_barrier((shifted(low, "heads", 1), beside))
    return low.astype(F32) + got.astype(F32), beside


def chip_tokens(x):
    return jnp.concatenate([x, shifted(x, "core", 1)], axis=0)


def layer_norm(residual, gain_row, shift_row):
    centred = residual - jnp.mean(residual, axis=-1, keepdims=True)
    inverse = lax.rsqrt(jnp.mean(centred * centred, axis=-1, keepdims=True) + EPS)
    normed = centred * inverse
    return (normed * gain_row + shift_row, normed, inverse)


def norm_back(incoming, normed, inverse, gain_row):
    scaled = incoming * gain_row
    projected = (
        scaled
        - jnp.mean(scaled, axis=-1, keepdims=True)
        - normed * jnp.mean(scaled * normed, axis=-1, keepdims=True)
    )
    return inverse * projected


def exact_gelu(pre_act):
    return jax.nn.gelu(pre_act, approximate=False)


def pieces_of(column):
    high = column.astype(BF16).astype(F32)
    middle = (column - high).astype(BF16).astype(F32)
    return high, middle, column - high - middle


def head_columns(h):
    return slice(h * HEAD_DIM, (h + 1) * HEAD_DIM)


def head_block(h):
    return slice(h * 128, (h + 1) * 128)


def diagonal_scores(q_ref, kv_ref, h):
    product = q_ref[h].astype(F32) * kv_ref[:, head_block(h)].astype(F32)
    return jnp.sum(product, axis=1, keepdims=True)


def copies_in(sources, buffer, sems):
    at = 0
    for source in sources:
        size = source.shape[0]
        pltpu.make_async_copy(source, buffer.at[pl.ds(at, size)], sems.at[at // 2]).start()
        at += size


def block_of(buffer, sems, j):
    block = buffer.at[pl.ds(2 * j, 2)]
    pltpu.make_async_copy(block, block, sems.at[j]).wait()
    return buffer[pl.ds(2 * j, 2)].reshape(-1, buffer.shape[2])


def attend_blocks(q_ref, tags_ref, seg_ref, top, total, acc, buffer, sems, row_of):
    rows = q_ref.shape[1]
    seg_wide = jnp.broadcast_to(seg_ref[...], (rows, 128))

    def step(j, carry):
        whole = block_of(buffer, sems, j)
        tags = tags_ref[pl.ds(row_of(j), 1), :]
        keys = tags.shape[1]
        allowed = jnp.tile(seg_wide, (1, keys // 128)) == tags
        for h in range(HEADS_DEV):
            kv = whole[:, head_block(h)]
            scores = lax.dot_general(q_ref[h], kv, NT, preferred_element_type=F32)
            scores = jnp.where(allowed, scores, NEG)
            before = top[h]
            now = jnp.maximum(before, jnp.max(scores, axis=1, keepdims=True))
            weights = jnp.exp(scores - jnp.tile(now, (1, keys // 128)))
            fade = jnp.exp(before - now)
            sums = weights[:, :128]
            for k in range(1, keys // 128):
                sums = sums + weights[:, k * 128 : (k + 1) * 128]
            total[h] = total[h] * fade + sums
            acc[h] = acc[h] * fade + jnp.dot(weights.astype(BF16), kv, preferred_element_type=F32)
            top[h] = now
        return carry

    lax.fori_loop(0, sems.shape[0], step, 0)


def near_row(j):
    return j + (j >= 3).astype(jnp.int32)


def far_row(j):
    return 4 * j + 3


def attend_near_kernel(q_ref, own_ref, tags_ref, seg_ref, tag_ref, *rest):
    blocks, (top, total, acc, buffer, sems) = rest[:6], rest[6:]
    copies_in(blocks, buffer, sems)
    rows = q_ref.shape[1]
    padded = tag_ref[...] < 0
    for h in range(HEADS_DEV):
        diagonal = diagonal_scores(q_ref, own_ref, h)
        top[h] = jnp.broadcast_to(jnp.where(padded, diagonal, NEG), (rows, 128))
        lane = lax.broadcasted_iota(jnp.int32, (rows, 128), 1)
        total[h] = jnp.where((lane == 0) & padded, 1.0, 0.0)
        acc[h] = jnp.where(padded, own_ref[:, head_block(h)].astype(F32), 0.0)
    attend_blocks(q_ref, tags_ref, seg_ref, top, total, acc, buffer, sems, near_row)


def attend_far_kernel(q_ref, tags_ref, seg_ref, top_in, total_in, acc_in, *rest):
    blocks, (out_ref, stat_ref, top, total, acc, buffer, sems) = rest[:4], rest[4:]
    copies_in(blocks, buffer, sems)
    top[...], total[...], acc[...] = top_in[...], total_in[...], acc_in[...]
    attend_blocks(q_ref, tags_ref, seg_ref, top, total, acc, buffer, sems, far_row)
    outs = []
    for h in range(HEADS_DEV):
        sums = jnp.sum(total[h], axis=1, keepdims=True)
        outs.append((acc[h] / sums)[:, HEAD_DIM:])
        stat_ref[h] = top[h] + jnp.log(sums)
    out_ref[...] = jnp.concatenate(outs, axis=1)


def vmem_specs(n):
    return [pl.BlockSpec(memory_space=pltpu.VMEM)] * n


def any_specs(n):
    return [pl.BlockSpec(memory_space=pl.ANY)] * n


def head_state(rows, lanes=128):
    return jax.ShapeDtypeStruct((HEADS_DEV, rows, lanes), F32)


def cost(rows, blocks, flops):
    keys = sum(b.shape[0] * b.shape[1] for b in blocks)
    pairs = rows * keys * HEADS_DEV
    return pl.CostEstimate(
        flops=pairs * flops, bytes_accessed=keys * 1024, transcendentals=pairs
    )


def buffers(blocks, lanes):
    count = sum(b.shape[0] for b in blocks)
    return [
        pltpu.VMEM((count, blocks[0].shape[1], lanes), BF16),
        pltpu.SemaphoreType.DMA((count // 2,)),
    ]


def attend_near(q_heads, kv_own, tags, seg, tag, blocks):
    rows = kv_own.shape[0]
    return pl.pallas_call(
        attend_near_kernel,
        out_shape=(head_state(rows),) * 3,
        in_specs=vmem_specs(5) + any_specs(6),
        out_specs=tuple(vmem_specs(3)),
        scratch_shapes=buffers(blocks, kv_own.shape[1]),
        compiler_params=pltpu.CompilerParams(vmem_limit_bytes=VMEM_LIMIT),
        cost_estimate=cost(rows, blocks, 512),
        name="attend_near",
    )(q_heads, kv_own, tags, seg, tag, *blocks)


def attend_far(q_heads, tags, seg, state, blocks):
    rows = q_heads.shape[1]
    return pl.pallas_call(
        attend_far_kernel,
        out_shape=(jax.ShapeDtypeStruct((rows, HEADS_DEV * HEAD_DIM), F32), head_state(rows)),
        in_specs=vmem_specs(6) + any_specs(4),
        out_specs=tuple(vmem_specs(2)),
        scratch_shapes=[pltpu.VMEM((HEADS_DEV, rows, 128), F32)] * 3
        + buffers(blocks, HEADS_DEV * 128),
        compiler_params=pltpu.CompilerParams(vmem_limit_bytes=VMEM_LIMIT),
        cost_estimate=cost(rows, blocks, 512),
        name="attend_far",
    )(q_heads, tags, seg, *state, *blocks)


def query_back_kernel(q_ref, g_ref, own_ref, tags_ref, seg_ref, tag_ref, stat_ref, delta_ref, *rest):
    blocks, (dq_ref, dkv_ref, buffer, sems, acc) = rest[:10], rest[10:]
    copies_in(blocks, buffer, sems)
    rows = q_ref.shape[1]
    seg_wide = jnp.broadcast_to(seg_ref[...], (rows, 128))
    padded = tag_ref[...] < 0
    for h in range(HEADS_DEV):
        own = own_ref[:, head_block(h)].astype(F32)
        prob = jnp.exp(diagonal_scores(q_ref, own_ref, h) - stat_ref[h][:, :1])
        prob = jnp.where(padded, prob, 0.0)
        grad = diagonal_scores(g_ref, own_ref, h) - delta_ref[h][:, :1]
        score = (prob * grad).astype(BF16).astype(F32)
        acc[h] = score * own
        dkv_ref[:, head_block(h)] = score * q_ref[h].astype(F32) + prob.astype(BF16).astype(
            F32
        ) * g_ref[h].astype(F32)

    def step(j, carry):
        whole = block_of(buffer, sems, j)
        tags = tags_ref[pl.ds(jnp.where(j < 6, near_row(j), far_row(j - 6)), 1), :]
        keys = tags.shape[1]
        allowed = jnp.tile(seg_wide, (1, keys // 128)) == tags
        for h in range(HEADS_DEV):
            kv = whole[:, head_block(h)]
            scores = lax.dot_general(q_ref[h], kv, NT, preferred_element_type=F32)
            scores = jnp.where(allowed, scores, NEG)
            probs = jnp.exp(scores - jnp.tile(stat_ref[h], (1, keys // 128)))
            grads = lax.dot_general(g_ref[h], kv, NT, preferred_element_type=F32)
            back = probs * (grads - jnp.tile(delta_ref[h], (1, keys // 128)))
            acc[h] = acc[h] + jnp.dot(back.astype(BF16), kv, preferred_element_type=F32)
        return carry

    lax.fori_loop(0, 8, step, 0)
    dq_ref[...] = (
        jnp.concatenate([acc[h][:, :HEAD_DIM] for h in range(HEADS_DEV)], axis=1)
        * HEAD_DIM ** (-0.5)
    ).astype(BF16)


def query_back(q_heads, g_heads, kv_own, tags, seg, tag, stat, delta, blocks):
    rows = kv_own.shape[0]
    return pl.pallas_call(
        query_back_kernel,
        out_shape=(
            jax.ShapeDtypeStruct((rows, HEADS_DEV * HEAD_DIM), BF16),
            jax.ShapeDtypeStruct(kv_own.shape, F32),
        ),
        in_specs=vmem_specs(8) + any_specs(10),
        out_specs=tuple(vmem_specs(2)),
        scratch_shapes=buffers(blocks, kv_own.shape[1]) + [pltpu.VMEM((HEADS_DEV, rows, 128), F32)],
        compiler_params=pltpu.CompilerParams(vmem_limit_bytes=VMEM_LIMIT),
        cost_estimate=cost(rows, blocks, 768),
        name="query_back",
    )(q_heads, g_heads, kv_own, tags, seg, tag, stat, delta, *blocks)


def grad_rows_kernel(
    mixed_ref, out_ref, attended_ref, stat_ref, seg_ref, sent_ref, g_ref, delta_ref
):
    rows = mixed_ref.shape[0]
    grad = jnp.dot(mixed_ref[...], out_ref[...], preferred_element_type=F32).astype(BF16)
    grad = grad.astype(F32)
    product = grad * attended_ref[...]
    lane = lax.broadcasted_iota(jnp.int32, (rows, HEAD_DIM), 1)
    seg = seg_ref[...]
    extra = jnp.where(lane == 21, 1.0, 0.0)
    for s in range(3):
        extra = extra + jnp.where((lane == 18 + s) & (seg != s), 1.0, 0.0)
    zeros = jnp.zeros((rows, HEAD_DIM), BF16)
    for h in range(HEADS_DEV):
        delta = jnp.sum(product[:, head_columns(h)], axis=1, keepdims=True)
        delta_ref[h] = jnp.broadcast_to(delta, (rows, 128))
        for i, piece in enumerate(pieces_of(delta)):
            extra = extra + jnp.where(lane == 3 * h + i, piece, 0.0)
        for i, piece in enumerate(pieces_of(stat_ref[h][:, :1])):
            extra = extra + jnp.where(lane == 9 + 3 * h + i, piece, 0.0)
        g_ref[h] = jnp.concatenate([zeros, grad[:, head_columns(h)].astype(BF16)], axis=1)
    sent_ref[...] = jnp.concatenate([grad, extra], axis=1).astype(BF16)


def grad_rows(mixed, w_out, attended, stat, seg):
    rows = mixed.shape[0]
    return pl.pallas_call(
        grad_rows_kernel,
        out_shape=(
            jax.ShapeDtypeStruct((rows, 256), BF16),
            jax.ShapeDtypeStruct((HEADS_DEV, rows, 128), BF16),
            jax.ShapeDtypeStruct((HEADS_DEV, rows, 128), F32),
        ),
        in_specs=vmem_specs(5),
        out_specs=tuple(vmem_specs(3)),
        compiler_params=pltpu.CompilerParams(vmem_limit_bytes=VMEM_LIMIT),
        name="grad_rows",
    )(mixed, w_out, attended, stat, seg)


def send_out(held, out_ref, sem):
    copy = pltpu.make_async_copy(held, out_ref, sem)
    copy.start()
    copy.wait()


def last_rows(x, group):
    parts = x.reshape(64, 16, x.shape[1])[:, 4 * group : 4 * group + 4]
    return jnp.concatenate([jnp.zeros((64, 12, x.shape[1]), F32), parts], axis=1).reshape(x.shape)


def early_grads_kernel(spread_ref, branch_ref, activated_ref, first_ref, up_ref, out_ref, held, sem):
    quarter = held.shape[1] // 3
    made = []
    for left, right in ((first_ref, up_ref), (branch_ref, activated_ref)):
        wide = jnp.dot(left[...], spread_ref[...], preferred_element_type=F32).astype(BF16)
        for half in range(2):
            made.append(dot_tn(wide, right[:, half * quarter : (half + 1) * quarter]))
    for g in range(3):
        held[:, g * quarter : (g + 1) * quarter] = (made[g] + last_rows(made[3], g)).astype(BF16)
    send_out(held, out_ref, sem)


def early_grads(spread, branch, activated, first, up):
    shape = (spread.shape[1], up.shape[1] * 3 // 2)
    return pl.pallas_call(
        early_grads_kernel,
        out_shape=jax.ShapeDtypeStruct(shape, BF16),
        in_specs=vmem_specs(5),
        out_specs=pl.BlockSpec(memory_space=pltpu.HBM),
        scratch_shapes=[pltpu.VMEM(shape, BF16), pltpu.SemaphoreType.DMA],
        compiler_params=pltpu.CompilerParams(vmem_limit_bytes=VMEM_LIMIT),
        name="early_grads",
    )(spread, branch, activated, first, up)


def out_rows_kernel(spread_ref, mixed_ref, attended_ref, out_ref):
    wide = jnp.dot(mixed_ref[...], spread_ref[...], preferred_element_type=F32).astype(BF16)
    made = dot_tn(wide, attended_ref[...].astype(BF16))
    out_ref[...] = jnp.concatenate([last_rows(made, g) for g in range(3)], axis=1).astype(BF16)


def out_rows(spread, mixed, attended):
    return pl.pallas_call(
        out_rows_kernel,
        out_shape=jax.ShapeDtypeStruct((spread.shape[1], 3 * attended.shape[1]), BF16),
        in_specs=vmem_specs(3),
        out_specs=vmem_specs(1)[0],
        compiler_params=pltpu.CompilerParams(vmem_limit_bytes=VMEM_LIMIT),
        name="out_rows",
    )(spread, mixed, attended)


def vector_rows_kernel(
    cot_ref, two_ref, resid_two_ref, first_ref, one_ref, resid_one_ref, up_ref, spread_ref, bias_ref,
    parts_ref, out_ref,
):
    cot, first = cot_ref[...].astype(F32), first_ref[...]
    columns = (
        first * one_ref[...],
        cot * two_ref[...],
        resid_one_ref[...],
        first,
        resid_two_ref[...],
        cot,
    )
    rows = jnp.concatenate([jnp.sum(c, axis=0, keepdims=True) for c in columns], axis=0)
    bias = jnp.sum(up_ref[...].astype(F32), axis=0, keepdims=True) * parts_ref[...]
    made = [
        jnp.dot(rows.astype(BF16), spread_ref[...], preferred_element_type=F32),
        jnp.dot(bias.astype(BF16), bias_ref[...], preferred_element_type=F32),
    ]
    out_ref[...] = jnp.concatenate(made, axis=0)


def vector_rows(spread, *args):
    return pl.pallas_call(
        vector_rows_kernel,
        out_shape=jax.ShapeDtypeStruct((8, spread.shape[1]), F32),
        in_specs=vmem_specs(10),
        out_specs=vmem_specs(1)[0],
        compiler_params=pltpu.CompilerParams(vmem_limit_bytes=VMEM_LIMIT),
        name="vector_rows",
    )(*args)


def late_grads_kernel(
    hid_ref, dkv_ref, dq_ref, rows_ref, q_place_ref, v_place_ref, placed_ref, w_ref, spread_ref,
    out_ref, back_ref, held, sem,
):
    wide = hid_ref.shape[1]
    grads = jnp.concatenate([dkv_ref[...], dq_ref[...]], axis=1)
    cols = grads.shape[1]
    made = dot_tn(hid_ref[...], grads) + placed_ref[...].astype(F32)
    sums = [rows_ref[...]]
    for grad, place in ((dq_ref, q_place_ref), (dkv_ref, v_place_ref)):
        row = jnp.sum(grad[...].astype(F32), axis=0, keepdims=True).astype(BF16)
        sums.append(jnp.dot(row, place[...], preferred_element_type=F32))
    sums.append(jnp.zeros((128 - 10, wide), F32))
    small = jnp.transpose(jnp.concatenate(sums, axis=0))[:, :64]
    held[...] = jnp.concatenate([made, small], axis=1).astype(BF16)
    copy = pltpu.make_async_copy(held, out_ref, sem)
    copy.start()
    back = dot_nt(grads, w_ref[:, :cols]).astype(BF16)
    back_ref[...] = dot_nt(back, spread_ref[...]).astype(BF16)
    copy.wait()


def late_grads(hid, dkv, dq, rows, q_place, v_place, placed, w, spread):
    shape = (hid.shape[1], dkv.shape[1] + dq.shape[1] + 64)
    return pl.pallas_call(
        late_grads_kernel,
        out_shape=(
            jax.ShapeDtypeStruct(shape, BF16),
            jax.ShapeDtypeStruct((hid.shape[0], spread.shape[0]), BF16),
        ),
        in_specs=vmem_specs(9),
        out_specs=(pl.BlockSpec(memory_space=pltpu.HBM), vmem_specs(1)[0]),
        scratch_shapes=[pltpu.VMEM(shape, BF16), pltpu.SemaphoreType.DMA],
        compiler_params=pltpu.CompilerParams(vmem_limit_bytes=VMEM_LIMIT),
        name="late_grads",
    )(hid, dkv, dq, rows, q_place, v_place, placed, w, spread)


def project_kernel(hid_ref, w_ref, bias_ref, scale_ref, kv_ref, wide_ref, q_ref):
    made = jnp.dot(hid_ref[...], w_ref[...], preferred_element_type=F32) + bias_ref[...]
    made = (made.astype(BF16).astype(F32) * scale_ref[...]).astype(BF16)
    kv_cols = kv_ref.shape[1]
    kv_ref[...] = made[:, :kv_cols]
    wide_ref[...] = made[:, kv_cols:]
    zeros = jnp.zeros((made.shape[0], HEAD_DIM), BF16)
    for h in range(HEADS_DEV):
        at = kv_cols + h * HEAD_DIM
        q_ref[h] = jnp.concatenate([made[:, at : at + HEAD_DIM], zeros], axis=1)


def project(hid, w, bias, scale):
    rows = hid.shape[0]
    return pl.pallas_call(
        project_kernel,
        out_shape=(
            jax.ShapeDtypeStruct((rows, HEADS_DEV * 128), BF16),
            jax.ShapeDtypeStruct((rows, w.shape[1] - HEADS_DEV * 128), BF16),
            jax.ShapeDtypeStruct((HEADS_DEV, rows, 128), BF16),
        ),
        in_specs=vmem_specs(4),
        out_specs=tuple(vmem_specs(3)),
        compiler_params=pltpu.CompilerParams(vmem_limit_bytes=VMEM_LIMIT),
        name="project",
    )(hid, w, bias, scale)


def queries_in(order_ref, q_ref, q_buffer, q_sems):
    for i in range(64):
        source = q_ref.at[order_ref[i]]
        pltpu.make_async_copy(source, q_buffer.at[i], q_sems.at[i // 8]).start()


def key_back_blocks(k_ref, v_ref, k_acc, v_acc, q_buffer, g_buffer, q_sems, g_sems):
    def step(j, carry):
        eight = q_buffer.at[pl.ds(8 * j, 8)]
        pltpu.make_async_copy(eight, eight, q_sems.at[j]).wait()
        queries = q_buffer[pl.ds(8 * j, 8)].reshape(-1, q_buffer.shape[2])
        grads = block_of(g_buffer, g_sems, j)
        lane = lax.broadcasted_iota(jnp.int32, queries.shape, 1)
        queries = jnp.where(lane < HEADS_DEV * HEAD_DIM, queries, grads)
        for h in range(HEADS_DEV):
            scores = lax.dot_general(k_ref[h], queries, NT, preferred_element_type=F32)
            probs = jnp.exp(scores)
            v_acc[h] = v_acc[h] + jnp.dot(probs.astype(BF16), grads, preferred_element_type=F32)
            back = probs * lax.dot_general(v_ref[h], grads, NT, preferred_element_type=F32)
            k_acc[h] = k_acc[h] + jnp.dot(back.astype(BF16), queries, preferred_element_type=F32)
        return carry

    lax.fori_loop(0, q_sems.shape[0], step, 0)


def key_heads(kv_ref, tag_ref, k_heads, v_heads):
    rows = kv_ref.shape[0]
    feat = HEADS_DEV * HEAD_DIM
    lane = lax.broadcasted_iota(jnp.int32, (rows, HEAD_DIM), 1)
    tag = tag_ref[...]
    masks = jnp.where((lane == 21) & (tag < 0), NEG, 0.0)
    for s in range(3):
        masks = masks + jnp.where((lane == 18 + s) & (tag == s), NEG, 0.0)
    for h in range(HEADS_DEV):
        block = kv_ref[:, head_block(h)].astype(F32)
        before = [jnp.zeros((rows, h * HEAD_DIM), F32)] if h else []
        left = feat - (h + 1) * HEAD_DIM
        after = [jnp.zeros((rows, left), F32)] if left else []
        k_extra = masks - jnp.where((lane >= 9 + 3 * h) & (lane < 12 + 3 * h), 1.0, 0.0)
        v_extra = -jnp.where((lane >= 3 * h) & (lane < 3 * h + 3), 1.0, 0.0)
        for heads, part, extra in (
            (k_heads, block[:, :HEAD_DIM], k_extra),
            (v_heads, block[:, HEAD_DIM:], v_extra),
        ):
            heads[h] = jnp.concatenate(before + [part] + after + [extra], axis=1).astype(BF16)


def key_back_kernel(order_ref, kv_ref, tag_ref, diag_ref, q_ref, *rest):
    g_blocks = rest[:8]
    dkv_ref, k_heads, v_heads, k_acc, v_acc, q_buffer, q_sems, g_buffer, g_sems = rest[8:]
    queries_in(order_ref, q_ref, q_buffer, q_sems)
    copies_in(g_blocks, g_buffer, g_sems)
    key_heads(kv_ref, tag_ref, k_heads, v_heads)
    k_acc[...] = jnp.zeros_like(k_acc)
    v_acc[...] = jnp.zeros_like(v_acc)
    key_back_blocks(k_heads, v_heads, k_acc, v_acc, q_buffer, g_buffer, q_sems, g_sems)
    parts = []
    for h in range(HEADS_DEV):
        parts += [k_acc[h][:, head_columns(h)], v_acc[h][:, head_columns(h)]]
    dkv_ref[...] = (jnp.concatenate(parts, axis=1) + diag_ref[...]).astype(BF16)


def query_buffers(q_all):
    return [pltpu.VMEM(q_all.shape, BF16), pltpu.SemaphoreType.DMA((8,))]


def smem_spec():
    return [pl.BlockSpec(memory_space=pltpu.SMEM)]


def key_back(order, kv_own, tag, diagonal, q_all, g_blocks):
    rows, width = kv_own.shape[0], g_blocks[0].shape[2]
    return pl.pallas_call(
        key_back_kernel,
        out_shape=jax.ShapeDtypeStruct(diagonal.shape, BF16),
        in_specs=smem_spec() + vmem_specs(3) + [pl.BlockSpec(memory_space=pltpu.HBM)] * 9,
        out_specs=vmem_specs(1)[0],
        scratch_shapes=[pltpu.VMEM((HEADS_DEV, rows, width), BF16)] * 2
        + [pltpu.VMEM((HEADS_DEV, rows, width), F32)] * 2
        + query_buffers(q_all)
        + buffers(g_blocks, width),
        compiler_params=pltpu.CompilerParams(vmem_limit_bytes=VMEM_LIMIT),
        cost_estimate=cost(rows, g_blocks, 2048),
        name="key_back",
    )(order, kv_own, tag, diagonal, q_all, *g_blocks)


def dot(a, b):
    return jnp.dot(a, b, preferred_element_type=F32)


def dot_nt(a, b):
    return lax.dot_general(a, b, NT, preferred_element_type=F32)


def dot_tn(a, b):
    return lax.dot_general(a, b, (((0,), (0,)), ((), ())), preferred_element_type=F32)


def core_half(x, axis, at):
    size = x.shape[axis] // 2
    return lax.dynamic_slice_in_dim(x, at * size, size, axis)


def interleaved(k, v):
    shape = (*k.shape[:-1], -1, HEAD_DIM)
    return jnp.stack([k.reshape(shape), v.reshape(shape)], axis=-2).reshape(*k.shape[:-1], -1)


def per_device(
    hidden,
    w_qkv,
    w_out,
    b_qv,
    w_up,
    w_down,
    b_up,
    norm_gains,
    norm_shifts,
    segments,
    lengths,
    cotangent,
):
    core = lax.axis_index("core")
    heads_at = lax.axis_index("heads")
    own_ctx = ((lax.axis_index("z") * 4 + lax.axis_index("y")) * 2 + lax.axis_index("xh")) * 2 + core
    tok = hidden.shape[0]
    rows = w_up.shape[0]
    feat = HEADS_DEV * HEAD_DIM
    hidden_units = w_up.shape[1] // 2

    hid = chip_tokens(hidden)
    out_turned, down_turned = w_out.T, w_down.T
    low_tok = segments.astype(BF16).reshape(2, tok // 2)
    kv_cols = 2 * feat

    def halves(x):
        return jnp.swapaxes(x.reshape(rows, 2, -1), 0, 1)

    q_half, k_half, v_half = (halves(w_qkv[i]) for i in range(3))
    tail = jnp.broadcast_to(jnp.pad(low_tok, ((0, rows - 2), (0, 0))), (2, rows, tok // 2))
    urgent = jnp.concatenate([interleaved(k_half, v_half), q_half, tail], axis=2)
    urgent = jnp.pad(urgent, ((0, 0), (0, 16 - rows), (0, 0)))
    urgent = jnp.broadcast_to(urgent[None], (32, *urgent.shape)).reshape(64, 16, -1)
    urgent, *later = lax.optimization_barrier((urgent, out_turned, w_up, down_turned))
    later = jnp.concatenate([halves(w) for w in later], axis=2)
    mine = lax.dynamic_index_in_dim(later, core, 0, keepdims=False)
    theirs = shifted(lax.dynamic_index_in_dim(later, 1 - core, 0, keepdims=False), "core", 1)
    later = pair_ordered(mine, theirs, "core").reshape(2 * rows, -1)
    rest = lax.all_gather(later, CHIPS, axis=0, tiled=True)
    w_urgent = lax.all_to_all(urgent, CTX, 0, 0, tiled=True)
    seg_all = w_urgent[:, :2, kv_cols + feat :].reshape(-1, tok).astype(jnp.int32)
    w_urgent = w_urgent.reshape(64 * 16, -1)
    at_wide = jnp.arange(64 * 16, dtype=jnp.int32)
    at_feature = jnp.arange(64 * rows, dtype=jnp.int32)
    spread = (
        (at_feature // rows * 16 + at_feature % rows)[:, None] == at_wide[None, :]
    ).astype(BF16)
    hid_wide = dot(hid, spread).astype(BF16)
    at_bias = jnp.arange(hidden_units, dtype=jnp.int32)
    at_half = jnp.arange(feat, dtype=jnp.int32)
    at_kv = jnp.arange(kv_cols, dtype=jnp.int32)

    def placed(owner, row):
        return ((owner * 16 + row)[:, None] == at_wide[None, :]).astype(BF16)

    first_owner = 32 * core
    bias_place = placed(first_owner + at_bias // 24, at_bias % 12)
    q_place = placed(first_owner + at_half // 6, at_half % 6)
    at_value = at_kv // 128 * HEAD_DIM + at_kv % 128 - HEAD_DIM
    is_value = at_kv % 128 >= HEAD_DIM
    v_place = placed(jnp.where(is_value, first_owner + at_value // 6, -1), at_value % 6)
    parts = jnp.arange(2, dtype=jnp.int32)[:, None] == (at_bias % 24 // 12)[None, :]
    hid_wide, q_place, v_place, bias_place = lax.optimization_barrier(
        (hid_wide, q_place, v_place, bias_place)
    )

    w_out_t = rest[:, :feat]
    w_up_all = rest[:, feat : feat + hidden_units]
    w_down_t = rest[:, feat + hidden_units :]

    bias = b_qv.astype(F32)
    q_bias, v_bias = core_half(bias[0], 0, core), core_half(bias[1], 0, core)
    no_bias = jnp.zeros((tok // 2,), F32)
    bias_row = jnp.concatenate([interleaved(jnp.zeros_like(v_bias), v_bias), q_bias, no_bias])
    column = jnp.arange(bias_row.shape[0], dtype=jnp.int32)
    scale_row = jnp.where(
        column < kv_cols, 1.0, jnp.where(column < kv_cols + feat, HEAD_DIM ** (-0.5), 0.0)
    ).astype(F32)
    kv_own, q_wide, q_heads = project(hid_wide, w_urgent, bias_row[None], scale_row[None])
    q_all = lax.all_gather(q_wide, CHIPS, axis=0, tiled=True).reshape(64, tok, -1)
    starts = [jnp.sum((seg_all < s).astype(jnp.int32)) for s in range(3)]
    places = jnp.arange(seg_all.size, dtype=jnp.int32).reshape(seg_all.shape)
    run_end = jnp.zeros_like(seg_all)
    for s in range(3):
        run_end = jnp.where(seg_all == s, starts[s] + lengths[s], run_end)
    tag_all = jnp.where(places < run_end, seg_all, -1).astype(F32)
    order = jnp.concatenate([relative_order("z", "y", 0), relative_order("y", "z", 1)])
    q_order = jnp.where(core == 0, order, order + 1 - 2 * (order % 2))
    tags = jnp.take(tag_all, order, axis=0).reshape(8, -1)
    both = jnp.stack([own_ctx, own_ctx + 1 - 2 * core])
    tag_own = jnp.take(tag_all, both, axis=0).reshape(-1, 1)
    seg_own = jnp.take(seg_all, both, axis=0).astype(F32).reshape(-1, 1)

    sent_z, sent_y = lax.optimization_barrier(gather_first(kv_own))
    blocks = gather_second(sent_z, sent_y)
    near, far = near_blocks(blocks), far_blocks(blocks)
    state = attend_near(q_heads, kv_own, tags, seg_own, tag_own, near)
    attended, stat = attend_far(q_heads, tags, seg_own, state, far)
    attended_low = attended.astype(BF16)

    gain_rows = norm_gains.astype(F32)
    shifts = norm_shifts.astype(F32)
    attn_mixed, _ = team_sum(dot_nt(attended_low, w_out_t))
    first_out, normed_one, inverse_one = layer_norm(
        hidden.astype(F32) + attn_mixed + shifts[0], gain_rows[0], shifts[1]
    )
    first_low = chip_tokens(first_out.astype(BF16))
    up_bias = core_half(b_up, 0, core).astype(F32)
    up_proj = dot(first_low, w_up_all) + up_bias
    activated = exact_gelu(up_proj).astype(BF16)
    second, _ = team_sum(dot_nt(activated, w_down_t))
    output, normed_two, inverse_two = layer_norm(
        first_out + second + shifts[2], gain_rows[1], shifts[3]
    )
    resid_two = norm_back(
        cotangent.astype(F32), normed_two, inverse_two, gain_rows[1]
    )
    branch_low = chip_tokens(resid_two.astype(BF16))
    act_grad = dot(branch_low, w_down_t)
    up_low = jax.vjp(exact_gelu, up_proj)[1](act_grad)[0].astype(BF16)
    made = early_grads(spread, branch_low, activated, first_low, up_low)
    first_sum, made = team_sum(dot_nt(up_low, w_up_all), made)
    first_grad = resid_two + first_sum
    resid_one = norm_back(first_grad, normed_one, inverse_one, gain_rows[0])
    mixed_low = chip_tokens(resid_one.astype(BF16))
    g_sent, g_heads, delta = grad_rows(mixed_low, w_out_t, attended, stat, seg_own)
    (g_z, g_y), g_heads = lax.optimization_barrier((gather_first(g_sent), g_heads))
    g_near = ring_near(g_z, "y") + ring_near(g_y, "z")
    g_far = [paired(shifted(g_z, "y", 2)), paired(shifted(g_y, "z", 2))]
    dq, diagonal = query_back(
        q_heads, g_heads, kv_own, tags, seg_own, tag_own, stat, delta, near + far
    )
    g_near, g_far, made, dq, spread = lax.optimization_barrier(
        (g_near, g_far, made, dq, spread)
    )
    g_blocks = [*g_near[:3], g_far[0], *g_near[3:], g_far[1]]
    early = to_owners(made)
    out_placed = out_rows(spread, mixed_low, attended_low)
    rows_made = vector_rows(
        spread,
        cotangent,
        normed_two,
        resid_two,
        first_grad,
        normed_one,
        resid_one,
        up_low,
        spread,
        bias_place,
        parts.astype(F32),
    )

    dkv = key_back(q_order, kv_own, tag_own, diagonal, q_all, g_blocks)
    dkv, early = lax.optimization_barrier((dkv, early))
    late, back = late_grads(
        hid_wide, dkv, dq, rows_made, q_place, v_place, out_placed, w_urgent, spread
    )
    late, early = lax.optimization_barrier((late, early))
    late = to_owners(late)
    hidden_grad = resid_one + team_sum(back.astype(F32))[0]

    early_sums, late_sums = owner_sums(early), owner_sums(late)

    def columns(x, start, size):
        return jnp.concatenate([x[c, :rows, start : start + size] for c in range(2)], axis=1)

    kv_pairs = columns(late_sums, 0, kv_cols).reshape(rows, 2 * HEADS_DEV, 2, HEAD_DIM)
    k_cols = kv_pairs[:, :, 0].reshape(rows, -1)
    v_cols = kv_pairs[:, :, 1].reshape(rows, -1)
    q_cols = columns(late_sums, kv_cols, feat)

    def last(x, size):
        return jnp.concatenate(
            [x[:, rows:, g * size : (g + 1) * size] for g in range(3)], axis=1
        )

    quarter = hidden_units // 2
    up_cols = columns(early_sums, 0, hidden_units)
    down_first, down_last = early_sums[:, :rows, hidden_units:], last(early_sums, quarter)
    down_cols = jnp.concatenate(
        [down_first[0], down_last[0], down_first[1], down_last[1]], axis=1
    )
    out_last = last(late_sums, feat)
    out_cols = jnp.concatenate([out_last[0], out_last[1]], axis=1)
    small = (late_sums[0] + late_sums[1])[:rows, kv_cols + feat :].T
    vec_out = small[:6].reshape(6, 2, 6)
    bias_out = small[6:8].reshape(-1)
    qv_out = small[8:10, :6]
    vec_out = lax.dynamic_index_in_dim(vec_out, heads_at, 1, keepdims=False)
    return (
        output.astype(BF16),
        hidden_grad,
        jnp.stack([q_cols, k_cols, v_cols]),
        out_cols.T,
        qv_out,
        up_cols,
        down_cols.T,
        bias_out,
        vec_out[:2],
        vec_out[2:],
    )


def solution(mesh):
    fine = Mesh(mesh.devices.reshape(4, 4, 2, 2, 2), ("z", "y", "xh", "core", "heads"))
    return jax.shard_map(
        per_device,
        mesh=fine,
        in_specs=(
            P(CTX, None),
            P(None, CTX, "heads"),
            P("heads", CTX),
            P(None, "heads"),
            P(CTX, "heads"),
            P("heads", CTX),
            P("heads"),
            P(),
            P(),
            P(CTX),
            P(),
            P(CTX, None),
        ),
        out_specs=(
            P(CTX, None),
            P(CTX, None),
            P(None, CTX, "heads"),
            P("heads", CTX),
            P(None, ("heads", *CTX)),
            P(CTX, "heads"),
            P("heads", CTX),
            P(("heads", *CTX)),
            P(None, (*CTX, "heads")),
            P(None, (*CTX, "heads")),
        ),
        check_vma=False,
    )
```

```python
import jax
import jax.numpy as jnp
from jax import lax
from jax.experimental import pallas as pl
from jax.experimental.pallas import tpu as pltpu
from jax.sharding import Mesh, PartitionSpec as P

HEAD_DIM = 64
HEADS_DEV = 3
EPS = 1e-06
NEG = -1e30
CTX = ("z", "y", "xh", "core")
CHIPS = ("z", "y", "xh")
F32 = jnp.float32
BF16 = jnp.bfloat16
NT = (((1,), (1,)), ((), ()))
VMEM_LIMIT = 50 * 1024 * 1024
OFFSETS = (0, -1, 1, 2)


def shifted(x, axis, step):
    n = lax.axis_size(axis)
    return lax.ppermute(x, axis, [(i, (i + step) % n) for i in range(n)])


def ring_halves(x, axis):
    half = x.shape[0] // 2
    before, after = shifted(x, axis, 1), shifted(x, axis, -1)
    return [x, before, after, shifted(before[:half], axis, 1), shifted(after[half:], axis, -1)]


def ring_near(x, axis):
    return [paired(b) for b in (x, shifted(x, axis, 1), shifted(x, axis, -1))]


def paired(x):
    return x.reshape(2, x.shape[0] // 2, x.shape[1])


def gather_first(x):
    half = x.shape[0] // 2
    streams = []
    for part, axis in ((x[:half], "z"), (x[half:], "y")):
        both = jnp.concatenate([part, shifted(part, "xh", 1)], axis=0)
        streams.append(jnp.concatenate(ring_halves(both, axis), axis=0))
    return tuple(streams)


def gather_second(z_stream, y_stream):
    blocks = ring_halves(z_stream, "y") + ring_halves(y_stream, "z")
    return [b.reshape(-1, z_stream.shape[0] // 2, b.shape[1]) for b in blocks]


def near_blocks(blocks):
    return blocks[:3] + blocks[5:8]


def far_blocks(blocks):
    return blocks[3:5] + blocks[8:]


def relative_order(first, second, core_at):
    place = {a: lax.axis_index(a) for a in CHIPS}
    core = lax.axis_index("core")
    order = []
    for second_step in OFFSETS:
        for first_step in OFFSETS:
            for xh_step in (0, 1):
                at = dict(place)
                at[first] = (at[first] + first_step) % 4
                at[second] = (at[second] + second_step) % 4
                at["xh"] = (at["xh"] + xh_step) % 2
                order.append(((at["z"] * 4 + at["y"]) * 2 + at["xh"]) * 2 + (core + core_at) % 2)
    return jnp.stack(order)


def pair_ordered(own, other, axis):
    first = lax.axis_index(axis) == 0
    return jnp.stack([jnp.where(first, own, other), jnp.where(first, other, own)])


def to_owners(x):
    return lax.all_to_all(x.reshape(64, 16, -1), CTX, 0, 0, tiled=True)


def owner_sums(parts):
    return jnp.sum(parts.reshape(-1, 2, *parts.shape[1:]).astype(F32), axis=0)


def team_sum(partial, beside=()):
    rows = partial.shape[0] // 2
    near = partial[:rows] + shifted(partial[rows:].astype(BF16), "core", 1).astype(F32)
    low = lax.optimization_barrier(near.astype(BF16))
    got, beside = lax.optimization_barrier((shifted(low, "heads", 1), beside))
    return low.astype(F32) + got.astype(F32), beside


def chip_tokens(x):
    return jnp.concatenate([x, shifted(x, "core", 1)], axis=0)


def layer_norm(residual, gain_row, shift_row):
    centred = residual - jnp.mean(residual, axis=-1, keepdims=True)
    inverse = lax.rsqrt(jnp.mean(centred * centred, axis=-1, keepdims=True) + EPS)
    normed = centred * inverse
    return (normed * gain_row + shift_row, normed, inverse)


def norm_back(incoming, normed, inverse, gain_row):
    scaled = incoming * gain_row
    projected = (
        scaled
        - jnp.mean(scaled, axis=-1, keepdims=True)
        - normed * jnp.mean(scaled * normed, axis=-1, keepdims=True)
    )
    return inverse * projected


def exact_gelu(pre_act):
    return jax.nn.gelu(pre_act, approximate=False)


def pieces_of(column):
    high = column.astype(BF16).astype(F32)
    middle = (column - high).astype(BF16).astype(F32)
    return high, middle, column - high - middle


def head_columns(h):
    return slice(h * HEAD_DIM, (h + 1) * HEAD_DIM)


def head_block(h):
    return slice(h * 128, (h + 1) * 128)


def diagonal_scores(q_ref, kv_ref, h):
    product = q_ref[h].astype(F32) * kv_ref[:, head_block(h)].astype(F32)
    return jnp.sum(product, axis=1, keepdims=True)


def copies_in(sources, buffer, sems):
    at = 0
    for source in sources:
        size = source.shape[0]
        pltpu.make_async_copy(source, buffer.at[pl.ds(at, size)], sems.at[at // 2]).start()
        at += size


def block_of(buffer, sems, j):
    block = buffer.at[pl.ds(2 * j, 2)]
    pltpu.make_async_copy(block, block, sems.at[j]).wait()
    return buffer[pl.ds(2 * j, 2)].reshape(-1, buffer.shape[2])


def attend_blocks(q_ref, tags_ref, seg_ref, top, total, acc, buffer, sems, row_of):
    rows = q_ref.shape[1]
    seg_wide = jnp.broadcast_to(seg_ref[...], (rows, 128))

    def step(j, carry):
        whole = block_of(buffer, sems, j)
        tags = tags_ref[pl.ds(row_of(j), 1), :]
        keys = tags.shape[1]
        allowed = jnp.tile(seg_wide, (1, keys // 128)) == tags
        for h in range(HEADS_DEV):
            kv = whole[:, head_block(h)]
            scores = lax.dot_general(q_ref[h], kv, NT, preferred_element_type=F32)
            scores = jnp.where(allowed, scores, NEG)
            before = top[h]
            now = jnp.maximum(before, jnp.max(scores, axis=1, keepdims=True))
            weights = jnp.exp(scores - jnp.tile(now, (1, keys // 128)))
            fade = jnp.exp(before - now)
            sums = weights[:, :128]
            for k in range(1, keys // 128):
                sums = sums + weights[:, k * 128 : (k + 1) * 128]
            total[h] = total[h] * fade + sums
            acc[h] = acc[h] * fade + jnp.dot(weights.astype(BF16), kv, preferred_element_type=F32)
            top[h] = now
        return carry

    lax.fori_loop(0, sems.shape[0], step, 0)


def near_row(j):
    return j + (j >= 3).astype(jnp.int32)


def far_row(j):
    return 4 * j + 3


def attend_near_kernel(q_ref, own_ref, tags_ref, seg_ref, tag_ref, *rest):
    blocks, (top, total, acc, buffer, sems) = rest[:6], rest[6:]
    copies_in(blocks, buffer, sems)
    rows = q_ref.shape[1]
    padded = tag_ref[...] < 0
    for h in range(HEADS_DEV):
        diagonal = diagonal_scores(q_ref, own_ref, h)
        top[h] = jnp.broadcast_to(jnp.where(padded, diagonal, NEG), (rows, 128))
        lane = lax.broadcasted_iota(jnp.int32, (rows, 128), 1)
        total[h] = jnp.where((lane == 0) & padded, 1.0, 0.0)
        acc[h] = jnp.where(padded, own_ref[:, head_block(h)].astype(F32), 0.0)
    attend_blocks(q_ref, tags_ref, seg_ref, top, total, acc, buffer, sems, near_row)


def attend_far_kernel(q_ref, tags_ref, seg_ref, top_in, total_in, acc_in, *rest):
    blocks, (out_ref, stat_ref, top, total, acc, buffer, sems) = rest[:4], rest[4:]
    copies_in(blocks, buffer, sems)
    top[...], total[...], acc[...] = top_in[...], total_in[...], acc_in[...]
    attend_blocks(q_ref, tags_ref, seg_ref, top, total, acc, buffer, sems, far_row)
    outs = []
    for h in range(HEADS_DEV):
        sums = jnp.sum(total[h], axis=1, keepdims=True)
        outs.append((acc[h] / sums)[:, HEAD_DIM:])
        stat_ref[h] = top[h] + jnp.log(sums)
    out_ref[...] = jnp.concatenate(outs, axis=1)


def vmem_specs(n):
    return [pl.BlockSpec(memory_space=pltpu.VMEM)] * n


def any_specs(n):
    return [pl.BlockSpec(memory_space=pl.ANY)] * n


def head_state(rows, lanes=128):
    return jax.ShapeDtypeStruct((HEADS_DEV, rows, lanes), F32)


def cost(rows, blocks, flops):
    keys = sum(b.shape[0] * b.shape[1] for b in blocks)
    pairs = rows * keys * HEADS_DEV
    return pl.CostEstimate(
        flops=pairs * flops, bytes_accessed=keys * 1024, transcendentals=pairs
    )


def buffers(blocks, lanes):
    count = sum(b.shape[0] for b in blocks)
    return [
        pltpu.VMEM((count, blocks[0].shape[1], lanes), BF16),
        pltpu.SemaphoreType.DMA((count // 2,)),
    ]


def attend_near(q_heads, kv_own, tags, seg, tag, blocks):
    rows = kv_own.shape[0]
    return pl.pallas_call(
        attend_near_kernel,
        out_shape=(head_state(rows),) * 3,
        in_specs=vmem_specs(5) + any_specs(6),
        out_specs=tuple(vmem_specs(3)),
        scratch_shapes=buffers(blocks, kv_own.shape[1]),
        compiler_params=pltpu.CompilerParams(vmem_limit_bytes=VMEM_LIMIT),
        cost_estimate=cost(rows, blocks, 512),
        name="attend_near",
    )(q_heads, kv_own, tags, seg, tag, *blocks)


def attend_far(q_heads, tags, seg, state, blocks):
    rows = q_heads.shape[1]
    return pl.pallas_call(
        attend_far_kernel,
        out_shape=(jax.ShapeDtypeStruct((rows, HEADS_DEV * HEAD_DIM), F32), head_state(rows)),
        in_specs=vmem_specs(6) + any_specs(4),
        out_specs=tuple(vmem_specs(2)),
        scratch_shapes=[pltpu.VMEM((HEADS_DEV, rows, 128), F32)] * 3
        + buffers(blocks, HEADS_DEV * 128),
        compiler_params=pltpu.CompilerParams(vmem_limit_bytes=VMEM_LIMIT),
        cost_estimate=cost(rows, blocks, 512),
        name="attend_far",
    )(q_heads, tags, seg, *state, *blocks)


def query_back_kernel(q_ref, g_ref, own_ref, tags_ref, seg_ref, tag_ref, stat_ref, delta_ref, *rest):
    blocks, (dq_ref, dkv_ref, buffer, sems, acc) = rest[:10], rest[10:]
    copies_in(blocks, buffer, sems)
    rows = q_ref.shape[1]
    seg_wide = jnp.broadcast_to(seg_ref[...], (rows, 128))
    padded = tag_ref[...] < 0
    for h in range(HEADS_DEV):
        own = own_ref[:, head_block(h)].astype(F32)
        prob = jnp.exp(diagonal_scores(q_ref, own_ref, h) - stat_ref[h][:, :1])
        prob = jnp.where(padded, prob, 0.0)
        grad = diagonal_scores(g_ref, own_ref, h) - delta_ref[h][:, :1]
        score = (prob * grad).astype(BF16).astype(F32)
        acc[h] = score * own
        dkv_ref[:, head_block(h)] = score * q_ref[h].astype(F32) + prob.astype(BF16).astype(
            F32
        ) * g_ref[h].astype(F32)

    def step(j, carry):
        whole = block_of(buffer, sems, j)
        tags = tags_ref[pl.ds(jnp.where(j < 6, near_row(j), far_row(j - 6)), 1), :]
        keys = tags.shape[1]
        allowed = jnp.tile(seg_wide, (1, keys // 128)) == tags
        for h in range(HEADS_DEV):
            kv = whole[:, head_block(h)]
            scores = lax.dot_general(q_ref[h], kv, NT, preferred_element_type=F32)
            scores = jnp.where(allowed, scores, NEG)
            probs = jnp.exp(scores - jnp.tile(stat_ref[h], (1, keys // 128)))
            grads = lax.dot_general(g_ref[h], kv, NT, preferred_element_type=F32)
            back = probs * (grads - jnp.tile(delta_ref[h], (1, keys // 128)))
            acc[h] = acc[h] + jnp.dot(back.astype(BF16), kv, preferred_element_type=F32)
        return carry

    lax.fori_loop(0, 8, step, 0)
    dq_ref[...] = (
        jnp.concatenate([acc[h][:, :HEAD_DIM] for h in range(HEADS_DEV)], axis=1)
        * HEAD_DIM ** (-0.5)
    ).astype(BF16)


def query_back(q_heads, g_heads, kv_own, tags, seg, tag, stat, delta, blocks):
    rows = kv_own.shape[0]
    return pl.pallas_call(
        query_back_kernel,
        out_shape=(
            jax.ShapeDtypeStruct((rows, HEADS_DEV * HEAD_DIM), BF16),
            jax.ShapeDtypeStruct(kv_own.shape, F32),
        ),
        in_specs=vmem_specs(8) + any_specs(10),
        out_specs=tuple(vmem_specs(2)),
        scratch_shapes=buffers(blocks, kv_own.shape[1]) + [pltpu.VMEM((HEADS_DEV, rows, 128), F32)],
        compiler_params=pltpu.CompilerParams(vmem_limit_bytes=VMEM_LIMIT),
        cost_estimate=cost(rows, blocks, 768),
        name="query_back",
    )(q_heads, g_heads, kv_own, tags, seg, tag, stat, delta, *blocks)


def grad_rows_kernel(
    mixed_ref, out_ref, attended_ref, stat_ref, seg_ref, sent_ref, g_ref, delta_ref
):
    rows = mixed_ref.shape[0]
    grad = jnp.dot(mixed_ref[...], out_ref[...], preferred_element_type=F32).astype(BF16)
    grad = grad.astype(F32)
    product = grad * attended_ref[...]
    lane = lax.broadcasted_iota(jnp.int32, (rows, HEAD_DIM), 1)
    seg = seg_ref[...]
    extra = jnp.where(lane == 21, 1.0, 0.0)
    for s in range(3):
        extra = extra + jnp.where((lane == 18 + s) & (seg != s), 1.0, 0.0)
    zeros = jnp.zeros((rows, HEAD_DIM), BF16)
    for h in range(HEADS_DEV):
        delta = jnp.sum(product[:, head_columns(h)], axis=1, keepdims=True)
        delta_ref[h] = jnp.broadcast_to(delta, (rows, 128))
        for i, piece in enumerate(pieces_of(delta)):
            extra = extra + jnp.where(lane == 3 * h + i, piece, 0.0)
        for i, piece in enumerate(pieces_of(stat_ref[h][:, :1])):
            extra = extra + jnp.where(lane == 9 + 3 * h + i, piece, 0.0)
        g_ref[h] = jnp.concatenate([zeros, grad[:, head_columns(h)].astype(BF16)], axis=1)
    sent_ref[...] = jnp.concatenate([grad, extra], axis=1).astype(BF16)


def grad_rows(mixed, w_out, attended, stat, seg):
    rows = mixed.shape[0]
    return pl.pallas_call(
        grad_rows_kernel,
        out_shape=(
            jax.ShapeDtypeStruct((rows, 256), BF16),
            jax.ShapeDtypeStruct((HEADS_DEV, rows, 128), BF16),
            jax.ShapeDtypeStruct((HEADS_DEV, rows, 128), F32),
        ),
        in_specs=vmem_specs(5),
        out_specs=tuple(vmem_specs(3)),
        compiler_params=pltpu.CompilerParams(vmem_limit_bytes=VMEM_LIMIT),
        name="grad_rows",
    )(mixed, w_out, attended, stat, seg)


def send_out(held, out_ref, sem):
    copy = pltpu.make_async_copy(held, out_ref, sem)
    copy.start()
    copy.wait()


def last_rows(x, group):
    parts = x.reshape(64, 16, x.shape[1])[:, 4 * group : 4 * group + 4]
    return jnp.concatenate([jnp.zeros((64, 12, x.shape[1]), F32), parts], axis=1).reshape(x.shape)


def early_grads_kernel(spread_ref, branch_ref, activated_ref, first_ref, up_ref, out_ref, held, sem):
    quarter = held.shape[1] // 3
    made = []
    for left, right in ((first_ref, up_ref), (branch_ref, activated_ref)):
        wide = jnp.dot(left[...], spread_ref[...], preferred_element_type=F32).astype(BF16)
        for half in range(2):
            made.append(dot_tn(wide, right[:, half * quarter : (half + 1) * quarter]))
    for g in range(3):
        held[:, g * quarter : (g + 1) * quarter] = (made[g] + last_rows(made[3], g)).astype(BF16)
    send_out(held, out_ref, sem)


def early_grads(spread, branch, activated, first, up):
    shape = (spread.shape[1], up.shape[1] * 3 // 2)
    return pl.pallas_call(
        early_grads_kernel,
        out_shape=jax.ShapeDtypeStruct(shape, BF16),
        in_specs=vmem_specs(5),
        out_specs=pl.BlockSpec(memory_space=pltpu.HBM),
        scratch_shapes=[pltpu.VMEM(shape, BF16), pltpu.SemaphoreType.DMA],
        compiler_params=pltpu.CompilerParams(vmem_limit_bytes=VMEM_LIMIT),
        name="early_grads",
    )(spread, branch, activated, first, up)


def out_rows_kernel(spread_ref, mixed_ref, attended_ref, out_ref):
    wide = jnp.dot(mixed_ref[...], spread_ref[...], preferred_element_type=F32).astype(BF16)
    made = dot_tn(wide, attended_ref[...].astype(BF16))
    out_ref[...] = jnp.concatenate([last_rows(made, g) for g in range(3)], axis=1).astype(BF16)


def out_rows(spread, mixed, attended):
    return pl.pallas_call(
        out_rows_kernel,
        out_shape=jax.ShapeDtypeStruct((spread.shape[1], 3 * attended.shape[1]), BF16),
        in_specs=vmem_specs(3),
        out_specs=vmem_specs(1)[0],
        compiler_params=pltpu.CompilerParams(vmem_limit_bytes=VMEM_LIMIT),
        name="out_rows",
    )(spread, mixed, attended)


def vector_rows_kernel(
    cot_ref, two_ref, resid_two_ref, first_ref, one_ref, resid_one_ref, up_ref, spread_ref, bias_ref,
    parts_ref, out_ref,
):
    cot, first = cot_ref[...].astype(F32), first_ref[...]
    columns = (
        first * one_ref[...],
        cot * two_ref[...],
        resid_one_ref[...],
        first,
        resid_two_ref[...],
        cot,
    )
    rows = jnp.concatenate([jnp.sum(c, axis=0, keepdims=True) for c in columns], axis=0)
    bias = jnp.sum(up_ref[...].astype(F32), axis=0, keepdims=True) * parts_ref[...]
    made = [
        jnp.dot(rows.astype(BF16), spread_ref[...], preferred_element_type=F32),
        jnp.dot(bias.astype(BF16), bias_ref[...], preferred_element_type=F32),
    ]
    out_ref[...] = jnp.concatenate(made, axis=0)


def vector_rows(spread, *args):
    return pl.pallas_call(
        vector_rows_kernel,
        out_shape=jax.ShapeDtypeStruct((8, spread.shape[1]), F32),
        in_specs=vmem_specs(10),
        out_specs=vmem_specs(1)[0],
        compiler_params=pltpu.CompilerParams(vmem_limit_bytes=VMEM_LIMIT),
        name="vector_rows",
    )(*args)


def late_grads_kernel(
    hid_ref, dkv_ref, dq_ref, rows_ref, q_place_ref, v_place_ref, placed_ref, w_ref, spread_ref,
    out_ref, back_ref, held, sem,
):
    wide = hid_ref.shape[1]
    grads = jnp.concatenate([dkv_ref[...], dq_ref[...]], axis=1)
    cols = grads.shape[1]
    made = dot_tn(hid_ref[...], grads) + placed_ref[...].astype(F32)
    sums = [rows_ref[...]]
    for grad, place in ((dq_ref, q_place_ref), (dkv_ref, v_place_ref)):
        row = jnp.sum(grad[...].astype(F32), axis=0, keepdims=True).astype(BF16)
        sums.append(jnp.dot(row, place[...], preferred_element_type=F32))
    sums.append(jnp.zeros((128 - 10, wide), F32))
    small = jnp.transpose(jnp.concatenate(sums, axis=0))[:, :64]
    held[...] = jnp.concatenate([made, small], axis=1).astype(BF16)
    copy = pltpu.make_async_copy(held, out_ref, sem)
    copy.start()
    back = dot_nt(grads, w_ref[:, :cols]).astype(BF16)
    back_ref[...] = dot_nt(back, spread_ref[...]).astype(BF16)
    copy.wait()


def late_grads(hid, dkv, dq, rows, q_place, v_place, placed, w, spread):
    shape = (hid.shape[1], dkv.shape[1] + dq.shape[1] + 64)
    return pl.pallas_call(
        late_grads_kernel,
        out_shape=(
            jax.ShapeDtypeStruct(shape, BF16),
            jax.ShapeDtypeStruct((hid.shape[0], spread.shape[0]), BF16),
        ),
        in_specs=vmem_specs(9),
        out_specs=(pl.BlockSpec(memory_space=pltpu.HBM), vmem_specs(1)[0]),
        scratch_shapes=[pltpu.VMEM(shape, BF16), pltpu.SemaphoreType.DMA],
        compiler_params=pltpu.CompilerParams(vmem_limit_bytes=VMEM_LIMIT),
        name="late_grads",
    )(hid, dkv, dq, rows, q_place, v_place, placed, w, spread)


def project_kernel(hid_ref, w_ref, bias_ref, scale_ref, kv_ref, wide_ref, q_ref):
    made = jnp.dot(hid_ref[...], w_ref[...], preferred_element_type=F32) + bias_ref[...]
    made = (made.astype(BF16).astype(F32) * scale_ref[...]).astype(BF16)
    kv_cols = kv_ref.shape[1]
    kv_ref[...] = made[:, :kv_cols]
    wide_ref[...] = made[:, kv_cols:]
    zeros = jnp.zeros((made.shape[0], HEAD_DIM), BF16)
    for h in range(HEADS_DEV):
        at = kv_cols + h * HEAD_DIM
        q_ref[h] = jnp.concatenate([made[:, at : at + HEAD_DIM], zeros], axis=1)


def project(hid, w, bias, scale):
    rows = hid.shape[0]
    return pl.pallas_call(
        project_kernel,
        out_shape=(
            jax.ShapeDtypeStruct((rows, HEADS_DEV * 128), BF16),
            jax.ShapeDtypeStruct((rows, w.shape[1] - HEADS_DEV * 128), BF16),
            jax.ShapeDtypeStruct((HEADS_DEV, rows, 128), BF16),
        ),
        in_specs=vmem_specs(4),
        out_specs=tuple(vmem_specs(3)),
        compiler_params=pltpu.CompilerParams(vmem_limit_bytes=VMEM_LIMIT),
        name="project",
    )(hid, w, bias, scale)


def queries_in(order_ref, q_ref, q_buffer, q_sems):
    for i in range(64):
        source = q_ref.at[order_ref[i]]
        pltpu.make_async_copy(source, q_buffer.at[i], q_sems.at[i // 8]).start()


def key_back_blocks(k_ref, v_ref, k_acc, v_acc, q_buffer, g_buffer, q_sems, g_sems):
    def step(j, carry):
        eight = q_buffer.at[pl.ds(8 * j, 8)]
        pltpu.make_async_copy(eight, eight, q_sems.at[j]).wait()
        queries = q_buffer[pl.ds(8 * j, 8)].reshape(-1, q_buffer.shape[2])
        grads = block_of(g_buffer, g_sems, j)
        lane = lax.broadcasted_iota(jnp.int32, queries.shape, 1)
        queries = jnp.where(lane < HEADS_DEV * HEAD_DIM, queries, grads)
        for h in range(HEADS_DEV):
            scores = lax.dot_general(k_ref[h], queries, NT, preferred_element_type=F32)
            probs = jnp.exp(scores)
            v_acc[h] = v_acc[h] + jnp.dot(probs.astype(BF16), grads, preferred_element_type=F32)
            back = probs * lax.dot_general(v_ref[h], grads, NT, preferred_element_type=F32)
            k_acc[h] = k_acc[h] + jnp.dot(back.astype(BF16), queries, preferred_element_type=F32)
        return carry

    lax.fori_loop(0, q_sems.shape[0], step, 0)


def key_heads(kv_ref, tag_ref, k_heads, v_heads):
    rows = kv_ref.shape[0]
    feat = HEADS_DEV * HEAD_DIM
    lane = lax.broadcasted_iota(jnp.int32, (rows, HEAD_DIM), 1)
    tag = tag_ref[...]
    masks = jnp.where((lane == 21) & (tag < 0), NEG, 0.0)
    for s in range(3):
        masks = masks + jnp.where((lane == 18 + s) & (tag == s), NEG, 0.0)
    for h in range(HEADS_DEV):
        block = kv_ref[:, head_block(h)].astype(F32)
        before = [jnp.zeros((rows, h * HEAD_DIM), F32)] if h else []
        left = feat - (h + 1) * HEAD_DIM
        after = [jnp.zeros((rows, left), F32)] if left else []
        k_extra = masks - jnp.where((lane >= 9 + 3 * h) & (lane < 12 + 3 * h), 1.0, 0.0)
        v_extra = -jnp.where((lane >= 3 * h) & (lane < 3 * h + 3), 1.0, 0.0)
        for heads, part, extra in (
            (k_heads, block[:, :HEAD_DIM], k_extra),
            (v_heads, block[:, HEAD_DIM:], v_extra),
        ):
            heads[h] = jnp.concatenate(before + [part] + after + [extra], axis=1).astype(BF16)


def key_back_kernel(order_ref, kv_ref, tag_ref, diag_ref, q_ref, *rest):
    g_blocks = rest[:8]
    dkv_ref, k_heads, v_heads, k_acc, v_acc, q_buffer, q_sems, g_buffer, g_sems = rest[8:]
    queries_in(order_ref, q_ref, q_buffer, q_sems)
    copies_in(g_blocks, g_buffer, g_sems)
    key_heads(kv_ref, tag_ref, k_heads, v_heads)
    k_acc[...] = jnp.zeros_like(k_acc)
    v_acc[...] = jnp.zeros_like(v_acc)
    key_back_blocks(k_heads, v_heads, k_acc, v_acc, q_buffer, g_buffer, q_sems, g_sems)
    parts = []
    for h in range(HEADS_DEV):
        parts += [k_acc[h][:, head_columns(h)], v_acc[h][:, head_columns(h)]]
    dkv_ref[...] = (jnp.concatenate(parts, axis=1) + diag_ref[...]).astype(BF16)


def query_buffers(q_all):
    return [pltpu.VMEM(q_all.shape, BF16), pltpu.SemaphoreType.DMA((8,))]


def smem_spec():
    return [pl.BlockSpec(memory_space=pltpu.SMEM)]


def key_back(order, kv_own, tag, diagonal, q_all, g_blocks):
    rows, width = kv_own.shape[0], g_blocks[0].shape[2]
    return pl.pallas_call(
        key_back_kernel,
        out_shape=jax.ShapeDtypeStruct(diagonal.shape, BF16),
        in_specs=smem_spec() + vmem_specs(3) + [pl.BlockSpec(memory_space=pltpu.HBM)] * 9,
        out_specs=vmem_specs(1)[0],
        scratch_shapes=[pltpu.VMEM((HEADS_DEV, rows, width), BF16)] * 2
        + [pltpu.VMEM((HEADS_DEV, rows, width), F32)] * 2
        + query_buffers(q_all)
        + buffers(g_blocks, width),
        compiler_params=pltpu.CompilerParams(vmem_limit_bytes=VMEM_LIMIT),
        cost_estimate=cost(rows, g_blocks, 2048),
        name="key_back",
    )(order, kv_own, tag, diagonal, q_all, *g_blocks)


def dot(a, b):
    return jnp.dot(a, b, preferred_element_type=F32)


def dot_nt(a, b):
    return lax.dot_general(a, b, NT, preferred_element_type=F32)


def dot_tn(a, b):
    return lax.dot_general(a, b, (((0,), (0,)), ((), ())), preferred_element_type=F32)


def core_half(x, axis, at):
    size = x.shape[axis] // 2
    return lax.dynamic_slice_in_dim(x, at * size, size, axis)


def interleaved(k, v):
    shape = (*k.shape[:-1], -1, HEAD_DIM)
    return jnp.stack([k.reshape(shape), v.reshape(shape)], axis=-2).reshape(*k.shape[:-1], -1)


def per_device(
    hidden,
    w_qkv,
    w_out,
    b_qv,
    w_up,
    w_down,
    b_up,
    norm_gains,
    norm_shifts,
    segments,
    lengths,
    cotangent,
):
    core = lax.axis_index("core")
    heads_at = lax.axis_index("heads")
    own_ctx = ((lax.axis_index("z") * 4 + lax.axis_index("y")) * 2 + lax.axis_index("xh")) * 2 + core
    tok = hidden.shape[0]
    rows = w_up.shape[0]
    feat = HEADS_DEV * HEAD_DIM
    hidden_units = w_up.shape[1] // 2

    hid = chip_tokens(hidden)
    out_turned, down_turned = w_out.T, w_down.T
    low_tok = segments.astype(BF16).reshape(2, tok // 2)
    kv_cols = 2 * feat

    def halves(x):
        return jnp.swapaxes(x.reshape(rows, 2, -1), 0, 1)

    q_half, k_half, v_half = (halves(w_qkv[i]) for i in range(3))
    tail = jnp.broadcast_to(jnp.pad(low_tok, ((0, rows - 2), (0, 0))), (2, rows, tok // 2))
    urgent = jnp.concatenate([interleaved(k_half, v_half), q_half, tail], axis=2)
    urgent = jnp.pad(urgent, ((0, 0), (0, 16 - rows), (0, 0)))
    urgent = jnp.broadcast_to(urgent[None], (32, *urgent.shape)).reshape(64, 16, -1)
    urgent, *later = lax.optimization_barrier((urgent, out_turned, w_up, down_turned))
    later = jnp.concatenate([halves(w) for w in later], axis=2)
    mine = lax.dynamic_index_in_dim(later, core, 0, keepdims=False)
    theirs = shifted(lax.dynamic_index_in_dim(later, 1 - core, 0, keepdims=False), "core", 1)
    later = pair_ordered(mine, theirs, "core").reshape(2 * rows, -1)
    rest = lax.all_gather(later, CHIPS, axis=0, tiled=True)
    w_urgent = lax.all_to_all(urgent, CTX, 0, 0, tiled=True)
    seg_all = w_urgent[:, :2, kv_cols + feat :].reshape(-1, tok).astype(jnp.int32)
    w_urgent = w_urgent.reshape(64 * 16, -1)
    at_wide = jnp.arange(64 * 16, dtype=jnp.int32)
    at_feature = jnp.arange(64 * rows, dtype=jnp.int32)
    spread = (
        (at_feature // rows * 16 + at_feature % rows)[:, None] == at_wide[None, :]
    ).astype(BF16)
    hid_wide = dot(hid, spread).astype(BF16)
    at_bias = jnp.arange(hidden_units, dtype=jnp.int32)
    at_half = jnp.arange(feat, dtype=jnp.int32)
    at_kv = jnp.arange(kv_cols, dtype=jnp.int32)

    def placed(owner, row):
        return ((owner * 16 + row)[:, None] == at_wide[None, :]).astype(BF16)

    first_owner = 32 * core
    bias_place = placed(first_owner + at_bias // 24, at_bias % 12)
    q_place = placed(first_owner + at_half // 6, at_half % 6)
    at_value = at_kv // 128 * HEAD_DIM + at_kv % 128 - HEAD_DIM
    is_value = at_kv % 128 >= HEAD_DIM
    v_place = placed(jnp.where(is_value, first_owner + at_value // 6, -1), at_value % 6)
    parts = jnp.arange(2, dtype=jnp.int32)[:, None] == (at_bias % 24 // 12)[None, :]
    hid_wide, q_place, v_place, bias_place = lax.optimization_barrier(
        (hid_wide, q_place, v_place, bias_place)
    )

    w_out_t = rest[:, :feat]
    w_up_all = rest[:, feat : feat + hidden_units]
    w_down_t = rest[:, feat + hidden_units :]

    bias = b_qv.astype(F32)
    q_bias, v_bias = core_half(bias[0], 0, core), core_half(bias[1], 0, core)
    no_bias = jnp.zeros((tok // 2,), F32)
    bias_row = jnp.concatenate([interleaved(jnp.zeros_like(v_bias), v_bias), q_bias, no_bias])
    column = jnp.arange(bias_row.shape[0], dtype=jnp.int32)
    scale_row = jnp.where(
        column < kv_cols, 1.0, jnp.where(column < kv_cols + feat, HEAD_DIM ** (-0.5), 0.0)
    ).astype(F32)
    kv_own, q_wide, q_heads = project(hid_wide, w_urgent, bias_row[None], scale_row[None])
    q_all = lax.all_gather(q_wide, CHIPS, axis=0, tiled=True).reshape(64, tok, -1)
    starts = [jnp.sum((seg_all < s).astype(jnp.int32)) for s in range(3)]
    places = jnp.arange(seg_all.size, dtype=jnp.int32).reshape(seg_all.shape)
    run_end = jnp.zeros_like(seg_all)
    for s in range(3):
        run_end = jnp.where(seg_all == s, starts[s] + lengths[s], run_end)
    tag_all = jnp.where(places < run_end, seg_all, -1).astype(F32)
    order = jnp.concatenate([relative_order("z", "y", 0), relative_order("y", "z", 1)])
    q_order = jnp.where(core == 0, order, order + 1 - 2 * (order % 2))
    tags = jnp.take(tag_all, order, axis=0).reshape(8, -1)
    both = jnp.stack([own_ctx, own_ctx + 1 - 2 * core])
    tag_own = jnp.take(tag_all, both, axis=0).reshape(-1, 1)
    seg_own = jnp.take(seg_all, both, axis=0).astype(F32).reshape(-1, 1)

    sent_z, sent_y = lax.optimization_barrier(gather_first(kv_own))
    blocks = gather_second(sent_z, sent_y)
    near, far = near_blocks(blocks), far_blocks(blocks)
    state = attend_near(q_heads, kv_own, tags, seg_own, tag_own, near)
    attended, stat = attend_far(q_heads, tags, seg_own, state, far)
    attended_low = attended.astype(BF16)

    gain_rows = norm_gains.astype(F32)
    shifts = norm_shifts.astype(F32)
    attn_mixed, _ = team_sum(dot_nt(attended_low, w_out_t))
    first_out, normed_one, inverse_one = layer_norm(
        hidden.astype(F32) + attn_mixed + shifts[0], gain_rows[0], shifts[1]
    )
    first_low = chip_tokens(first_out.astype(BF16))
    up_bias = core_half(b_up, 0, core).astype(F32)
    up_proj = dot(first_low, w_up_all) + up_bias
    activated = exact_gelu(up_proj).astype(BF16)
    second, _ = team_sum(dot_nt(activated, w_down_t))
    output, normed_two, inverse_two = layer_norm(
        first_out + second + shifts[2], gain_rows[1], shifts[3]
    )
    resid_two = norm_back(
        cotangent.astype(F32), normed_two, inverse_two, gain_rows[1]
    )
    branch_low = chip_tokens(resid_two.astype(BF16))
    act_grad = dot(branch_low, w_down_t)
    up_low = jax.vjp(exact_gelu, up_proj)[1](act_grad)[0].astype(BF16)
    made = early_grads(spread, branch_low, activated, first_low, up_low)
    first_sum, made = team_sum(dot_nt(up_low, w_up_all), made)
    first_grad = resid_two + first_sum
    resid_one = norm_back(first_grad, normed_one, inverse_one, gain_rows[0])
    mixed_low = chip_tokens(resid_one.astype(BF16))
    g_sent, g_heads, delta = grad_rows(mixed_low, w_out_t, attended, stat, seg_own)
    (g_z, g_y), g_heads = lax.optimization_barrier((gather_first(g_sent), g_heads))
    g_near = ring_near(g_z, "y") + ring_near(g_y, "z")
    z_far = paired(shifted(g_z, "y", 2))
    dq, diagonal = query_back(
        q_heads, g_heads, kv_own, tags, seg_own, tag_own, stat, delta, near + far
    )
    g_near, g_y, dq, spread = lax.optimization_barrier((g_near, g_y, dq, spread))
    g_far = [z_far, paired(shifted(g_y, "z", 2))]
    g_near, g_far, made = lax.optimization_barrier((g_near, g_far, made))
    g_blocks = [*g_near[:3], g_far[0], *g_near[3:], g_far[1]]
    early = to_owners(made)
    out_placed = out_rows(spread, mixed_low, attended_low)
    rows_made = vector_rows(
        spread,
        cotangent,
        normed_two,
        resid_two,
        first_grad,
        normed_one,
        resid_one,
        up_low,
        spread,
        bias_place,
        parts.astype(F32),
    )

    dkv = key_back(q_order, kv_own, tag_own, diagonal, q_all, g_blocks)
    dkv, early = lax.optimization_barrier((dkv, early))
    late, back = late_grads(
        hid_wide, dkv, dq, rows_made, q_place, v_place, out_placed, w_urgent, spread
    )
    late, early = lax.optimization_barrier((late, early))
    late = to_owners(late)
    hidden_grad = resid_one + team_sum(back.astype(F32))[0]

    early_sums, late_sums = owner_sums(early), owner_sums(late)

    def columns(x, start, size):
        return jnp.concatenate([x[c, :rows, start : start + size] for c in range(2)], axis=1)

    kv_pairs = columns(late_sums, 0, kv_cols).reshape(rows, 2 * HEADS_DEV, 2, HEAD_DIM)
    k_cols = kv_pairs[:, :, 0].reshape(rows, -1)
    v_cols = kv_pairs[:, :, 1].reshape(rows, -1)
    q_cols = columns(late_sums, kv_cols, feat)

    def last(x, size):
        return jnp.concatenate(
            [x[:, rows:, g * size : (g + 1) * size] for g in range(3)], axis=1
        )

    quarter = hidden_units // 2
    up_cols = columns(early_sums, 0, hidden_units)
    down_first, down_last = early_sums[:, :rows, hidden_units:], last(early_sums, quarter)
    down_cols = jnp.concatenate(
        [down_first[0], down_last[0], down_first[1], down_last[1]], axis=1
    )
    out_last = last(late_sums, feat)
    out_cols = jnp.concatenate([out_last[0], out_last[1]], axis=1)
    small = (late_sums[0] + late_sums[1])[:rows, kv_cols + feat :].T
    vec_out = small[:6].reshape(6, 2, 6)
    bias_out = small[6:8].reshape(-1)
    qv_out = small[8:10, :6]
    vec_out = lax.dynamic_index_in_dim(vec_out, heads_at, 1, keepdims=False)
    return (
        output.astype(BF16),
        hidden_grad,
        jnp.stack([q_cols, k_cols, v_cols]),
        out_cols.T,
        qv_out,
        up_cols,
        down_cols.T,
        bias_out,
        vec_out[:2],
        vec_out[2:],
    )


def solution(mesh):
    fine = Mesh(mesh.devices.reshape(4, 4, 2, 2, 2), ("z", "y", "xh", "core", "heads"))
    return jax.shard_map(
        per_device,
        mesh=fine,
        in_specs=(
            P(CTX, None),
            P(None, CTX, "heads"),
            P("heads", CTX),
            P(None, "heads"),
            P(CTX, "heads"),
            P("heads", CTX),
            P("heads"),
            P(),
            P(),
            P(CTX),
            P(),
            P(CTX, None),
        ),
        out_specs=(
            P(CTX, None),
            P(CTX, None),
            P(None, CTX, "heads"),
            P("heads", CTX),
            P(None, ("heads", *CTX)),
            P(CTX, "heads"),
            P("heads", CTX),
            P(("heads", *CTX)),
            P(None, (*CTX, "heads")),
            P(None, (*CTX, "heads")),
        ),
        check_vma=False,
    )
```
